32 devices in a mesh: dp: 4 (over y, core), seq: 8 (over z, x).
Axes of the slice: x: 2, y: 2, z: 4, core: 2. Of those that a mesh axis runs over, the one named last changes fastest.
Arguments:
- tokens: bfloat16 [2, 8, 1024, 768], P(None, 'dp', 'seq'), may hold values from -6 to 6
- cotangent: bfloat16 [2, 8, 1024, 768], P(None, 'dp', 'seq'), may hold values from -6 to 6
- stretch_size: int32 [2, 8], P(None, 'dp'), may hold values from 128 to 1024, as said below
- w_value: bfloat16 [768, 1536], P(('dp', 'seq')), may hold values from -0.21875 to 0.21875
- w_base: bfloat16 [768, 3200], P(('dp', 'seq')), may hold values from -0.21875 to 0.21875
- w_out: bfloat16 [1536, 768], P(('dp', 'seq')), may hold values from -1.25 to 1.25
- w_up: bfloat16 [768, 1536], P(('dp', 'seq')), may hold values from -0.21875 to 0.21875
- w_down: bfloat16 [1536, 768], P(('dp', 'seq')), may hold values from -0.15625 to 0.15625
- ema_delta: bfloat16 [768, 16], P(('dp', 'seq')), may hold values from -8 to 0.1
- ema_alpha: bfloat16 [768, 16], P(('dp', 'seq')), may hold values from -9 to -1
- ema_beta: bfloat16 [768, 16], P(('dp', 'seq')), may hold values from -4 to 4
- ema_gamma: bfloat16 [768, 16], P(('dp', 'seq')), may hold values from -4 to 4
- ema_omega: bfloat16 [768], P(('dp', 'seq')), may hold values from -4 to 4
- first_gain: bfloat16 [768], P(('dp', 'seq')), may hold values from 0.5 to 1.5
- second_gain: bfloat16 [768], P(('dp', 'seq')), may hold values from 0.5 to 1.5
- query_gain: float32 [128], replicated, may hold values from -8 to 8
- query_bias: float32 [128], replicated, may hold values from -4 to 4
- key_gain: float32 [128], replicated, may hold values from -8 to 8
- relative_bias: float32 [32], replicated, may hold values from -4 to 4
Outputs:
- block_out: bfloat16 [2, 8, 1024, 768], P(None, 'dp', 'seq')
- grad_tokens: float32 [2, 8, 1024, 768], P(None, 'dp', 'seq')
- grad_w_value: float32 [768, 1536], P(('dp', 'seq'))
- grad_w_base: float32 [768, 3200], P(('dp', 'seq'))
- grad_w_out: float32 [1536, 768], P(('dp', 'seq'))
- grad_w_up: float32 [768, 1536], P(('dp', 'seq'))
- grad_w_down: float32 [1536, 768], P(('dp', 'seq'))
- grad_ema_delta: float32 [768, 16], P(('dp', 'seq'))
- grad_ema_alpha: float32 [768, 16], P(('dp', 'seq'))
- grad_ema_beta: float32 [768, 16], P(('dp', 'seq'))
- grad_ema_gamma: float32 [768, 16], P(('dp', 'seq'))
- grad_ema_omega: float32 [768], P(('dp', 'seq'))
- grad_first_gain: float32 [768], P(('dp', 'seq'))
- grad_second_gain: float32 [768], P(('dp', 'seq'))
- grad_query_gain: float32 [128], replicated
- grad_query_bias: float32 [128], replicated
- grad_key_gain: float32 [128], replicated
- grad_relative_bias: float32 [32], replicated
The draws below stay inside these ranges and needn't reach their ends.
Inputs may be any that keep to these rules, and one draw needn't show every extreme that they name: `stretch_size`: in each micro-batch, exactly one of the 2 sequences of each index of dp has the value 1024; the others have 128.
All inputs are finite; a program needn't handle non-finite values.
Results may differ from the reference program's by a relative error of at most 0.033.
The reference program's roundings to bfloat16 on the way count: a program that leaves them out, or rounds other values in their place, can miss the bound.
Values may be sent and summed in bfloat16 or wider, within the bound.
A program may use at most 384 MiB of HBM per device.

```python
import math
import jax
import jax.numpy as jnp
import numpy as np
from jax import lax

D = 768
Z = 128
V = 1536
H = 16
FF = 1536
NB = 32
STRETCH = 128
EMA_BLOCK = 64
SEQ_DP = 2
MICRO = 2
LENGTH = 1024
SEQS = 8


def draw_stretch_size(key, part):
    groups = SEQS // SEQ_DP
    chosen = jax.random.randint(key, (MICRO, groups), 0, SEQ_DP)
    columns = jnp.arange(SEQ_DP, dtype=jnp.int32)
    full_slot = chosen[:, :, None] == columns[None, None, :]
    return jnp.where(full_slot, LENGTH, STRETCH).reshape(MICRO, SEQS).astype(jnp.int32)


def rate_parts(key):
    rate_key = jax.random.fold_in(key, 17)
    ratio_key = jax.random.fold_in(key, 29)
    low_end = math.log(0.02 / LENGTH)
    high_end = math.log(0.05)
    rate_values = jnp.exp(jax.random.uniform(rate_key, (D, H), jnp.float32, low_end, high_end))
    ratio_values = jnp.exp(jax.random.uniform(ratio_key, (D, H), jnp.float32, math.log(0.5), math.log(2.0)))
    leak_rate = jnp.sqrt(2.0 * rate_values * ratio_values)
    keep_rate = jnp.sqrt(rate_values / (2.0 * ratio_values))
    return (leak_rate, keep_rate)


def draw_ema_delta(key, part):
    leak_rate, keep_rate = rate_parts(key)
    return jnp.log(leak_rate / (1.0 - leak_rate)).astype(jnp.bfloat16)


def draw_ema_alpha(key, part):
    leak_rate, keep_rate = rate_parts(key)
    return jnp.log(keep_rate / (1.0 - keep_rate)).astype(jnp.bfloat16)


def block_levels(own_key, shape, cuts, low, top_value):
    factor_of = 1.0
    for position, parts in cuts:
        draws = jax.random.uniform(jax.random.fold_in(jax.random.fold_in(own_key, 6), position), (parts,), jnp.float32, low / len(cuts), top_value / len(cuts))
        factor_of = factor_of * jnp.repeat(jnp.exp(draws), shape[position] // parts).reshape((-1,) + (1,) * (len(shape) - 1 - position))
    return factor_of


def centred(rng, extent, scale, reach, split=(), kind=jnp.bfloat16):
    values = jax.random.normal(rng, extent, jnp.float32) * scale
    if len(split) > 0:
        values = block_levels(rng, extent, split, -0.22, 0.18) * values
    return jnp.clip(values, min=-reach, max=reach).astype(kind)


def setup_inputs(seed: int = 0) -> dict:
    splits = jax.random.split(jax.random.key(seed), 20)
    return {
        "tokens": centred(splits[0], (MICRO, SEQS, LENGTH, D), 1.0, 6.0, ((1, 4), (2, 8))),
        "cotangent": centred(splits[1], (MICRO, SEQS, LENGTH, D), 1.0, 6.0, ((1, 4), (2, 8))),
        "stretch_size": draw_stretch_size(jax.random.fold_in(splits[19], 71), 0),
        "w_value": centred(splits[3], (D, V), D ** -0.5, 0.21875, ((0, 32),)),
        "w_base": centred(splits[4], (D, Z + V + 2 * D), D ** -0.5, 0.21875, ((0, 32),)),
        "w_out": centred(splits[5], (V, D), (V // 64) ** -0.5, 1.25, ((0, 32),)),
        "w_up": centred(splits[6], (D, FF), D ** -0.5, 0.21875, ((0, 32),)),
        "w_down": centred(splits[7], (FF, D), FF ** -0.5, 0.15625, ((0, 32),)),
        "ema_delta": draw_ema_delta(jax.random.fold_in(splits[19], 71), 0),
        "ema_alpha": draw_ema_alpha(jax.random.fold_in(splits[19], 71), 0),
        "ema_beta": centred(splits[10], (D, H), 1.0, 4.0, ((0, 32),)),
        "ema_gamma": centred(splits[11], (D, H), 1.0, 4.0, ((0, 32),)),
        "ema_omega": centred(splits[12], (D,), 1.0, 4.0, ((0, 32),)),
        "first_gain": jnp.clip(1.0 + 0.1 * jax.random.normal(splits[13], (D,), jnp.float32), 0.5, 1.5).astype(jnp.bfloat16),
        "second_gain": jnp.clip(1.0 + 0.1 * jax.random.normal(splits[14], (D,), jnp.float32), 0.5, 1.5).astype(jnp.bfloat16),
        "query_gain": centred(splits[15], (Z,), 2.0, 8.0, (), jnp.float32),
        "query_bias": centred(splits[16], (Z,), 1.0, 4.0, (), jnp.float32),
        "key_gain": centred(splits[17], (Z,), 2.0, 8.0, (), jnp.float32),
        "relative_bias": centred(splits[18], (NB,), 1.0, 4.0, (), jnp.float32),
    }


highest = lax.Precision.HIGHEST
epsilon = 1e-05
masked_fill = -1e+30

@jax.custom_vjp
def low(v):
    return lax.optimization_barrier(v.astype(jnp.bfloat16)).astype(jnp.float32)

@jax.custom_vjp
def low_back(v):
    return v

def low_keep(v):
    return (low(v), None)

def low_pass(kept, grad):
    return (grad,)

def back_keep(v):
    return (v, None)

def back_low(kept, grad):
    return (low(grad),)
low.defvjp(low_keep, low_pass)
low_back.defvjp(back_keep, back_low)

def bucket_edges(bucket_count):
    edge_list = [0]
    middle = bucket_count // 2
    for number in range(1, bucket_count):
        edge_list.append(number if number < middle else int(middle * 2 ** ((number - middle) / 2)))
    return np.array(edge_list, np.int32)

def ema_tables(params, ema_steps):
    delta_raw, alpha_raw, beta_raw, gamma_raw = (params[0], params[1], params[2], params[3])
    leak_rate = jax.nn.sigmoid(delta_raw)
    log_decay = jnp.log(1.0 - leak_rate * jax.nn.sigmoid(alpha_raw))
    drive_gain = leak_rate * beta_raw
    readout = gamma_raw * gamma_raw.shape[1] ** (-0.5)
    offsets = jnp.arange(ema_steps, dtype=jnp.float32)
    powers = jnp.exp((offsets + 1.0)[:, None, None] * log_decay) * readout
    inject = jnp.exp((ema_steps - 1.0 - offsets)[:, None, None] * log_decay) * drive_gain
    kernel = jnp.einsum('tdh,dh->td', jnp.exp(offsets[:, None, None] * log_decay), readout * drive_gain, precision=highest)
    lag_grid = offsets[:, None] - offsets[None, :]
    onehot = (lag_grid[:, :, None] == offsets[None, None, :]).astype(jnp.float32)
    toeplitz = jnp.einsum('rst,td->rsd', onehot, kernel, precision=highest)
    return (powers, inject, toeplitz, jnp.exp(ema_steps * log_decay))

def ema_step(tables, ema_state, block_input):
    powers, inject, toeplitz, block_decay = tables
    output = jnp.einsum('rsd,...sd->...rd', toeplitz, block_input, precision=highest)
    output = output + jnp.einsum('rdh,...dh->...rd', powers, ema_state, precision=highest)
    ema_state = block_decay * ema_state + jnp.einsum('rdh,...rd->...dh', inject, block_input, precision=highest)
    return (ema_state, output)

def ema_sequence(seq_rows, params, ema_steps):
    tables = ema_tables(params, ema_steps)
    row_total, model_width = seq_rows.shape
    blocks = seq_rows.reshape(row_total // ema_steps, ema_steps, model_width)

    def advance(ema_state, block_input):
        return ema_step(tables, ema_state, block_input)
    start_state = jnp.zeros(params[0].shape, jnp.float32)
    unused_end, outputs = lax.scan(jax.checkpoint(advance), start_state, blocks)
    return outputs.reshape(row_total, model_width) + params[4] * seq_rows

def normalize(seq_rows):
    centered = seq_rows - lax.optimization_barrier(jnp.mean(seq_rows, axis=-1, keepdims=True))
    return centered * lax.rsqrt(lax.optimization_barrier(jnp.mean(centered * centered, axis=-1, keepdims=True)) + epsilon)

def attention(queries, keys_low, values, relative_bias, stretch_width):
    length = queries.shape[0]
    block_rows = min(512, length)
    edge_values = jnp.asarray(bucket_edges(relative_bias.shape[0])[1:])
    key_pos = jnp.arange(length, dtype=jnp.int32)

    def one_block(query_start):
        query_rows = lax.dynamic_slice_in_dim(queries, query_start, block_rows, 0)
        query_pos = query_start + jnp.arange(block_rows, dtype=jnp.int32)
        lag_grid = query_pos[:, None] - key_pos[None, :]
        allowed = (lag_grid >= 0) & (query_pos[:, None] // stretch_width == key_pos[None, :] // stretch_width)
        buckets = jnp.searchsorted(edge_values, lag_grid, side='right').astype(jnp.int32)
        scores = low_back(jnp.dot(query_rows, keys_low.T, precision=highest) * queries.shape[1] ** (-0.5)) + relative_bias[buckets]
        weights = jax.nn.softmax(jnp.where(allowed, scores, masked_fill), axis=-1)
        return jnp.dot(low(weights), values, precision=highest)
    starts = jnp.arange(0, length, block_rows, dtype=jnp.int32)
    blocks = lax.map(jax.checkpoint(one_block), starts)
    return blocks.reshape(length, values.shape[1])

def mega_layer(seq_rows, params, stretch_width):
    mat_value, mat_base, mat_out, mat_up, mat_down, delta_raw, alpha_raw, beta_raw, gamma_raw, omega_raw, gain_first, gain_second, query_gain, query_bias, key_gain, relative_bias = params
    z_width = query_gain.shape[0]
    v_width = mat_value.shape[1]
    model_width = seq_rows.shape[1]
    value_pre = low_back(jnp.dot(seq_rows, mat_value, precision=highest))
    values = low(jax.nn.silu(value_pre))
    ema_out = ema_sequence(seq_rows, (delta_raw, alpha_raw, beta_raw, gamma_raw, omega_raw), EMA_BLOCK)
    mixed = low(jax.nn.silu(ema_out))
    base_out = low_back(jnp.dot(mixed, mat_base, precision=highest))
    z_pre = base_out[:, :z_width]
    reset_pre = base_out[:, z_width:z_width + v_width]
    cand_pre = base_out[:, z_width + v_width:z_width + v_width + model_width]
    update_pre = base_out[:, z_width + v_width + model_width:]
    shared = jax.nn.silu(z_pre)
    queries = low(shared * query_gain + query_bias)
    keys_low = low(shared * key_gain)
    attended = low_back(attention(queries, keys_low, values, relative_bias, stretch_width))
    gated = low(attended * jax.nn.silu(reset_pre))
    cand_in = low_back(cand_pre + jnp.dot(gated, mat_out, precision=highest))
    update = jax.nn.sigmoid(update_pre)
    first_sum = seq_rows + update * (jax.nn.silu(cand_in) - seq_rows)
    normed = normalize(first_sum) * gain_first
    hidden_pre = low_back(jnp.dot(low(normed), mat_up, precision=highest))
    branch = low_back(jnp.dot(low(jax.nn.silu(hidden_pre)), mat_down, precision=highest))
    return normalize(normed + branch) * gain_second

def reference(tokens, cotangent, stretch_size, w_value, w_base, w_out, w_up, w_down, ema_delta, ema_alpha, ema_beta, ema_gamma, ema_omega, first_gain, second_gain, query_gain, query_bias, key_gain, relative_bias):
    params = tuple((member.astype(jnp.float32) for member in (w_value, w_base, w_out, w_up, w_down, ema_delta, ema_alpha, ema_beta, ema_gamma, ema_omega, first_gain, second_gain, query_gain, query_bias, key_gain, relative_bias)))
    model_width = tokens.shape[3]
    sequences = tokens.reshape(-1, tokens.shape[2], model_width).astype(jnp.float32)
    cotangents = cotangent.reshape(sequences.shape).astype(jnp.float32)
    widths = stretch_size.reshape(-1).astype(jnp.int32)

    def one_item(totals, item_parts):
        seq_rows, seq_cot, stretch_width = item_parts

        def forward(rows_in, params_in):
            return mega_layer(rows_in, params_in, stretch_width)
        output, pullback = jax.vjp(forward, seq_rows, params)
        grad_rows, grad_params = pullback(seq_cot)
        return (jax.tree.map(jnp.add, totals, grad_params), (output, grad_rows))
    start_totals = jax.tree.map(jnp.zeros_like, params)
    totals, (outputs, grad_rows) = lax.scan(one_item, start_totals, (sequences, cotangents, widths))
    return (outputs.reshape(tokens.shape).astype(jnp.bfloat16), grad_rows.reshape(tokens.shape), totals[0], totals[1], totals[2], totals[3], totals[4], totals[5], totals[6], totals[7], totals[8], totals[9], totals[10], totals[11], totals[12], totals[13], totals[14], totals[15])
```

```python
import functools

import jax
import jax.numpy as jnp
import numpy as np
from jax import lax
from jax.experimental import pallas as pl
from jax.experimental.pallas import tpu as pltpu
from jax.sharding import PartitionSpec as P

epsilon = 1e-05
masked_fill = -1e30
MESH = pl.DeviceIdType.MESH
ANY = pl.BlockSpec(memory_space=pl.ANY)
VM = pl.BlockSpec(memory_space=pltpu.VMEM)
SM = pl.BlockSpec(memory_space=pltpu.SMEM)
F32 = jnp.float32
BF16 = jnp.bfloat16
SEG = 8
LANES = 128


def bucket_edges(bucket_count):
    edge_list = [0]
    middle = bucket_count // 2
    for number in range(1, bucket_count):
        edge_list.append(number if number < middle else int(middle * 2 ** ((number - middle) / 2)))
    return edge_list


class Layout:
    def __init__(self, dp, seq, micro, items):
        self.dp, self.S = dp, seq
        self.C = 2
        self.Y = dp // 2
        self.X = min(self.Y, seq)
        self.Z = seq // self.X
        self.items = items
        self.MS = micro * items
        self.Q = 2 * self.MS
        self.Cq = seq // self.Q
        self.G = 2 * self.Cq
        self.BL = seq // self.G

    def here(self):
        d, b = lax.axis_index("dp"), lax.axis_index("seq")
        return d // 2, d % 2, b // self.X, b % self.X, b


class Wire:
    def __init__(self, lay, send, recv):
        self.lay, self.send, self.recv, self.count = lay, send, recv, 0
        self.sent = []

    def to(self, y, c, z, x):
        return (y * 2 + c, z * self.lay.X + x)

    def start(self, src, dst, target):
        number = self.count
        self.count += 1
        copy = pltpu.make_async_remote_copy(
            src_ref=src,
            dst_ref=dst,
            send_sem=self.send.at[number],
            recv_sem=self.recv.at[number],
            device_id=target,
            device_id_type=MESH,
        )
        copy.start()
        self.sent.append(copy)
        return copy

    def finish(self):
        for copy in self.sent:
            copy.wait_send()


def greet(lay):
    y, c, z, x, b = lay.here()
    barrier = pltpu.get_barrier_semaphore()
    plane = 2 * lay.S

    def one(k, carry):
        other = (c * lay.S + b + k) % plane
        pl.semaphore_signal(
            barrier, inc=1, device_id=(y * 2 + other // lay.S, other % lay.S), device_id_type=MESH
        )
        return carry

    lax.fori_loop(1, plane, one, 0)
    for k in range(1, lay.Y):
        pl.semaphore_signal(
            barrier, inc=1, device_id=(((y + k) % lay.Y) * 2 + c, b), device_id_type=MESH
        )
    pl.semaphore_wait(barrier, plane - 1 + lay.Y - 1)


def half_columns(columns):
    return ((columns // LANES + 1) // 2) * LANES


def reshard_in(lay, sources, targets, send, recv, local):
    y, c, z, x, b = lay.here()
    g = b // lay.BL
    slot = b % lay.BL
    qm = b // lay.Cq
    gm = (b % lay.Cq) * 2 + c

    def begin():
        for n, (source, target) in enumerate(zip(sources, targets)):
            for ms in range(lay.MS):
                seq_to = (ms * 2 + c) * lay.Cq + g // 2
                mine = jnp.logical_and(seq_to == b, g % 2 == c)
                block = source.at[ms // lay.items, ms % lay.items]

                @pl.when(jnp.logical_not(mine))
                def _():
                    pltpu.make_async_remote_copy(
                        src_ref=block,
                        dst_ref=target.at[slot],
                        send_sem=send.at[n, ms],
                        recv_sem=recv.at[n, slot],
                        device_id=(y * 2 + g % 2, seq_to),
                        device_id_type=MESH,
                    ).start()

                @pl.when(mine)
                def _():
                    pltpu.make_async_copy(block, target.at[slot], local.at[n]).start()

    def wait(n):
        source, target = sources[n], targets[n]
        for ms in range(lay.MS):
            seq_to = (ms * 2 + c) * lay.Cq + g // 2
            mine = jnp.logical_and(seq_to == b, g % 2 == c)
            block = source.at[ms // lay.items, ms % lay.items]

            @pl.when(jnp.logical_not(mine))
            def _():
                pltpu.make_async_remote_copy(
                    src_ref=block,
                    dst_ref=target.at[slot],
                    send_sem=send.at[n, ms],
                    recv_sem=recv.at[n, slot],
                    device_id=(y * 2 + g % 2, seq_to),
                    device_id_type=MESH,
                ).wait_send()

            @pl.when(mine)
            def _():
                pltpu.make_async_copy(block, target.at[slot], local.at[n]).wait()

        for j in range(lay.BL):
            from_b = gm * lay.BL + j
            own = jnp.logical_and(from_b == b, qm % 2 == c)

            @pl.when(jnp.logical_not(own))
            def _():
                pltpu.make_async_remote_copy(
                    src_ref=source.at[0, 0],
                    dst_ref=target.at[j],
                    send_sem=send.at[n, 0],
                    recv_sem=recv.at[n, j],
                    device_id=(y * 2 + qm % 2, from_b),
                    device_id_type=MESH,
                ).wait_recv()

    return begin, wait


def reshard_out(lay, sources, targets, send, recv, local):
    y, c, z, x, b = lay.here()
    g = b // lay.BL
    qm = b // lay.Cq
    gm = (b % lay.Cq) * 2 + c
    ms_to = qm // 2
    m_to, s_to = ms_to // lay.items, ms_to % lay.items

    def copies(n, j):
        from_b = gm * lay.BL + j
        own = jnp.logical_and(from_b == b, qm % 2 == c)
        remote = pltpu.make_async_remote_copy(
            src_ref=sources[n].at[j],
            dst_ref=targets[n].at[m_to, s_to],
            send_sem=send.at[n, j],
            recv_sem=recv.at[n, ms_to],
            device_id=(y * 2 + qm % 2, from_b),
            device_id_type=MESH,
        )
        near = pltpu.make_async_copy(sources[n].at[j], targets[n].at[m_to, s_to], local.at[n])
        return own, remote, near

    def begin(n):
        for j in range(lay.BL):
            own, remote, near = copies(n, j)
            pl.when(jnp.logical_not(own))(remote.start)
            pl.when(own)(near.start)

    def wait(n):
        for j in range(lay.BL):
            own, remote, near = copies(n, j)
            pl.when(jnp.logical_not(own))(remote.wait_send)
            pl.when(own)(near.wait)
        for ms in range(lay.MS):
            seq_at = (ms * 2 + c) * lay.Cq + g // 2
            own = jnp.logical_and(seq_at == b, g % 2 == c)

            @pl.when(jnp.logical_not(own))
            def _():
                pltpu.make_async_remote_copy(
                    src_ref=sources[n].at[0],
                    dst_ref=targets[n].at[ms // lay.items, ms % lay.items],
                    send_sem=send.at[n, 0],
                    recv_sem=recv.at[n, ms],
                    device_id=(y * 2 + g % 2, seq_at),
                    device_id_type=MESH,
                ).wait_recv()

    return begin, wait


def gather_kernel(lay, count, refs):
    tok, cot = refs[0], refs[1]
    shards = refs[2 : 2 + count]
    tok_out, cot_out = refs[2 + count], refs[3 + count]
    fulls = refs[4 + count : 4 + 2 * count]
    send, recv, local, t_send, t_recv, t_local = refs[4 + 2 * count :]
    y, c, z, x, b = lay.here()
    X, Y, Z = lay.X, lay.Y, lay.Z
    greet(lay)
    wire = Wire(lay, send, recv)
    begin, wait = reshard_in(lay, (tok, cot), (tok_out, cot_out), t_send, t_recv, t_local)

    def own(n):
        copy = pltpu.make_async_copy(shards[n], fulls[n].at[y, c, z, x], local.at[n])
        copy.start()
        return copy

    owns = [own(n) for n in range(count)]
    arrived = [dict() for n in range(count)]

    def stage_z(n):
        arrived[n]["z"] = [
            wire.start(shards[n], fulls[n].at[y, c, z, x], wire.to(y, c, (z + k) % Z, x))
            for k in range(1, Z)
        ]

    def parts(n):
        columns = shards[n].shape[1]
        left = half_columns(columns)
        result = [(0, left)]
        if left < columns:
            result.append((left, columns - left))
        return result

    def to_core(n, block):
        arrived[n].setdefault("core", []).append(wire.start(block, block, wire.to(y, 1 - c, z, x)))

    def stage_one(n):
        owns[n].wait()
        for copy in arrived[n]["z"]:
            copy.wait_recv()
        full = fulls[n]
        for half, (at, width) in enumerate(parts(n)):
            block = full.at[y, c, :, x, :, pl.ds(at, width)]
            if half == 0:
                arrived[n]["x0"] = [
                    wire.start(block, block, wire.to(y, c, z, (x + k) % X)) for k in range(1, X)
                ]
            else:
                arrived[n]["y1"] = [
                    wire.start(block, block, wire.to((y + k) % Y, c, z, x)) for k in range(1, Y)
                ]
        to_core(n, full.at[y, c, :, x])

    def stage_two(n):
        full = fulls[n]
        for half, (at, width) in enumerate(parts(n)):
            cols = pl.ds(at, width)
            if half == 0:
                for copy in arrived[n]["x0"]:
                    copy.wait_recv()
                block = full.at[y, c, :, :, :, cols]
                arrived[n]["y0"] = [
                    wire.start(block, block, wire.to((y + k) % Y, c, z, x)) for k in range(1, Y)
                ]
                for k in range(1, X):
                    to_core(n, full.at[y, c, :, (x + X - k) % X, :, cols])
            else:
                for copy in arrived[n]["y1"]:
                    copy.wait_recv()
                block = full.at[:, c, :, x, :, cols]
                arrived[n]["x1"] = [
                    wire.start(block, block, wire.to(y, c, z, (x + k) % X)) for k in range(1, X)
                ]
                for k in range(1, Y):
                    to_core(n, full.at[(y + Y - k) % Y, c, :, x, :, cols])

    def stage_three(n):
        full = fulls[n]
        for half, (at, width) in enumerate(parts(n)):
            cols = pl.ds(at, width)
            if half == 0:
                for k, copy in enumerate(arrived[n]["y0"], 1):
                    copy.wait_recv()
                    to_core(n, full.at[(y + Y - k) % Y, c, :, :, :, cols])
            else:
                for k, copy in enumerate(arrived[n]["x1"], 1):
                    copy.wait_recv()
                    to_core(n, full.at[:, c, :, (x + X - k) % X, :, cols])

    stage_z(0)
    begin()
    for n in range(1, count):
        stage_z(n)
    for turn in range(count + 2):
        if turn < count:
            stage_one(turn)
        if 0 <= turn - 1 < count:
            stage_two(turn - 1)
        if 0 <= turn - 2:
            stage_three(turn - 2)
    for n in range(count):
        for copy in arrived[n]["core"]:
            copy.wait_recv()
    wait(0)
    wait(1)
    wire.finish()


def gather_all(lay, tokens, cotangent, shards):
    count = len(shards)
    micro, items, rows, width = tokens.shape
    per = (lay.Z - 1) + 2 * (lay.X - 1 + lay.Y - 1) + 1 + 2 * (lay.X - 1 + lay.Y - 1)
    blocks = jax.ShapeDtypeStruct((lay.BL, rows, width), BF16)
    outs = [blocks, blocks] + [
        jax.ShapeDtypeStruct((lay.Y, 2, lay.Z, lay.X) + shard.shape, shard.dtype)
        for shard in shards
    ]

    def body(*refs):
        gather_kernel(lay, count, refs)

    result = pl.pallas_call(
        body,
        out_shape=outs,
        in_specs=[ANY] * (2 + count),
        out_specs=[ANY] * (2 + count),
        scratch_shapes=[
            pltpu.SemaphoreType.DMA((count * per,)),
            pltpu.SemaphoreType.DMA((count * per,)),
            pltpu.SemaphoreType.DMA((count,)),
            pltpu.SemaphoreType.DMA((2, lay.MS)),
            pltpu.SemaphoreType.DMA((2, lay.BL)),
            pltpu.SemaphoreType.DMA((2,)),
        ],
        compiler_params=pltpu.CompilerParams(
            collective_id=0, has_side_effects=True, vmem_limit_bytes=16 * 2**20
        ),
        name="gather_all",
    )(tokens, cotangent, *shards)
    return result[0], result[1], result[2:]


def add_blocks(total, index, extra, extra_index, counts, width_at):
    size = int(np.prod(counts)) if counts else 1

    def one(i, carry):
        places = []
        for extent in reversed(counts):
            places.insert(0, i % extent)
            i = i // extent
        a, e = index(*places), extra_index(*places)
        summed = total[a].astype(F32) + extra[e].astype(F32)
        total[a] = summed.astype(total.dtype)
        return carry

    lax.fori_loop(0, size, one, 0)


def scatter_kernel(lay, count, out_count, refs):
    grads = refs[:count]
    small = refs[count]
    outs_in = refs[count + 1 : count + 1 + out_count]
    at = count + 1 + out_count
    results = refs[at : at + count]
    small_out = refs[at + count]
    outs_to = refs[at + count + 1 : at + count + 1 + out_count]
    at = at + count + 1 + out_count
    bufs = refs[at : at + 7 * count]
    at += 7 * count
    small_acc, small_recv = refs[at], refs[at + 1]
    send, recv, local, t_send, t_recv, t_local = refs[at + 2 :]
    y, c, z, x, b = lay.here()
    X, Y, Z = lay.X, lay.Y, lay.Z
    greet(lay)
    wire = Wire(lay, send, recv)
    begin, wait = reshard_out(lay, outs_in, outs_to, t_send, t_recv, t_local)
    arrived = [dict() for n in range(count)]

    def buf(n, name):
        return bufs[7 * n + ("acc", "core", "x0", "y1", "y0", "x1", "z").index(name)]

    def parts(n):
        columns = grads[n].shape[-1]
        left = half_columns(columns)
        result = [(0, left)]
        if left < columns:
            result.append((left, columns - left))
        return result

    def stage_core(n):
        arrived[n]["core"] = [
            wire.start(grads[n].at[:, 1 - c], buf(n, "core"), wire.to(y, 1 - c, z, x))
        ]
        copy = pltpu.make_async_copy(grads[n].at[:, c], buf(n, "acc"), local.at[n])
        copy.start()
        arrived[n]["own"] = copy

    def stage_one(n):
        arrived[n]["own"].wait()
        arrived[n]["core"][0].wait_recv()
        acc = buf(n, "acc")
        add_blocks(acc, lambda i, j, k: (i, j, k), buf(n, "core"), lambda i, j, k: (i, j, k), (Y, Z, X), None)
        for half, (at, width) in enumerate(parts(n)):
            cols = pl.ds(at, width)
            if half == 0:
                arrived[n]["x0"] = [
                    wire.start(
                        acc.at[:, :, (x + k) % X, :, cols],
                        buf(n, "x0").at[k - 1],
                        wire.to(y, c, z, (x + k) % X),
                    )
                    for k in range(1, X)
                ]
            else:
                arrived[n]["y1"] = [
                    wire.start(
                        acc.at[(y + k) % Y, :, :, :, cols],
                        buf(n, "y1").at[k - 1],
                        wire.to((y + k) % Y, c, z, x),
                    )
                    for k in range(1, Y)
                ]

    def stage_two(n):
        acc = buf(n, "acc")
        for half, (at, width) in enumerate(parts(n)):
            cols = slice(at, at + width)
            view = pl.ds(at, width)
            if half == 0:
                for k, copy in enumerate(arrived[n]["x0"]):
                    copy.wait_recv()
                    add_blocks(
                        acc,
                        lambda i, j: (i, j, x, slice(None), cols),
                        buf(n, "x0"),
                        lambda i, j: (k, i, j),
                        (Y, Z),
                        None,
                    )
                arrived[n]["y0"] = [
                    wire.start(
                        acc.at[(y + k) % Y, :, x, :, view],
                        buf(n, "y0").at[k - 1],
                        wire.to((y + k) % Y, c, z, x),
                    )
                    for k in range(1, Y)
                ]
            else:
                for k, copy in enumerate(arrived[n]["y1"]):
                    copy.wait_recv()
                    add_blocks(
                        acc,
                        lambda i, j: (y, i, j, slice(None), cols),
                        buf(n, "y1"),
                        lambda i, j: (k, i, j),
                        (Z, X),
                        None,
                    )
                arrived[n]["x1"] = [
                    wire.start(
                        acc.at[y, :, (x + k) % X, :, view],
                        buf(n, "x1").at[k - 1],
                        wire.to(y, c, z, (x + k) % X),
                    )
                    for k in range(1, X)
                ]

    def stage_three(n):
        acc = buf(n, "acc")
        for half, (at, width) in enumerate(parts(n)):
            cols = slice(at, at + width)
            name = "y0" if half == 0 else "x1"
            for k, copy in enumerate(arrived[n][name]):
                copy.wait_recv()
                add_blocks(
                    acc,
                    lambda i: (y, i, x, slice(None), cols),
                    buf(n, name),
                    lambda i: (k, i),
                    (Z,),
                    None,
                )
        arrived[n]["z"] = [
            wire.start(
                acc.at[y, (z + k) % Z, x], buf(n, "z").at[k - 1], wire.to(y, c, (z + k) % Z, x)
            )
            for k in range(1, Z)
        ]

    def stage_four(n):
        acc = buf(n, "acc")
        total = acc[y, z, x].astype(F32)
        for k, copy in enumerate(arrived[n]["z"]):
            copy.wait_recv()
            total = total + buf(n, "z")[k].astype(F32)
        results[n][...] = total

    small_at = [0]

    def small_stage(moves):
        copies = []
        for target in moves:
            slot = small_at[0]
            small_at[0] += 1
            copies.append((slot, wire.start(small_acc, small_recv.at[slot], target)))
        for slot, copy in copies:
            copy.wait_send()
            wire.sent = [other for other in wire.sent if other is not copy]
        for slot, copy in copies:
            copy.wait_recv()
            small_acc[...] += small_recv[slot]

    small_acc[...] = small[...]
    for n in range(count):
        stage_core(n)
    begin(0)
    small_stage([wire.to(y, 1 - c, z, x)])
    for turn in range(count + 3):
        if turn < count:
            stage_one(turn)
        if 0 <= turn - 1 < count:
            stage_two(turn - 1)
        if 0 <= turn - 2 < count:
            stage_three(turn - 2)
        if 0 <= turn - 3:
            stage_four(turn - 3)
        if turn == 0:
            small_stage([wire.to(y, c, z, (x + k) % X) for k in range(1, X)])
            small_stage([wire.to((y + k) % Y, c, z, x) for k in range(1, Y)])
            small_stage([wire.to(y, c, (z + k) % Z, x) for k in range(1, Z)])
            begin(1)
    small_out[...] = small_acc[...]
    wait(0)
    wait(1)
    wire.finish()


def scatter_all(lay, grads, small, blocks, rows, width):
    count = len(grads)
    X, Y, Z = lay.X, lay.Y, lay.Z
    out_count = len(blocks)
    micro = lay.MS // lay.items
    scratch = []
    outs = []
    for grad in grads:
        r, cols = grad.shape[-2:]
        left = half_columns(cols)
        right = cols - left if cols > left else LANES
        kind = grad.dtype
        scratch += [
            pltpu.VMEM((Y, Z, X, r, cols), kind),
            pltpu.VMEM((Y, Z, X, r, cols), kind),
            pltpu.VMEM((X - 1, Y, Z, r, left), kind),
            pltpu.VMEM((Y - 1, Z, X, r, right), kind),
            pltpu.VMEM((Y - 1, Z, r, left), kind),
            pltpu.VMEM((X - 1, Z, r, right), kind),
            pltpu.VMEM((Z - 1, r, cols), kind),
        ]
        outs.append(jax.ShapeDtypeStruct((r, cols), F32))
    hops = 1 + (X - 1) + (Y - 1) + (Z - 1)
    per = 1 + 2 * (X - 1 + Y - 1) + Z - 1
    outs.append(jax.ShapeDtypeStruct(small.shape, F32))
    outs += [jax.ShapeDtypeStruct((micro, lay.items, rows, width), b.dtype) for b in blocks]
    scratch += [pltpu.VMEM(small.shape, F32), pltpu.VMEM((hops,) + small.shape, F32)]
    scratch += [
        pltpu.SemaphoreType.DMA((count * per + hops,)),
        pltpu.SemaphoreType.DMA((count * per + hops,)),
        pltpu.SemaphoreType.DMA((count,)),
        pltpu.SemaphoreType.DMA((out_count, lay.BL)),
        pltpu.SemaphoreType.DMA((out_count, lay.MS)),
        pltpu.SemaphoreType.DMA((out_count,)),
    ]

    def body(*refs):
        scatter_kernel(lay, count, out_count, refs)

    result = pl.pallas_call(
        body,
        out_shape=outs,
        in_specs=[ANY] * count + [VM] + [ANY] * out_count,
        out_specs=[VM] * (count + 1) + [ANY] * out_count,
        scratch_shapes=scratch,
        compiler_params=pltpu.CompilerParams(
            collective_id=1, has_side_effects=True, vmem_limit_bytes=52 * 2**20
        ),
        name="scatter_all",
    )(*grads, small, *blocks)
    return result[:count], result[count], result[count + 1 :]


def row(ref, index, lanes):
    return jnp.broadcast_to(ref[pl.ds(index, 1), lanes], (SEG, LANES))


def lane_call(kernel, outs, args, name):
    def spec(a):
        lead = len(a.shape) - 1
        return pl.BlockSpec(a.shape[:-1] + (LANES,), lambda i: (0,) * lead + (i,))

    return pl.pallas_call(
        kernel,
        out_shape=outs,
        grid=(args[0].shape[-1] // LANES,),
        in_specs=[spec(a) for a in args],
        out_specs=jax.tree.map(spec, outs),
        compiler_params=pltpu.CompilerParams(vmem_limit_bytes=32 * 2**20),
        name=name,
    )(*args)


def shifted(value, by):
    where = lax.broadcasted_iota(jnp.int32, (SEG, LANES), 0)
    if by > 0:
        return jnp.where(where >= by, pltpu.roll(value, by, 0), 0.0)
    return jnp.where(where < SEG + by, pltpu.roll(value, SEG + by, 0), 0.0)


def ema_ends_kernel(H, x_ref, tab_ref, s_ref, r_ref):
    rows, width = x_ref.shape
    steps = rows // SEG

    def tile(lanes):
        decay = [row(tab_ref, h, lanes) for h in range(H)]

        def step(t, state):
            s, r = state
            xt = x_ref[pl.ds(t, SEG, stride=steps), lanes]
            r = tuple(decay[h] * r[h] + s[h] for h in range(H))
            s = tuple(decay[h] * s[h] + xt for h in range(H))
            return s, r

        zero = tuple(tab_ref[0:SEG, lanes] * 0.0 for h in range(H))
        s, r = lax.fori_loop(0, steps, step, (zero, zero))
        for h in range(H):
            log = row(tab_ref, H + h, lanes)
            sh, rh = s[h], r[h]
            for d in (1, 2, 4):
                span = d * steps
                sd, rd = shifted(sh, d), shifted(rh, d)
                power = jnp.exp(span * log)
                rh = rh + power * rd + (span * jnp.exp((span - 1) * log)) * sd
                sh = sh + power * sd
            s_ref[h, :, lanes] = sh
            r_ref[h, :, lanes] = rh

    tile(slice(None))


def ema_out_kernel(H, x_ref, tab_ref, omega_ref, s_ref, r_ref, inc_ref, ema_ref, mixed_ref, si_ref, ri_ref):
    rows, width = x_ref.shape
    steps = rows // SEG

    def tile(lanes):
        decay = [row(tab_ref, h, lanes) for h in range(H)]
        gain = [row(tab_ref, 2 * H + h, lanes) for h in range(H)]
        omega = row(omega_ref, 0, lanes)
        start = []
        span = (lax.broadcasted_iota(jnp.int32, (SEG, LANES), 0) * steps).astype(F32)
        for h in range(H):
            log = row(tab_ref, H + h, lanes)
            s_dev = jnp.broadcast_to(inc_ref[0, pl.ds(h, 1), lanes], (SEG, LANES))
            r_dev = jnp.broadcast_to(inc_ref[1, pl.ds(h, 1), lanes], (SEG, LANES))
            power = jnp.exp(span * log)
            s_in = shifted(s_ref[h, :, lanes], 1) + power * s_dev
            r_in = (
                shifted(r_ref[h, :, lanes], 1)
                + power * r_dev
                + (span * jnp.exp((span - 1.0) * log)) * s_dev
            )
            si_ref[h, :, lanes] = s_in
            ri_ref[h, :, lanes] = r_in
            start.append(s_in)

        def step(t, s):
            xt = x_ref[pl.ds(t, SEG, stride=steps), lanes]
            s = tuple(decay[h] * s[h] + xt for h in range(H))
            parts = [gain[h] * s[h] for h in range(H)]
            while len(parts) > 1:
                parts = [parts[i] + parts[i + 1] for i in range(0, len(parts), 2)]
            ema_ref[pl.ds(t, SEG, stride=steps), lanes] = parts[0] + omega * xt
            return s

        lax.fori_loop(0, steps, step, tuple(start))

    tile(slice(None))

    def finish(i, carry):
        at = pl.ds(pl.multiple_of(i * 64, 64), 64)
        value = ema_ref[at, :]
        mixed_ref[at, :] = (value * jax.nn.sigmoid(value)).astype(BF16)
        return carry

    lax.fori_loop(0, rows // 64, finish, 0)


def ema_back_ends_kernel(H, d_ref, tab_ref, l_ref):
    rows, width = d_ref.shape
    steps = rows // SEG

    def tile(lanes):
        decay = [row(tab_ref, h, lanes) for h in range(H)]

        def step(i, lam):
            dt = d_ref[pl.ds(steps - 1 - i, SEG, stride=steps), lanes]
            return tuple(decay[h] * lam[h] + dt for h in range(H))

        zero = tuple(tab_ref[0:SEG, lanes] * 0.0 for h in range(H))
        lam = lax.fori_loop(0, steps, step, zero)
        for h in range(H):
            log = row(tab_ref, H + h, lanes)
            lh = lam[h]
            for d in (1, 2, 4):
                lh = lh + jnp.exp(d * steps * log) * shifted(lh, -d)
            l_ref[h, :, lanes] = lh

    tile(slice(None))


def ema_sums_kernel(H, x_ref, d_ref, tab_ref, si_ref, ri_ref, out_ref):
    rows, width = x_ref.shape
    steps = rows // SEG
    group = H // 2

    def tile(lanes):
        for first in range(0, H, group):
            decay = [row(tab_ref, first + h, lanes) for h in range(group)]

            def step(t, state):
                s, r, c, q, o = state
                xt = x_ref[pl.ds(t, SEG, stride=steps), lanes]
                dt = d_ref[pl.ds(t, SEG, stride=steps), lanes]
                r = tuple(decay[h] * r[h] + s[h] for h in range(group))
                s = tuple(decay[h] * s[h] + xt for h in range(group))
                c = tuple(c[h] + dt * s[h] for h in range(group))
                q = tuple(q[h] + dt * r[h] for h in range(group))
                return s, r, c, q, o + dt * xt

            zero = tuple(tab_ref[0:SEG, lanes] * 0.0 for h in range(group))
            s = tuple(si_ref[first + h, :, lanes] for h in range(group))
            r = tuple(ri_ref[first + h, :, lanes] for h in range(group))
            s, r, c, q, o = lax.fori_loop(0, steps, step, (s, r, zero, zero, zero[0]))
            for h in range(group):
                out_ref[pl.ds(first + h, 1), lanes] = jnp.sum(c[h], axis=0, keepdims=True)
                out_ref[pl.ds(H + first + h, 1), lanes] = jnp.sum(q[h], axis=0, keepdims=True)
            out_ref[pl.ds(2 * H, 1), lanes] = jnp.sum(o, axis=0, keepdims=True)

    tile(slice(None))


def ema_back_kernel(H, d_ref, tab_ref, omega_ref, l_ref, inc_ref, dx_ref):
    rows, width = d_ref.shape
    steps = rows // SEG

    def tile(lanes):
        decay = [row(tab_ref, h, lanes) for h in range(H)]
        gain = [row(tab_ref, 2 * H + h, lanes) for h in range(H)]
        omega = row(omega_ref, 0, lanes)
        start = []
        span = ((SEG - 1 - lax.broadcasted_iota(jnp.int32, (SEG, LANES), 0)) * steps).astype(F32)
        for h in range(H):
            log = row(tab_ref, H + h, lanes)
            l_dev = jnp.broadcast_to(inc_ref[pl.ds(h, 1), lanes], (SEG, LANES))
            start.append(shifted(l_ref[h, :, lanes], -1) + jnp.exp(span * log) * l_dev)

        def step(i, lam):
            at = pl.ds(steps - 1 - i, SEG, stride=steps)
            dt = d_ref[at, lanes]
            lam = tuple(decay[h] * lam[h] + dt for h in range(H))
            parts = [gain[h] * lam[h] for h in range(H)]
            while len(parts) > 1:
                parts = [parts[i] + parts[i + 1] for i in range(0, len(parts), 2)]
            dx_ref[at, lanes] = parts[0] + omega * dt
            return lam

        lax.fori_loop(0, steps, step, tuple(start))

    tile(slice(None))


def call(kernel, outs, args, specs=None, scratch=(), vmem=58, name=None):
    return pl.pallas_call(
        kernel,
        out_shape=outs,
        in_specs=specs or [VM] * len(args),
        out_specs=jax.tree.map(lambda o: VM, outs),
        scratch_shapes=list(scratch),
        compiler_params=pltpu.CompilerParams(vmem_limit_bytes=vmem * 2**20),
        name=name,
    )(*args)


QB = 256


def bias_kernel(length, bucket_count, bias_ref, strip_ref):
    edges = bucket_edges(bucket_count)
    tiles = length // LANES + QB // LANES
    lag0 = lax.broadcasted_iota(jnp.int32, (QB, LANES), 0) - lax.broadcasted_iota(
        jnp.int32, (QB, LANES), 1
    )
    for t in range(strip_ref.shape[1] // LANES):
        base = length - t * LANES
        low, high = base - LANES + 1, base + QB - 1
        start = max([k for k in range(bucket_count) if edges[k] <= low], default=0)
        value = jnp.full((QB, LANES), bias_ref[start], F32)
        for k in range(start + 1, bucket_count):
            if edges[k] <= high:
                value = jnp.where(lag0 + base >= edges[k], bias_ref[k], value)
        strip_ref[:, t * LANES : (t + 1) * LANES] = value


def attend_kernel(lay, flag_ref, q_ref, strip_ref, *refs):
    G = lay.G
    keys, vals = refs[:G], refs[G : 2 * G]
    att_ref, probs_ref, scores = refs[2 * G :]
    rows, zw = q_ref.shape
    length = G * rows
    full = flag_ref[0] > 0
    g = flag_ref[1]
    r0 = lax.broadcasted_iota(jnp.int32, (QB, rows), 0)
    c0 = lax.broadcasted_iota(jnp.int32, (QB, rows), 1)

    def one(i, carry):
        at = pl.multiple_of(i * QB, QB)
        q = q_ref[pl.ds(at, QB), :]
        for k in range(G):
            owner = lax.rem(g - k + G, G)
            s = lax.dot_general(q, keys[k][...], (((1,), (1,)), ((), ())), preferred_element_type=F32)
            off = jnp.clip(length - rows * (g - owner) - at, 0, length)
            s = s * (zw ** (-0.5)) + strip_ref[:, pl.ds(pl.multiple_of(off, LANES), rows)]
            if k == 0:
                pos = r0 + at
                ok = (c0 <= pos) & (full | (pos // 128 == c0 // 128))
            else:
                ok = jnp.logical_and(full, k <= g)
            scores[:, k * rows : (k + 1) * rows] = jnp.where(ok, s, masked_fill)
        s = scores[...]
        p = jnp.exp(s - jnp.max(s, axis=1, keepdims=True))
        p = p * (1.0 / jnp.sum(p, axis=1, keepdims=True))
        total = jnp.zeros((QB, att_ref.shape[1]), F32)
        for k in range(G):
            part = p[:, k * rows : (k + 1) * rows]
            probs_ref[k, pl.ds(at, QB), :] = part
            total += jnp.dot(part.astype(BF16), vals[k][...], preferred_element_type=F32)
        att_ref[pl.ds(at, QB), :] = total
        return carry

    lax.fori_loop(0, rows // QB, one, 0)


def attend_back_kernel(lay, bucket_count, flag_ref, q_ref, da_ref, delta_ref, probs_ref, *refs):
    G = lay.G
    keys, vals = refs[:G], refs[G : 2 * G]
    dq_ref, dk_ref, dv_ref, dko_ref, dvo_ref, bucket_ref, strip, ds_ref, pb_ref = refs[2 * G :]
    rows, zw = q_ref.shape
    length = G * rows
    g = flag_ref[1]
    scale = zw ** (-0.5)
    edges = bucket_edges(bucket_count)
    strip[...] = jnp.zeros(strip.shape, F32)

    def one(i, carry):
        at = pl.multiple_of(i * QB, QB)
        da = da_ref[pl.ds(at, QB), :]
        dq = jnp.zeros((QB, zw), F32)
        for k in range(G):
            owner = lax.rem(g - k + G, G)
            dw = lax.dot_general(da, vals[k][...], (((1,), (1,)), ((), ())), preferred_element_type=F32)
            p = probs_ref[k, pl.ds(at, QB), :]
            ds = p * (dw - delta_ref[pl.ds(at, QB), :])
            off = jnp.clip(length - rows * (g - owner) - at, 0, length)
            strip[:, pl.ds(pl.multiple_of(off, LANES), rows)] += ds
            low = ds.astype(BF16)
            dq += jnp.dot(low, keys[k][...], preferred_element_type=F32)
            ds_ref[k, pl.ds(at, QB), :] = low
            pb_ref[k, pl.ds(at, QB), :] = p.astype(BF16)
        dq_ref[pl.ds(at, QB), :] = dq * scale
        return carry

    lax.fori_loop(0, rows // QB, one, 0)
    for k in range(G):
        dk = lax.dot_general(
            ds_ref[k], q_ref[...], (((0,), (0,)), ((), ())), preferred_element_type=F32
        )
        dv = lax.dot_general(
            pb_ref[k], da_ref[...], (((0,), (0,)), ((), ())), preferred_element_type=F32
        )
        if k == 0:
            dk_ref[...] = dk * scale
            dv_ref[...] = dv
        else:
            dko_ref[k - 1] = (dk * scale).astype(BF16)
            dvo_ref[k - 1] = dv.astype(BF16)
    lag0 = lax.broadcasted_iota(jnp.int32, (QB, LANES), 0) - lax.broadcasted_iota(
        jnp.int32, (QB, LANES), 1
    )
    sums = [jnp.zeros((1, LANES), F32) for k in range(bucket_count)]
    for t in range((length + QB) // LANES):
        base = length - t * LANES
        low, high = base - LANES + 1, base + QB - 1
        if high < 0:
            continue
        value = strip[:, t * LANES : (t + 1) * LANES]
        for k in range(bucket_count):
            top = edges[k + 1] if k + 1 < bucket_count else length
            if edges[k] <= high and top > low:
                lag = lag0 + base
                inside = (lag >= edges[k]) & (lag < top)
                sums[k] = sums[k] + jnp.sum(jnp.where(inside, value, 0.0), axis=0, keepdims=True)
    for k in range(bucket_count):
        bucket_ref[pl.ds(k, 1), :] = sums[k]


def silu_slope(values):
    gate_value = jax.nn.sigmoid(values)
    return gate_value * (1.0 + values * (1.0 - gate_value))


def normalize(seq_rows):
    centered = seq_rows - jnp.mean(seq_rows, axis=-1, keepdims=True)
    inverse = lax.rsqrt(jnp.mean(centered * centered, axis=-1, keepdims=True) + epsilon)
    return (centered * inverse, inverse)


def normalize_back(grad_scaled, unit_rows, inverse):
    return inverse * (
        grad_scaled
        - jnp.mean(grad_scaled, axis=-1, keepdims=True)
        - unit_rows * jnp.mean(grad_scaled * unit_rows, axis=-1, keepdims=True)
    )


def mm(a, b):
    return jnp.dot(a, b, preferred_element_type=F32)


def mm_t(a, b):
    return lax.dot_general(a, b, (((1,), (1,)), ((), ())), preferred_element_type=F32)


def wgrad(a, b):
    return lax.dot_general(a, b, (((0,), (0,)), ((), ())), preferred_element_type=F32).astype(BF16)


def shards(
    lay,
    tokens,
    cotangent,
    stretch_size,
    w_value,
    w_base,
    w_out,
    w_up,
    w_down,
    ema_delta,
    ema_alpha,
    ema_beta,
    ema_gamma,
    ema_omega,
    first_gain,
    second_gain,
    query_gain,
    query_bias,
    key_gain,
    relative_bias,
):
    micro, items, seq_len, D = tokens.shape
    H = ema_delta.shape[1]
    zw = query_gain.shape[0]
    V = w_value.shape[1]
    NB = relative_bias.shape[0]
    length = seq_len * lay.S
    G = lay.G
    R = lay.BL * seq_len
    d_at, b_at = lax.axis_index("dp"), lax.axis_index("seq")
    c_at, y_at = d_at % 2, d_at // 2
    q_at = b_at // lay.Cq
    g_at = (b_at % lay.Cq) * 2 + c_at
    share = ema_delta.shape[0]

    def group_perm(k):
        pairs = []
        for y in range(lay.Y):
            for q in range(lay.Q):
                for g in range(G):
                    t = (g + k) % G
                    src = (y * 2 + g % 2) * lay.S + q * lay.Cq + g // 2
                    dst = (y * 2 + t % 2) * lay.S + q * lay.Cq + t // 2
                    pairs.append((src, dst))
        return pairs

    def shift(value, k):
        return lax.ppermute(value, ("dp", "seq"), group_perm(k % G))

    marks = jnp.broadcast_to(
        stretch_size.reshape(1, -1).astype(BF16), (share, lay.MS)
    )
    used = 4 * H + 3 + lay.MS
    pack = jnp.concatenate(
        [
            ema_delta,
            ema_alpha,
            ema_beta,
            ema_gamma,
            ema_omega[:, None],
            first_gain[:, None],
            second_gain[:, None],
            marks,
            jnp.zeros((share, LANES - used), BF16),
        ],
        1,
    )
    x_blocks, cot_blocks, fulls = gather_all(
        lay, tokens, cotangent, (pack, w_value, w_base, w_out, w_up, w_down)
    )
    pack_full = fulls[0]
    mark = pack_full[y_at, q_at % 2, 0, 0, 0, 4 * H + 3 + q_at // 2]
    flags = jnp.stack([(mark.astype(jnp.int32) == length).astype(jnp.int32), g_at])
    mats = [full.reshape(D if full.shape[-2] == share else -1, full.shape[-1]) for full in fulls[1:]]
    mat_value, mat_base, mat_out, mat_up, mat_down = mats
    raw = pack_full.reshape(D, LANES).astype(F32).T
    leak = jax.nn.sigmoid(raw[:H])
    decay = 1.0 - leak * jax.nn.sigmoid(raw[H : 2 * H])
    log_decay = jnp.log(decay)
    gain = leak * raw[2 * H : 3 * H] * raw[3 * H : 4 * H] * (H ** (-0.5))
    table = jnp.concatenate([decay, log_decay, gain])
    omega = raw[4 * H : 4 * H + 1]
    gain_first = raw[4 * H + 1]
    gain_second = raw[4 * H + 2]

    x_low = x_blocks.reshape(R, D)
    x = x_low.astype(F32)
    grad_out = cot_blocks.reshape(R, D).astype(F32)

    state = jax.ShapeDtypeStruct((H, SEG, D), F32)
    ends_s, ends_r = lane_call(
        functools.partial(ema_ends_kernel, H), [state, state], (x, table), name="ema_ends"
    )
    mine = jnp.stack([ends_s[:, SEG - 1], ends_r[:, SEG - 1]])
    inc = jnp.zeros_like(mine)
    for k in range(1, G):
        other = shift(mine, k)
        span = (k - 1) * R
        s_part, r_part = other[0], other[1]
        if span:
            power = jnp.exp(span * log_decay)
            r_part = power * r_part + span * jnp.exp((span - 1) * log_decay) * s_part
            s_part = power * s_part
        inc = inc + jnp.where(k <= g_at, jnp.stack([s_part, r_part]), 0.0)
    value_pre = mm(x_low, mat_value)
    values = jax.nn.silu(value_pre).astype(BF16)
    ema, mixed, s_in, r_in = lane_call(
        functools.partial(ema_out_kernel, H),
        [jax.ShapeDtypeStruct((R, D), F32), jax.ShapeDtypeStruct((R, D), BF16), state, state],
        (x, table, omega, ends_s, ends_r, inc),
        name="ema_out",
    )
    base = mm(mixed, mat_base)
    z_pre = base[:, :zw]
    reset_pre = base[:, zw : zw + V]
    cand_pre = base[:, zw + V : zw + V + D]
    update_pre = base[:, zw + V + D :]
    shared = jax.nn.silu(z_pre)
    queries = (shared * query_gain + query_bias).astype(BF16)
    keys = (shared * key_gain).astype(BF16)
    keys_all = [keys] + [shift(keys, k) for k in range(1, G)]
    vals_all = [values] + [shift(values, k) for k in range(1, G)]
    strip = call(
        functools.partial(bias_kernel, length, NB),
        jax.ShapeDtypeStruct((QB, length + R), F32),
        (relative_bias,),
        specs=[SM],
        name="bias_strip",
    )
    attended, probs = call(
        functools.partial(attend_kernel, lay),
        [jax.ShapeDtypeStruct((R, V), F32), jax.ShapeDtypeStruct((G, R, R), F32)],
        (flags, queries, strip, *keys_all, *vals_all),
        specs=[SM] + [VM] * (2 + 2 * G),
        scratch=[pltpu.VMEM((QB, length), F32)],
        name="attend",
    )
    reset_gate = jax.nn.silu(reset_pre)
    update = jax.nn.sigmoid(update_pre)
    gated = (attended * reset_gate).astype(BF16)
    cand_in = cand_pre + mm(gated, mat_out)
    candidate = jax.nn.silu(cand_in)
    first_sum = x + update * (candidate - x)
    unit_first, inverse_first = normalize(first_sum)
    normed = unit_first * gain_first
    normed_low = normed.astype(BF16)
    hidden_pre = mm(normed_low, mat_up)
    hidden = jax.nn.silu(hidden_pre).astype(BF16)
    second_sum = normed + mm(hidden, mat_down)
    unit_second, inverse_second = normalize(second_sum)
    block_out = (unit_second * gain_second).astype(BF16)

    grad_gain_second = jnp.sum(grad_out * unit_second, axis=0)
    grad_second = normalize_back(grad_out * gain_second, unit_second, inverse_second)
    branch = grad_second.astype(BF16)
    grad_mat_down = wgrad(hidden, branch)
    hidden_grad = (mm_t(branch, mat_down) * silu_slope(hidden_pre)).astype(BF16)
    grad_mat_up = wgrad(normed_low, hidden_grad)
    grad_normed = grad_second + mm_t(hidden_grad, mat_up)
    grad_gain_first = jnp.sum(grad_normed * unit_first, axis=0)
    grad_first = normalize_back(grad_normed * gain_first, unit_first, inverse_first)
    cand_low = (grad_first * update * silu_slope(cand_in)).astype(BF16)
    grad_mat_out = wgrad(gated, cand_low)
    grad_gated = mm_t(cand_low, mat_out)
    att_low = (grad_gated * reset_gate).astype(BF16)
    grad_reset = grad_gated * attended * silu_slope(reset_pre)
    grad_update = grad_first * (candidate - x) * update * (1.0 - update)
    delta = jnp.sum(att_low.astype(F32) * attended, axis=1, keepdims=True)
    dq, grad_keys, grad_values, dk_out, dv_out, buckets = call(
        functools.partial(attend_back_kernel, lay, NB),
        [
            jax.ShapeDtypeStruct((R, zw), F32),
            jax.ShapeDtypeStruct((R, zw), F32),
            jax.ShapeDtypeStruct((R, V), F32),
            jax.ShapeDtypeStruct((G - 1, R, zw), BF16),
            jax.ShapeDtypeStruct((G - 1, R, V), BF16),
            jax.ShapeDtypeStruct((NB, LANES), F32),
        ],
        (flags, queries, att_low, delta, probs, *keys_all, *vals_all),
        specs=[SM] + [VM] * (4 + 2 * G),
        scratch=[
            pltpu.VMEM((QB, length + R), F32),
            pltpu.VMEM((G, R, R), BF16),
            pltpu.VMEM((G, R, R), BF16),
        ],
        name="attend_back",
    )
    for k in range(1, G):
        grad_keys = grad_keys + shift(dk_out[k - 1], -k).astype(F32)
        grad_values = grad_values + shift(dv_out[k - 1], -k).astype(F32)
    grad_query_gain = jnp.sum(dq * shared, axis=0)
    grad_query_bias = jnp.sum(dq, axis=0)
    grad_key_gain = jnp.sum(grad_keys * shared, axis=0)
    grad_relative = jnp.sum(buckets, axis=1)
    grad_z = (dq * query_gain + grad_keys * key_gain) * silu_slope(z_pre)
    base_low = jnp.concatenate(
        [grad_z.astype(BF16), grad_reset.astype(BF16), cand_low, grad_update.astype(BF16)], 1
    )
    grad_mat_base = wgrad(mixed, base_low)
    grad_ema = mm_t(base_low, mat_base) * silu_slope(ema)
    lam_ends = lane_call(
        functools.partial(ema_back_ends_kernel, H), state, (grad_ema, table), name="ema_back_ends"
    )
    lam_mine = lam_ends[:, 0]
    lam_inc = jnp.zeros_like(lam_mine)
    for k in range(1, G):
        part = shift(lam_mine, -k)
        span = (k - 1) * R
        if span:
            part = jnp.exp(span * log_decay) * part
        lam_inc = lam_inc + jnp.where(g_at + k < G, part, 0.0)
    ema_sums = lane_call(
        functools.partial(ema_sums_kernel, H),
        jax.ShapeDtypeStruct((2 * H + 8, D), F32),
        (x, grad_ema, table, s_in, r_in),
        name="ema_sums",
    )
    value_low = (grad_values * silu_slope(value_pre)).astype(BF16)
    grad_mat_value = wgrad(x_low, value_low)
    grad_x_value = mm_t(value_low, mat_value)
    grad_x_ema = lane_call(
        functools.partial(ema_back_kernel, H),
        jax.ShapeDtypeStruct((R, D), F32),
        (grad_ema, table, omega, lam_ends, lam_inc),
        name="ema_back",
    )
    grad_x = (grad_first * (1.0 - update) + grad_x_ema + grad_x_value).astype(BF16)

    sums = jnp.concatenate(
        [
            ema_sums[: 2 * H + 1],
            grad_gain_first[None],
            grad_gain_second[None],
            jnp.zeros((LANES - 2 * H - 3, D), F32),
        ]
    ).T
    small = jnp.zeros((8, LANES), F32)
    small = small.at[0, :zw].set(grad_query_gain)
    small = small.at[1, :zw].set(grad_query_bias)
    small = small.at[2, :zw].set(grad_key_gain)
    small = small.at[3, :NB].set(grad_relative)
    shape = (lay.Y, 2, lay.Z, lay.X)

    def split(grad):
        return grad.reshape(shape + (-1, grad.shape[-1]))

    reduced, small_total, moved = scatter_all(
        lay,
        [
            split(grad_mat_down),
            split(grad_mat_up),
            split(grad_mat_out),
            split(grad_mat_base),
            split(grad_mat_value),
            split(sums),
        ],
        small,
        [block_out.reshape(lay.BL, seq_len, D), grad_x.reshape(lay.BL, seq_len, D)],
        seq_len,
        D,
    )
    own = reduced[5]
    corr, lagged = own[:, :H], own[:, H : 2 * H]
    p = jax.nn.sigmoid(ema_delta.astype(F32))
    a = jax.nn.sigmoid(ema_alpha.astype(F32))
    beta = ema_beta.astype(F32)
    read = ema_gamma.astype(F32) * (H ** (-0.5))
    q_grad = read * p * beta * lagged
    return (
        moved[0],
        moved[1].astype(F32),
        reduced[4],
        reduced[3],
        reduced[2],
        reduced[1],
        reduced[0],
        (read * beta * corr - a * q_grad) * p * (1.0 - p),
        -p * q_grad * a * (1.0 - a),
        p * read * corr,
        p * beta * corr * (H ** (-0.5)),
        own[:, 2 * H],
        own[:, 2 * H + 1],
        own[:, 2 * H + 2],
        small_total[0, :zw],
        small_total[1, :zw],
        small_total[2, :zw],
        small_total[3, :NB],
    )


def solution(mesh):
    rows = P(None, "dp", "seq", None)
    part2, part1 = P(("dp", "seq"), None), P(("dp", "seq"))
    in_specs = (rows, rows, P(None, "dp")) + (part2,) * 9 + (part1,) * 3 + (P(),) * 4
    out_specs = (rows, rows) + (part2,) * 9 + (part1,) * 3 + (P(),) * 4

    def whole(tokens, *rest):
        micro, seqs = tokens.shape[:2]
        lay = Layout(mesh.shape["dp"], mesh.shape["seq"], micro, seqs // mesh.shape["dp"])
        return jax.shard_map(
            functools.partial(shards, lay),
            mesh=mesh,
            in_specs=in_specs,
            out_specs=out_specs,
            check_vma=False,
        )(tokens, *rest)

    return whole
```

```python
import functools

import jax
import jax.numpy as jnp
import numpy as np
from jax import lax
from jax.experimental import pallas as pl
from jax.experimental.pallas import tpu as pltpu
from jax.sharding import PartitionSpec as P

epsilon = 1e-05
masked_fill = -1e30
MESH = pl.DeviceIdType.MESH
ANY = pl.BlockSpec(memory_space=pl.ANY)
VM = pl.BlockSpec(memory_space=pltpu.VMEM)
SM = pl.BlockSpec(memory_space=pltpu.SMEM)
F32 = jnp.float32
BF16 = jnp.bfloat16
SEG = 8
LANES = 128


def bucket_edges(bucket_count):
    edge_list = [0]
    middle = bucket_count // 2
    for number in range(1, bucket_count):
        edge_list.append(number if number < middle else int(middle * 2 ** ((number - middle) / 2)))
    return edge_list


class Layout:
    def __init__(self, dp, seq, micro, items):
        self.dp, self.S = dp, seq
        self.C = 2
        self.Y = dp // 2
        self.X = min(self.Y, seq)
        self.Z = seq // self.X
        self.items = items
        self.MS = micro * items
        self.Q = 2 * self.MS
        self.Cq = seq // self.Q
        self.G = 2 * self.Cq
        self.BL = seq // self.G

    def here(self):
        d, b = lax.axis_index("dp"), lax.axis_index("seq")
        return d // 2, d % 2, b // self.X, b % self.X, b


class Wire:
    def __init__(self, lay, send, recv):
        self.lay, self.send, self.recv, self.count = lay, send, recv, 0
        self.sent = []

    def to(self, y, c, z, x):
        return (y * 2 + c, z * self.lay.X + x)

    def start(self, src, dst, target):
        number = self.count
        self.count += 1
        copy = pltpu.make_async_remote_copy(
            src_ref=src,
            dst_ref=dst,
            send_sem=self.send.at[number],
            recv_sem=self.recv.at[number],
            device_id=target,
            device_id_type=MESH,
        )
        copy.start()
        self.sent.append(copy)
        return copy

    def finish(self):
        for copy in self.sent:
            copy.wait_send()


def greet(lay):
    y, c, z, x, b = lay.here()
    barrier = pltpu.get_barrier_semaphore()
    plane = 2 * lay.S

    def one(k, carry):
        other = (c * lay.S + b + k) % plane
        pl.semaphore_signal(
            barrier, inc=1, device_id=(y * 2 + other // lay.S, other % lay.S), device_id_type=MESH
        )
        return carry

    lax.fori_loop(1, plane, one, 0)
    for k in range(1, lay.Y):
        pl.semaphore_signal(
            barrier, inc=1, device_id=(((y + k) % lay.Y) * 2 + c, b), device_id_type=MESH
        )
    pl.semaphore_wait(barrier, plane - 1 + lay.Y - 1)


def half_columns(columns):
    return ((columns // LANES + 1) // 2) * LANES


def reshard_in(lay, sources, targets, send, recv, local):
    y, c, z, x, b = lay.here()
    g = b // lay.BL
    slot = b % lay.BL
    qm = b // lay.Cq
    gm = (b % lay.Cq) * 2 + c

    def begin(n):
        for source, target in ((sources[n], targets[n]),):
            for ms in range(lay.MS):
                seq_to = (ms * 2 + c) * lay.Cq + g // 2
                mine = jnp.logical_and(seq_to == b, g % 2 == c)
                block = source.at[ms // lay.items, ms % lay.items]

                @pl.when(jnp.logical_not(mine))
                def _():
                    pltpu.make_async_remote_copy(
                        src_ref=block,
                        dst_ref=target.at[slot],
                        send_sem=send.at[n, ms],
                        recv_sem=recv.at[n, slot],
                        device_id=(y * 2 + g % 2, seq_to),
                        device_id_type=MESH,
                    ).start()

                @pl.when(mine)
                def _():
                    pltpu.make_async_copy(block, target.at[slot], local.at[n]).start()

    def wait(n):
        source, target = sources[n], targets[n]
        for ms in range(lay.MS):
            seq_to = (ms * 2 + c) * lay.Cq + g // 2
            mine = jnp.logical_and(seq_to == b, g % 2 == c)
            block = source.at[ms // lay.items, ms % lay.items]

            @pl.when(jnp.logical_not(mine))
            def _():
                pltpu.make_async_remote_copy(
                    src_ref=block,
                    dst_ref=target.at[slot],
                    send_sem=send.at[n, ms],
                    recv_sem=recv.at[n, slot],
                    device_id=(y * 2 + g % 2, seq_to),
                    device_id_type=MESH,
                ).wait_send()

            @pl.when(mine)
            def _():
                pltpu.make_async_copy(block, target.at[slot], local.at[n]).wait()

        for j in range(lay.BL):
            from_b = gm * lay.BL + j
            own = jnp.logical_and(from_b == b, qm % 2 == c)

            @pl.when(jnp.logical_not(own))
            def _():
                pltpu.make_async_remote_copy(
                    src_ref=source.at[0, 0],
                    dst_ref=target.at[j],
                    send_sem=send.at[n, 0],
                    recv_sem=recv.at[n, j],
                    device_id=(y * 2 + qm % 2, from_b),
                    device_id_type=MESH,
                ).wait_recv()

    return begin, wait


def reshard_out(lay, sources, targets, send, recv, local):
    y, c, z, x, b = lay.here()
    g = b // lay.BL
    qm = b // lay.Cq
    gm = (b % lay.Cq) * 2 + c
    ms_to = qm // 2
    m_to, s_to = ms_to // lay.items, ms_to % lay.items

    def copies(n, j):
        from_b = gm * lay.BL + j
        own = jnp.logical_and(from_b == b, qm % 2 == c)
        remote = pltpu.make_async_remote_copy(
            src_ref=sources[n].at[j],
            dst_ref=targets[n].at[m_to, s_to],
            send_sem=send.at[n, j],
            recv_sem=recv.at[n, ms_to],
            device_id=(y * 2 + qm % 2, from_b),
            device_id_type=MESH,
        )
        near = pltpu.make_async_copy(sources[n].at[j], targets[n].at[m_to, s_to], local.at[n])
        return own, remote, near

    def begin(n):
        for j in range(lay.BL):
            own, remote, near = copies(n, j)
            pl.when(jnp.logical_not(own))(remote.start)
            pl.when(own)(near.start)

    def wait(n):
        for j in range(lay.BL):
            own, remote, near = copies(n, j)
            pl.when(jnp.logical_not(own))(remote.wait_send)
            pl.when(own)(near.wait)
        for ms in range(lay.MS):
            seq_at = (ms * 2 + c) * lay.Cq + g // 2
            own = jnp.logical_and(seq_at == b, g % 2 == c)

            @pl.when(jnp.logical_not(own))
            def _():
                pltpu.make_async_remote_copy(
                    src_ref=sources[n].at[0],
                    dst_ref=targets[n].at[ms // lay.items, ms % lay.items],
                    send_sem=send.at[n, 0],
                    recv_sem=recv.at[n, ms],
                    device_id=(y * 2 + g % 2, seq_at),
                    device_id_type=MESH,
                ).wait_recv()

    return begin, wait


def chunks_of(shapes, limit):
    result = []
    for n, shape in enumerate(shapes):
        tiles = shape[-1] // LANES
        cuts = max(1, -(-shape[0] * shape[-1] // limit))
        at = 0
        for cut in range(cuts):
            width = (tiles - at) // (cuts - cut) if cut == cuts - 1 else -(-(tiles - at) // (cuts - cut))
            result.append((n, at * LANES, width * LANES))
            at += width
    return result


def gather_kernel(lay, count, chunks, refs):
    tok, cot = refs[0], refs[1]
    shards = refs[2 : 2 + count]
    tok_out, cot_out = refs[2 + count], refs[3 + count]
    fulls = refs[4 + count : 4 + 2 * count]
    send, recv, local, t_send, t_recv, t_local = refs[4 + 2 * count :]
    y, c, z, x, b = lay.here()
    X, Y, Z = lay.X, lay.Y, lay.Z
    greet(lay)
    wire = Wire(lay, send, recv)
    begin, wait = reshard_in(lay, (tok, cot), (tok_out, cot_out), t_send, t_recv, t_local)
    total = len(chunks)
    owns = []
    for i, (n, at, width) in enumerate(chunks):
        cols = pl.ds(at, width)
        copy = pltpu.make_async_copy(
            shards[n].at[:, cols], fulls[n].at[y, c, z, x, :, cols], local.at[i]
        )
        copy.start()
        owns.append(copy)
    arrived = [dict() for i in range(total)]

    def stage_z(i):
        n, at, width = chunks[i]
        cols = pl.ds(at, width)
        arrived[i]["z"] = [
            wire.start(
                shards[n].at[:, cols],
                fulls[n].at[y, c, z, x, :, cols],
                wire.to(y, c, (z + k) % Z, x),
            )
            for k in range(1, Z)
        ]

    def parts(i):
        n, at, width = chunks[i]
        left = half_columns(width)
        result = [(at, left)]
        if left < width:
            result.append((at + left, width - left))
        return result

    def to_core(i, block):
        arrived[i].setdefault("core", []).append(wire.start(block, block, wire.to(y, 1 - c, z, x)))

    def stage_one(i):
        owns[i].wait()
        for copy in arrived[i]["z"]:
            copy.wait_recv()
        n, first, columns = chunks[i]
        full = fulls[n]
        for half, (at, width) in enumerate(parts(i)):
            block = full.at[y, c, :, x, :, pl.ds(at, width)]
            if half == 0:
                arrived[i]["x0"] = [
                    wire.start(block, block, wire.to(y, c, z, (x + k) % X)) for k in range(1, X)
                ]
            else:
                arrived[i]["y1"] = [
                    wire.start(block, block, wire.to((y + k) % Y, c, z, x)) for k in range(1, Y)
                ]
        to_core(i, full.at[y, c, :, x, :, pl.ds(first, columns)])

    def stage_two(i):
        full = fulls[chunks[i][0]]
        for half, (at, width) in enumerate(parts(i)):
            cols = pl.ds(at, width)
            if half == 0:
                for copy in arrived[i]["x0"]:
                    copy.wait_recv()
                block = full.at[y, c, :, :, :, cols]
                arrived[i]["y0"] = [
                    wire.start(block, block, wire.to((y + k) % Y, c, z, x)) for k in range(1, Y)
                ]
                for k in range(1, X):
                    to_core(i, full.at[y, c, :, (x + X - k) % X, :, cols])
            else:
                for copy in arrived[i]["y1"]:
                    copy.wait_recv()
                block = full.at[:, c, :, x, :, cols]
                arrived[i]["x1"] = [
                    wire.start(block, block, wire.to(y, c, z, (x + k) % X)) for k in range(1, X)
                ]
                for k in range(1, Y):
                    to_core(i, full.at[(y + Y - k) % Y, c, :, x, :, cols])

    def stage_three(i):
        full = fulls[chunks[i][0]]
        for half, (at, width) in enumerate(parts(i)):
            cols = pl.ds(at, width)
            if half == 0:
                for k, copy in enumerate(arrived[i]["y0"], 1):
                    copy.wait_recv()
                    to_core(i, full.at[(y + Y - k) % Y, c, :, :, :, cols])
            else:
                for k, copy in enumerate(arrived[i]["x1"], 1):
                    copy.wait_recv()
                    to_core(i, full.at[:, c, :, (x + X - k) % X, :, cols])

    def finish():
        for i in range(total):
            for copy in arrived[i]["core"]:
                copy.wait_recv()
        wire.finish()

    def gathered(n):
        for i in range(total):
            if chunks[i][0] == n:
                for copy in arrived[i].pop("core"):
                    copy.wait_recv()
                arrived[i]["core"] = []

    return wire, (begin, wait), (stage_z, stage_one, stage_two, stage_three), gathered, finish


def group_copies(lay, send, recv, source, inbox, forward):
    y, c, z, x, b = lay.here()
    q = b // lay.Cq
    g = (b % lay.Cq) * 2 + c
    copies = []
    for k in range(1, lay.G):
        t = (g + (k if forward else lay.G - k)) % lay.G
        copies.append(
            pltpu.make_async_remote_copy(
                src_ref=source,
                dst_ref=inbox.at[k - 1],
                send_sem=send.at[k - 1],
                recv_sem=recv.at[k - 1],
                device_id=(y * 2 + t % 2, q * lay.Cq + t // 2),
                device_id_type=MESH,
            )
        )
    return copies, g


def to_tiles(low, tiles, r0, rows):
    for t in range(tiles.shape[0]):
        tiles[t, pl.ds(r0, rows), :] = low[:, t * LANES : (t + 1) * LANES].astype(F32)


def make_tables(lay, H, pack, raw, table, turned):
    r = pack.shape[4]
    total = lay.Y * 2 * lay.Z * lay.X

    def one(i, carry):
        block = pack[i // (2 * lay.Z * lay.X), i // (lay.Z * lay.X) % 2, i // lay.X % lay.Z, i % lay.X]
        raw[pl.ds(i * r, r), :] = block.astype(F32)
        return carry

    lax.fori_loop(0, total, one, 0)
    for t in range(table.shape[0]):
        v = raw[t * LANES : (t + 1) * LANES, :].T
        turned[t] = v
        leak = jax.nn.sigmoid(v[:H])
        decay = 1.0 - leak * jax.nn.sigmoid(v[H : 2 * H])
        table[t, :H] = decay
        table[t, H : 2 * H] = jnp.log(decay)
        table[t, 2 * H : 3 * H] = leak * v[2 * H : 3 * H] * v[3 * H : 4 * H] * (H ** (-0.5))


def carry_in(lay, H, rows, g, inbox, table, inc, t, later):
    log = table[t, H : 2 * H]
    state = jnp.zeros((H, LANES), F32)
    slope = jnp.zeros((H, LANES), F32)
    for k in range(1, lay.G):
        span = (k - 1) * rows
        valid = (g + k < lay.G) if later else (k <= g)
        s_part = inbox[k - 1, t, :H]
        r_part = s_part * 0.0 if later else inbox[k - 1, t, H : 2 * H]
        if span:
            power = jnp.exp(span * log)
            r_part = power * r_part + (span * jnp.exp((span - 1) * log)) * s_part
            s_part = power * s_part
        state = state + jnp.where(valid, s_part, 0.0)
        slope = slope + jnp.where(valid, r_part, 0.0)
    inc[t, :H] = state
    if not later:
        inc[t, H : 2 * H] = slope


def forward_kernel(lay, count, chunks, H, refs):
    n_in, n_out = 2 + count, 8 + count
    ins, outs, scratch = refs[:n_in], refs[n_in : n_in + n_out], refs[n_in + n_out :]
    tok_out, cot_out = outs[0], outs[1]
    fulls = outs[2 : 2 + count]
    mixed, ema, si, ri, table, turned = outs[2 + count :]
    sems, work = scratch[:6], scratch[6:]
    xt, pack, raw, s_end, r_end, mine, inbox, inc, load, c_send, c_recv = work
    wire, (begin, wait), stages, gathered, finish = gather_kernel(
        lay, count, chunks, ins + (tok_out, cot_out) + tuple(fulls) + sems
    )
    stage_z, stage_one, stage_two, stage_three = stages
    total = len(chunks)
    rows = xt.shape[1]
    tiles = xt.shape[0]
    copies, g = group_copies(lay, c_send, c_recv, mine, inbox, True)

    def tables():
        gathered(0)
        copy = pltpu.make_async_copy(fulls[0], pack, load)
        copy.start()
        copy.wait()
        make_tables(lay, H, pack, raw, table, turned)

    def tokens():
        wait(0)
        for j in range(lay.BL):
            to_tiles(tok_out[j], xt, j * (rows // lay.BL), rows // lay.BL)

    def ends(first, last):
        def one(t, carry):
            ema_ends_kernel(H, xt.at[t], table.at[t], s_end.at[t], r_end.at[t])
            for h in range(H):
                mine[t, pl.ds(h, 1), :] = s_end[t, h, SEG - 1 : SEG, :]
                mine[t, pl.ds(H + h, 1), :] = r_end[t, h, SEG - 1 : SEG, :]
            return carry

        lax.fori_loop(first, last, one, 0)

    def exchange():
        for copy in copies:
            copy.start()

    def carries():
        for copy in copies:
            copy.wait()
        for t in range(tiles):
            carry_in(lay, H, rows, g, inbox, table, inc, t, False)

    def out(first, last):
        def one(t, carry):
            ema_out_kernel(
                H, xt.at[t], table.at[t], turned.at[t, pl.ds(4 * H, 1)], s_end.at[t], r_end.at[t],
                inc.at[t], ema.at[t], si.at[t], ri.at[t],
            )
            return carry

        lax.fori_loop(first, last, one, 0)
        for t in range(first, last):
            for r0 in range(0, rows, 128):
                v = ema[t, pl.ds(r0, 128), :]
                mixed[pl.ds(r0, 128), t * LANES : (t + 1) * LANES] = (
                    v * jax.nn.sigmoid(v)
                ).astype(BF16)

    third = tiles // 3
    hooks = {
        HOOK[0]: [tables],
        HOOK[1]: [tokens, lambda: ends(0, third)],
        HOOK[2]: [lambda: ends(third, tiles), exchange],
        HOOK[3]: [carries, lambda: out(0, third)],
        HOOK[4]: [lambda: out(third, 2 * third)],
        HOOK[5]: [lambda: out(2 * third, tiles)],
    }
    AHEAD = 2
    begin(0)
    for i in range(min(AHEAD, total)):
        stage_z(i)
    for turn in range(total + 2):
        if turn < total:
            stage_one(turn)
        if turn + AHEAD < total:
            stage_z(turn + AHEAD)
        if turn == HOOK[6]:
            begin(1)
        if 0 <= turn - 1 < total:
            stage_two(turn - 1)
        if 0 <= turn - 2:
            stage_three(turn - 2)
        for hook in hooks.get(turn, []):
            hook()
    finish()
    wait(1)


HOOK = (2, 3, 4, 5, 6, 7, 6)


def forward_all(lay, H, tokens, cotangent, shards):
    count = len(shards)
    chunks = chunks_of([shard.shape for shard in shards], shards[0].shape[0] * 800)
    micro, items, rows, width = tokens.shape
    per = (lay.Z - 1) + 2 * (lay.X - 1 + lay.Y - 1) + 1 + 2 * (lay.X - 1 + lay.Y - 1)
    blocks = jax.ShapeDtypeStruct((lay.BL, rows, width), BF16)
    fulls = [
        jax.ShapeDtypeStruct((lay.Y, 2, lay.Z, lay.X) + shard.shape, shard.dtype)
        for shard in shards
    ]
    T, R = width // LANES, lay.BL * rows
    state = (T, H, SEG, LANES)
    outs = [blocks, blocks] + fulls
    outs += [
        jax.ShapeDtypeStruct((R, width), BF16),
        jax.ShapeDtypeStruct((T, R, LANES), F32),
        jax.ShapeDtypeStruct(state, F32),
        jax.ShapeDtypeStruct(state, F32),
        jax.ShapeDtypeStruct((T, 3 * H, LANES), F32),
        jax.ShapeDtypeStruct((T, LANES, LANES), F32),
    ]

    def body(*refs):
        forward_kernel(lay, count, chunks, H, refs)

    result = pl.pallas_call(
        body,
        out_shape=outs,
        in_specs=[ANY] * (2 + count),
        out_specs=[VM] + [ANY] * (1 + count) + [VM] * 6,
        scratch_shapes=[
            pltpu.SemaphoreType.DMA((len(chunks) * per,)),
            pltpu.SemaphoreType.DMA((len(chunks) * per,)),
            pltpu.SemaphoreType.DMA((len(chunks),)),
            pltpu.SemaphoreType.DMA((2, lay.MS)),
            pltpu.SemaphoreType.DMA((2, lay.BL)),
            pltpu.SemaphoreType.DMA((2,)),
            pltpu.VMEM((T, R, LANES), F32),
            pltpu.VMEM(fulls[0].shape, fulls[0].dtype),
            pltpu.VMEM((width, LANES), F32),
            pltpu.VMEM(state, F32),
            pltpu.VMEM(state, F32),
            pltpu.VMEM((T, 2 * H, LANES), F32),
            pltpu.VMEM((lay.G - 1, T, 2 * H, LANES), F32),
            pltpu.VMEM((T, 2 * H, LANES), F32),
            pltpu.SemaphoreType.DMA,
            pltpu.SemaphoreType.DMA((lay.G - 1,)),
            pltpu.SemaphoreType.DMA((lay.G - 1,)),
        ],
        compiler_params=pltpu.CompilerParams(
            collective_id=0, has_side_effects=True, vmem_limit_bytes=40 * 2**20
        ),
        name="forward_all",
    )(tokens, cotangent, *shards)
    return result[0], result[1], result[2 : 2 + count], result[2 + count :]


def add_blocks(total, index, extra, extra_index, counts, width_at):
    size = int(np.prod(counts)) if counts else 1

    def one(i, carry):
        places = []
        for extent in reversed(counts):
            places.insert(0, i % extent)
            i = i // extent
        a, e = index(*places), extra_index(*places)
        summed = total[a].astype(F32) + extra[e].astype(F32)
        total[a] = summed.astype(total.dtype)
        return carry

    lax.fori_loop(0, size, one, 0)


def scatter_kernel(lay, H, chunks, ins, outs, scratch):
    grads, small, x_low, d_in, pre, gains, table, turned, si, ri, block_out = ins
    results, small_out, outs_to = outs
    bufs, own = scratch[: 7 * len(chunks)], scratch[7 * len(chunks) :]
    small_acc, small_recv, send, recv, local, t_send, t_recv, t_local = own[:8]
    xt, dt, dx, sums, flat, split, l_end, mine, inbox, inc, gx, c_send, c_recv = own[8:]
    grads = grads + (split,)
    y, c, z, x, b = lay.here()
    X, Y, Z = lay.X, lay.Y, lay.Z
    greet(lay)
    wire = Wire(lay, send, recv)
    begin, wait = reshard_out(lay, (block_out, gx), outs_to, t_send, t_recv, t_local)
    total = len(chunks)
    arrived = [dict() for i in range(total)]

    def buf(i, name):
        return bufs[7 * i + ("acc", "core", "x0", "y1", "y0", "x1", "z").index(name)]

    def parts(i):
        n, at, width = chunks[i]
        left = half_columns(width)
        result = [(0, left)]
        if left < width:
            result.append((left, width - left))
        return result

    def stage_core(i):
        n, at, width = chunks[i]
        cols = pl.ds(at, width)
        arrived[i]["core"] = [
            wire.start(
                grads[n].at[:, 1 - c, :, :, :, cols], buf(i, "core"), wire.to(y, 1 - c, z, x)
            )
        ]
        copy = pltpu.make_async_copy(
            grads[n].at[:, c, :, :, :, cols], buf(i, "acc"), local.at[i]
        )
        copy.start()
        arrived[i]["own"] = copy

    def stage_one(i):
        arrived[i]["own"].wait()
        arrived[i]["core"][0].wait_recv()
        acc = buf(i, "acc")
        add_blocks(acc, lambda *p: p, buf(i, "core"), lambda *p: p, (Y, Z, X), None)
        for half, (at, width) in enumerate(parts(i)):
            cols = pl.ds(at, width)
            if half == 0:
                arrived[i]["x0"] = [
                    wire.start(
                        acc.at[:, :, (x + k) % X, :, cols],
                        buf(i, "x0").at[k - 1],
                        wire.to(y, c, z, (x + k) % X),
                    )
                    for k in range(1, X)
                ]
            else:
                arrived[i]["y1"] = [
                    wire.start(
                        acc.at[(y + k) % Y, :, :, :, cols],
                        buf(i, "y1").at[k - 1],
                        wire.to((y + k) % Y, c, z, x),
                    )
                    for k in range(1, Y)
                ]

    def stage_two(i):
        acc = buf(i, "acc")
        for half, (at, width) in enumerate(parts(i)):
            cols = slice(at, at + width)
            view = pl.ds(at, width)
            if half == 0:
                for k, copy in enumerate(arrived[i]["x0"]):
                    copy.wait_recv()
                    add_blocks(
                        acc,
                        lambda p, q: (p, q, x, slice(None), cols),
                        buf(i, "x0"),
                        lambda p, q: (k, p, q),
                        (Y, Z),
                        None,
                    )
                arrived[i]["y0"] = [
                    wire.start(
                        acc.at[(y + k) % Y, :, x, :, view],
                        buf(i, "y0").at[k - 1],
                        wire.to((y + k) % Y, c, z, x),
                    )
                    for k in range(1, Y)
                ]
            else:
                for k, copy in enumerate(arrived[i]["y1"]):
                    copy.wait_recv()
                    add_blocks(
                        acc,
                        lambda p, q: (y, p, q, slice(None), cols),
                        buf(i, "y1"),
                        lambda p, q: (k, p, q),
                        (Z, X),
                        None,
                    )
                arrived[i]["x1"] = [
                    wire.start(
                        acc.at[y, :, (x + k) % X, :, view],
                        buf(i, "x1").at[k - 1],
                        wire.to(y, c, z, (x + k) % X),
                    )
                    for k in range(1, X)
                ]

    def stage_three(i):
        acc = buf(i, "acc")
        for half, (at, width) in enumerate(parts(i)):
            cols = slice(at, at + width)
            name = "y0" if half == 0 else "x1"
            for k, copy in enumerate(arrived[i][name]):
                copy.wait_recv()
                add_blocks(
                    acc,
                    lambda p: (y, p, x, slice(None), cols),
                    buf(i, name),
                    lambda p: (k, p),
                    (Z,),
                    None,
                )
        arrived[i]["z"] = [
            wire.start(
                acc.at[y, (z + k) % Z, x], buf(i, "z").at[k - 1], wire.to(y, c, (z + k) % Z, x)
            )
            for k in range(1, Z)
        ]

    def stage_four(i):
        n, at, width = chunks[i]
        total = buf(i, "acc")[y, z, x].astype(F32)
        for k, copy in enumerate(arrived[i]["z"]):
            copy.wait_recv()
            total = total + buf(i, "z")[k].astype(F32)
        results[n][:, pl.ds(at, width)] = total

    small_at = [0]

    def small_stage(moves):
        copies = []
        for target in moves:
            slot = small_at[0]
            small_at[0] += 1
            copies.append((slot, wire.start(small_acc, small_recv.at[slot], target)))
        for slot, copy in copies:
            copy.wait_send()
            wire.sent = [other for other in wire.sent if other is not copy]
        for slot, copy in copies:
            copy.wait_recv()
            small_acc[...] += small_recv[slot]

    rows, tiles = xt.shape[1], xt.shape[0]
    per_block = rows // lay.BL
    copies, g = group_copies(lay, c_send, c_recv, mine, inbox, False)

    def load():
        for j in range(lay.BL):
            to_tiles(d_in[j * per_block : (j + 1) * per_block, :], dt, j * per_block, per_block)

    def ends():
        def one(t, carry):
            ema_back_ends_kernel(H, dt.at[t], table.at[t], l_end.at[t])
            for h in range(H):
                mine[t, pl.ds(h, 1), :] = l_end[t, h, 0:1, :]
            return carry

        lax.fori_loop(0, tiles, one, 0)
        for copy in copies:
            copy.start()
        for j in range(lay.BL):
            to_tiles(x_low[j], xt, j * per_block, per_block)

    def correlate(first, last):
        def one(t, carry):
            ema_sums_kernel(H, xt.at[t], dt.at[t], table.at[t], si.at[t], ri.at[t], sums.at[t])
            return carry

        lax.fori_loop(first, last, one, 0)

    def back(first, last):
        if first == 0:
            for copy in copies:
                copy.wait()
            for t in range(tiles):
                carry_in(lay, H, rows, g, inbox, table, inc, t, True)

        def one(t, carry):
            ema_back_kernel(
                H, dt.at[t], table.at[t], turned.at[t, pl.ds(4 * H, 1)], l_end.at[t], inc.at[t], dx.at[t]
            )
            return carry

        lax.fori_loop(first, last, one, 0)
        for t in range(first, last):
            cols = slice(t * LANES, (t + 1) * LANES)
            for j in range(lay.BL):
                at = pl.ds(j * per_block, per_block)
                gx[j, :, cols] = (pre[at, cols] + dx[t, at, :]).astype(BF16)

    def share_sums():
        r = split.shape[4]
        for t in range(tiles):
            sums[t, pl.ds(2 * H + 1, 2), :] = gains[0:2, t * LANES : (t + 1) * LANES]
            flat[t * LANES : (t + 1) * LANES, :] = sums[t].T

        def one(i, carry):
            split[i // (2 * Z * X), i // (Z * X) % 2, i // X % Z, i % X] = flat[pl.ds(i * r, r), :]
            return carry

        lax.fori_loop(0, 2 * X * Y * Z, one, 0)

    half = tiles // 2
    small_acc[...] = small[...]
    sums[...] = jnp.zeros(sums.shape, F32)
    hooks = {
        BACK[0]: [load, ends],
        BACK[1]: [lambda: back(0, half)],
        BACK[2]: [lambda: back(half, tiles), lambda: begin(1)],
        BACK[3]: [lambda: correlate(0, half)],
        BACK[4]: [lambda: correlate(half, tiles), share_sums],
    }
    xs = [wire.to(y, c, z, (x + k) % X) for k in range(1, X)]
    ys = [wire.to((y + k) % Y, c, z, x) for k in range(1, Y)]
    zs = [wire.to(y, c, (z + k) % Z, x) for k in range(1, Z)]
    smalls = {5: [wire.to(y, 1 - c, z, x)], 6: xs, 7: ys, 8: zs}
    LEAD = 3
    for i in range(min(LEAD, total)):
        stage_core(i)
    begin(0)
    for turn in range(total + 3):
        if turn < total:
            stage_one(turn)
        if turn + LEAD < total:
            stage_core(turn + LEAD)
        if 0 <= turn - 1 < total:
            stage_two(turn - 1)
        if 0 <= turn - 2 < total:
            stage_three(turn - 2)
        if 0 <= turn - 3:
            stage_four(turn - 3)
        for hook in hooks.get(turn, []):
            hook()
        if turn in smalls:
            small_stage(smalls[turn])
    small_out[...] = small_acc[...]
    wait(0)
    wait(1)
    wire.finish()


BACK = (0, 1, 2, 3, 4)


def backward_all(lay, H, grads, small, x_blocks, grad_ema, pre, gains, table, turned, si, ri, block_out, share):
    X, Y, Z = lay.X, lay.Y, lay.Z
    T, R = table.shape[0], grad_ema.shape[0]
    width = grad_ema.shape[1]
    rows = R // lay.BL
    micro = lay.MS // lay.items
    shapes = [grad.shape[-2:] for grad in grads] + [(share, LANES)]
    kinds = [grad.dtype for grad in grads] + [F32]
    chunks = chunks_of(shapes, share * 800)
    scratch = []
    for n, at, cols in chunks:
        r = shapes[n][0]
        left = half_columns(cols)
        right = cols - left if cols > left else LANES
        kind = kinds[n]
        scratch += [
            pltpu.VMEM((Y, Z, X, r, cols), kind),
            pltpu.VMEM((Y, Z, X, r, cols), kind),
            pltpu.VMEM((X - 1, Y, Z, r, left), kind),
            pltpu.VMEM((Y - 1, Z, X, r, right), kind),
            pltpu.VMEM((Y - 1, Z, r, left), kind),
            pltpu.VMEM((X - 1, Z, r, right), kind),
            pltpu.VMEM((Z - 1, r, cols), kind),
        ]
    hops = 1 + (X - 1) + (Y - 1) + (Z - 1)
    per = 1 + 2 * (X - 1 + Y - 1) + Z - 1
    outs = [jax.ShapeDtypeStruct(shape, F32) for shape in shapes]
    outs.append(jax.ShapeDtypeStruct(small.shape, F32))
    outs += [jax.ShapeDtypeStruct((micro, lay.items, rows, width), BF16)] * 2
    scratch += [pltpu.VMEM(small.shape, F32), pltpu.VMEM((hops,) + small.shape, F32)]
    scratch += [
        pltpu.SemaphoreType.DMA((len(chunks) * per + hops,)),
        pltpu.SemaphoreType.DMA((len(chunks) * per + hops,)),
        pltpu.SemaphoreType.DMA((len(chunks),)),
        pltpu.SemaphoreType.DMA((2, lay.BL)),
        pltpu.SemaphoreType.DMA((2, lay.MS)),
        pltpu.SemaphoreType.DMA((2,)),
        pltpu.VMEM((T, R, LANES), F32),
        pltpu.VMEM((T, R, LANES), F32),
        pltpu.VMEM((T, R, LANES), F32),
        pltpu.VMEM((T, LANES, LANES), F32),
        pltpu.VMEM((width, LANES), F32),
        pltpu.VMEM((Y, 2, Z, X, share, LANES), F32),
        pltpu.VMEM((T, H, SEG, LANES), F32),
        pltpu.VMEM((T, H, LANES), F32),
        pltpu.VMEM((lay.G - 1, T, H, LANES), F32),
        pltpu.VMEM((T, H, LANES), F32),
        pltpu.VMEM((lay.BL, rows, width), BF16),
        pltpu.SemaphoreType.DMA((lay.G - 1,)),
        pltpu.SemaphoreType.DMA((lay.G - 1,)),
    ]
    count = len(grads)

    def body(*refs):
        ins = (refs[:count],) + refs[count : count + 10]
        rest = refs[count + 10 :]
        results, small_out, moved = rest[: count + 1], rest[count + 1], rest[count + 2 : count + 4]
        scatter_kernel(lay, H, chunks, ins, (results, small_out, moved), rest[count + 4 :])

    result = pl.pallas_call(
        body,
        out_shape=outs,
        in_specs=[ANY] * count + [VM] * 9 + [ANY],
        out_specs=[VM] * (count + 2) + [ANY] * 2,
        scratch_shapes=scratch,
        compiler_params=pltpu.CompilerParams(
            collective_id=1, has_side_effects=True, vmem_limit_bytes=58 * 2**20
        ),
        name="backward_all",
    )(*grads, small, x_blocks, grad_ema, pre, gains, table, turned, si, ri, block_out)
    return result[: count + 1], result[count + 1], result[count + 2 :]


def row(ref, index, lanes):
    return jnp.broadcast_to(ref[pl.ds(index, 1), lanes], (SEG, LANES))


def lane_call(kernel, outs, args, name):
    def spec(a):
        lead = len(a.shape) - 1
        return pl.BlockSpec(a.shape[:-1] + (LANES,), lambda i: (0,) * lead + (i,))

    return pl.pallas_call(
        kernel,
        out_shape=outs,
        grid=(args[0].shape[-1] // LANES,),
        in_specs=[spec(a) for a in args],
        out_specs=jax.tree.map(spec, outs),
        compiler_params=pltpu.CompilerParams(vmem_limit_bytes=32 * 2**20),
        name=name,
    )(*args)


def shifted(value, by):
    where = lax.broadcasted_iota(jnp.int32, (SEG, LANES), 0)
    if by > 0:
        return jnp.where(where >= by, pltpu.roll(value, by, 0), 0.0)
    return jnp.where(where < SEG + by, pltpu.roll(value, SEG + by, 0), 0.0)


def ema_ends_kernel(H, x_ref, tab_ref, s_ref, r_ref):
    rows, width = x_ref.shape
    steps = rows // SEG

    def tile(lanes):
        decay = [row(tab_ref, h, lanes) for h in range(H)]

        def step(t, state):
            s, r = state
            xt = x_ref[pl.ds(t, SEG, stride=steps), lanes]
            r = tuple(decay[h] * r[h] + s[h] for h in range(H))
            s = tuple(decay[h] * s[h] + xt for h in range(H))
            return s, r

        zero = tuple(tab_ref[0:SEG, lanes] * 0.0 for h in range(H))
        s, r = lax.fori_loop(0, steps, step, (zero, zero))
        for h in range(H):
            log = row(tab_ref, H + h, lanes)
            sh, rh = s[h], r[h]
            for d in (1, 2, 4):
                span = d * steps
                sd, rd = shifted(sh, d), shifted(rh, d)
                power = jnp.exp(span * log)
                rh = rh + power * rd + (span * jnp.exp((span - 1) * log)) * sd
                sh = sh + power * sd
            s_ref[h, :, lanes] = sh
            r_ref[h, :, lanes] = rh

    tile(slice(None))


def ema_out_kernel(H, x_ref, tab_ref, omega_ref, s_ref, r_ref, inc_ref, ema_ref, si_ref, ri_ref):
    rows, width = x_ref.shape
    steps = rows // SEG

    def tile(lanes):
        decay = [row(tab_ref, h, lanes) for h in range(H)]
        gain = [row(tab_ref, 2 * H + h, lanes) for h in range(H)]
        omega = row(omega_ref, 0, lanes)
        start = []
        span = (lax.broadcasted_iota(jnp.int32, (SEG, LANES), 0) * steps).astype(F32)
        for h in range(H):
            log = row(tab_ref, H + h, lanes)
            s_dev = row(inc_ref, h, lanes)
            r_dev = row(inc_ref, H + h, lanes)
            power = jnp.exp(span * log)
            s_in = shifted(s_ref[h, :, lanes], 1) + power * s_dev
            r_in = (
                shifted(r_ref[h, :, lanes], 1)
                + power * r_dev
                + (span * jnp.exp((span - 1.0) * log)) * s_dev
            )
            si_ref[h, :, lanes] = s_in
            ri_ref[h, :, lanes] = r_in
            start.append(s_in)

        def step(t, s):
            xt = x_ref[pl.ds(t, SEG, stride=steps), lanes]
            s = tuple(decay[h] * s[h] + xt for h in range(H))
            parts = [gain[h] * s[h] for h in range(H)]
            while len(parts) > 1:
                parts = [parts[i] + parts[i + 1] for i in range(0, len(parts), 2)]
            ema_ref[pl.ds(t, SEG, stride=steps), lanes] = parts[0] + omega * xt
            return s

        lax.fori_loop(0, steps, step, tuple(start))

    tile(slice(None))


def ema_back_ends_kernel(H, d_ref, tab_ref, l_ref):
    rows, width = d_ref.shape
    steps = rows // SEG

    def tile(lanes):
        decay = [row(tab_ref, h, lanes) for h in range(H)]

        def step(i, lam):
            dt = d_ref[pl.ds(steps - 1 - i, SEG, stride=steps), lanes]
            return tuple(decay[h] * lam[h] + dt for h in range(H))

        zero = tuple(tab_ref[0:SEG, lanes] * 0.0 for h in range(H))
        lam = lax.fori_loop(0, steps, step, zero)
        for h in range(H):
            log = row(tab_ref, H + h, lanes)
            lh = lam[h]
            for d in (1, 2, 4):
                lh = lh + jnp.exp(d * steps * log) * shifted(lh, -d)
            l_ref[h, :, lanes] = lh

    tile(slice(None))


def ema_sums_kernel(H, x_ref, d_ref, tab_ref, si_ref, ri_ref, out_ref):
    rows, width = x_ref.shape
    steps = rows // SEG
    group = H // 2

    def tile(lanes):
        for first in range(0, H, group):
            decay = [row(tab_ref, first + h, lanes) for h in range(group)]

            def step(t, state):
                s, r, c, q, o = state
                xt = x_ref[pl.ds(t, SEG, stride=steps), lanes]
                dt = d_ref[pl.ds(t, SEG, stride=steps), lanes]
                r = tuple(decay[h] * r[h] + s[h] for h in range(group))
                s = tuple(decay[h] * s[h] + xt for h in range(group))
                c = tuple(c[h] + dt * s[h] for h in range(group))
                q = tuple(q[h] + dt * r[h] for h in range(group))
                return s, r, c, q, o + dt * xt

            zero = tuple(tab_ref[0:SEG, lanes] * 0.0 for h in range(group))
            s = tuple(si_ref[first + h, :, lanes] for h in range(group))
            r = tuple(ri_ref[first + h, :, lanes] for h in range(group))
            s, r, c, q, o = lax.fori_loop(0, steps, step, (s, r, zero, zero, zero[0]))
            for h in range(group):
                out_ref[pl.ds(first + h, 1), lanes] = jnp.sum(c[h], axis=0, keepdims=True)
                out_ref[pl.ds(H + first + h, 1), lanes] = jnp.sum(q[h], axis=0, keepdims=True)
            out_ref[pl.ds(2 * H, 1), lanes] = jnp.sum(o, axis=0, keepdims=True)

    tile(slice(None))


def ema_back_kernel(H, d_ref, tab_ref, omega_ref, l_ref, inc_ref, dx_ref):
    rows, width = d_ref.shape
    steps = rows // SEG

    def tile(lanes):
        decay = [row(tab_ref, h, lanes) for h in range(H)]
        gain = [row(tab_ref, 2 * H + h, lanes) for h in range(H)]
        omega = row(omega_ref, 0, lanes)
        start = []
        span = ((SEG - 1 - lax.broadcasted_iota(jnp.int32, (SEG, LANES), 0)) * steps).astype(F32)
        for h in range(H):
            log = row(tab_ref, H + h, lanes)
            l_dev = row(inc_ref, h, lanes)
            start.append(shifted(l_ref[h, :, lanes], -1) + jnp.exp(span * log) * l_dev)

        def step(i, lam):
            at = pl.ds(steps - 1 - i, SEG, stride=steps)
            dt = d_ref[at, lanes]
            lam = tuple(decay[h] * lam[h] + dt for h in range(H))
            parts = [gain[h] * lam[h] for h in range(H)]
            while len(parts) > 1:
                parts = [parts[i] + parts[i + 1] for i in range(0, len(parts), 2)]
            dx_ref[at, lanes] = parts[0] + omega * dt
            return lam

        lax.fori_loop(0, steps, step, tuple(start))

    tile(slice(None))


def call(kernel, outs, args, specs=None, scratch=(), vmem=58, name=None):
    return pl.pallas_call(
        kernel,
        out_shape=outs,
        in_specs=specs or [VM] * len(args),
        out_specs=jax.tree.map(lambda o: VM, outs),
        scratch_shapes=list(scratch),
        compiler_params=pltpu.CompilerParams(vmem_limit_bytes=vmem * 2**20),
        name=name,
    )(*args)


QB = 256


def bias_kernel(length, bucket_count, bias_ref, strip_ref):
    edges = bucket_edges(bucket_count)
    tiles = length // LANES + QB // LANES
    lag0 = lax.broadcasted_iota(jnp.int32, (QB, LANES), 0) - lax.broadcasted_iota(
        jnp.int32, (QB, LANES), 1
    )
    for t in range(strip_ref.shape[1] // LANES):
        base = length - t * LANES
        low, high = base - LANES + 1, base + QB - 1
        start = max([k for k in range(bucket_count) if edges[k] <= low], default=0)
        value = jnp.full((QB, LANES), bias_ref[start], F32)
        for k in range(start + 1, bucket_count):
            if edges[k] <= high:
                value = jnp.where(lag0 + base >= edges[k], bias_ref[k], value)
        strip_ref[:, t * LANES : (t + 1) * LANES] = value


def attend_kernel(lay, flag_ref, q_ref, strip_ref, *refs):
    G = lay.G
    keys, vals = refs[:G], refs[G : 2 * G]
    att_ref, probs_ref, scores = refs[2 * G :]
    rows, zw = q_ref.shape
    length = G * rows
    full = flag_ref[0] > 0
    g = flag_ref[1]
    r0 = lax.broadcasted_iota(jnp.int32, (QB, rows), 0)
    c0 = lax.broadcasted_iota(jnp.int32, (QB, rows), 1)

    def one(i, carry):
        at = pl.multiple_of(i * QB, QB)
        q = q_ref[pl.ds(at, QB), :]
        for k in range(G):
            owner = lax.rem(g - k + G, G)
            s = lax.dot_general(q, keys[k][...], (((1,), (1,)), ((), ())), preferred_element_type=F32)
            off = jnp.clip(length - rows * (g - owner) - at, 0, length)
            s = s * (zw ** (-0.5)) + strip_ref[:, pl.ds(pl.multiple_of(off, LANES), rows)]
            if k == 0:
                pos = r0 + at
                ok = (c0 <= pos) & (full | (pos // 128 == c0 // 128))
            else:
                ok = jnp.logical_and(full, k <= g)
            scores[:, k * rows : (k + 1) * rows] = jnp.where(ok, s, masked_fill)
        s = scores[...]
        p = jnp.exp(s - jnp.max(s, axis=1, keepdims=True))
        p = p * (1.0 / jnp.sum(p, axis=1, keepdims=True))
        total = jnp.zeros((QB, att_ref.shape[1]), F32)
        for k in range(G):
            part = p[:, k * rows : (k + 1) * rows]
            probs_ref[k, pl.ds(at, QB), :] = part
            total += jnp.dot(part.astype(BF16), vals[k][...], preferred_element_type=F32)
        att_ref[pl.ds(at, QB), :] = total
        return carry

    lax.fori_loop(0, rows // QB, one, 0)


def attend_back_kernel(lay, bucket_count, flag_ref, q_ref, da_ref, delta_ref, probs_ref, *refs):
    G = lay.G
    keys, vals = refs[:G], refs[G : 2 * G]
    dq_ref, dk_ref, dv_ref, dko_ref, dvo_ref, bucket_ref, strip, ds_ref, pb_ref = refs[2 * G :]
    rows, zw = q_ref.shape
    length = G * rows
    g = flag_ref[1]
    scale = zw ** (-0.5)
    edges = bucket_edges(bucket_count)
    strip[...] = jnp.zeros(strip.shape, F32)

    def one(i, carry):
        at = pl.multiple_of(i * QB, QB)
        da = da_ref[pl.ds(at, QB), :]
        dq = jnp.zeros((QB, zw), F32)
        for k in range(G):
            owner = lax.rem(g - k + G, G)
            dw = lax.dot_general(da, vals[k][...], (((1,), (1,)), ((), ())), preferred_element_type=F32)
            p = probs_ref[k, pl.ds(at, QB), :]
            ds = p * (dw - delta_ref[pl.ds(at, QB), :])
            off = jnp.clip(length - rows * (g - owner) - at, 0, length)
            strip[:, pl.ds(pl.multiple_of(off, LANES), rows)] += ds
            low = ds.astype(BF16)
            dq += jnp.dot(low, keys[k][...], preferred_element_type=F32)
            ds_ref[k, pl.ds(at, QB), :] = low
            pb_ref[k, pl.ds(at, QB), :] = p.astype(BF16)
        dq_ref[pl.ds(at, QB), :] = dq * scale
        return carry

    lax.fori_loop(0, rows // QB, one, 0)
    for k in range(G):
        dk = lax.dot_general(
            ds_ref[k], q_ref[...], (((0,), (0,)), ((), ())), preferred_element_type=F32
        )
        dv = lax.dot_general(
            pb_ref[k], da_ref[...], (((0,), (0,)), ((), ())), preferred_element_type=F32
        )
        if k == 0:
            dk_ref[...] = dk * scale
            dv_ref[...] = dv
        else:
            dko_ref[k - 1] = (dk * scale).astype(BF16)
            dvo_ref[k - 1] = dv.astype(BF16)
    lag0 = lax.broadcasted_iota(jnp.int32, (QB, LANES), 0) - lax.broadcasted_iota(
        jnp.int32, (QB, LANES), 1
    )
    sums = [jnp.zeros((1, LANES), F32) for k in range(bucket_count)]
    for t in range((length + QB) // LANES):
        base = length - t * LANES
        low, high = base - LANES + 1, base + QB - 1
        if high < 0:
            continue
        value = strip[:, t * LANES : (t + 1) * LANES]
        for k in range(bucket_count):
            top = edges[k + 1] if k + 1 < bucket_count else length
            if edges[k] <= high and top > low:
                lag = lag0 + base
                inside = (lag >= edges[k]) & (lag < top)
                sums[k] = sums[k] + jnp.sum(jnp.where(inside, value, 0.0), axis=0, keepdims=True)
    for k in range(bucket_count):
        bucket_ref[pl.ds(k, 1), :] = sums[k]


def silu_slope(values):
    gate_value = jax.nn.sigmoid(values)
    return gate_value * (1.0 + values * (1.0 - gate_value))


def normalize(seq_rows):
    centered = seq_rows - jnp.mean(seq_rows, axis=-1, keepdims=True)
    inverse = lax.rsqrt(jnp.mean(centered * centered, axis=-1, keepdims=True) + epsilon)
    return (centered * inverse, inverse)


def normalize_back(grad_scaled, unit_rows, inverse):
    return inverse * (
        grad_scaled
        - jnp.mean(grad_scaled, axis=-1, keepdims=True)
        - unit_rows * jnp.mean(grad_scaled * unit_rows, axis=-1, keepdims=True)
    )


def mm(a, b):
    return jnp.dot(a, b, preferred_element_type=F32)


def mm_t(a, b):
    return lax.dot_general(a, b, (((1,), (1,)), ((), ())), preferred_element_type=F32)


def wgrad(a, b):
    return lax.dot_general(a, b, (((0,), (0,)), ((), ())), preferred_element_type=F32).astype(BF16)


def shards(
    lay,
    tokens,
    cotangent,
    stretch_size,
    w_value,
    w_base,
    w_out,
    w_up,
    w_down,
    ema_delta,
    ema_alpha,
    ema_beta,
    ema_gamma,
    ema_omega,
    first_gain,
    second_gain,
    query_gain,
    query_bias,
    key_gain,
    relative_bias,
):
    micro, items, seq_len, D = tokens.shape
    H = ema_delta.shape[1]
    zw = query_gain.shape[0]
    V = w_value.shape[1]
    NB = relative_bias.shape[0]
    length = seq_len * lay.S
    G = lay.G
    R = lay.BL * seq_len
    d_at, b_at = lax.axis_index("dp"), lax.axis_index("seq")
    c_at, y_at = d_at % 2, d_at // 2
    q_at = b_at // lay.Cq
    g_at = (b_at % lay.Cq) * 2 + c_at
    share = ema_delta.shape[0]

    def group_perm(k):
        pairs = []
        for y in range(lay.Y):
            for q in range(lay.Q):
                for g in range(G):
                    t = (g + k) % G
                    src = (y * 2 + g % 2) * lay.S + q * lay.Cq + g // 2
                    dst = (y * 2 + t % 2) * lay.S + q * lay.Cq + t // 2
                    pairs.append((src, dst))
        return pairs

    def shift(value, k):
        return lax.ppermute(value, ("dp", "seq"), group_perm(k % G))

    marks = jnp.broadcast_to(
        stretch_size.reshape(1, -1).astype(BF16), (share, lay.MS)
    )
    used = 4 * H + 3 + lay.MS
    pack = jnp.concatenate(
        [
            ema_delta,
            ema_alpha,
            ema_beta,
            ema_gamma,
            ema_omega[:, None],
            first_gain[:, None],
            second_gain[:, None],
            marks,
            jnp.zeros((share, LANES - used), BF16),
        ],
        1,
    )
    x_blocks, cot_blocks, fulls, rest = forward_all(
        lay, H, tokens, cotangent, (pack, w_value, w_base, w_out, w_up, w_down)
    )
    mixed, ema_tiles, s_in, r_in, table, turned = rest
    mark = fulls[0][y_at, q_at % 2, 0, 0, 0, 4 * H + 3 + q_at // 2]
    flags = jnp.stack([(mark.astype(jnp.int32) == length).astype(jnp.int32), g_at])
    mats = [full.reshape(-1, full.shape[-1]) for full in fulls[1:]]
    mat_value, mat_base, mat_out, mat_up, mat_down = mats
    gain_first = turned[:, 4 * H + 1].reshape(D)
    gain_second = turned[:, 4 * H + 2].reshape(D)
    ema = jnp.moveaxis(ema_tiles, 0, 1).reshape(R, D)

    x_low = x_blocks.reshape(R, D)
    x = x_low.astype(F32)
    grad_out = cot_blocks.reshape(R, D).astype(F32)

    value_pre = mm(x_low, mat_value)
    values = jax.nn.silu(value_pre).astype(BF16)
    base = mm(mixed, mat_base)
    z_pre = base[:, :zw]
    reset_pre = base[:, zw : zw + V]
    cand_pre = base[:, zw + V : zw + V + D]
    update_pre = base[:, zw + V + D :]
    shared = jax.nn.silu(z_pre)
    queries = (shared * query_gain + query_bias).astype(BF16)
    keys = (shared * key_gain).astype(BF16)
    keys_all = [keys] + [shift(keys, k) for k in range(1, G)]
    vals_all = [values] + [shift(values, k) for k in range(1, G)]
    strip = call(
        functools.partial(bias_kernel, length, NB),
        jax.ShapeDtypeStruct((QB, length + R), F32),
        (relative_bias,),
        specs=[SM],
        name="bias_strip",
    )
    attended, probs = call(
        functools.partial(attend_kernel, lay),
        [jax.ShapeDtypeStruct((R, V), F32), jax.ShapeDtypeStruct((G, R, R), F32)],
        (flags, queries, strip, *keys_all, *vals_all),
        specs=[SM] + [VM] * (2 + 2 * G),
        scratch=[pltpu.VMEM((QB, length), F32)],
        name="attend",
    )
    reset_gate = jax.nn.silu(reset_pre)
    update = jax.nn.sigmoid(update_pre)
    gated = (attended * reset_gate).astype(BF16)
    cand_in = cand_pre + mm(gated, mat_out)
    candidate = jax.nn.silu(cand_in)
    first_sum = x + update * (candidate - x)
    unit_first, inverse_first = normalize(first_sum)
    normed = unit_first * gain_first
    normed_low = normed.astype(BF16)
    hidden_pre = mm(normed_low, mat_up)
    hidden = jax.nn.silu(hidden_pre).astype(BF16)
    second_sum = normed + mm(hidden, mat_down)
    unit_second, inverse_second = normalize(second_sum)
    block_out = (unit_second * gain_second).astype(BF16)

    grad_gain_second = jnp.sum(grad_out * unit_second, axis=0)
    grad_second = normalize_back(grad_out * gain_second, unit_second, inverse_second)
    branch = grad_second.astype(BF16)
    grad_mat_down = wgrad(hidden, branch)
    hidden_grad = (mm_t(branch, mat_down) * silu_slope(hidden_pre)).astype(BF16)
    grad_mat_up = wgrad(normed_low, hidden_grad)
    grad_normed = grad_second + mm_t(hidden_grad, mat_up)
    grad_gain_first = jnp.sum(grad_normed * unit_first, axis=0)
    grad_first = normalize_back(grad_normed * gain_first, unit_first, inverse_first)
    cand_low = (grad_first * update * silu_slope(cand_in)).astype(BF16)
    grad_mat_out = wgrad(gated, cand_low)
    grad_gated = mm_t(cand_low, mat_out)
    att_low = (grad_gated * reset_gate).astype(BF16)
    grad_reset = grad_gated * attended * silu_slope(reset_pre)
    grad_update = grad_first * (candidate - x) * update * (1.0 - update)
    delta = jnp.sum(att_low.astype(F32) * attended, axis=1, keepdims=True)
    dq, grad_keys, grad_values, dk_out, dv_out, buckets = call(
        functools.partial(attend_back_kernel, lay, NB),
        [
            jax.ShapeDtypeStruct((R, zw), F32),
            jax.ShapeDtypeStruct((R, zw), F32),
            jax.ShapeDtypeStruct((R, V), F32),
            jax.ShapeDtypeStruct((G - 1, R, zw), BF16),
            jax.ShapeDtypeStruct((G - 1, R, V), BF16),
            jax.ShapeDtypeStruct((NB, LANES), F32),
        ],
        (flags, queries, att_low, delta, probs, *keys_all, *vals_all),
        specs=[SM] + [VM] * (4 + 2 * G),
        scratch=[
            pltpu.VMEM((QB, length + R), F32),
            pltpu.VMEM((G, R, R), BF16),
            pltpu.VMEM((G, R, R), BF16),
        ],
        name="attend_back",
    )
    for k in range(1, G):
        grad_keys = grad_keys + shift(dk_out[k - 1], -k).astype(F32)
        grad_values = grad_values + shift(dv_out[k - 1], -k).astype(F32)
    grad_query_gain = jnp.sum(dq * shared, axis=0)
    grad_query_bias = jnp.sum(dq, axis=0)
    grad_key_gain = jnp.sum(grad_keys * shared, axis=0)
    grad_relative = jnp.sum(buckets, axis=1)
    grad_z = (dq * query_gain + grad_keys * key_gain) * silu_slope(z_pre)
    base_low = jnp.concatenate(
        [grad_z.astype(BF16), grad_reset.astype(BF16), cand_low, grad_update.astype(BF16)], 1
    )
    grad_mat_base = wgrad(mixed, base_low)
    grad_ema = mm_t(base_low, mat_base) * silu_slope(ema)
    value_low = (grad_values * silu_slope(value_pre)).astype(BF16)
    grad_mat_value = wgrad(x_low, value_low)
    pre = grad_first * (1.0 - update) + mm_t(value_low, mat_value)
    gains = jnp.concatenate(
        [grad_gain_first[None], grad_gain_second[None], jnp.zeros((6, D), F32)]
    )
    small = jnp.zeros((8, LANES), F32)
    small = small.at[0, :zw].set(grad_query_gain)
    small = small.at[1, :zw].set(grad_query_bias)
    small = small.at[2, :zw].set(grad_key_gain)
    small = small.at[3, :NB].set(grad_relative)
    shape = (lay.Y, 2, lay.Z, lay.X)

    def split(grad):
        return grad.reshape(shape + (-1, grad.shape[-1]))

    reduced, small_total, moved = backward_all(
        lay,
        H,
        [
            split(grad_mat_down),
            split(grad_mat_up),
            split(grad_mat_out),
            split(grad_mat_base),
            split(grad_mat_value),
        ],
        small,
        x_blocks,
        grad_ema,
        pre,
        gains,
        table,
        turned,
        s_in,
        r_in,
        block_out.reshape(lay.BL, seq_len, D),
        share,
    )
    own = reduced[5]
    corr, lagged = own[:, :H], own[:, H : 2 * H]
    p = jax.nn.sigmoid(ema_delta.astype(F32))
    a = jax.nn.sigmoid(ema_alpha.astype(F32))
    beta = ema_beta.astype(F32)
    read = ema_gamma.astype(F32) * (H ** (-0.5))
    q_grad = read * p * beta * lagged
    return (
        moved[0],
        moved[1].astype(F32),
        reduced[4],
        reduced[3],
        reduced[2],
        reduced[1],
        reduced[0],
        (read * beta * corr - a * q_grad) * p * (1.0 - p),
        -p * q_grad * a * (1.0 - a),
        p * read * corr,
        p * beta * corr * (H ** (-0.5)),
        own[:, 2 * H],
        own[:, 2 * H + 1],
        own[:, 2 * H + 2],
        small_total[0, :zw],
        small_total[1, :zw],
        small_total[2, :zw],
        small_total[3, :NB],
    )


def solution(mesh):
    rows = P(None, "dp", "seq", None)
    part2, part1 = P(("dp", "seq"), None), P(("dp", "seq"))
    in_specs = (rows, rows, P(None, "dp")) + (part2,) * 9 + (part1,) * 3 + (P(),) * 4
    out_specs = (rows, rows) + (part2,) * 9 + (part1,) * 3 + (P(),) * 4

    def whole(tokens, *rest):
        micro, seqs = tokens.shape[:2]
        lay = Layout(mesh.shape["dp"], mesh.shape["seq"], micro, seqs // mesh.shape["dp"])
        return jax.shard_map(
            functools.partial(shards, lay),
            mesh=mesh,
            in_specs=in_specs,
            out_specs=out_specs,
            check_vma=False,
        )(tokens, *rest)

    return whole
```

```python
import functools

import jax
import jax.numpy as jnp
import numpy as np
from jax import lax
from jax.experimental import pallas as pl
from jax.experimental.pallas import tpu as pltpu
from jax.sharding import PartitionSpec as P

epsilon = 1e-05
masked_fill = -1e30
MESH = pl.DeviceIdType.MESH
ANY = pl.BlockSpec(memory_space=pl.ANY)
VM = pl.BlockSpec(memory_space=pltpu.VMEM)
SM = pl.BlockSpec(memory_space=pltpu.SMEM)
F32 = jnp.float32
BF16 = jnp.bfloat16
SEG = 8
LANES = 128


def bucket_edges(bucket_count):
    edge_list = [0]
    middle = bucket_count // 2
    for number in range(1, bucket_count):
        edge_list.append(number if number < middle else int(middle * 2 ** ((number - middle) / 2)))
    return edge_list


class Layout:
    def __init__(self, dp, seq, micro, items):
        self.dp, self.S = dp, seq
        self.C = 2
        self.Y = dp // 2
        self.X = min(self.Y, seq)
        self.Z = seq // self.X
        self.items = items
        self.MS = micro * items
        self.Q = 2 * self.MS
        self.Cq = seq // self.Q
        self.G = 2 * self.Cq
        self.BL = seq // self.G

    def here(self):
        d, b = lax.axis_index("dp"), lax.axis_index("seq")
        return d // 2, d % 2, b // self.X, b % self.X, b


class Wire:
    def __init__(self, lay, send, recv):
        self.lay, self.send, self.recv, self.count = lay, send, recv, 0
        self.sent = []

    def to(self, y, c, z, x):
        return (y * 2 + c, z * self.lay.X + x)

    def start(self, src, dst, target):
        number = self.count
        self.count += 1
        copy = pltpu.make_async_remote_copy(
            src_ref=src,
            dst_ref=dst,
            send_sem=self.send.at[number],
            recv_sem=self.recv.at[number],
            device_id=target,
            device_id_type=MESH,
        )
        copy.start()
        self.sent.append(copy)
        return copy

    def finish(self):
        for copy in self.sent:
            copy.wait_send()


def greet(lay):
    y, c, z, x, b = lay.here()
    barrier = pltpu.get_barrier_semaphore()
    plane = 2 * lay.S

    def one(k, carry):
        other = (c * lay.S + b + k) % plane
        pl.semaphore_signal(
            barrier, inc=1, device_id=(y * 2 + other // lay.S, other % lay.S), device_id_type=MESH
        )
        return carry

    lax.fori_loop(1, plane, one, 0)
    for k in range(1, lay.Y):
        pl.semaphore_signal(
            barrier, inc=1, device_id=(((y + k) % lay.Y) * 2 + c, b), device_id_type=MESH
        )
    pl.semaphore_wait(barrier, plane - 1 + lay.Y - 1)


ALPHA = 0.5
AHEAD = 2
LAG = 2
ORDER = 1
LIMIT = 800


def half_columns(columns):
    return max(1, int(columns // LANES * ALPHA + 0.5)) * LANES


def reshard_in(lay, sources, targets, send, recv, local):
    y, c, z, x, b = lay.here()
    g = b // lay.BL
    slot = b % lay.BL
    qm = b // lay.Cq
    gm = (b % lay.Cq) * 2 + c

    def begin(n):
        for source, target in ((sources[n], targets[n]),):
            for ms in range(lay.MS):
                seq_to = (ms * 2 + c) * lay.Cq + g // 2
                mine = jnp.logical_and(seq_to == b, g % 2 == c)
                block = source.at[ms // lay.items, ms % lay.items]

                @pl.when(jnp.logical_not(mine))
                def _():
                    pltpu.make_async_remote_copy(
                        src_ref=block,
                        dst_ref=target.at[slot],
                        send_sem=send.at[n, ms],
                        recv_sem=recv.at[n, slot],
                        device_id=(y * 2 + g % 2, seq_to),
                        device_id_type=MESH,
                    ).start()

                @pl.when(mine)
                def _():
                    pltpu.make_async_copy(block, target.at[slot], local.at[n]).start()

    def wait(n):
        source, target = sources[n], targets[n]
        for ms in range(lay.MS):
            seq_to = (ms * 2 + c) * lay.Cq + g // 2
            mine = jnp.logical_and(seq_to == b, g % 2 == c)
            block = source.at[ms // lay.items, ms % lay.items]

            @pl.when(jnp.logical_not(mine))
            def _():
                pltpu.make_async_remote_copy(
                    src_ref=block,
                    dst_ref=target.at[slot],
                    send_sem=send.at[n, ms],
                    recv_sem=recv.at[n, slot],
                    device_id=(y * 2 + g % 2, seq_to),
                    device_id_type=MESH,
                ).wait_send()

            @pl.when(mine)
            def _():
                pltpu.make_async_copy(block, target.at[slot], local.at[n]).wait()

        for j in range(lay.BL):
            from_b = gm * lay.BL + j
            own = jnp.logical_and(from_b == b, qm % 2 == c)

            @pl.when(jnp.logical_not(own))
            def _():
                pltpu.make_async_remote_copy(
                    src_ref=source.at[0, 0],
                    dst_ref=target.at[j],
                    send_sem=send.at[n, 0],
                    recv_sem=recv.at[n, j],
                    device_id=(y * 2 + qm % 2, from_b),
                    device_id_type=MESH,
                ).wait_recv()

    return begin, wait


def reshard_out(lay, sources, targets, send, recv, local):
    y, c, z, x, b = lay.here()
    g = b // lay.BL
    qm = b // lay.Cq
    gm = (b % lay.Cq) * 2 + c
    ms_to = qm // 2
    m_to, s_to = ms_to // lay.items, ms_to % lay.items

    def copies(n, j):
        from_b = gm * lay.BL + j
        own = jnp.logical_and(from_b == b, qm % 2 == c)
        remote = pltpu.make_async_remote_copy(
            src_ref=sources[n].at[j],
            dst_ref=targets[n].at[m_to, s_to],
            send_sem=send.at[n, j],
            recv_sem=recv.at[n, ms_to],
            device_id=(y * 2 + qm % 2, from_b),
            device_id_type=MESH,
        )
        near = pltpu.make_async_copy(sources[n].at[j], targets[n].at[m_to, s_to], local.at[n])
        return own, remote, near

    def begin(n):
        for j in range(lay.BL):
            own, remote, near = copies(n, j)
            pl.when(jnp.logical_not(own))(remote.start)
            pl.when(own)(near.start)

    def wait(n):
        for j in range(lay.BL):
            own, remote, near = copies(n, j)
            pl.when(jnp.logical_not(own))(remote.wait_send)
            pl.when(own)(near.wait)
        for ms in range(lay.MS):
            seq_at = (ms * 2 + c) * lay.Cq + g // 2
            own = jnp.logical_and(seq_at == b, g % 2 == c)

            @pl.when(jnp.logical_not(own))
            def _():
                pltpu.make_async_remote_copy(
                    src_ref=sources[n].at[0],
                    dst_ref=targets[n].at[ms // lay.items, ms % lay.items],
                    send_sem=send.at[n, 0],
                    recv_sem=recv.at[n, ms],
                    device_id=(y * 2 + g % 2, seq_at),
                    device_id_type=MESH,
                ).wait_recv()

    return begin, wait


def chunks_of(shapes, limit):
    result = []
    for n, shape in enumerate(shapes):
        tiles = shape[-1] // LANES
        cuts = max(1, -(-shape[0] * shape[-1] // limit))
        at = 0
        for cut in range(cuts):
            width = (tiles - at) // (cuts - cut) if cut == cuts - 1 else -(-(tiles - at) // (cuts - cut))
            result.append((n, at * LANES, width * LANES))
            at += width
    return result


def column_blocks(columns, most=768):
    cuts = -(-columns // most)
    while (columns // LANES) % cuts:
        cuts += 1
    width = columns // cuts
    return [(i * width, width) for i in range(cuts)]


def weight_block(full, stage, sem, at, width):
    target = stage.at[:, :, :, :, :, pl.ds(0, width)]
    copy = pltpu.make_async_copy(full.at[:, :, :, :, :, pl.ds(at, width)], target, sem)
    copy.start()
    copy.wait()
    block = stage[:, :, :, :, :, 0:width]
    return block.reshape(-1, width)


def gather_kernel(lay, count, chunks, refs):
    tok, cot = refs[0], refs[1]
    shards = refs[2 : 2 + count]
    tok_out, cot_out = refs[2 + count], refs[3 + count]
    fulls = refs[4 + count : 4 + 2 * count]
    send, recv, local, t_send, t_recv, t_local = refs[4 + 2 * count :]
    y, c, z, x, b = lay.here()
    X, Y, Z = lay.X, lay.Y, lay.Z
    greet(lay)
    wire = Wire(lay, send, recv)
    begin, wait = reshard_in(lay, (tok, cot), (tok_out, cot_out), t_send, t_recv, t_local)
    total = len(chunks)
    owns = []
    for i, (n, at, width) in enumerate(chunks):
        cols = pl.ds(at, width)
        copy = pltpu.make_async_copy(
            shards[n].at[:, cols], fulls[n].at[y, c, z, x, :, cols], local.at[i]
        )
        copy.start()
        owns.append(copy)
    arrived = [dict() for i in range(total)]

    def stage_z(i):
        n, at, width = chunks[i]
        cols = pl.ds(at, width)
        arrived[i]["z"] = [
            wire.start(
                shards[n].at[:, cols],
                fulls[n].at[y, c, z, x, :, cols],
                wire.to(y, c, (z + k) % Z, x),
            )
            for k in range(1, Z)
        ]

    def parts(i):
        n, at, width = chunks[i]
        left = half_columns(width)
        result = [(at, left)]
        if left < width:
            result.append((at + left, width - left))
        return result

    def to_core(i, block):
        arrived[i].setdefault("core", []).append(wire.start(block, block, wire.to(y, 1 - c, z, x)))

    def stage_one(i):
        owns[i].wait()
        for copy in arrived[i]["z"]:
            copy.wait_recv()
        n, first, columns = chunks[i]
        full = fulls[n]
        for half, (at, width) in enumerate(parts(i)):
            block = full.at[y, c, :, x, :, pl.ds(at, width)]
            if half == 0:
                arrived[i]["x0"] = [
                    wire.start(block, block, wire.to(y, c, z, (x + k) % X)) for k in range(1, X)
                ]
            else:
                arrived[i]["y1"] = [
                    wire.start(block, block, wire.to((y + k) % Y, c, z, x)) for k in range(1, Y)
                ]
        to_core(i, full.at[y, c, :, x, :, pl.ds(first, columns)])

    def stage_two(i):
        full = fulls[chunks[i][0]]
        for half, (at, width) in enumerate(parts(i)):
            cols = pl.ds(at, width)
            if half == 0:
                for copy in arrived[i]["x0"]:
                    copy.wait_recv()
                block = full.at[y, c, :, :, :, cols]
                arrived[i]["y0"] = [
                    wire.start(block, block, wire.to((y + k) % Y, c, z, x)) for k in range(1, Y)
                ]
                for k in range(1, X):
                    to_core(i, full.at[y, c, :, (x + X - k) % X, :, cols])
            else:
                for copy in arrived[i]["y1"]:
                    copy.wait_recv()
                block = full.at[:, c, :, x, :, cols]
                arrived[i]["x1"] = [
                    wire.start(block, block, wire.to(y, c, z, (x + k) % X)) for k in range(1, X)
                ]
                for k in range(1, Y):
                    to_core(i, full.at[(y + Y - k) % Y, c, :, x, :, cols])

    def stage_three(i):
        full = fulls[chunks[i][0]]
        for half, (at, width) in enumerate(parts(i)):
            cols = pl.ds(at, width)
            if half == 0:
                for k, copy in enumerate(arrived[i]["y0"], 1):
                    copy.wait_recv()
                    to_core(i, full.at[(y + Y - k) % Y, c, :, :, :, cols])
            else:
                for k, copy in enumerate(arrived[i]["x1"], 1):
                    copy.wait_recv()
                    to_core(i, full.at[:, c, :, (x + X - k) % X, :, cols])

    def finish():
        for i in range(total):
            for copy in arrived[i]["core"]:
                copy.wait_recv()
        wire.finish()

    def gathered(n):
        for i in range(total):
            if chunks[i][0] == n:
                for copy in arrived[i].pop("core"):
                    copy.wait_recv()
                arrived[i]["core"] = []

    return wire, (begin, wait), (stage_z, stage_one, stage_two, stage_three), gathered, finish


def group_copies(lay, send, recv, source, inbox, forward):
    y, c, z, x, b = lay.here()
    q = b // lay.Cq
    g = (b % lay.Cq) * 2 + c
    copies = []
    for k in range(1, lay.G):
        t = (g + (k if forward else lay.G - k)) % lay.G
        copies.append(
            pltpu.make_async_remote_copy(
                src_ref=source,
                dst_ref=inbox.at[k - 1],
                send_sem=send.at[k - 1],
                recv_sem=recv.at[k - 1],
                device_id=(y * 2 + t % 2, q * lay.Cq + t // 2),
                device_id_type=MESH,
            )
        )
    return copies, g


def to_tiles(low, tiles, r0, rows):
    for t in range(tiles.shape[0]):
        tiles[t, pl.ds(r0, rows), :] = low[:, t * LANES : (t + 1) * LANES].astype(F32)


def make_tables(lay, H, pack, raw, table, turned):
    r = pack.shape[4]
    total = lay.Y * 2 * lay.Z * lay.X

    def one(i, carry):
        block = pack[i // (2 * lay.Z * lay.X), i // (lay.Z * lay.X) % 2, i // lay.X % lay.Z, i % lay.X]
        raw[pl.ds(i * r, r), :] = block.astype(F32)
        return carry

    lax.fori_loop(0, total, one, 0)
    for t in range(table.shape[0]):
        v = raw[t * LANES : (t + 1) * LANES, :].T
        turned[t] = v
        leak = jax.nn.sigmoid(v[:H])
        decay = 1.0 - leak * jax.nn.sigmoid(v[H : 2 * H])
        table[t, :H] = decay
        table[t, H : 2 * H] = jnp.log(decay)
        table[t, 2 * H : 3 * H] = leak * v[2 * H : 3 * H] * v[3 * H : 4 * H] * (H ** (-0.5))


def carry_in(lay, H, rows, g, inbox, table, inc, t, later):
    log = table[t, H : 2 * H]
    state = jnp.zeros((H, LANES), F32)
    slope = jnp.zeros((H, LANES), F32)
    for k in range(1, lay.G):
        span = (k - 1) * rows
        valid = (g + k < lay.G) if later else (k <= g)
        s_part = inbox[k - 1, t, :H]
        r_part = s_part * 0.0 if later else inbox[k - 1, t, H : 2 * H]
        if span:
            power = jnp.exp(span * log)
            r_part = power * r_part + (span * jnp.exp((span - 1) * log)) * s_part
            s_part = power * s_part
        state = state + jnp.where(valid, s_part, 0.0)
        slope = slope + jnp.where(valid, r_part, 0.0)
    inc[t, :H] = state
    if not later:
        inc[t, H : 2 * H] = slope


def forward_kernel(lay, count, chunks, H, refs):
    n_in, n_out = 2 + count, 15 + count
    ins = refs[:n_in]
    query_gain, query_bias, key_gain, relative = refs[n_in : n_in + 4]
    refs = refs[n_in + 4 :]
    outs, scratch = refs[:n_out], refs[n_out:]
    tok_out, cot_out = outs[0], outs[1]
    fulls = outs[2 : 2 + count]
    mixed, ema, si, ri, table, turned = outs[2 + count : 8 + count]
    value_pre, base, queries, keys, vals, probs, attended = outs[8 + count :]
    sems, work = scratch[:6], scratch[6:]
    xt, pack, raw, s_end, r_end, mine, inbox, inc, stage, strip, scores, load, c_send, c_recv = work
    wire, (begin, wait), stages, gathered, finish = gather_kernel(
        lay, count, chunks, ins + (tok_out, cot_out) + tuple(fulls) + sems
    )
    stage_z, stage_one, stage_two, stage_three = stages
    total = len(chunks)
    rows = xt.shape[1]
    tiles = xt.shape[0]
    copies, g = group_copies(lay, c_send.at[0], c_recv.at[0], mine, inbox, True)
    others = pl.ds(1, lay.G - 1)
    vals_copies, g = group_copies(
        lay, c_send.at[1], c_recv.at[1], vals.at[0], vals.at[others], True
    )
    keys_copies, g = group_copies(
        lay, c_send.at[2], c_recv.at[2], keys.at[0], keys.at[others], True
    )
    width = tok_out.shape[2]
    zw = queries.shape[1]

    def value(at, cols):
        v = mm(tok_out[...].reshape(rows, width), weight_block(fulls[1], stage, load, at, cols))
        value_pre[:, at : at + cols] = v
        vals[0, :, at : at + cols] = (v * jax.nn.sigmoid(v)).astype(BF16)

    def send_values():
        for copy in vals_copies:
            copy.start()

    def bias():
        bias_kernel(lay.G * rows, relative.shape[0], relative, strip)

    def base_out(at, cols):
        base[:, at : at + cols] = mm(mixed[...], weight_block(fulls[2], stage, load, at, cols))

    def send_keys():
        z_pre = base[:, :zw]
        shared = z_pre * jax.nn.sigmoid(z_pre)
        queries[...] = (shared * query_gain[...] + query_bias[...]).astype(BF16)
        keys[0] = (shared * key_gain[...]).astype(BF16)
        for copy in keys_copies:
            copy.start()

    def keys_here():
        for copy in keys_copies + vals_copies:
            copy.wait()

    def attend(part):
        y, c, z, x, b = lay.here()
        q_at = b // lay.Cq
        first = ((y * 2 + q_at % 2) * lay.Z * lay.X) * pack.shape[4]
        marks = raw[pl.ds(first, 1), :]
        lane = lax.broadcasted_iota(jnp.int32, (1, LANES), 1)
        mark = jnp.sum(
            jnp.where(lane == 4 * H + 3 + q_at // 2, marks, 0.0), axis=1, keepdims=True
        )
        far = jnp.where(mark == float(lay.G * rows), 0.0, masked_fill)
        attend_body(lay, g, far, queries, strip, keys, vals, attended, probs, scores, part)

    def tables():
        gathered(0)
        copy = pltpu.make_async_copy(fulls[0], pack, load)
        copy.start()
        copy.wait()
        make_tables(lay, H, pack, raw, table, turned)

    def tokens():
        wait(0)
        for j in range(lay.BL):
            to_tiles(tok_out[j], xt, j * (rows // lay.BL), rows // lay.BL)

    def ends(first, last):
        def one(t, carry):
            ema_ends_kernel(H, xt.at[t], table.at[t], s_end.at[t], r_end.at[t])
            for h in range(H):
                mine[t, pl.ds(h, 1), :] = s_end[t, h, SEG - 1 : SEG, :]
                mine[t, pl.ds(H + h, 1), :] = r_end[t, h, SEG - 1 : SEG, :]
            return carry

        lax.fori_loop(first, last, one, 0)

    def exchange():
        for copy in copies:
            copy.start()

    def carries():
        for copy in copies:
            copy.wait()
        for t in range(tiles):
            carry_in(lay, H, rows, g, inbox, table, inc, t, False)

    def out(first, last):
        def one(t, carry):
            ema_out_kernel(
                H, xt.at[t], table.at[t], turned.at[t, pl.ds(4 * H, 1)], s_end.at[t], r_end.at[t],
                inc.at[t], ema.at[t], si.at[t], ri.at[t],
            )
            return carry

        lax.fori_loop(first, last, one, 0)
        for t in range(first, last):
            for r0 in range(0, rows, 128):
                v = ema[t, pl.ds(r0, 128), :]
                mixed[pl.ds(r0, 128), t * LANES : (t + 1) * LANES] = (
                    v * jax.nn.sigmoid(v)
                ).astype(BF16)

    steps = [lambda: begin(0)]
    last = {}
    for i in range(min(AHEAD, total)):
        steps.append(functools.partial(stage_z, i))
    for turn in range(total + 2 * LAG):
        if 0 <= turn - 2 * LAG < total:
            last[chunks[turn - 2 * LAG][0]] = len(steps)
            steps.append(functools.partial(stage_three, turn - 2 * LAG))
        if 0 <= turn - LAG < total:
            steps.append(functools.partial(stage_two, turn - LAG))
        if turn < total:
            steps.append(functools.partial(stage_one, turn))
        if turn + AHEAD < total:
            steps.append(functools.partial(stage_z, turn + AHEAD))
        if turn == PLAN[5]:
            steps.append(lambda: begin(1))
    base_blocks = column_blocks(base.shape[1])
    todo = [(last[0] + PLAN[0], tables), (PLAN[1], tokens)]
    todo += [(0, functools.partial(ends, t, t + 1)) for t in range(tiles)]
    todo += [(0, exchange)]
    todo += [(last[1] + PLAN[2], lambda: gathered(1))]
    todo += [(0, functools.partial(value, *block)) for block in column_blocks(vals.shape[2])]
    todo += [(0, send_values), (0, carries)]
    todo += [(0, functools.partial(out, t, t + 1)) for t in range(tiles)]
    todo += [(0, bias), (last[2] + PLAN[3], lambda: gathered(2))]
    todo += [(0, functools.partial(base_out, *base_blocks[0])), (0, send_keys)]
    todo += [(0, functools.partial(base_out, *block)) for block in base_blocks[1:]]
    todo += [(0, keys_here)]
    todo += [(0, functools.partial(attend, part)) for part in range(rows // QB)]
    interleave(steps, todo, PLAN[6])
    finish()
    wait(1)


def interleave(steps, todo, most):
    todo = list(todo)
    done = set()

    def run():
        first, piece, name = (todo.pop(0) + (None,))[:3]
        piece()
        done.add(name)

    for number, step in enumerate(steps):
        step, needs = step if isinstance(step, tuple) else (step, None)
        while needs is not None and needs not in done:
            run()
        step()
        for i in range(most):
            if todo and todo[0][0] <= number:
                run()
    while todo:
        run()


PLAN = (1, 12, 1, 1, 0, 9, 1)


def forward_all(lay, H, tokens, cotangent, shards, query_gain, query_bias, key_gain, relative):
    count = len(shards)
    chunks = chunks_of([shard.shape for shard in shards], shards[0].shape[0] * LIMIT)
    micro, items, rows, width = tokens.shape
    per = (lay.Z - 1) + 2 * (lay.X - 1 + lay.Y - 1) + 1 + 2 * (lay.X - 1 + lay.Y - 1)
    blocks = jax.ShapeDtypeStruct((lay.BL, rows, width), BF16)
    fulls = [
        jax.ShapeDtypeStruct((lay.Y, 2, lay.Z, lay.X) + shard.shape, shard.dtype)
        for shard in shards
    ]
    T, R = width // LANES, lay.BL * rows
    state = (T, H, SEG, LANES)
    outs = [blocks, blocks] + fulls
    outs += [
        jax.ShapeDtypeStruct((R, width), BF16),
        jax.ShapeDtypeStruct((T, R, LANES), F32),
        jax.ShapeDtypeStruct(state, F32),
        jax.ShapeDtypeStruct(state, F32),
        jax.ShapeDtypeStruct((T, 3 * H, LANES), F32),
        jax.ShapeDtypeStruct((T, LANES, LANES), F32),
    ]
    V, cols, zw, G = shards[1].shape[1], shards[2].shape[1], query_gain.shape[1], lay.G
    outs += [
        jax.ShapeDtypeStruct((R, V), F32),
        jax.ShapeDtypeStruct((R, cols), F32),
        jax.ShapeDtypeStruct((R, zw), BF16),
        jax.ShapeDtypeStruct((G, R, zw), BF16),
        jax.ShapeDtypeStruct((G, R, V), BF16),
        jax.ShapeDtypeStruct((G, R, R), BF16),
        jax.ShapeDtypeStruct((R, V), F32),
    ]

    def body(*refs):
        forward_kernel(lay, count, chunks, H, refs)

    result = pl.pallas_call(
        body,
        out_shape=outs,
        in_specs=[ANY] * (2 + count) + [VM] * 3 + [SM],
        out_specs=[VM] + [ANY] * (1 + count) + [VM] * 13,
        scratch_shapes=[
            pltpu.SemaphoreType.DMA((len(chunks) * per,)),
            pltpu.SemaphoreType.DMA((len(chunks) * per,)),
            pltpu.SemaphoreType.DMA((len(chunks),)),
            pltpu.SemaphoreType.DMA((2, lay.MS)),
            pltpu.SemaphoreType.DMA((2, lay.BL)),
            pltpu.SemaphoreType.DMA((2,)),
            pltpu.VMEM((T, R, LANES), F32),
            pltpu.VMEM(fulls[0].shape, fulls[0].dtype),
            pltpu.VMEM((width, LANES), F32),
            pltpu.VMEM(state, F32),
            pltpu.VMEM(state, F32),
            pltpu.VMEM((T, 2 * H, LANES), F32),
            pltpu.VMEM((lay.G - 1, T, 2 * H, LANES), F32),
            pltpu.VMEM((T, 2 * H, LANES), F32),
            pltpu.VMEM((lay.Y, 2, lay.Z, lay.X, shards[1].shape[0], 768), BF16),
            pltpu.VMEM((QB, (G + 1) * R), F32),
            pltpu.VMEM((QB, G * R), F32),
            pltpu.SemaphoreType.DMA,
            pltpu.SemaphoreType.DMA((3, lay.G - 1)),
            pltpu.SemaphoreType.DMA((3, lay.G - 1)),
        ],
        compiler_params=pltpu.CompilerParams(
            collective_id=0, has_side_effects=True, vmem_limit_bytes=58 * 2**20
        ),
        name="forward_all",
    )(tokens, cotangent, *shards, query_gain, query_bias, key_gain, relative)
    return result[0], result[1], result[2 : 2 + count], result[2 + count :]


def add_blocks(total, index, extra, extra_index, counts, width_at):
    size = int(np.prod(counts)) if counts else 1

    def one(i, carry):
        places = []
        for extent in reversed(counts):
            places.insert(0, i % extent)
            i = i // extent
        a, e = index(*places), extra_index(*places)
        summed = total[a].astype(F32) + extra[e].astype(F32)
        total[a] = summed.astype(total.dtype)
        return carry

    lax.fori_loop(0, size, one, 0)


def scatter_kernel(lay, H, NB, chunks, ins, outs, scratch):
    (
        grads, x_low, d_in, d_att, delta, queries, keys, vals, probs, z_pre, gains_small, mixed, ema,
        base_rest, value_pre, w_base, w_value, pre, gains, table, turned, si, ri, block_out,
    ) = ins
    results, small_out, outs_to, made, dvo, dvi = outs
    bufs, own = scratch[: 6 * len(chunks)], scratch[6 * len(chunks) :]
    small_acc, small_recv, send, recv, local, t_send, t_recv, t_local = own[:8]
    xt, dt, dx, sums, flat, split, l_end, mine, inbox, inc, gx, c_send, c_recv = own[8:21]
    stage, vstage, bstage, pstage, ds, strip, dq, dko, dki, zlow, vlow, mixed_acc, x_acc, load = own[21:35]
    halves = own[35:]
    grads = grads + made + (split,)
    y, c, z, x, b = lay.here()
    X, Y, Z = lay.X, lay.Y, lay.Z
    greet(lay)
    wire = Wire(lay, send, recv)
    begin, wait = reshard_out(lay, (block_out, gx), outs_to, t_send, t_recv, t_local)
    total = len(chunks)
    arrived = [dict() for i in range(total)]

    def buf(i, name):
        return bufs[6 * i + ("acc", "x0", "y1", "y0", "x1", "z").index(name)]

    def parts(i):
        n, at, width = chunks[i]
        left = half_columns(width)
        result = [(0, left)]
        if left < width:
            result.append((left, width - left))
        return result

    def own_half(i):
        n, at, width = chunks[i]
        if n == len(grads) - 1:
            return None
        source = grads[n].at[:, c, :, :, :, pl.ds(at, width)]
        return pltpu.make_async_copy(source, half_of(i), local.at[i])

    def half_of(i):
        n, at, width = chunks[i]
        r = grads[n].shape[4]
        room = [h for h in halves if h.shape[4] == r][0]
        return room.at[i % 2, :, :, :, :, pl.ds(0, width)]

    def stage_core(i):
        n, at, width = chunks[i]
        arrived[i]["core"] = wire.start(
            grads[n].at[:, 1 - c, :, :, :, pl.ds(at, width)],
            buf(i, "acc"),
            wire.to(y, 1 - c, z, x),
        )

    def stage_one(i):
        n, first, columns = chunks[i]
        acc = buf(i, "acc")
        near = own_half(i)
        if near is not None:
            near.start()
            near.wait()
        arrived[i]["core"].wait_recv()
        if near is not None:
            mine_half = half_of(i)
            add_blocks(acc, lambda *p: p, mine_half, lambda *p: p, (Y, Z, X), None)
        else:
            add_blocks(
                acc, lambda *p: p, split, lambda p, q, s: (p, c, q, s), (Y, Z, X), None
            )
        for half, (at, width) in enumerate(parts(i)):
            cols = pl.ds(at, width)
            if half == 0:
                arrived[i]["x0"] = [
                    wire.start(
                        acc.at[:, :, (x + k) % X, :, cols],
                        buf(i, "x0").at[k - 1],
                        wire.to(y, c, z, (x + k) % X),
                    )
                    for k in range(1, X)
                ]
            else:
                arrived[i]["y1"] = [
                    wire.start(
                        acc.at[(y + k) % Y, :, :, :, cols],
                        buf(i, "y1").at[k - 1],
                        wire.to((y + k) % Y, c, z, x),
                    )
                    for k in range(1, Y)
                ]

    def stage_two(i):
        acc = buf(i, "acc")
        for half, (at, width) in enumerate(parts(i)):
            cols = slice(at, at + width)
            view = pl.ds(at, width)
            if half == 0:
                for k, copy in enumerate(arrived[i]["x0"]):
                    copy.wait_recv()
                    add_blocks(
                        acc,
                        lambda p, q: (p, q, x, slice(None), cols),
                        buf(i, "x0"),
                        lambda p, q: (k, p, q),
                        (Y, Z),
                        None,
                    )
                arrived[i]["y0"] = [
                    wire.start(
                        acc.at[(y + k) % Y, :, x, :, view],
                        buf(i, "y0").at[k - 1],
                        wire.to((y + k) % Y, c, z, x),
                    )
                    for k in range(1, Y)
                ]
            else:
                for k, copy in enumerate(arrived[i]["y1"]):
                    copy.wait_recv()
                    add_blocks(
                        acc,
                        lambda p, q: (y, p, q, slice(None), cols),
                        buf(i, "y1"),
                        lambda p, q: (k, p, q),
                        (Z, X),
                        None,
                    )
                arrived[i]["x1"] = [
                    wire.start(
                        acc.at[y, :, (x + k) % X, :, view],
                        buf(i, "x1").at[k - 1],
                        wire.to(y, c, z, (x + k) % X),
                    )
                    for k in range(1, X)
                ]

    def stage_three(i):
        acc = buf(i, "acc")
        for half, (at, width) in enumerate(parts(i)):
            cols = slice(at, at + width)
            name = "y0" if half == 0 else "x1"
            for k, copy in enumerate(arrived[i][name]):
                copy.wait_recv()
                add_blocks(
                    acc,
                    lambda p: (y, p, x, slice(None), cols),
                    buf(i, name),
                    lambda p: (k, p),
                    (Z,),
                    None,
                )
        arrived[i]["z"] = [
            wire.start(
                acc.at[y, (z + k) % Z, x], buf(i, "z").at[k - 1], wire.to(y, c, (z + k) % Z, x)
            )
            for k in range(1, Z)
        ]

    def stage_four(i):
        n, at, width = chunks[i]
        total = buf(i, "acc")[y, z, x].astype(F32)
        for k, copy in enumerate(arrived[i]["z"]):
            copy.wait_recv()
            total = total + buf(i, "z")[k].astype(F32)
        results[n][:, pl.ds(at, width)] = total

    small_at = [0]

    def small_stage(moves):
        copies = []
        for target in moves:
            slot = small_at[0]
            small_at[0] += 1
            copies.append((slot, wire.start(small_acc, small_recv.at[slot], target)))
        for slot, copy in copies:
            copy.wait_send()
            wire.sent = [other for other in wire.sent if other is not copy]
        for slot, copy in copies:
            copy.wait_recv()
            small_acc[...] += small_recv[slot]

    rows, tiles = xt.shape[1], xt.shape[0]
    per_block = rows // lay.BL
    copies, g = group_copies(lay, c_send.at[0], c_recv.at[0], mine, inbox, False)
    G, zw = lay.G, queries.shape[1]
    D = x_low.shape[2]
    scale = zw ** (-0.5)
    n_base, n_value = len(grads) - 3, len(grads) - 2
    q_at = b // lay.Cq

    def back_copy(k, source, target, kind):
        t = (g + G - k) % G
        return pltpu.make_async_remote_copy(
            src_ref=source,
            dst_ref=target,
            send_sem=c_send.at[kind, k - 1],
            recv_sem=c_recv.at[kind, k - 1],
            device_id=(y * 2 + t % 2, q_at * lay.Cq + t // 2),
            device_id_type=MESH,
        )

    key_copies = [back_copy(k, dko.at[k - 1], dki.at[k - 1], 1) for k in range(1, G)]
    val_copies = [back_copy(k, dvo.at[k - 1], dvi.at[k - 1], 2) for k in range(1, G)]

    def fetch(source, target):
        copy = pltpu.make_async_copy(source, target, load)
        copy.start()
        copy.wait()

    def keep_grad(n, at, grad):
        columns = grad.shape[1]
        r = made[n].shape[4]
        low = grad.astype(BF16).reshape(Y, 2, Z, X, r, columns)
        stage[:, :, :, :, :, :columns] = low
        fetch(stage.at[:, :, :, :, :, pl.ds(0, columns)], made[n].at[:, :, :, :, :, pl.ds(at, columns)])

    def base_block(at, columns, first):
        block = bstage.at[:, pl.ds(0, columns)]
        if at == 0:
            bstage[:, :zw] = zlow[...]
            fetch(base_rest.at[:, pl.ds(0, columns - zw)], bstage.at[:, pl.ds(zw, columns - zw)])
        else:
            fetch(base_rest.at[:, pl.ds(at - zw, columns)], block)
        low = block[...]
        keep_grad(0, at, dot_t(mixed[...], low))
        part = mm_t(low, weight_block(w_base, stage, load, at, columns))
        mixed_acc[...] = part if first else mixed_acc[...] + part

    def load_values(k):
        fetch(vals.at[k], vstage)
        if k == G - 1:
            strip[...] = jnp.zeros(strip.shape, F32)

    def scores_back(k, i):
        at = i * QB
        here = pl.ds(at, QB)
        owner = lax.rem(g - k + G, G)
        dw = mm_t(d_att[here, :], vstage[...])
        p = probs[k, here, :].astype(F32)
        grad = p * (dw - delta[here, :])
        off = jnp.clip(G * rows - rows * (g - owner) - at, 0, G * rows)
        strip[:, pl.ds(pl.multiple_of(off, LANES), rows)] += grad
        low = grad.astype(BF16)
        ds[here, :] = low
        part = mm(low, keys[k]) * scale
        dq[here, :] = part if k == G - 1 else dq[here, :] + part

    def keys_back(k):
        grad = dot_t(ds[...], queries[...]) * scale
        if k:
            dko[k - 1] = grad.astype(BF16)
            key_copies[k - 1].start()
        else:
            for copy in key_copies:
                copy.wait()
            for j in range(1, G):
                grad = grad + dki[j - 1].astype(F32)
            pre_z = z_pre[...]
            gate = jax.nn.sigmoid(pre_z)
            shared = pre_z * gate
            small_acc[0:1, :] = jnp.sum(dq[...] * shared, axis=0, keepdims=True)
            small_acc[1:2, :] = jnp.sum(dq[...], axis=0, keepdims=True)
            small_acc[2:3, :] = jnp.sum(grad * shared, axis=0, keepdims=True)
            d_shared = dq[...] * gains_small[0:1, :] + grad * gains_small[1:2, :]
            zlow[...] = (d_shared * (gate * (1.0 + pre_z * (1.0 - gate)))).astype(BF16)

    def values_back(k):
        for at, columns in column_blocks(vstage.shape[1]):
            vstage[:, at : at + columns] = dot_t(
                probs[k], d_att[:, at : at + columns]
            ).astype(BF16)
        fetch(vstage, dvo.at[k - 1])
        val_copies[k - 1].start()

    def buckets():
        sums_of = bucket_sums(G * rows, NB, strip)
        lane = lax.broadcasted_iota(jnp.int32, (1, LANES), 1)
        line = jnp.zeros((1, LANES), F32)
        for k in range(NB):
            line = jnp.where(lane == k, jnp.sum(sums_of[k], axis=1, keepdims=True), line)
        small_acc[3:4, :] = line
        small_acc[4:8, :] = jnp.zeros((4, LANES), F32)

    def values_here():
        for copy in val_copies:
            copy.wait()

    def value_block(at, columns, first):
        cols = pl.ds(at, columns)
        grad = dot_t(probs[0], d_att[:, at : at + columns])
        for k in range(1, G):
            fetch(dvi.at[k - 1, :, cols], bstage.at[:, pl.ds(0, columns)])
            grad = grad + bstage[:, :columns].astype(F32)
        fetch(value_pre.at[:, cols], pstage.at[:, pl.ds(0, columns)])
        v = pstage[:, :columns]
        gate = jax.nn.sigmoid(v)
        vlow[:, :columns] = (grad * (gate * (1.0 + v * (1.0 - gate)))).astype(BF16)
        keep_grad(1, at, dot_t(x_low[...].reshape(rows, D), vlow[:, :columns]))
        part = mm_t(vlow[:, :columns], weight_block(w_value, stage, load, at, columns))
        if first:
            fetch(pre, x_acc)
        x_acc[...] += part

    def d_ema(t):
        v = ema[t]
        gate = jax.nn.sigmoid(v)
        dt[t] = mixed_acc[:, t * LANES : (t + 1) * LANES] * (gate * (1.0 + v * (1.0 - gate)))

    def tile_x():
        for j in range(lay.BL):
            to_tiles(x_low[j], xt, j * per_block, per_block)

    def ends(t):
        ema_back_ends_kernel(H, dt.at[t], table.at[t], l_end.at[t])
        for h in range(H):
            mine[t, pl.ds(h, 1), :] = l_end[t, h, 0:1, :]

    def exchange():
        for copy in copies:
            copy.start()

    def carries():
        for copy in copies:
            copy.wait()
        for t in range(tiles):
            carry_in(lay, H, rows, g, inbox, table, inc, t, True)

    def correlate(t):
        ema_sums_kernel(H, xt.at[t], dt.at[t], table.at[t], si.at[t], ri.at[t], sums.at[t])

    def back(t):
        ema_back_kernel(
            H, dt.at[t], table.at[t], turned.at[t, pl.ds(4 * H, 1)], l_end.at[t], inc.at[t], dx.at[t]
        )
        cols = slice(t * LANES, (t + 1) * LANES)
        for j in range(lay.BL):
            at = pl.ds(j * per_block, per_block)
            gx[j, :, cols] = (x_acc[at, cols] + dx[t, at, :]).astype(BF16)

    def share_sums():
        r = split.shape[4]
        for t in range(tiles):
            sums[t, pl.ds(2 * H + 1, 2), :] = gains[0:2, t * LANES : (t + 1) * LANES]
            flat[t * LANES : (t + 1) * LANES, :] = sums[t].T

        def one(i, carry):
            split[i // (2 * Z * X), i // (Z * X) % 2, i // X % Z, i % X] = flat[pl.ds(i * r, r), :]
            return carry

        lax.fori_loop(0, 2 * X * Y * Z, one, 0)

    sums[...] = jnp.zeros(sums.shape, F32)
    xs = [wire.to(y, c, z, (x + k) % X) for k in range(1, X)]
    ys = [wire.to((y + k) % Y, c, z, x) for k in range(1, Y)]
    zs = [wire.to(y, c, (z + k) % Z, x) for k in range(1, Z)]

    run = functools.partial
    base_blocks = column_blocks(w_base.shape[5])
    value_blocks = column_blocks(w_value.shape[5])
    todo = []
    for number, block in enumerate(base_blocks[1:]):
        todo.append((0, run(base_block, *block, number == 0), (n_base, block[0])))
    for k in list(range(1, G))[::-1] + [0]:
        todo.append((0, run(load_values, k)))
        todo += [(0, run(scores_back, k, i)) for i in range(rows // QB)]
        todo.append((0, run(keys_back, k)))
        if k:
            todo.append((0, run(values_back, k)))
    todo.append((0, run(base_block, *base_blocks[0], False), (n_base, 0)))
    todo += [(0, run(d_ema, t)) for t in range(tiles)]
    todo += [(0, run(ends, t)) for t in range(tiles)]
    todo += [(0, exchange), (0, values_here)]
    for number, block in enumerate(value_blocks):
        todo.append((0, run(value_block, *block, number == 0), (n_value, block[0])))
    todo.append((0, carries))
    todo += [(0, run(back, t)) for t in range(tiles)]
    todo += [(0, lambda: begin(1)), (0, tile_x), (0, buckets, "small")]
    todo += [(0, run(correlate, t)) for t in range(tiles)]
    todo.append((0, share_sums, (len(grads) - 1, 0)))

    def needs(i):
        n, at, width = chunks[i]
        return (n, at) if n >= n_base else None

    steps = []
    for i in range(min(LEAD, total)):
        steps.append((run(stage_core, i), needs(i)))
    steps.append(lambda: begin(0))
    for turn in range(total + 3 * LAG):
        for what, lag in ((stage_four, 3), (stage_three, 2), (stage_two, 1), (stage_one, 0)):
            if 0 <= turn - lag * LAG < total:
                steps.append(run(what, turn - lag * LAG))
        if turn + LEAD < total:
            steps.append((run(stage_core, turn + LEAD), needs(turn + LEAD)))
        if turn >= total:
            late = turn - total
            moves = ([wire.to(y, 1 - c, z, x)], xs, ys, zs)
            if late < 4:
                steps.append((run(small_stage, moves[late]), "small"))
    interleave(steps, todo, MOST)
    small_out[...] = small_acc[...]
    wait(0)
    wait(1)
    wire.finish()


LEAD = 3
MOST = 1


def dot_t(a, b):
    return lax.dot_general(a, b, (((0,), (0,)), ((), ())), preferred_element_type=F32)


def bucket_sums(length, bucket_count, strip):
    edges = bucket_edges(bucket_count)
    lag0 = lax.broadcasted_iota(jnp.int32, (QB, LANES), 0) - lax.broadcasted_iota(
        jnp.int32, (QB, LANES), 1
    )
    totals = [jnp.zeros((1, LANES), F32) for k in range(bucket_count)]
    for t in range((length + QB) // LANES):
        base = length - t * LANES
        low, high = base - LANES + 1, base + QB - 1
        if high < 0:
            continue
        value = strip[:, t * LANES : (t + 1) * LANES]
        for k in range(bucket_count):
            top = edges[k + 1] if k + 1 < bucket_count else length
            if edges[k] <= high and top > low:
                lag = lag0 + base
                inside = (lag >= edges[k]) & (lag < top)
                totals[k] = totals[k] + jnp.sum(jnp.where(inside, value, 0.0), axis=0, keepdims=True)
    return totals


def backward_all(lay, H, NB, grads, fulls, values, share):
    X, Y, Z, G = lay.X, lay.Y, lay.Z, lay.G
    R, V = values["d_att"].shape
    D = values["pre"].shape[1]
    T, zw = D // LANES, values["queries"].shape[1]
    rows = R // lay.BL
    micro = lay.MS // lay.items
    shapes = [grad.shape[-2:] for grad in grads] + [full.shape[-2:] for full in fulls] + [(share, LANES)]
    kinds = [grad.dtype for grad in grads] + [BF16, BF16, F32]
    known = len(grads)
    chunks = chunks_of([shape for shape in shapes[:known]], share * LIMIT)
    base_blocks = column_blocks(shapes[known][1])
    chunks += [(known,) + block for block in base_blocks[1:]]
    chunks += [(known,) + base_blocks[0]]
    chunks += [(known + 1,) + block for block in column_blocks(shapes[known + 1][1])]
    chunks += [(known + 2, 0, LANES)]
    scratch = []
    for n, at, cols in chunks:
        r = shapes[n][0]
        left = half_columns(cols)
        right = cols - left if cols > left else LANES
        kind = kinds[n]
        scratch += [
            pltpu.VMEM((Y, Z, X, r, cols), kind),
            pltpu.VMEM((X - 1, Y, Z, r, left), kind),
            pltpu.VMEM((Y - 1, Z, X, r, right), kind),
            pltpu.VMEM((Y - 1, Z, r, left), kind),
            pltpu.VMEM((X - 1, Z, r, right), kind),
            pltpu.VMEM((Z - 1, r, cols), kind),
        ]
    hops = 1 + (X - 1) + (Y - 1) + (Z - 1)
    per = 1 + 2 * (X - 1 + Y - 1) + Z - 1
    small = (8, LANES)
    outs = [jax.ShapeDtypeStruct(shape, F32) for shape in shapes]
    outs.append(jax.ShapeDtypeStruct(small, F32))
    outs += [jax.ShapeDtypeStruct((micro, lay.items, rows, D), BF16)] * 2
    outs += [jax.ShapeDtypeStruct(full.shape, BF16) for full in fulls]
    outs += [jax.ShapeDtypeStruct((G - 1, R, V), BF16)] * 2
    scratch += [pltpu.VMEM(small, F32), pltpu.VMEM((hops,) + small, F32)]
    heights = sorted({shapes[n][0] for n, at, width in chunks})
    widest = {r: max(w for n, at, w in chunks if shapes[n][0] == r) for r in heights}
    scratch += [
        pltpu.SemaphoreType.DMA((len(chunks) * per + hops,)),
        pltpu.SemaphoreType.DMA((len(chunks) * per + hops,)),
        pltpu.SemaphoreType.DMA((len(chunks),)),
        pltpu.SemaphoreType.DMA((2, lay.BL)),
        pltpu.SemaphoreType.DMA((2, lay.MS)),
        pltpu.SemaphoreType.DMA((2,)),
        pltpu.VMEM((T, R, LANES), F32),
        pltpu.VMEM((T, R, LANES), F32),
        pltpu.VMEM((T, R, LANES), F32),
        pltpu.VMEM((T, LANES, LANES), F32),
        pltpu.VMEM((D, LANES), F32),
        pltpu.VMEM((Y, 2, Z, X, share, LANES), F32),
        pltpu.VMEM((T, H, SEG, LANES), F32),
        pltpu.VMEM((T, H, LANES), F32),
        pltpu.VMEM((G - 1, T, H, LANES), F32),
        pltpu.VMEM((T, H, LANES), F32),
        pltpu.VMEM((lay.BL, rows, D), BF16),
        pltpu.SemaphoreType.DMA((3, G - 1)),
        pltpu.SemaphoreType.DMA((3, G - 1)),
        pltpu.VMEM((Y, 2, Z, X, share, 768), BF16),
        pltpu.VMEM((R, V), BF16),
        pltpu.VMEM((R, 768), BF16),
        pltpu.VMEM((R, 768), F32),
        pltpu.VMEM((R, R), BF16),
        pltpu.VMEM((QB, (G + 1) * R), F32),
        pltpu.VMEM((R, zw), F32),
        pltpu.VMEM((G - 1, R, zw), BF16),
        pltpu.VMEM((G - 1, R, zw), BF16),
        pltpu.VMEM((R, zw), BF16),
        pltpu.VMEM((R, 768), BF16),
        pltpu.VMEM((R, D), F32),
        pltpu.VMEM((R, D), F32),
        pltpu.SemaphoreType.DMA,
    ]
    scratch += [pltpu.VMEM((2, Y, Z, X, r, widest[r]), BF16) for r in heights]
    order = (
        ("x_blocks", VM), ("d_in", ANY), ("d_att", VM), ("delta", VM), ("queries", VM), ("keys", VM),
        ("vals", ANY), ("probs", VM), ("z_pre", VM), ("gains_small", VM), ("mixed", VM), ("ema", VM),
        ("base_rest", ANY), ("value_pre", ANY), ("w_base", ANY), ("w_value", ANY), ("pre", ANY),
        ("gains", VM), ("table", VM), ("turned", VM), ("si", VM), ("ri", VM), ("block_out", ANY),
    )
    values = dict(values, w_base=fulls[0], w_value=fulls[1])
    order = tuple(item for item in order if item[0] != "d_in")

    def body(*refs):
        named = refs[known : known + len(order)]
        ins = (tuple(refs[:known]), named[0], None) + tuple(named[1:])
        rest = refs[known + len(order) :]
        results, small_out, moved = rest[: known + 3], rest[known + 3], rest[known + 4 : known + 6]
        made, dvo, dvi = rest[known + 6 : known + 8], rest[known + 8], rest[known + 9]
        scatter_kernel(
            lay, H, NB, chunks, ins, (results, small_out, moved, tuple(made), dvo, dvi), rest[known + 10 :]
        )

    result = pl.pallas_call(
        body,
        out_shape=outs,
        in_specs=[ANY] * known + [spec for name, spec in order],
        out_specs=[VM] * (known + 4) + [ANY] * 6,
        scratch_shapes=scratch,
        compiler_params=pltpu.CompilerParams(
            collective_id=1, has_side_effects=True, vmem_limit_bytes=60 * 2**20
        ),
        name="backward_all",
    )(*grads, *[values[name] for name, spec in order])
    return result[: known + 3], result[known + 3], result[known + 4 : known + 6]


def row(ref, index, lanes):
    return jnp.broadcast_to(ref[pl.ds(index, 1), lanes], (SEG, LANES))


def lane_call(kernel, outs, args, name):
    def spec(a):
        lead = len(a.shape) - 1
        return pl.BlockSpec(a.shape[:-1] + (LANES,), lambda i: (0,) * lead + (i,))

    return pl.pallas_call(
        kernel,
        out_shape=outs,
        grid=(args[0].shape[-1] // LANES,),
        in_specs=[spec(a) for a in args],
        out_specs=jax.tree.map(spec, outs),
        compiler_params=pltpu.CompilerParams(vmem_limit_bytes=32 * 2**20),
        name=name,
    )(*args)


def shifted(value, by):
    where = lax.broadcasted_iota(jnp.int32, (SEG, LANES), 0)
    if by > 0:
        return jnp.where(where >= by, pltpu.roll(value, by, 0), 0.0)
    return jnp.where(where < SEG + by, pltpu.roll(value, SEG + by, 0), 0.0)


def ema_ends_kernel(H, x_ref, tab_ref, s_ref, r_ref):
    rows, width = x_ref.shape
    steps = rows // SEG

    def tile(lanes):
        decay = [row(tab_ref, h, lanes) for h in range(H)]

        def step(t, state):
            s, r = state
            xt = x_ref[pl.ds(t, SEG, stride=steps), lanes]
            r = tuple(decay[h] * r[h] + s[h] for h in range(H))
            s = tuple(decay[h] * s[h] + xt for h in range(H))
            return s, r

        zero = tuple(tab_ref[0:SEG, lanes] * 0.0 for h in range(H))
        s, r = lax.fori_loop(0, steps, step, (zero, zero))
        for h in range(H):
            log = row(tab_ref, H + h, lanes)
            sh, rh = s[h], r[h]
            for d in (1, 2, 4):
                span = d * steps
                sd, rd = shifted(sh, d), shifted(rh, d)
                power = jnp.exp(span * log)
                rh = rh + power * rd + (span * jnp.exp((span - 1) * log)) * sd
                sh = sh + power * sd
            s_ref[h, :, lanes] = sh
            r_ref[h, :, lanes] = rh

    tile(slice(None))


def ema_out_kernel(H, x_ref, tab_ref, omega_ref, s_ref, r_ref, inc_ref, ema_ref, si_ref, ri_ref):
    rows, width = x_ref.shape
    steps = rows // SEG

    def tile(lanes):
        decay = [row(tab_ref, h, lanes) for h in range(H)]
        gain = [row(tab_ref, 2 * H + h, lanes) for h in range(H)]
        omega = row(omega_ref, 0, lanes)
        start = []
        span = (lax.broadcasted_iota(jnp.int32, (SEG, LANES), 0) * steps).astype(F32)
        for h in range(H):
            log = row(tab_ref, H + h, lanes)
            s_dev = row(inc_ref, h, lanes)
            r_dev = row(inc_ref, H + h, lanes)
            power = jnp.exp(span * log)
            s_in = shifted(s_ref[h, :, lanes], 1) + power * s_dev
            r_in = (
                shifted(r_ref[h, :, lanes], 1)
                + power * r_dev
                + (span * jnp.exp((span - 1.0) * log)) * s_dev
            )
            si_ref[h, :, lanes] = s_in
            ri_ref[h, :, lanes] = r_in
            start.append(s_in)

        def step(t, s):
            xt = x_ref[pl.ds(t, SEG, stride=steps), lanes]
            s = tuple(decay[h] * s[h] + xt for h in range(H))
            parts = [gain[h] * s[h] for h in range(H)]
            while len(parts) > 1:
                parts = [parts[i] + parts[i + 1] for i in range(0, len(parts), 2)]
            ema_ref[pl.ds(t, SEG, stride=steps), lanes] = parts[0] + omega * xt
            return s

        lax.fori_loop(0, steps, step, tuple(start))

    tile(slice(None))


def ema_back_ends_kernel(H, d_ref, tab_ref, l_ref):
    rows, width = d_ref.shape
    steps = rows // SEG

    def tile(lanes):
        decay = [row(tab_ref, h, lanes) for h in range(H)]

        def step(i, lam):
            dt = d_ref[pl.ds(steps - 1 - i, SEG, stride=steps), lanes]
            return tuple(decay[h] * lam[h] + dt for h in range(H))

        zero = tuple(tab_ref[0:SEG, lanes] * 0.0 for h in range(H))
        lam = lax.fori_loop(0, steps, step, zero)
        for h in range(H):
            log = row(tab_ref, H + h, lanes)
            lh = lam[h]
            for d in (1, 2, 4):
                lh = lh + jnp.exp(d * steps * log) * shifted(lh, -d)
            l_ref[h, :, lanes] = lh

    tile(slice(None))


def ema_sums_kernel(H, x_ref, d_ref, tab_ref, si_ref, ri_ref, out_ref):
    rows, width = x_ref.shape
    steps = rows // SEG
    group = H // 2

    def tile(lanes):
        for first in range(0, H, group):
            decay = [row(tab_ref, first + h, lanes) for h in range(group)]

            def step(t, state):
                s, r, c, q, o = state
                xt = x_ref[pl.ds(t, SEG, stride=steps), lanes]
                dt = d_ref[pl.ds(t, SEG, stride=steps), lanes]
                r = tuple(decay[h] * r[h] + s[h] for h in range(group))
                s = tuple(decay[h] * s[h] + xt for h in range(group))
                c = tuple(c[h] + dt * s[h] for h in range(group))
                q = tuple(q[h] + dt * r[h] for h in range(group))
                return s, r, c, q, o + dt * xt

            zero = tuple(tab_ref[0:SEG, lanes] * 0.0 for h in range(group))
            s = tuple(si_ref[first + h, :, lanes] for h in range(group))
            r = tuple(ri_ref[first + h, :, lanes] for h in range(group))
            s, r, c, q, o = lax.fori_loop(0, steps, step, (s, r, zero, zero, zero[0]))
            for h in range(group):
                out_ref[pl.ds(first + h, 1), lanes] = jnp.sum(c[h], axis=0, keepdims=True)
                out_ref[pl.ds(H + first + h, 1), lanes] = jnp.sum(q[h], axis=0, keepdims=True)
            out_ref[pl.ds(2 * H, 1), lanes] = jnp.sum(o, axis=0, keepdims=True)

    tile(slice(None))


def ema_back_kernel(H, d_ref, tab_ref, omega_ref, l_ref, inc_ref, dx_ref):
    rows, width = d_ref.shape
    steps = rows // SEG

    def tile(lanes):
        decay = [row(tab_ref, h, lanes) for h in range(H)]
        gain = [row(tab_ref, 2 * H + h, lanes) for h in range(H)]
        omega = row(omega_ref, 0, lanes)
        start = []
        span = ((SEG - 1 - lax.broadcasted_iota(jnp.int32, (SEG, LANES), 0)) * steps).astype(F32)
        for h in range(H):
            log = row(tab_ref, H + h, lanes)
            l_dev = row(inc_ref, h, lanes)
            start.append(shifted(l_ref[h, :, lanes], -1) + jnp.exp(span * log) * l_dev)

        def step(i, lam):
            at = pl.ds(steps - 1 - i, SEG, stride=steps)
            dt = d_ref[at, lanes]
            lam = tuple(decay[h] * lam[h] + dt for h in range(H))
            parts = [gain[h] * lam[h] for h in range(H)]
            while len(parts) > 1:
                parts = [parts[i] + parts[i + 1] for i in range(0, len(parts), 2)]
            dx_ref[at, lanes] = parts[0] + omega * dt
            return lam

        lax.fori_loop(0, steps, step, tuple(start))

    tile(slice(None))


def call(kernel, outs, args, specs=None, scratch=(), vmem=58, name=None):
    return pl.pallas_call(
        kernel,
        out_shape=outs,
        in_specs=specs or [VM] * len(args),
        out_specs=jax.tree.map(lambda o: VM, outs),
        scratch_shapes=list(scratch),
        compiler_params=pltpu.CompilerParams(vmem_limit_bytes=vmem * 2**20),
        name=name,
    )(*args)


QB = 256
STRETCH = 128


def bias_kernel(length, bucket_count, bias_ref, strip_ref):
    edges = bucket_edges(bucket_count)
    tiles = length // LANES + QB // LANES
    lag0 = lax.broadcasted_iota(jnp.int32, (QB, LANES), 0) - lax.broadcasted_iota(
        jnp.int32, (QB, LANES), 1
    )
    for t in range(strip_ref.shape[1] // LANES):
        base = length - t * LANES
        low, high = base - LANES + 1, base + QB - 1
        start = max([k for k in range(bucket_count) if edges[k] <= low], default=0)
        value = jnp.full((QB, LANES), bias_ref[start], F32)
        for k in range(start + 1, bucket_count):
            if edges[k] <= high:
                value = jnp.where(lag0 + base >= edges[k], bias_ref[k], value)
        strip_ref[:, t * LANES : (t + 1) * LANES] = value


def attend_body(lay, g, far, q_ref, strip_ref, keys, vals, att_ref, probs_ref, scores, part):
    G = lay.G
    rows, zw = q_ref.shape
    length = G * rows
    r0 = lax.broadcasted_iota(jnp.int32, (QB, rows), 0)
    c0 = lax.broadcasted_iota(jnp.int32, (QB, rows), 1)

    def one(i, carry):
        at = i * QB
        q = q_ref[pl.ds(at, QB), :]
        for k in range(G):
            owner = lax.rem(g - k + G, G)
            s = mm_t(q, keys[k])
            off = jnp.clip(length - rows * (g - owner) - at, 0, length)
            s = s * (zw ** (-0.5)) + strip_ref[:, pl.ds(pl.multiple_of(off, LANES), rows)]
            if k == 0:
                pos = r0 + at
                s = jnp.where(pos // STRETCH == c0 // STRETCH, s, s + far)
                s = jnp.where(c0 <= pos, s, masked_fill)
            else:
                s = s + jnp.where(k <= g, far, masked_fill)
            scores[:, k * rows : (k + 1) * rows] = s
        s = scores[...]
        p = jnp.exp(s - jnp.max(s, axis=1, keepdims=True))
        p = p * (1.0 / jnp.sum(p, axis=1, keepdims=True))
        total = jnp.zeros((QB, att_ref.shape[1]), F32)
        for k in range(G):
            low = p[:, k * rows : (k + 1) * rows].astype(BF16)
            probs_ref[k, pl.ds(at, QB), :] = low
            total += mm(low, vals[k])
        att_ref[pl.ds(at, QB), :] = total
        return carry

    one(part, 0)


def attend_back_kernel(lay, bucket_count, flag_ref, q_ref, da_ref, delta_ref, probs_ref, *refs):
    G = lay.G
    keys, vals, dq_ref, dk_ref, dv_ref, dko_ref, dvo_ref, bucket_ref, strip, ds_ref = refs
    rows, zw = q_ref.shape
    length = G * rows
    g = flag_ref[1]
    scale = zw ** (-0.5)
    edges = bucket_edges(bucket_count)
    strip[...] = jnp.zeros(strip.shape, F32)

    def one(i, carry):
        at = pl.multiple_of(i * QB, QB)
        da = da_ref[pl.ds(at, QB), :]
        dq = jnp.zeros((QB, zw), F32)
        for k in range(G):
            owner = lax.rem(g - k + G, G)
            dw = mm_t(da, vals[k])
            p = probs_ref[k, pl.ds(at, QB), :].astype(F32)
            ds = p * (dw - delta_ref[pl.ds(at, QB), :])
            off = jnp.clip(length - rows * (g - owner) - at, 0, length)
            strip[:, pl.ds(pl.multiple_of(off, LANES), rows)] += ds
            low = ds.astype(BF16)
            dq += mm(low, keys[k])
            ds_ref[k, pl.ds(at, QB), :] = low
        dq_ref[pl.ds(at, QB), :] = dq * scale
        return carry

    lax.fori_loop(0, rows // QB, one, 0)
    for k in range(G):
        dk = lax.dot_general(
            ds_ref[k], q_ref[...], (((0,), (0,)), ((), ())), preferred_element_type=F32
        )
        dv = lax.dot_general(
            probs_ref[k], da_ref[...], (((0,), (0,)), ((), ())), preferred_element_type=F32
        )
        if k == 0:
            dk_ref[...] = dk * scale
            dv_ref[...] = dv
        else:
            dko_ref[k - 1] = (dk * scale).astype(BF16)
            dvo_ref[k - 1] = dv.astype(BF16)
    lag0 = lax.broadcasted_iota(jnp.int32, (QB, LANES), 0) - lax.broadcasted_iota(
        jnp.int32, (QB, LANES), 1
    )
    sums = [jnp.zeros((1, LANES), F32) for k in range(bucket_count)]
    for t in range((length + QB) // LANES):
        base = length - t * LANES
        low, high = base - LANES + 1, base + QB - 1
        if high < 0:
            continue
        value = strip[:, t * LANES : (t + 1) * LANES]
        for k in range(bucket_count):
            top = edges[k + 1] if k + 1 < bucket_count else length
            if edges[k] <= high and top > low:
                lag = lag0 + base
                inside = (lag >= edges[k]) & (lag < top)
                sums[k] = sums[k] + jnp.sum(jnp.where(inside, value, 0.0), axis=0, keepdims=True)
    for k in range(bucket_count):
        bucket_ref[pl.ds(k, 1), :] = sums[k]


def silu_slope(values):
    gate_value = jax.nn.sigmoid(values)
    return gate_value * (1.0 + values * (1.0 - gate_value))


def normalize(seq_rows):
    centered = seq_rows - jnp.mean(seq_rows, axis=-1, keepdims=True)
    inverse = lax.rsqrt(jnp.mean(centered * centered, axis=-1, keepdims=True) + epsilon)
    return (centered * inverse, inverse)


def normalize_back(grad_scaled, unit_rows, inverse):
    return inverse * (
        grad_scaled
        - jnp.mean(grad_scaled, axis=-1, keepdims=True)
        - unit_rows * jnp.mean(grad_scaled * unit_rows, axis=-1, keepdims=True)
    )


def mm(a, b):
    return jnp.dot(a, b, preferred_element_type=F32)


def mm_t(a, b):
    return lax.dot_general(a, b, (((1,), (1,)), ((), ())), preferred_element_type=F32)


def wgrad(a, b):
    return lax.dot_general(a, b, (((0,), (0,)), ((), ())), preferred_element_type=F32).astype(BF16)


def shards(
    lay,
    tokens,
    cotangent,
    stretch_size,
    w_value,
    w_base,
    w_out,
    w_up,
    w_down,
    ema_delta,
    ema_alpha,
    ema_beta,
    ema_gamma,
    ema_omega,
    first_gain,
    second_gain,
    query_gain,
    query_bias,
    key_gain,
    relative_bias,
):
    micro, items, seq_len, D = tokens.shape
    H = ema_delta.shape[1]
    zw = query_gain.shape[0]
    V = w_value.shape[1]
    NB = relative_bias.shape[0]
    length = seq_len * lay.S
    G = lay.G
    R = lay.BL * seq_len
    d_at, b_at = lax.axis_index("dp"), lax.axis_index("seq")
    c_at, y_at = d_at % 2, d_at // 2
    q_at = b_at // lay.Cq
    g_at = (b_at % lay.Cq) * 2 + c_at
    share = ema_delta.shape[0]

    def group_perm(k):
        pairs = []
        for y in range(lay.Y):
            for q in range(lay.Q):
                for g in range(G):
                    t = (g + k) % G
                    src = (y * 2 + g % 2) * lay.S + q * lay.Cq + g // 2
                    dst = (y * 2 + t % 2) * lay.S + q * lay.Cq + t // 2
                    pairs.append((src, dst))
        return pairs

    def shift(value, k):
        return lax.ppermute(value, ("dp", "seq"), group_perm(k % G))

    marks = jnp.broadcast_to(
        stretch_size.reshape(1, -1).astype(BF16), (share, lay.MS)
    )
    used = 4 * H + 3 + lay.MS
    pack = jnp.concatenate(
        [
            ema_delta,
            ema_alpha,
            ema_beta,
            ema_gamma,
            ema_omega[:, None],
            first_gain[:, None],
            second_gain[:, None],
            marks,
            jnp.zeros((share, LANES - used), BF16),
        ],
        1,
    )
    x_blocks, cot_blocks, fulls, rest = forward_all(
        lay, H, tokens, cotangent, (pack, w_value, w_base, w_out, w_up, w_down),
        query_gain[None], query_bias[None], key_gain[None], relative_bias,
    )
    mixed, ema_tiles, s_in, r_in, table, turned = rest[:6]
    value_pre, base, queries, keys_all, vals_all, probs, attended = rest[6:]
    flags = jnp.stack([g_at, g_at])
    mats = [full.reshape(-1, full.shape[-1]) for full in fulls[1:]]
    mat_value, mat_base, mat_out, mat_up, mat_down = mats
    gain_first = turned[:, 4 * H + 1].reshape(D)
    gain_second = turned[:, 4 * H + 2].reshape(D)

    x_low = x_blocks.reshape(R, D)
    x = x_low.astype(F32)
    grad_out = cot_blocks.reshape(R, D).astype(F32)

    z_pre = base[:, :zw]
    reset_pre = base[:, zw : zw + V]
    cand_pre = base[:, zw + V : zw + V + D]
    update_pre = base[:, zw + V + D :]
    reset_gate = jax.nn.silu(reset_pre)
    update = jax.nn.sigmoid(update_pre)
    gated = (attended * reset_gate).astype(BF16)
    cand_in = cand_pre + mm(gated, mat_out)
    candidate = jax.nn.silu(cand_in)
    first_sum = x + update * (candidate - x)
    unit_first, inverse_first = normalize(first_sum)
    normed = unit_first * gain_first
    normed_low = normed.astype(BF16)
    hidden_pre = mm(normed_low, mat_up)
    hidden = jax.nn.silu(hidden_pre).astype(BF16)
    second_sum = normed + mm(hidden, mat_down)
    unit_second, inverse_second = normalize(second_sum)
    block_out = (unit_second * gain_second).astype(BF16)

    grad_gain_second = jnp.sum(grad_out * unit_second, axis=0)
    grad_second = normalize_back(grad_out * gain_second, unit_second, inverse_second)
    branch = grad_second.astype(BF16)
    grad_mat_down = wgrad(hidden, branch)
    hidden_grad = (mm_t(branch, mat_down) * silu_slope(hidden_pre)).astype(BF16)
    grad_mat_up = wgrad(normed_low, hidden_grad)
    grad_normed = grad_second + mm_t(hidden_grad, mat_up)
    grad_gain_first = jnp.sum(grad_normed * unit_first, axis=0)
    grad_first = normalize_back(grad_normed * gain_first, unit_first, inverse_first)
    cand_low = (grad_first * update * silu_slope(cand_in)).astype(BF16)
    grad_mat_out = wgrad(gated, cand_low)
    grad_gated = mm_t(cand_low, mat_out)
    att_low = (grad_gated * reset_gate).astype(BF16)
    grad_reset = grad_gated * attended * silu_slope(reset_pre)
    grad_update = grad_first * (candidate - x) * update * (1.0 - update)
    delta = jnp.sum(att_low.astype(F32) * attended, axis=1, keepdims=True)
    base_rest = jnp.concatenate(
        [grad_reset.astype(BF16), cand_low, grad_update.astype(BF16)], 1
    )
    pre = grad_first * (1.0 - update)
    gains = jnp.concatenate(
        [grad_gain_first[None], grad_gain_second[None], jnp.zeros((6, D), F32)]
    )
    shape = (lay.Y, 2, lay.Z, lay.X)

    def split(grad):
        return grad.reshape(shape + (-1, grad.shape[-1]))

    reduced, small_total, moved = backward_all(
        lay,
        H,
        NB,
        [split(grad_mat_down), split(grad_mat_up), split(grad_mat_out)],
        [fulls[2], fulls[1]],
        dict(
            x_blocks=x_blocks, d_att=att_low, delta=delta, queries=queries, keys=keys_all,
            vals=vals_all, probs=probs, z_pre=z_pre,
            gains_small=jnp.concatenate([query_gain[None], key_gain[None], jnp.zeros((6, zw), F32)]),
            mixed=mixed, ema=ema_tiles, base_rest=base_rest, value_pre=value_pre, pre=pre, gains=gains,
            table=table, turned=turned, si=s_in, ri=r_in,
            block_out=block_out.reshape(lay.BL, seq_len, D),
        ),
        share,
    )
    own = reduced[5]
    corr, lagged = own[:, :H], own[:, H : 2 * H]
    p = jax.nn.sigmoid(ema_delta.astype(F32))
    a = jax.nn.sigmoid(ema_alpha.astype(F32))
    beta = ema_beta.astype(F32)
    read = ema_gamma.astype(F32) * (H ** (-0.5))
    q_grad = read * p * beta * lagged
    return (
        moved[0],
        moved[1].astype(F32),
        reduced[4],
        reduced[3],
        reduced[2],
        reduced[1],
        reduced[0],
        (read * beta * corr - a * q_grad) * p * (1.0 - p),
        -p * q_grad * a * (1.0 - a),
        p * read * corr,
        p * beta * corr * (H ** (-0.5)),
        own[:, 2 * H],
        own[:, 2 * H + 1],
        own[:, 2 * H + 2],
        small_total[0, :zw],
        small_total[1, :zw],
        small_total[2, :zw],
        small_total[3, :NB],
    )


def solution(mesh):
    rows = P(None, "dp", "seq", None)
    part2, part1 = P(("dp", "seq"), None), P(("dp", "seq"))
    in_specs = (rows, rows, P(None, "dp")) + (part2,) * 9 + (part1,) * 3 + (P(),) * 4
    out_specs = (rows, rows) + (part2,) * 9 + (part1,) * 3 + (P(),) * 4

    def whole(tokens, *rest):
        micro, seqs = tokens.shape[:2]
        lay = Layout(mesh.shape["dp"], mesh.shape["seq"], micro, seqs // mesh.shape["dp"])
        return jax.shard_map(
            functools.partial(shards, lay),
            mesh=mesh,
            in_specs=in_specs,
            out_specs=out_specs,
            check_vma=False,
        )(tokens, *rest)

    return whole
```

```python
import functools

import jax
import jax.numpy as jnp
import numpy as np
from jax import lax
from jax.experimental import pallas as pl
from jax.experimental.pallas import tpu as pltpu
from jax.sharding import PartitionSpec as P

epsilon = 1e-05
masked_fill = -1e30
MESH = pl.DeviceIdType.MESH
ANY = pl.BlockSpec(memory_space=pl.ANY)
VM = pl.BlockSpec(memory_space=pltpu.VMEM)
SM = pl.BlockSpec(memory_space=pltpu.SMEM)
F32 = jnp.float32
BF16 = jnp.bfloat16
SEG = 8
LANES = 128


def bucket_edges(bucket_count):
    edge_list = [0]
    middle = bucket_count // 2
    for number in range(1, bucket_count):
        edge_list.append(number if number < middle else int(middle * 2 ** ((number - middle) / 2)))
    return edge_list


class Layout:
    def __init__(self, dp, seq, micro, items):
        self.dp, self.S = dp, seq
        self.C = 2
        self.Y = dp // 2
        self.X = min(self.Y, seq)
        self.Z = seq // self.X
        self.items = items
        self.MS = micro * items
        self.Q = 2 * self.MS
        self.Cq = seq // self.Q
        self.G = 2 * self.Cq
        self.BL = seq // self.G

    def here(self):
        d, b = lax.axis_index("dp"), lax.axis_index("seq")
        return d // 2, d % 2, b // self.X, b % self.X, b


class Wire:
    def __init__(self, lay, send, recv):
        self.lay, self.send, self.recv, self.count = lay, send, recv, 0
        self.sent = []

    def to(self, y, c, z, x):
        return (y * 2 + c, z * self.lay.X + x)

    def start(self, src, dst, target):
        number = self.count
        self.count += 1
        copy = pltpu.make_async_remote_copy(
            src_ref=src,
            dst_ref=dst,
            send_sem=self.send.at[number],
            recv_sem=self.recv.at[number],
            device_id=target,
            device_id_type=MESH,
        )
        copy.start()
        self.sent.append(copy)
        return copy

    def finish(self):
        for copy in self.sent:
            copy.wait_send()


def greet(lay):
    y, c, z, x, b = lay.here()
    barrier = pltpu.get_barrier_semaphore()
    plane = 2 * lay.S

    def one(k, carry):
        other = (c * lay.S + b + k) % plane
        pl.semaphore_signal(
            barrier, inc=1, device_id=(y * 2 + other // lay.S, other % lay.S), device_id_type=MESH
        )
        return carry

    lax.fori_loop(1, plane, one, 0)
    for k in range(1, lay.Y):
        pl.semaphore_signal(
            barrier, inc=1, device_id=(((y + k) % lay.Y) * 2 + c, b), device_id_type=MESH
        )
    pl.semaphore_wait(barrier, plane - 1 + lay.Y - 1)


ALPHA = 0.5
AHEAD = 2
LAG = 2
ORDER = 1
LIMIT = 800


def half_columns(columns):
    return max(1, int(columns // LANES * ALPHA + 0.5)) * LANES


def reshard_in(lay, sources, targets, send, recv, local):
    y, c, z, x, b = lay.here()
    g = b // lay.BL
    slot = b % lay.BL
    qm = b // lay.Cq
    gm = (b % lay.Cq) * 2 + c

    def begin(n):
        for source, target in ((sources[n], targets[n]),):
            for ms in range(lay.MS):
                seq_to = (ms * 2 + c) * lay.Cq + g // 2
                mine = jnp.logical_and(seq_to == b, g % 2 == c)
                block = source.at[ms // lay.items, ms % lay.items]

                @pl.when(jnp.logical_not(mine))
                def _():
                    pltpu.make_async_remote_copy(
                        src_ref=block,
                        dst_ref=target.at[slot],
                        send_sem=send.at[n, ms],
                        recv_sem=recv.at[n, slot],
                        device_id=(y * 2 + g % 2, seq_to),
                        device_id_type=MESH,
                    ).start()

                @pl.when(mine)
                def _():
                    pltpu.make_async_copy(block, target.at[slot], local.at[n]).start()

    def wait(n):
        source, target = sources[n], targets[n]
        for ms in range(lay.MS):
            seq_to = (ms * 2 + c) * lay.Cq + g // 2
            mine = jnp.logical_and(seq_to == b, g % 2 == c)
            block = source.at[ms // lay.items, ms % lay.items]

            @pl.when(jnp.logical_not(mine))
            def _():
                pltpu.make_async_remote_copy(
                    src_ref=block,
                    dst_ref=target.at[slot],
                    send_sem=send.at[n, ms],
                    recv_sem=recv.at[n, slot],
                    device_id=(y * 2 + g % 2, seq_to),
                    device_id_type=MESH,
                ).wait_send()

            @pl.when(mine)
            def _():
                pltpu.make_async_copy(block, target.at[slot], local.at[n]).wait()

        for j in range(lay.BL):
            from_b = gm * lay.BL + j
            own = jnp.logical_and(from_b == b, qm % 2 == c)

            @pl.when(jnp.logical_not(own))
            def _():
                pltpu.make_async_remote_copy(
                    src_ref=source.at[0, 0],
                    dst_ref=target.at[j],
                    send_sem=send.at[n, 0],
                    recv_sem=recv.at[n, j],
                    device_id=(y * 2 + qm % 2, from_b),
                    device_id_type=MESH,
                ).wait_recv()

    return begin, wait


def reshard_out(lay, sources, targets, send, recv, local):
    y, c, z, x, b = lay.here()
    g = b // lay.BL
    qm = b // lay.Cq
    gm = (b % lay.Cq) * 2 + c
    ms_to = qm // 2
    m_to, s_to = ms_to // lay.items, ms_to % lay.items

    def copies(n, j):
        from_b = gm * lay.BL + j
        own = jnp.logical_and(from_b == b, qm % 2 == c)
        remote = pltpu.make_async_remote_copy(
            src_ref=sources[n].at[j],
            dst_ref=targets[n].at[m_to, s_to],
            send_sem=send.at[n, j],
            recv_sem=recv.at[n, ms_to],
            device_id=(y * 2 + qm % 2, from_b),
            device_id_type=MESH,
        )
        near = pltpu.make_async_copy(sources[n].at[j], targets[n].at[m_to, s_to], local.at[n])
        return own, remote, near

    def begin(n):
        for j in range(lay.BL):
            own, remote, near = copies(n, j)
            pl.when(jnp.logical_not(own))(remote.start)
            pl.when(own)(near.start)

    def wait(n):
        for j in range(lay.BL):
            own, remote, near = copies(n, j)
            pl.when(jnp.logical_not(own))(remote.wait_send)
            pl.when(own)(near.wait)
        for ms in range(lay.MS):
            seq_at = (ms * 2 + c) * lay.Cq + g // 2
            own = jnp.logical_and(seq_at == b, g % 2 == c)

            @pl.when(jnp.logical_not(own))
            def _():
                pltpu.make_async_remote_copy(
                    src_ref=sources[n].at[0],
                    dst_ref=targets[n].at[ms // lay.items, ms % lay.items],
                    send_sem=send.at[n, 0],
                    recv_sem=recv.at[n, ms],
                    device_id=(y * 2 + g % 2, seq_at),
                    device_id_type=MESH,
                ).wait_recv()

    return begin, wait


def chunks_of(shapes, limit):
    result = []
    for n, shape in enumerate(shapes):
        tiles = shape[-1] // LANES
        cuts = max(1, -(-shape[0] * shape[-1] // limit))
        at = 0
        for cut in range(cuts):
            width = (tiles - at) // (cuts - cut) if cut == cuts - 1 else -(-(tiles - at) // (cuts - cut))
            result.append((n, at * LANES, width * LANES))
            at += width
    return result


def column_blocks(columns, most=768):
    cuts = -(-columns // most)
    while (columns // LANES) % cuts:
        cuts += 1
    width = columns // cuts
    return [(i * width, width) for i in range(cuts)]


def weight_block(full, stage, sem, at, width):
    target = stage.at[:, :, :, :, :, pl.ds(0, width)]
    copy = pltpu.make_async_copy(full.at[:, :, :, :, :, pl.ds(at, width)], target, sem)
    copy.start()
    copy.wait()
    block = stage[:, :, :, :, :, 0:width]
    return block.reshape(-1, width)


def gather_kernel(lay, count, chunks, refs):
    tok, cot = refs[0], refs[1]
    shards = refs[2 : 2 + count]
    tok_out, cot_out = refs[2 + count], refs[3 + count]
    fulls = refs[4 + count : 4 + 2 * count]
    send, recv, local, t_send, t_recv, t_local = refs[4 + 2 * count :]
    y, c, z, x, b = lay.here()
    X, Y, Z = lay.X, lay.Y, lay.Z
    greet(lay)
    wire = Wire(lay, send, recv)
    begin, wait = reshard_in(lay, (tok, cot), (tok_out, cot_out), t_send, t_recv, t_local)
    total = len(chunks)
    owns = []
    for i, (n, at, width) in enumerate(chunks):
        cols = pl.ds(at, width)
        copy = pltpu.make_async_copy(
            shards[n].at[:, cols], fulls[n].at[y, c, z, x, :, cols], local.at[i]
        )
        copy.start()
        owns.append(copy)
    arrived = [dict() for i in range(total)]

    def stage_z(i):
        n, at, width = chunks[i]
        cols = pl.ds(at, width)
        arrived[i]["z"] = [
            wire.start(
                shards[n].at[:, cols],
                fulls[n].at[y, c, z, x, :, cols],
                wire.to(y, c, (z + k) % Z, x),
            )
            for k in range(1, Z)
        ]

    def parts(i):
        n, at, width = chunks[i]
        left = half_columns(width)
        result = [(at, left)]
        if left < width:
            result.append((at + left, width - left))
        return result

    def to_core(i, block):
        arrived[i].setdefault("core", []).append(wire.start(block, block, wire.to(y, 1 - c, z, x)))

    def stage_one(i):
        owns[i].wait()
        for copy in arrived[i]["z"]:
            copy.wait_recv()
        n, first, columns = chunks[i]
        full = fulls[n]
        for half, (at, width) in enumerate(parts(i)):
            block = full.at[y, c, :, x, :, pl.ds(at, width)]
            if half == 0:
                arrived[i]["x0"] = [
                    wire.start(block, block, wire.to(y, c, z, (x + k) % X)) for k in range(1, X)
                ]
            else:
                arrived[i]["y1"] = [
                    wire.start(block, block, wire.to((y + k) % Y, c, z, x)) for k in range(1, Y)
                ]
        to_core(i, full.at[y, c, :, x, :, pl.ds(first, columns)])

    def stage_two(i):
        full = fulls[chunks[i][0]]
        for half, (at, width) in enumerate(parts(i)):
            cols = pl.ds(at, width)
            if half == 0:
                for copy in arrived[i]["x0"]:
                    copy.wait_recv()
                block = full.at[y, c, :, :, :, cols]
                arrived[i]["y0"] = [
                    wire.start(block, block, wire.to((y + k) % Y, c, z, x)) for k in range(1, Y)
                ]
                for k in range(1, X):
                    to_core(i, full.at[y, c, :, (x + X - k) % X, :, cols])
            else:
                for copy in arrived[i]["y1"]:
                    copy.wait_recv()
                block = full.at[:, c, :, x, :, cols]
                arrived[i]["x1"] = [
                    wire.start(block, block, wire.to(y, c, z, (x + k) % X)) for k in range(1, X)
                ]
                for k in range(1, Y):
                    to_core(i, full.at[(y + Y - k) % Y, c, :, x, :, cols])

    def stage_three(i):
        full = fulls[chunks[i][0]]
        for half, (at, width) in enumerate(parts(i)):
            cols = pl.ds(at, width)
            if half == 0:
                for k, copy in enumerate(arrived[i]["y0"], 1):
                    copy.wait_recv()
                    to_core(i, full.at[(y + Y - k) % Y, c, :, :, :, cols])
            else:
                for k, copy in enumerate(arrived[i]["x1"], 1):
                    copy.wait_recv()
                    to_core(i, full.at[:, c, :, (x + X - k) % X, :, cols])

    def finish():
        for i in range(total):
            for copy in arrived[i]["core"]:
                copy.wait_recv()
        wire.finish()

    def gathered(n):
        for i in range(total):
            if chunks[i][0] == n:
                for copy in arrived[i].pop("core"):
                    copy.wait_recv()
                arrived[i]["core"] = []

    return wire, (begin, wait), (stage_z, stage_one, stage_two, stage_three), gathered, finish


def group_copies(lay, send, recv, source, inbox, forward):
    y, c, z, x, b = lay.here()
    q = b // lay.Cq
    g = (b % lay.Cq) * 2 + c
    copies = []
    for k in range(1, lay.G):
        t = (g + (k if forward else lay.G - k)) % lay.G
        copies.append(
            pltpu.make_async_remote_copy(
                src_ref=source,
                dst_ref=inbox.at[k - 1],
                send_sem=send.at[k - 1],
                recv_sem=recv.at[k - 1],
                device_id=(y * 2 + t % 2, q * lay.Cq + t // 2),
                device_id_type=MESH,
            )
        )
    return copies, g


def to_tiles(low, tiles, r0, rows):
    for t in range(tiles.shape[0]):
        tiles[t, pl.ds(r0, rows), :] = low[:, t * LANES : (t + 1) * LANES].astype(F32)


def make_tables(lay, H, pack, raw, table, turned):
    r = pack.shape[4]
    total = lay.Y * 2 * lay.Z * lay.X

    def one(i, carry):
        block = pack[i // (2 * lay.Z * lay.X), i // (lay.Z * lay.X) % 2, i // lay.X % lay.Z, i % lay.X]
        raw[pl.ds(i * r, r), :] = block.astype(F32)
        return carry

    lax.fori_loop(0, total, one, 0)
    for t in range(table.shape[0]):
        v = raw[t * LANES : (t + 1) * LANES, :].T
        turned[t] = v
        leak = jax.nn.sigmoid(v[:H])
        decay = 1.0 - leak * jax.nn.sigmoid(v[H : 2 * H])
        table[t, :H] = decay
        table[t, H : 2 * H] = jnp.log(decay)
        table[t, 2 * H : 3 * H] = leak * v[2 * H : 3 * H] * v[3 * H : 4 * H] * (H ** (-0.5))


def carry_in(lay, H, rows, g, inbox, table, inc, t, later):
    log = table[t, H : 2 * H]
    state = jnp.zeros((H, LANES), F32)
    slope = jnp.zeros((H, LANES), F32)
    for k in range(1, lay.G):
        span = (k - 1) * rows
        valid = (g + k < lay.G) if later else (k <= g)
        s_part = inbox[k - 1, t, :H]
        r_part = s_part * 0.0 if later else inbox[k - 1, t, H : 2 * H]
        if span:
            power = jnp.exp(span * log)
            r_part = power * r_part + (span * jnp.exp((span - 1) * log)) * s_part
            s_part = power * s_part
        state = state + jnp.where(valid, s_part, 0.0)
        slope = slope + jnp.where(valid, r_part, 0.0)
    inc[t, :H] = state
    if not later:
        inc[t, H : 2 * H] = slope


def forward_kernel(lay, count, chunks, H, refs):
    n_in, n_out = 2 + count, 15 + count
    ins = refs[:n_in]
    query_gain, query_bias, key_gain, relative = refs[n_in : n_in + 4]
    refs = refs[n_in + 4 :]
    outs, scratch = refs[:n_out], refs[n_out:]
    tok_out, cot_out = outs[0], outs[1]
    fulls = outs[2 : 2 + count]
    mixed, ema, si, ri, table, turned = outs[2 + count : 8 + count]
    value_pre, base, queries, keys, vals, probs, attended = outs[8 + count :]
    sems, work = scratch[:6], scratch[6:]
    xt, pack, raw, s_end, r_end, mine, inbox, inc, stage, strip, scores, load, c_send, c_recv = work
    wire, (begin, wait), stages, gathered, finish = gather_kernel(
        lay, count, chunks, ins + (tok_out, cot_out) + tuple(fulls) + sems
    )
    stage_z, stage_one, stage_two, stage_three = stages
    total = len(chunks)
    rows = xt.shape[1]
    tiles = xt.shape[0]
    copies, g = group_copies(lay, c_send.at[0], c_recv.at[0], mine, inbox, True)
    others = pl.ds(1, lay.G - 1)
    vals_copies, g = group_copies(
        lay, c_send.at[1], c_recv.at[1], vals.at[0], vals.at[others], True
    )
    keys_copies, g = group_copies(
        lay, c_send.at[2], c_recv.at[2], keys.at[0], keys.at[others], True
    )
    width = tok_out.shape[2]
    zw = queries.shape[1]

    def value(at, cols):
        v = mm(tok_out[...].reshape(rows, width), weight_block(fulls[1], stage, load, at, cols))
        value_pre[:, at : at + cols] = v
        vals[0, :, at : at + cols] = (v * jax.nn.sigmoid(v)).astype(BF16)

    def send_values():
        for copy in vals_copies:
            copy.start()

    def bias():
        bias_kernel(lay.G * rows, relative.shape[0], relative, strip)

    def base_out(at, cols):
        base[:, at : at + cols] = mm(mixed[...], weight_block(fulls[2], stage, load, at, cols))

    def send_keys():
        z_pre = base[:, :zw]
        shared = z_pre * jax.nn.sigmoid(z_pre)
        queries[...] = (shared * query_gain[...] + query_bias[...]).astype(BF16)
        keys[0] = (shared * key_gain[...]).astype(BF16)
        for copy in keys_copies:
            copy.start()

    def keys_here():
        for copy in keys_copies + vals_copies:
            copy.wait()

    def attend(part):
        y, c, z, x, b = lay.here()
        q_at = b // lay.Cq
        first = ((y * 2 + q_at % 2) * lay.Z * lay.X) * pack.shape[4]
        marks = raw[pl.ds(first, 1), :]
        lane = lax.broadcasted_iota(jnp.int32, (1, LANES), 1)
        mark = jnp.sum(
            jnp.where(lane == 4 * H + 3 + q_at // 2, marks, 0.0), axis=1, keepdims=True
        )
        far = jnp.where(mark == float(lay.G * rows), 0.0, masked_fill)
        attend_body(lay, g, far, queries, strip, keys, vals, attended, probs, scores, part)

    def tables():
        gathered(0)
        copy = pltpu.make_async_copy(fulls[0], pack, load)
        copy.start()
        copy.wait()
        make_tables(lay, H, pack, raw, table, turned)

    def tokens():
        wait(0)
        for j in range(lay.BL):
            to_tiles(tok_out[j], xt, j * (rows // lay.BL), rows // lay.BL)

    def ends(first, last):
        def one(t, carry):
            ema_ends_kernel(H, xt.at[t], table.at[t], s_end.at[t], r_end.at[t])
            for h in range(H):
                mine[t, pl.ds(h, 1), :] = s_end[t, h, SEG - 1 : SEG, :]
                mine[t, pl.ds(H + h, 1), :] = r_end[t, h, SEG - 1 : SEG, :]
            return carry

        lax.fori_loop(first, last, one, 0)

    def exchange():
        for copy in copies:
            copy.start()

    def carries():
        for copy in copies:
            copy.wait()
        for t in range(tiles):
            carry_in(lay, H, rows, g, inbox, table, inc, t, False)

    def out(first, last):
        def one(t, carry):
            ema_out_kernel(
                H, xt.at[t], table.at[t], turned.at[t, pl.ds(4 * H, 1)], s_end.at[t], r_end.at[t],
                inc.at[t], ema.at[t], si.at[t], ri.at[t],
            )
            return carry

        lax.fori_loop(first, last, one, 0)
        for t in range(first, last):
            for r0 in range(0, rows, 128):
                v = ema[t, pl.ds(r0, 128), :]
                mixed[pl.ds(r0, 128), t * LANES : (t + 1) * LANES] = (
                    v * jax.nn.sigmoid(v)
                ).astype(BF16)

    steps = [lambda: begin(0)]
    last = {}
    for i in range(min(AHEAD, total)):
        steps.append(functools.partial(stage_z, i))
    for turn in range(total + 2 * LAG):
        if 0 <= turn - 2 * LAG < total:
            last[chunks[turn - 2 * LAG][0]] = len(steps)
            steps.append(functools.partial(stage_three, turn - 2 * LAG))
        if 0 <= turn - LAG < total:
            steps.append(functools.partial(stage_two, turn - LAG))
        if turn < total:
            steps.append(functools.partial(stage_one, turn))
        if turn + AHEAD < total:
            steps.append(functools.partial(stage_z, turn + AHEAD))
        if turn == PLAN[5]:
            steps.append(lambda: begin(1))
    base_blocks = column_blocks(base.shape[1])
    todo = [(last[0] + PLAN[0], tables), (PLAN[1], tokens)]
    todo += [(0, functools.partial(ends, t, t + 1)) for t in range(tiles)]
    todo += [(0, exchange)]
    todo += [(last[1] + PLAN[2], lambda: gathered(1))]
    todo += [(0, functools.partial(value, *block)) for block in column_blocks(vals.shape[2])]
    todo += [(0, send_values), (0, carries)]
    todo += [(0, functools.partial(out, t, t + 1)) for t in range(tiles)]
    todo += [(0, bias), (last[2] + PLAN[3], lambda: gathered(2))]
    todo += [(0, functools.partial(base_out, *base_blocks[0])), (0, send_keys)]
    todo += [(0, functools.partial(base_out, *block)) for block in base_blocks[1:]]
    todo += [(0, keys_here)]
    todo += [(0, functools.partial(attend, part)) for part in range(rows // QB)]
    interleave(steps, todo, PLAN[6])
    finish()
    wait(1)


def interleave(steps, todo, most):
    todo = list(todo)
    done = set()

    def run():
        first, piece, name = (todo.pop(0) + (None,))[:3]
        piece()
        done.add(name)

    for number, step in enumerate(steps):
        step, needs = step if isinstance(step, tuple) else (step, None)
        while needs is not None and needs not in done:
            run()
        step()
        for i in range(most):
            if todo and todo[0][0] <= number:
                run()
    while todo:
        run()


PLAN = (1, 12, 1, 1, 0, 9, 1)


def forward_all(lay, H, tokens, cotangent, shards, query_gain, query_bias, key_gain, relative):
    count = len(shards)
    chunks = chunks_of([shard.shape for shard in shards], shards[0].shape[0] * LIMIT)
    micro, items, rows, width = tokens.shape
    per = (lay.Z - 1) + 2 * (lay.X - 1 + lay.Y - 1) + 1 + 2 * (lay.X - 1 + lay.Y - 1)
    blocks = jax.ShapeDtypeStruct((lay.BL, rows, width), BF16)
    fulls = [
        jax.ShapeDtypeStruct((lay.Y, 2, lay.Z, lay.X) + shard.shape, shard.dtype)
        for shard in shards
    ]
    T, R = width // LANES, lay.BL * rows
    state = (T, H, SEG, LANES)
    outs = [blocks, blocks] + fulls
    outs += [
        jax.ShapeDtypeStruct((R, width), BF16),
        jax.ShapeDtypeStruct((T, R, LANES), F32),
        jax.ShapeDtypeStruct(state, F32),
        jax.ShapeDtypeStruct(state, F32),
        jax.ShapeDtypeStruct((T, 3 * H, LANES), F32),
        jax.ShapeDtypeStruct((T, LANES, LANES), F32),
    ]
    V, cols, zw, G = shards[1].shape[1], shards[2].shape[1], query_gain.shape[1], lay.G
    outs += [
        jax.ShapeDtypeStruct((R, V), F32),
        jax.ShapeDtypeStruct((R, cols), F32),
        jax.ShapeDtypeStruct((R, zw), BF16),
        jax.ShapeDtypeStruct((G, R, zw), BF16),
        jax.ShapeDtypeStruct((G, R, V), BF16),
        jax.ShapeDtypeStruct((G, R, R), BF16),
        jax.ShapeDtypeStruct((R, V), F32),
    ]

    def body(*refs):
        forward_kernel(lay, count, chunks, H, refs)

    result = pl.pallas_call(
        body,
        out_shape=outs,
        in_specs=[ANY] * (2 + count) + [VM] * 3 + [SM],
        out_specs=[VM] + [ANY] * (1 + count) + [VM] * 13,
        scratch_shapes=[
            pltpu.SemaphoreType.DMA((len(chunks) * per,)),
            pltpu.SemaphoreType.DMA((len(chunks) * per,)),
            pltpu.SemaphoreType.DMA((len(chunks),)),
            pltpu.SemaphoreType.DMA((2, lay.MS)),
            pltpu.SemaphoreType.DMA((2, lay.BL)),
            pltpu.SemaphoreType.DMA((2,)),
            pltpu.VMEM((T, R, LANES), F32),
            pltpu.VMEM(fulls[0].shape, fulls[0].dtype),
            pltpu.VMEM((width, LANES), F32),
            pltpu.VMEM(state, F32),
            pltpu.VMEM(state, F32),
            pltpu.VMEM((T, 2 * H, LANES), F32),
            pltpu.VMEM((lay.G - 1, T, 2 * H, LANES), F32),
            pltpu.VMEM((T, 2 * H, LANES), F32),
            pltpu.VMEM((lay.Y, 2, lay.Z, lay.X, shards[1].shape[0], 768), BF16),
            pltpu.VMEM((QB, (G + 1) * R), F32),
            pltpu.VMEM((QB, G * R), F32),
            pltpu.SemaphoreType.DMA,
            pltpu.SemaphoreType.DMA((3, lay.G - 1)),
            pltpu.SemaphoreType.DMA((3, lay.G - 1)),
        ],
        compiler_params=pltpu.CompilerParams(
            collective_id=0, has_side_effects=True, vmem_limit_bytes=58 * 2**20
        ),
        name="forward_all",
    )(tokens, cotangent, *shards, query_gain, query_bias, key_gain, relative)
    return result[0], result[1], result[2 : 2 + count], result[2 + count :]


def add_blocks(total, index, extra, extra_index, counts, width_at):
    size = int(np.prod(counts)) if counts else 1

    def one(i, carry):
        places = []
        for extent in reversed(counts):
            places.insert(0, i % extent)
            i = i // extent
        a, e = index(*places), extra_index(*places)
        total[a] = total[a] + extra[e]
        return carry

    lax.fori_loop(0, size, one, 0)


def scatter_kernel(lay, H, NB, chunks, ins, outs, scratch):
    (
        grads, x_low, d_in, d_att, delta, queries, keys, vals, probs, z_pre, gains_small, mixed, ema,
        base_rest, value_pre, w_base, w_value, pre, gains, table, turned, si, ri, block_out,
    ) = ins
    results, small_out, outs_to, made, dvo, dvi = outs
    bufs, own = scratch[: 6 * len(chunks)], scratch[6 * len(chunks) :]
    small_acc, small_recv, send, recv, local, t_send, t_recv, t_local = own[:8]
    xt, dt, sums, flat, split, l_end, mine, inbox, inc, gx, c_send, c_recv = own[8:20]
    dx = xt
    stage, vstage, bstage, pstage, ds, strip, dq, dko, dki, zlow, mixed_acc, x_acc, load = own[20:33]
    gstage, mixed_t, loads = own[33:36]
    halves = own[36:]
    grads = grads + made + (split,)
    y, c, z, x, b = lay.here()
    X, Y, Z = lay.X, lay.Y, lay.Z
    greet(lay)
    wire = Wire(lay, send, recv)
    begin, wait = reshard_out(lay, (block_out, gx), outs_to, t_send, t_recv, t_local)
    total = len(chunks)
    arrived = [dict() for i in range(total)]

    def buf(i, name):
        return bufs[6 * i + ("acc", "x0", "y1", "y0", "x1", "z").index(name)]

    def parts(i):
        n, at, width = chunks[i]
        left = half_columns(width)
        result = [(0, left)]
        if left < width:
            result.append((left, width - left))
        return result

    def own_half(i):
        n, at, width = chunks[i]
        if n == len(grads) - 1:
            return None
        source = grads[n].at[:, c, :, :, :, pl.ds(at, width)]
        return pltpu.make_async_copy(source, half_of(i), local.at[i])

    def half_of(i):
        n, at, width = chunks[i]
        r = grads[n].shape[4]
        room = [h for h in halves if h.shape[4] == r][0]
        return room.at[i % 2, :, :, :, :, pl.ds(0, width)]

    def prefetch_half(i):
        near = own_half(i) if i < total else None
        if near is not None:
            near.start()

    def stage_core(i):
        n, at, width = chunks[i]
        if n_base <= n < n_base + 2:
            settle()
        if i == 0:
            prefetch_half(0)
        arrived[i]["core"] = wire.start(
            grads[n].at[:, 1 - c, :, :, :, pl.ds(at, width)],
            buf(i, "acc"),
            wire.to(y, 1 - c, z, x),
        )

    def stage_one(i):
        n, first, columns = chunks[i]
        acc = buf(i, "acc")
        near = own_half(i)
        if near is not None:
            near.wait()
        arrived[i]["core"].wait_recv()
        if near is not None:
            mine_half = half_of(i)
            add_blocks(acc, lambda *p: p, mine_half, lambda *p: p, (Y, Z, X), None)
        else:
            add_blocks(
                acc, lambda *p: p, split, lambda p, q, s: (p, c, q, s), (Y, Z, X), None
            )
        prefetch_half(i + 1)
        for half, (at, width) in enumerate(parts(i)):
            cols = pl.ds(at, width)
            if half == 0:
                arrived[i]["x0"] = [
                    wire.start(
                        acc.at[:, :, (x + k) % X, :, cols],
                        buf(i, "x0").at[k - 1],
                        wire.to(y, c, z, (x + k) % X),
                    )
                    for k in range(1, X)
                ]
            else:
                arrived[i]["y1"] = [
                    wire.start(
                        acc.at[(y + k) % Y, :, :, :, cols],
                        buf(i, "y1").at[k - 1],
                        wire.to((y + k) % Y, c, z, x),
                    )
                    for k in range(1, Y)
                ]

    def stage_two(i):
        acc = buf(i, "acc")
        for half, (at, width) in enumerate(parts(i)):
            cols = slice(at, at + width)
            view = pl.ds(at, width)
            if half == 0:
                for k, copy in enumerate(arrived[i]["x0"]):
                    copy.wait_recv()
                    add_blocks(
                        acc,
                        lambda p, q: (p, q, x, slice(None), cols),
                        buf(i, "x0"),
                        lambda p, q: (k, p, q),
                        (Y, Z),
                        None,
                    )
                arrived[i]["y0"] = [
                    wire.start(
                        acc.at[(y + k) % Y, :, x, :, view],
                        buf(i, "y0").at[k - 1],
                        wire.to((y + k) % Y, c, z, x),
                    )
                    for k in range(1, Y)
                ]
            else:
                for k, copy in enumerate(arrived[i]["y1"]):
                    copy.wait_recv()
                    add_blocks(
                        acc,
                        lambda p, q: (y, p, q, slice(None), cols),
                        buf(i, "y1"),
                        lambda p, q: (k, p, q),
                        (Z, X),
                        None,
                    )
                arrived[i]["x1"] = [
                    wire.start(
                        acc.at[y, :, (x + k) % X, :, view],
                        buf(i, "x1").at[k - 1],
                        wire.to(y, c, z, (x + k) % X),
                    )
                    for k in range(1, X)
                ]

    def stage_three(i):
        acc = buf(i, "acc")
        for half, (at, width) in enumerate(parts(i)):
            cols = slice(at, at + width)
            name = "y0" if half == 0 else "x1"
            for k, copy in enumerate(arrived[i][name]):
                copy.wait_recv()
                add_blocks(
                    acc,
                    lambda p: (y, p, x, slice(None), cols),
                    buf(i, name),
                    lambda p: (k, p),
                    (Z,),
                    None,
                )
        arrived[i]["z"] = [
            wire.start(
                acc.at[y, (z + k) % Z, x], buf(i, "z").at[k - 1], wire.to(y, c, (z + k) % Z, x)
            )
            for k in range(1, Z)
        ]

    def stage_four(i):
        n, at, width = chunks[i]
        total = buf(i, "acc")[y, z, x].astype(F32)
        for k, copy in enumerate(arrived[i]["z"]):
            copy.wait_recv()
            total = total + buf(i, "z")[k].astype(F32)
        results[n][:, pl.ds(at, width)] = total

    small_at = [0]

    def small_stage(moves):
        copies = []
        for target in moves:
            slot = small_at[0]
            small_at[0] += 1
            copies.append((slot, wire.start(small_acc, small_recv.at[slot], target)))
        for slot, copy in copies:
            copy.wait_send()
            wire.sent = [other for other in wire.sent if other is not copy]
        for slot, copy in copies:
            copy.wait_recv()
            small_acc[...] += small_recv[slot]

    rows, tiles = xt.shape[1], xt.shape[0]
    per_block = rows // lay.BL
    copies, g = group_copies(lay, c_send.at[0], c_recv.at[0], mine, inbox, False)
    G, zw = lay.G, queries.shape[1]
    D = x_low.shape[2]
    scale = zw ** (-0.5)
    n_base, n_value = len(grads) - 3, len(grads) - 2
    q_at = b // lay.Cq

    def back_copy(k, source, target, kind):
        t = (g + G - k) % G
        return pltpu.make_async_remote_copy(
            src_ref=source,
            dst_ref=target,
            send_sem=c_send.at[kind, k - 1],
            recv_sem=c_recv.at[kind, k - 1],
            device_id=(y * 2 + t % 2, q_at * lay.Cq + t // 2),
            device_id_type=MESH,
        )

    key_copies = [back_copy(k, dko.at[k - 1], dki.at[k - 1], 1) for k in range(1, G)]
    val_copies = [back_copy(k, dvo.at[k - 1], dvi.at[k - 1], 2) for k in range(1, G)]

    def fetch(source, target):
        copy = pltpu.make_async_copy(source, target, load)
        copy.start()
        copy.wait()

    storing = []

    def settle():
        while storing:
            storing.pop().wait()

    def keep_grad(n, at, grad):
        columns = grad.shape[1]
        r = made[n].shape[4]
        low = grad.astype(BF16).reshape(Y, 2, Z, X, r, columns)
        settle()
        gstage[:, :, :, :, :, :columns] = low
        copy = pltpu.make_async_copy(
            gstage.at[:, :, :, :, :, pl.ds(0, columns)],
            made[n].at[:, :, :, :, :, pl.ds(at, columns)],
            loads.at[0],
        )
        copy.start()
        storing.append(copy)

    all_base, all_value = column_blocks(w_base.shape[5]), column_blocks(w_value.shape[5])
    weight_order = [(w_base,) + block for block in all_base[1:] + all_base[:1]]
    weight_order += [(w_value,) + block for block in all_value]
    coming = {}

    def weight_copy(number):
        full, at, columns = weight_order[number]
        return pltpu.make_async_copy(
            full.at[:, :, :, :, :, pl.ds(at, columns)],
            stage.at[:, :, :, :, :, pl.ds(0, columns)],
            loads.at[1],
        )

    def next_weight(number):
        if number < len(weight_order):
            coming["weight"] = weight_copy(number)
            coming["weight"].start()

    def rest_copy(number):
        full, at, columns = weight_order[number]
        if at == 0:
            return pltpu.make_async_copy(
                base_rest.at[:, pl.ds(0, columns - zw)],
                bstage.at[:, pl.ds(zw, columns - zw)],
                loads.at[2],
            )
        return pltpu.make_async_copy(
            base_rest.at[:, pl.ds(at - zw, columns)], bstage.at[:, pl.ds(0, columns)], loads.at[2]
        )

    def next_rest(number):
        if number < len(all_base):
            coming["rest"] = rest_copy(number)
            coming["rest"].start()

    def next_pre(number):
        if number < len(all_value):
            at, columns = all_value[number]
            coming["pre"] = pltpu.make_async_copy(
                value_pre.at[:, pl.ds(at, columns)], pstage.at[:, pl.ds(0, columns)], loads.at[3]
            )
            coming["pre"].start()

    def begin_fetch():
        next_weight(0)
        next_rest(0)
        next_pre(0)
        coming["x"] = pltpu.make_async_copy(pre, x_acc, loads.at[4])
        coming["x"].start()
        mixed_t[...] = mixed[...].astype(F32).T.astype(BF16)

    def weight_here(columns):
        coming["weight"].wait()
        return stage[:, :, :, :, :, 0:columns].reshape(-1, columns)

    def base_block(number):
        full, at, columns = weight_order[number]
        coming["rest"].wait()
        if at == 0:
            bstage[:, :zw] = zlow[...]
        low = bstage[:, :columns]
        keep_grad(0, at, mm(mixed_t[...], low))
        part = mm_t(low, weight_here(columns))
        mixed_acc[...] = part if number == 0 else mixed_acc[...] + part
        next_weight(number + 1)
        next_rest(number + 1)

    def load_values(k):
        fetch(vals.at[k], vstage)
        if k == G - 1:
            strip[...] = jnp.zeros(strip.shape, F32)

    def scores_back(k, i):
        at = i * QB
        here = pl.ds(at, QB)
        owner = lax.rem(g - k + G, G)
        dw = mm_t(d_att[here, :], vstage[...])
        p = probs[k, here, :].astype(F32)
        grad = p * (dw - delta[here, :])
        off = jnp.clip(G * rows - rows * (g - owner) - at, 0, G * rows)
        strip[:, pl.ds(pl.multiple_of(off, LANES), rows)] += grad
        low = grad.astype(BF16)
        ds[here, :] = low
        part = mm(low, keys[k]) * scale
        dq[here, :] = part if k == G - 1 else dq[here, :] + part

    def keys_back(k):
        grad = dot_t(ds[...], queries[...]) * scale
        if k:
            dko[k - 1] = grad.astype(BF16)
            key_copies[k - 1].start()
        else:
            for copy in key_copies:
                copy.wait()
            for j in range(1, G):
                grad = grad + dki[j - 1].astype(F32)
            pre_z = z_pre[...]
            gate = jax.nn.sigmoid(pre_z)
            shared = pre_z * gate
            small_acc[0:1, :] = jnp.sum(dq[...] * shared, axis=0, keepdims=True)
            small_acc[1:2, :] = jnp.sum(dq[...], axis=0, keepdims=True)
            small_acc[2:3, :] = jnp.sum(grad * shared, axis=0, keepdims=True)
            d_shared = dq[...] * gains_small[0:1, :] + grad * gains_small[1:2, :]
            zlow[...] = (d_shared * (gate * (1.0 + pre_z * (1.0 - gate)))).astype(BF16)

    def values_back(k):
        for at, columns in column_blocks(vstage.shape[1]):
            vstage[:, at : at + columns] = dot_t(
                probs[k], d_att[:, at : at + columns]
            ).astype(BF16)
        fetch(vstage, dvo.at[k - 1])
        val_copies[k - 1].start()

    def buckets():
        sums_of = bucket_sums(G * rows, NB, strip)
        lane = lax.broadcasted_iota(jnp.int32, (1, LANES), 1)
        line = jnp.zeros((1, LANES), F32)
        for k in range(NB):
            line = jnp.where(lane == k, jnp.sum(sums_of[k], axis=1, keepdims=True), line)
        small_acc[3:4, :] = line
        small_acc[4:8, :] = jnp.zeros((4, LANES), F32)

    def values_here():
        for copy in val_copies:
            copy.wait()

    def value_block(number):
        full, at, columns = weight_order[len(all_base) + number]
        cols = pl.ds(at, columns)
        if number == 0:
            mixed_t[...] = x_low[...].reshape(rows, D).astype(F32).T.astype(BF16)
            coming["x"].wait()
        grad = dot_t(probs[0], d_att[:, at : at + columns])
        for k in range(1, G):
            fetch(dvi.at[k - 1, :, cols], bstage.at[:, pl.ds(0, columns)])
            grad = grad + bstage[:, :columns].astype(F32)
        coming["pre"].wait()
        v = pstage[:, :columns]
        gate = jax.nn.sigmoid(v)
        low = (grad * (gate * (1.0 + v * (1.0 - gate)))).astype(BF16)
        next_pre(number + 1)
        keep_grad(1, at, mm(mixed_t[...], low))
        x_acc[...] += mm_t(low, weight_here(columns))
        next_weight(len(all_base) + number + 1)

    def d_ema(t):
        v = ema[t]
        gate = jax.nn.sigmoid(v)
        dt[t] = mixed_acc[:, t * LANES : (t + 1) * LANES] * (gate * (1.0 + v * (1.0 - gate)))

    def tile_x():
        for j in range(lay.BL):
            to_tiles(x_low[j], xt, j * per_block, per_block)

    def ends(t):
        ema_back_ends_kernel(H, dt.at[t], table.at[t], l_end.at[t])
        for h in range(H):
            mine[t, pl.ds(h, 1), :] = l_end[t, h, 0:1, :]

    def exchange():
        for copy in copies:
            copy.start()

    def carries():
        for copy in copies:
            copy.wait()
        for t in range(tiles):
            carry_in(lay, H, rows, g, inbox, table, inc, t, True)

    def correlate(t):
        ema_sums_kernel(H, xt.at[t], dt.at[t], table.at[t], si.at[t], ri.at[t], sums.at[t])

    def back(t):
        ema_back_kernel(
            H, dt.at[t], table.at[t], turned.at[t, pl.ds(4 * H, 1)], l_end.at[t], inc.at[t], dx.at[t]
        )
        cols = slice(t * LANES, (t + 1) * LANES)
        for j in range(lay.BL):
            at = pl.ds(j * per_block, per_block)
            gx[j, :, cols] = (x_acc[at, cols] + dx[t, at, :]).astype(BF16)

    def share_sums():
        r = split.shape[4]
        for t in range(tiles):
            sums[t, pl.ds(2 * H + 1, 2), :] = gains[0:2, t * LANES : (t + 1) * LANES]
            flat[t * LANES : (t + 1) * LANES, :] = sums[t].T

        def one(i, carry):
            split[i // (2 * Z * X), i // (Z * X) % 2, i // X % Z, i % X] = flat[pl.ds(i * r, r), :]
            return carry

        lax.fori_loop(0, 2 * X * Y * Z, one, 0)

    sums[...] = jnp.zeros(sums.shape, F32)
    xs = [wire.to(y, c, z, (x + k) % X) for k in range(1, X)]
    ys = [wire.to((y + k) % Y, c, z, x) for k in range(1, Y)]
    zs = [wire.to(y, c, (z + k) % Z, x) for k in range(1, Z)]

    run = functools.partial
    todo = [(0, begin_fetch)]
    for number in range(len(all_base) - 1):
        todo.append((0, run(base_block, number), (n_base, weight_order[number][1])))
    for k in list(range(1, G))[::-1] + [0]:
        todo.append((0, run(load_values, k)))
        todo += [(0, run(scores_back, k, i)) for i in range(rows // QB)]
        todo.append((0, run(keys_back, k)))
        if k:
            todo.append((0, run(values_back, k)))
    todo.append((0, run(base_block, len(all_base) - 1), (n_base, 0)))
    todo += [(0, run(d_ema, t)) for t in range(tiles)]
    todo += [(0, run(ends, t)) for t in range(tiles)]
    todo += [(0, exchange), (0, values_here)]
    for number, block in enumerate(all_value):
        todo.append((0, run(value_block, number), (n_value, block[0])))
    todo.append((0, carries))
    todo += [(0, run(back, t)) for t in range(tiles)]
    todo += [(0, lambda: begin(1)), (0, tile_x), (0, buckets, "small")]
    todo += [(0, run(correlate, t)) for t in range(tiles)]
    todo.append((0, share_sums, (len(grads) - 1, 0)))

    def needs(i):
        n, at, width = chunks[i]
        return (n, at) if n >= n_base else None

    steps = []
    for i in range(min(LEAD, total)):
        steps.append((run(stage_core, i), needs(i)))
    steps.append(lambda: begin(0))
    for turn in range(total + 3 * BLAG):
        for what, lag in ((stage_four, 3), (stage_three, 2), (stage_two, 1), (stage_one, 0)):
            if 0 <= turn - lag * BLAG < total:
                steps.append(run(what, turn - lag * BLAG))
        if turn + LEAD < total:
            steps.append((run(stage_core, turn + LEAD), needs(turn + LEAD)))
        if turn >= total:
            late = turn - total
            moves = ([wire.to(y, 1 - c, z, x)], xs, ys, zs)
            if late < 4:
                steps.append((run(small_stage, moves[late]), "small"))
    interleave(steps, todo, MOST)
    small_out[...] = small_acc[...]
    wait(0)
    wait(1)
    wire.finish()


LEAD = 3
MOST = 1
BLAG = 2


def dot_t(a, b):
    return lax.dot_general(a, b, (((0,), (0,)), ((), ())), preferred_element_type=F32)


def bucket_sums(length, bucket_count, strip):
    edges = bucket_edges(bucket_count)
    lag0 = lax.broadcasted_iota(jnp.int32, (QB, LANES), 0) - lax.broadcasted_iota(
        jnp.int32, (QB, LANES), 1
    )
    totals = [jnp.zeros((1, LANES), F32) for k in range(bucket_count)]
    for t in range((length + QB) // LANES):
        base = length - t * LANES
        low, high = base - LANES + 1, base + QB - 1
        if high < 0:
            continue
        value = strip[:, t * LANES : (t + 1) * LANES]
        for k in range(bucket_count):
            top = edges[k + 1] if k + 1 < bucket_count else length
            if edges[k] <= high and top > low:
                lag = lag0 + base
                inside = (lag >= edges[k]) & (lag < top)
                totals[k] = totals[k] + jnp.sum(jnp.where(inside, value, 0.0), axis=0, keepdims=True)
    return totals


def backward_all(lay, H, NB, grads, fulls, values, share):
    X, Y, Z, G = lay.X, lay.Y, lay.Z, lay.G
    R, V = values["d_att"].shape
    D = values["pre"].shape[1]
    T, zw = D // LANES, values["queries"].shape[1]
    rows = R // lay.BL
    micro = lay.MS // lay.items
    shapes = [grad.shape[-2:] for grad in grads] + [full.shape[-2:] for full in fulls] + [(share, LANES)]
    kinds = [grad.dtype for grad in grads] + [BF16, BF16, F32]
    known = len(grads)
    chunks = chunks_of([shape for shape in shapes[:known]], share * LIMIT)
    base_blocks = column_blocks(shapes[known][1])
    chunks += [(known,) + block for block in base_blocks[1:]]
    chunks += [(known,) + base_blocks[0]]
    chunks += [(known + 1,) + block for block in column_blocks(shapes[known + 1][1])]
    chunks += [(known + 2, 0, LANES)]
    scratch = []
    for n, at, cols in chunks:
        r = shapes[n][0]
        left = half_columns(cols)
        right = cols - left if cols > left else LANES
        kind = kinds[n]
        scratch += [
            pltpu.VMEM((Y, Z, X, r, cols), kind),
            pltpu.VMEM((X - 1, Y, Z, r, left), kind),
            pltpu.VMEM((Y - 1, Z, X, r, right), kind),
            pltpu.VMEM((Y - 1, Z, r, left), kind),
            pltpu.VMEM((X - 1, Z, r, right), kind),
            pltpu.VMEM((Z - 1, r, cols), kind),
        ]
    hops = 1 + (X - 1) + (Y - 1) + (Z - 1)
    per = 1 + 2 * (X - 1 + Y - 1) + Z - 1
    small = (8, LANES)
    outs = [jax.ShapeDtypeStruct(shape, F32) for shape in shapes]
    outs.append(jax.ShapeDtypeStruct(small, F32))
    outs += [jax.ShapeDtypeStruct((micro, lay.items, rows, D), BF16)] * 2
    outs += [jax.ShapeDtypeStruct(full.shape, BF16) for full in fulls]
    outs += [jax.ShapeDtypeStruct((G - 1, R, V), BF16)] * 2
    scratch += [pltpu.VMEM(small, F32), pltpu.VMEM((hops,) + small, F32)]
    heights = sorted({shapes[n][0] for n, at, width in chunks})
    widest = {r: max(w for n, at, w in chunks if shapes[n][0] == r) for r in heights}
    scratch += [
        pltpu.SemaphoreType.DMA((len(chunks) * per + hops,)),
        pltpu.SemaphoreType.DMA((len(chunks) * per + hops,)),
        pltpu.SemaphoreType.DMA((len(chunks),)),
        pltpu.SemaphoreType.DMA((2, lay.BL)),
        pltpu.SemaphoreType.DMA((2, lay.MS)),
        pltpu.SemaphoreType.DMA((2,)),
        pltpu.VMEM((T, R, LANES), F32),
        pltpu.VMEM((T, R, LANES), F32),
        pltpu.VMEM((T, LANES, LANES), F32),
        pltpu.VMEM((D, LANES), F32),
        pltpu.VMEM((Y, 2, Z, X, share, LANES), F32),
        pltpu.VMEM((T, H, SEG, LANES), F32),
        pltpu.VMEM((T, H, LANES), F32),
        pltpu.VMEM((G - 1, T, H, LANES), F32),
        pltpu.VMEM((T, H, LANES), F32),
        pltpu.VMEM((lay.BL, rows, D), BF16),
        pltpu.SemaphoreType.DMA((3, G - 1)),
        pltpu.SemaphoreType.DMA((3, G - 1)),
        pltpu.VMEM((Y, 2, Z, X, share, 768), BF16),
        pltpu.VMEM((R, V), BF16),
        pltpu.VMEM((R, 768), BF16),
        pltpu.VMEM((R, 768), F32),
        pltpu.VMEM((R, R), BF16),
        pltpu.VMEM((QB, (G + 1) * R), F32),
        pltpu.VMEM((R, zw), F32),
        pltpu.VMEM((G - 1, R, zw), BF16),
        pltpu.VMEM((G - 1, R, zw), BF16),
        pltpu.VMEM((R, zw), BF16),
        pltpu.VMEM((R, D), F32),
        pltpu.VMEM((R, D), F32),
        pltpu.SemaphoreType.DMA,
        pltpu.VMEM((Y, 2, Z, X, share, 768), BF16),
        pltpu.VMEM((D, R), BF16),
        pltpu.SemaphoreType.DMA((5,)),
    ]
    scratch += [pltpu.VMEM((2, Y, Z, X, r, widest[r]), BF16) for r in heights]
    order = (
        ("x_blocks", VM), ("d_in", ANY), ("d_att", VM), ("delta", VM), ("queries", VM), ("keys", VM),
        ("vals", ANY), ("probs", VM), ("z_pre", VM), ("gains_small", VM), ("mixed", VM), ("ema", VM),
        ("base_rest", ANY), ("value_pre", ANY), ("w_base", ANY), ("w_value", ANY), ("pre", ANY),
        ("gains", VM), ("table", VM), ("turned", VM), ("si", VM), ("ri", VM), ("block_out", ANY),
    )
    values = dict(values, w_base=fulls[0], w_value=fulls[1])
    order = tuple(item for item in order if item[0] != "d_in")

    def body(*refs):
        named = refs[known : known + len(order)]
        ins = (tuple(refs[:known]), named[0], None) + tuple(named[1:])
        rest = refs[known + len(order) :]
        results, small_out, moved = rest[: known + 3], rest[known + 3], rest[known + 4 : known + 6]
        made, dvo, dvi = rest[known + 6 : known + 8], rest[known + 8], rest[known + 9]
        scatter_kernel(
            lay, H, NB, chunks, ins, (results, small_out, moved, tuple(made), dvo, dvi), rest[known + 10 :]
        )

    result = pl.pallas_call(
        body,
        out_shape=outs,
        in_specs=[ANY] * known + [spec for name, spec in order],
        out_specs=[VM] * (known + 4) + [ANY] * 6,
        scratch_shapes=scratch,
        compiler_params=pltpu.CompilerParams(
            collective_id=1, has_side_effects=True, vmem_limit_bytes=60 * 2**20
        ),
        name="backward_all",
    )(*grads, *[values[name] for name, spec in order])
    return result[: known + 3], result[known + 3], result[known + 4 : known + 6]


def row(ref, index, lanes):
    return jnp.broadcast_to(ref[pl.ds(index, 1), lanes], (SEG, LANES))


def lane_call(kernel, outs, args, name):
    def spec(a):
        lead = len(a.shape) - 1
        return pl.BlockSpec(a.shape[:-1] + (LANES,), lambda i: (0,) * lead + (i,))

    return pl.pallas_call(
        kernel,
        out_shape=outs,
        grid=(args[0].shape[-1] // LANES,),
        in_specs=[spec(a) for a in args],
        out_specs=jax.tree.map(spec, outs),
        compiler_params=pltpu.CompilerParams(vmem_limit_bytes=32 * 2**20),
        name=name,
    )(*args)


def shifted(value, by):
    where = lax.broadcasted_iota(jnp.int32, (SEG, LANES), 0)
    if by > 0:
        return jnp.where(where >= by, pltpu.roll(value, by, 0), 0.0)
    return jnp.where(where < SEG + by, pltpu.roll(value, SEG + by, 0), 0.0)


def ema_ends_kernel(H, x_ref, tab_ref, s_ref, r_ref):
    rows, width = x_ref.shape
    steps = rows // SEG

    def tile(lanes):
        decay = [row(tab_ref, h, lanes) for h in range(H)]

        def step(t, state):
            s, r = state
            xt = x_ref[pl.ds(t, SEG, stride=steps), lanes]
            r = tuple(decay[h] * r[h] + s[h] for h in range(H))
            s = tuple(decay[h] * s[h] + xt for h in range(H))
            return s, r

        zero = tuple(tab_ref[0:SEG, lanes] * 0.0 for h in range(H))
        s, r = lax.fori_loop(0, steps, step, (zero, zero))
        for h in range(H):
            log = row(tab_ref, H + h, lanes)
            sh, rh = s[h], r[h]
            for d in (1, 2, 4):
                span = d * steps
                sd, rd = shifted(sh, d), shifted(rh, d)
                power = jnp.exp(span * log)
                rh = rh + power * rd + (span * jnp.exp((span - 1) * log)) * sd
                sh = sh + power * sd
            s_ref[h, :, lanes] = sh
            r_ref[h, :, lanes] = rh

    tile(slice(None))


def ema_out_kernel(H, x_ref, tab_ref, omega_ref, s_ref, r_ref, inc_ref, ema_ref, si_ref, ri_ref):
    rows, width = x_ref.shape
    steps = rows // SEG

    def tile(lanes):
        decay = [row(tab_ref, h, lanes) for h in range(H)]
        gain = [row(tab_ref, 2 * H + h, lanes) for h in range(H)]
        omega = row(omega_ref, 0, lanes)
        start = []
        span = (lax.broadcasted_iota(jnp.int32, (SEG, LANES), 0) * steps).astype(F32)
        for h in range(H):
            log = row(tab_ref, H + h, lanes)
            s_dev = row(inc_ref, h, lanes)
            r_dev = row(inc_ref, H + h, lanes)
            power = jnp.exp(span * log)
            s_in = shifted(s_ref[h, :, lanes], 1) + power * s_dev
            r_in = (
                shifted(r_ref[h, :, lanes], 1)
                + power * r_dev
                + (span * jnp.exp((span - 1.0) * log)) * s_dev
            )
            si_ref[h, :, lanes] = s_in
            ri_ref[h, :, lanes] = r_in
            start.append(s_in)

        def step(t, s):
            xt = x_ref[pl.ds(t, SEG, stride=steps), lanes]
            s = tuple(decay[h] * s[h] + xt for h in range(H))
            parts = [gain[h] * s[h] for h in range(H)]
            while len(parts) > 1:
                parts = [parts[i] + parts[i + 1] for i in range(0, len(parts), 2)]
            ema_ref[pl.ds(t, SEG, stride=steps), lanes] = parts[0] + omega * xt
            return s

        lax.fori_loop(0, steps, step, tuple(start))

    tile(slice(None))


def ema_back_ends_kernel(H, d_ref, tab_ref, l_ref):
    rows, width = d_ref.shape
    steps = rows // SEG

    def tile(lanes):
        decay = [row(tab_ref, h, lanes) for h in range(H)]

        def step(i, lam):
            dt = d_ref[pl.ds(steps - 1 - i, SEG, stride=steps), lanes]
            return tuple(decay[h] * lam[h] + dt for h in range(H))

        zero = tuple(tab_ref[0:SEG, lanes] * 0.0 for h in range(H))
        lam = lax.fori_loop(0, steps, step, zero)
        for h in range(H):
            log = row(tab_ref, H + h, lanes)
            lh = lam[h]
            for d in (1, 2, 4):
                lh = lh + jnp.exp(d * steps * log) * shifted(lh, -d)
            l_ref[h, :, lanes] = lh

    tile(slice(None))


def ema_sums_kernel(H, x_ref, d_ref, tab_ref, si_ref, ri_ref, out_ref):
    rows, width = x_ref.shape
    steps = rows // SEG
    group = H // 2

    def tile(lanes):
        for first in range(0, H, group):
            decay = [row(tab_ref, first + h, lanes) for h in range(group)]

            def step(t, state):
                s, r, c, q, o = state
                xt = x_ref[pl.ds(t, SEG, stride=steps), lanes]
                dt = d_ref[pl.ds(t, SEG, stride=steps), lanes]
                r = tuple(decay[h] * r[h] + s[h] for h in range(group))
                s = tuple(decay[h] * s[h] + xt for h in range(group))
                c = tuple(c[h] + dt * s[h] for h in range(group))
                q = tuple(q[h] + dt * r[h] for h in range(group))
                return s, r, c, q, o + dt * xt

            zero = tuple(tab_ref[0:SEG, lanes] * 0.0 for h in range(group))
            s = tuple(si_ref[first + h, :, lanes] for h in range(group))
            r = tuple(ri_ref[first + h, :, lanes] for h in range(group))
            s, r, c, q, o = lax.fori_loop(0, steps, step, (s, r, zero, zero, zero[0]))
            for h in range(group):
                out_ref[pl.ds(first + h, 1), lanes] = jnp.sum(c[h], axis=0, keepdims=True)
                out_ref[pl.ds(H + first + h, 1), lanes] = jnp.sum(q[h], axis=0, keepdims=True)
            out_ref[pl.ds(2 * H, 1), lanes] = jnp.sum(o, axis=0, keepdims=True)

    tile(slice(None))


def ema_back_kernel(H, d_ref, tab_ref, omega_ref, l_ref, inc_ref, dx_ref):
    rows, width = d_ref.shape
    steps = rows // SEG

    def tile(lanes):
        decay = [row(tab_ref, h, lanes) for h in range(H)]
        gain = [row(tab_ref, 2 * H + h, lanes) for h in range(H)]
        omega = row(omega_ref, 0, lanes)
        start = []
        span = ((SEG - 1 - lax.broadcasted_iota(jnp.int32, (SEG, LANES), 0)) * steps).astype(F32)
        for h in range(H):
            log = row(tab_ref, H + h, lanes)
            l_dev = row(inc_ref, h, lanes)
            start.append(shifted(l_ref[h, :, lanes], -1) + jnp.exp(span * log) * l_dev)

        def step(i, lam):
            at = pl.ds(steps - 1 - i, SEG, stride=steps)
            dt = d_ref[at, lanes]
            lam = tuple(decay[h] * lam[h] + dt for h in range(H))
            parts = [gain[h] * lam[h] for h in range(H)]
            while len(parts) > 1:
                parts = [parts[i] + parts[i + 1] for i in range(0, len(parts), 2)]
            dx_ref[at, lanes] = parts[0] + omega * dt
            return lam

        lax.fori_loop(0, steps, step, tuple(start))

    tile(slice(None))


def call(kernel, outs, args, specs=None, scratch=(), vmem=58, name=None):
    return pl.pallas_call(
        kernel,
        out_shape=outs,
        in_specs=specs or [VM] * len(args),
        out_specs=jax.tree.map(lambda o: VM, outs),
        scratch_shapes=list(scratch),
        compiler_params=pltpu.CompilerParams(vmem_limit_bytes=vmem * 2**20),
        name=name,
    )(*args)


QB = 256
STRETCH = 128


def bias_kernel(length, bucket_count, bias_ref, strip_ref):
    edges = bucket_edges(bucket_count)
    tiles = length // LANES + QB // LANES
    lag0 = lax.broadcasted_iota(jnp.int32, (QB, LANES), 0) - lax.broadcasted_iota(
        jnp.int32, (QB, LANES), 1
    )
    for t in range(strip_ref.shape[1] // LANES):
        base = length - t * LANES
        low, high = base - LANES + 1, base + QB - 1
        start = max([k for k in range(bucket_count) if edges[k] <= low], default=0)
        value = jnp.full((QB, LANES), bias_ref[start], F32)
        for k in range(start + 1, bucket_count):
            if edges[k] <= high:
                value = jnp.where(lag0 + base >= edges[k], bias_ref[k], value)
        strip_ref[:, t * LANES : (t + 1) * LANES] = value


def attend_body(lay, g, far, q_ref, strip_ref, keys, vals, att_ref, probs_ref, scores, part):
    G = lay.G
    rows, zw = q_ref.shape
    length = G * rows
    r0 = lax.broadcasted_iota(jnp.int32, (QB, rows), 0)
    c0 = lax.broadcasted_iota(jnp.int32, (QB, rows), 1)

    def one(i, carry):
        at = i * QB
        q = q_ref[pl.ds(at, QB), :]
        for k in range(G):
            owner = lax.rem(g - k + G, G)
            s = mm_t(q, keys[k])
            off = jnp.clip(length - rows * (g - owner) - at, 0, length)
            s = s * (zw ** (-0.5)) + strip_ref[:, pl.ds(pl.multiple_of(off, LANES), rows)]
            if k == 0:
                pos = r0 + at
                s = jnp.where(pos // STRETCH == c0 // STRETCH, s, s + far)
                s = jnp.where(c0 <= pos, s, masked_fill)
            else:
                s = s + jnp.where(k <= g, far, masked_fill)
            scores[:, k * rows : (k + 1) * rows] = s
        s = scores[...]
        p = jnp.exp(s - jnp.max(s, axis=1, keepdims=True))
        p = p * (1.0 / jnp.sum(p, axis=1, keepdims=True))
        total = jnp.zeros((QB, att_ref.shape[1]), F32)
        for k in range(G):
            low = p[:, k * rows : (k + 1) * rows].astype(BF16)
            probs_ref[k, pl.ds(at, QB), :] = low
            total += mm(low, vals[k])
        att_ref[pl.ds(at, QB), :] = total
        return carry

    one(part, 0)


def attend_back_kernel(lay, bucket_count, flag_ref, q_ref, da_ref, delta_ref, probs_ref, *refs):
    G = lay.G
    keys, vals, dq_ref, dk_ref, dv_ref, dko_ref, dvo_ref, bucket_ref, strip, ds_ref = refs
    rows, zw = q_ref.shape
    length = G * rows
    g = flag_ref[1]
    scale = zw ** (-0.5)
    edges = bucket_edges(bucket_count)
    strip[...] = jnp.zeros(strip.shape, F32)

    def one(i, carry):
        at = pl.multiple_of(i * QB, QB)
        da = da_ref[pl.ds(at, QB), :]
        dq = jnp.zeros((QB, zw), F32)
        for k in range(G):
            owner = lax.rem(g - k + G, G)
            dw = mm_t(da, vals[k])
            p = probs_ref[k, pl.ds(at, QB), :].astype(F32)
            ds = p * (dw - delta_ref[pl.ds(at, QB), :])
            off = jnp.clip(length - rows * (g - owner) - at, 0, length)
            strip[:, pl.ds(pl.multiple_of(off, LANES), rows)] += ds
            low = ds.astype(BF16)
            dq += mm(low, keys[k])
            ds_ref[k, pl.ds(at, QB), :] = low
        dq_ref[pl.ds(at, QB), :] = dq * scale
        return carry

    lax.fori_loop(0, rows // QB, one, 0)
    for k in range(G):
        dk = lax.dot_general(
            ds_ref[k], q_ref[...], (((0,), (0,)), ((), ())), preferred_element_type=F32
        )
        dv = lax.dot_general(
            probs_ref[k], da_ref[...], (((0,), (0,)), ((), ())), preferred_element_type=F32
        )
        if k == 0:
            dk_ref[...] = dk * scale
            dv_ref[...] = dv
        else:
            dko_ref[k - 1] = (dk * scale).astype(BF16)
            dvo_ref[k - 1] = dv.astype(BF16)
    lag0 = lax.broadcasted_iota(jnp.int32, (QB, LANES), 0) - lax.broadcasted_iota(
        jnp.int32, (QB, LANES), 1
    )
    sums = [jnp.zeros((1, LANES), F32) for k in range(bucket_count)]
    for t in range((length + QB) // LANES):
        base = length - t * LANES
        low, high = base - LANES + 1, base + QB - 1
        if high < 0:
            continue
        value = strip[:, t * LANES : (t + 1) * LANES]
        for k in range(bucket_count):
            top = edges[k + 1] if k + 1 < bucket_count else length
            if edges[k] <= high and top > low:
                lag = lag0 + base
                inside = (lag >= edges[k]) & (lag < top)
                sums[k] = sums[k] + jnp.sum(jnp.where(inside, value, 0.0), axis=0, keepdims=True)
    for k in range(bucket_count):
        bucket_ref[pl.ds(k, 1), :] = sums[k]


def silu_slope(values):
    gate_value = jax.nn.sigmoid(values)
    return gate_value * (1.0 + values * (1.0 - gate_value))


def normalize(seq_rows):
    centered = seq_rows - jnp.mean(seq_rows, axis=-1, keepdims=True)
    inverse = lax.rsqrt(jnp.mean(centered * centered, axis=-1, keepdims=True) + epsilon)
    return (centered * inverse, inverse)


def normalize_back(grad_scaled, unit_rows, inverse):
    return inverse * (
        grad_scaled
        - jnp.mean(grad_scaled, axis=-1, keepdims=True)
        - unit_rows * jnp.mean(grad_scaled * unit_rows, axis=-1, keepdims=True)
    )


def mm(a, b):
    return jnp.dot(a, b, preferred_element_type=F32)


def mm_t(a, b):
    return lax.dot_general(a, b, (((1,), (1,)), ((), ())), preferred_element_type=F32)


def wgrad(a, b):
    return lax.dot_general(a, b, (((0,), (0,)), ((), ())), preferred_element_type=F32).astype(BF16)


def shards(
    lay,
    tokens,
    cotangent,
    stretch_size,
    w_value,
    w_base,
    w_out,
    w_up,
    w_down,
    ema_delta,
    ema_alpha,
    ema_beta,
    ema_gamma,
    ema_omega,
    first_gain,
    second_gain,
    query_gain,
    query_bias,
    key_gain,
    relative_bias,
):
    micro, items, seq_len, D = tokens.shape
    H = ema_delta.shape[1]
    zw = query_gain.shape[0]
    V = w_value.shape[1]
    NB = relative_bias.shape[0]
    length = seq_len * lay.S
    G = lay.G
    R = lay.BL * seq_len
    d_at, b_at = lax.axis_index("dp"), lax.axis_index("seq")
    c_at, y_at = d_at % 2, d_at // 2
    q_at = b_at // lay.Cq
    g_at = (b_at % lay.Cq) * 2 + c_at
    share = ema_delta.shape[0]

    def group_perm(k):
        pairs = []
        for y in range(lay.Y):
            for q in range(lay.Q):
                for g in range(G):
                    t = (g + k) % G
                    src = (y * 2 + g % 2) * lay.S + q * lay.Cq + g // 2
                    dst = (y * 2 + t % 2) * lay.S + q * lay.Cq + t // 2
                    pairs.append((src, dst))
        return pairs

    def shift(value, k):
        return lax.ppermute(value, ("dp", "seq"), group_perm(k % G))

    marks = jnp.broadcast_to(
        stretch_size.reshape(1, -1).astype(BF16), (share, lay.MS)
    )
    used = 4 * H + 3 + lay.MS
    pack = jnp.concatenate(
        [
            ema_delta,
            ema_alpha,
            ema_beta,
            ema_gamma,
            ema_omega[:, None],
            first_gain[:, None],
            second_gain[:, None],
            marks,
            jnp.zeros((share, LANES - used), BF16),
        ],
        1,
    )
    x_blocks, cot_blocks, fulls, rest = forward_all(
        lay, H, tokens, cotangent, (pack, w_value, w_base, w_out, w_up, w_down),
        query_gain[None], query_bias[None], key_gain[None], relative_bias,
    )
    mixed, ema_tiles, s_in, r_in, table, turned = rest[:6]
    value_pre, base, queries, keys_all, vals_all, probs, attended = rest[6:]
    flags = jnp.stack([g_at, g_at])
    mats = [full.reshape(-1, full.shape[-1]) for full in fulls[1:]]
    mat_value, mat_base, mat_out, mat_up, mat_down = mats
    gain_first = turned[:, 4 * H + 1].reshape(D)
    gain_second = turned[:, 4 * H + 2].reshape(D)

    x_low = x_blocks.reshape(R, D)
    x = x_low.astype(F32)
    grad_out = cot_blocks.reshape(R, D).astype(F32)

    z_pre = base[:, :zw]
    reset_pre = base[:, zw : zw + V]
    cand_pre = base[:, zw + V : zw + V + D]
    update_pre = base[:, zw + V + D :]
    reset_gate = jax.nn.silu(reset_pre)
    update = jax.nn.sigmoid(update_pre)
    gated = (attended * reset_gate).astype(BF16)
    cand_in = cand_pre + mm(gated, mat_out)
    candidate = jax.nn.silu(cand_in)
    first_sum = x + update * (candidate - x)
    unit_first, inverse_first = normalize(first_sum)
    normed = unit_first * gain_first
    normed_low = normed.astype(BF16)
    hidden_pre = mm(normed_low, mat_up)
    hidden = jax.nn.silu(hidden_pre).astype(BF16)
    second_sum = normed + mm(hidden, mat_down)
    unit_second, inverse_second = normalize(second_sum)
    block_out = (unit_second * gain_second).astype(BF16)

    grad_gain_second = jnp.sum(grad_out * unit_second, axis=0)
    grad_second = normalize_back(grad_out * gain_second, unit_second, inverse_second)
    branch = grad_second.astype(BF16)
    grad_mat_down = wgrad(hidden, branch)
    hidden_grad = (mm_t(branch, mat_down) * silu_slope(hidden_pre)).astype(BF16)
    grad_mat_up = wgrad(normed_low, hidden_grad)
    grad_normed = grad_second + mm_t(hidden_grad, mat_up)
    grad_gain_first = jnp.sum(grad_normed * unit_first, axis=0)
    grad_first = normalize_back(grad_normed * gain_first, unit_first, inverse_first)
    cand_low = (grad_first * update * silu_slope(cand_in)).astype(BF16)
    grad_mat_out = wgrad(gated, cand_low)
    grad_gated = mm_t(cand_low, mat_out)
    att_low = (grad_gated * reset_gate).astype(BF16)
    grad_reset = grad_gated * attended * silu_slope(reset_pre)
    grad_update = grad_first * (candidate - x) * update * (1.0 - update)
    delta = jnp.sum(att_low.astype(F32) * attended, axis=1, keepdims=True)
    base_rest = jnp.concatenate(
        [grad_reset.astype(BF16), cand_low, grad_update.astype(BF16)], 1
    )
    pre = grad_first * (1.0 - update)
    gains = jnp.concatenate(
        [grad_gain_first[None], grad_gain_second[None], jnp.zeros((6, D), F32)]
    )
    shape = (lay.Y, 2, lay.Z, lay.X)

    def split(grad):
        return grad.reshape(shape + (-1, grad.shape[-1]))

    reduced, small_total, moved = backward_all(
        lay,
        H,
        NB,
        [split(grad_mat_down), split(grad_mat_up), split(grad_mat_out)],
        [fulls[2], fulls[1]],
        dict(
            x_blocks=x_blocks, d_att=att_low, delta=delta, queries=queries, keys=keys_all,
            vals=vals_all, probs=probs, z_pre=z_pre,
            gains_small=jnp.concatenate([query_gain[None], key_gain[None], jnp.zeros((6, zw), F32)]),
            mixed=mixed, ema=ema_tiles, base_rest=base_rest, value_pre=value_pre, pre=pre, gains=gains,
            table=table, turned=turned, si=s_in, ri=r_in,
            block_out=block_out.reshape(lay.BL, seq_len, D),
        ),
        share,
    )
    own = reduced[5]
    corr, lagged = own[:, :H], own[:, H : 2 * H]
    p = jax.nn.sigmoid(ema_delta.astype(F32))
    a = jax.nn.sigmoid(ema_alpha.astype(F32))
    beta = ema_beta.astype(F32)
    read = ema_gamma.astype(F32) * (H ** (-0.5))
    q_grad = read * p * beta * lagged
    return (
        moved[0],
        moved[1].astype(F32),
        reduced[4],
        reduced[3],
        reduced[2],
        reduced[1],
        reduced[0],
        (read * beta * corr - a * q_grad) * p * (1.0 - p),
        -p * q_grad * a * (1.0 - a),
        p * read * corr,
        p * beta * corr * (H ** (-0.5)),
        own[:, 2 * H],
        own[:, 2 * H + 1],
        own[:, 2 * H + 2],
        small_total[0, :zw],
        small_total[1, :zw],
        small_total[2, :zw],
        small_total[3, :NB],
    )


def solution(mesh):
    rows = P(None, "dp", "seq", None)
    part2, part1 = P(("dp", "seq"), None), P(("dp", "seq"))
    in_specs = (rows, rows, P(None, "dp")) + (part2,) * 9 + (part1,) * 3 + (P(),) * 4
    out_specs = (rows, rows) + (part2,) * 9 + (part1,) * 3 + (P(),) * 4

    def whole(tokens, *rest):
        micro, seqs = tokens.shape[:2]
        lay = Layout(mesh.shape["dp"], mesh.shape["seq"], micro, seqs // mesh.shape["dp"])
        return jax.shard_map(
            functools.partial(shards, lay),
            mesh=mesh,
            in_specs=in_specs,
            out_specs=out_specs,
            check_vma=False,
        )(tokens, *rest)

    return whole
```

```python
import functools

import jax
import jax.numpy as jnp
import numpy as np
from jax import lax
from jax.experimental import pallas as pl
from jax.experimental.pallas import tpu as pltpu
from jax.sharding import PartitionSpec as P

epsilon = 1e-05
masked_fill = -1e30
MESH = pl.DeviceIdType.MESH
ANY = pl.BlockSpec(memory_space=pl.ANY)
VM = pl.BlockSpec(memory_space=pltpu.VMEM)
SM = pl.BlockSpec(memory_space=pltpu.SMEM)
F32 = jnp.float32
BF16 = jnp.bfloat16
SEG = 8
LANES = 128


def bucket_edges(bucket_count):
    edge_list = [0]
    middle = bucket_count // 2
    for number in range(1, bucket_count):
        edge_list.append(number if number < middle else int(middle * 2 ** ((number - middle) / 2)))
    return edge_list


class Layout:
    def __init__(self, dp, seq, micro, items):
        self.dp, self.S = dp, seq
        self.C = 2
        self.Y = dp // 2
        self.X = min(self.Y, seq)
        self.Z = seq // self.X
        self.items = items
        self.MS = micro * items
        self.Q = 2 * self.MS
        self.Cq = seq // self.Q
        self.G = 2 * self.Cq
        self.BL = seq // self.G

    def here(self):
        d, b = lax.axis_index("dp"), lax.axis_index("seq")
        return d // 2, d % 2, b // self.X, b % self.X, b


class Wire:
    def __init__(self, lay, send, recv):
        self.lay, self.send, self.recv, self.count = lay, send, recv, 0
        self.sent = []

    def to(self, y, c, z, x):
        return (y * 2 + c, z * self.lay.X + x)

    def start(self, src, dst, target):
        number = self.count
        self.count += 1
        copy = pltpu.make_async_remote_copy(
            src_ref=src,
            dst_ref=dst,
            send_sem=self.send.at[number],
            recv_sem=self.recv.at[number],
            device_id=target,
            device_id_type=MESH,
        )
        copy.start()
        self.sent.append(copy)
        return copy

    def finish(self):
        for copy in self.sent:
            copy.wait_send()


def greet(lay):
    y, c, z, x, b = lay.here()
    barrier = pltpu.get_barrier_semaphore()
    plane = 2 * lay.S

    def one(k, carry):
        other = (c * lay.S + b + k) % plane
        pl.semaphore_signal(
            barrier, inc=1, device_id=(y * 2 + other // lay.S, other % lay.S), device_id_type=MESH
        )
        return carry

    lax.fori_loop(1, plane, one, 0)
    for k in range(1, lay.Y):
        pl.semaphore_signal(
            barrier, inc=1, device_id=(((y + k) % lay.Y) * 2 + c, b), device_id_type=MESH
        )
    pl.semaphore_wait(barrier, plane - 1 + lay.Y - 1)


ALPHA = 0.5
AHEAD = 3
LAG = 3
ORDER = 1
LIMIT = 800


def half_columns(columns):
    return max(1, int(columns // LANES * ALPHA + 0.5)) * LANES


def reshard_in(lay, sources, targets, send, recv, local):
    y, c, z, x, b = lay.here()
    g = b // lay.BL
    slot = b % lay.BL
    qm = b // lay.Cq
    gm = (b % lay.Cq) * 2 + c

    def begin(n):
        for source, target in ((sources[n], targets[n]),):
            for ms in range(lay.MS):
                seq_to = (ms * 2 + c) * lay.Cq + g // 2
                mine = jnp.logical_and(seq_to == b, g % 2 == c)
                block = source.at[ms // lay.items, ms % lay.items]

                @pl.when(jnp.logical_not(mine))
                def _():
                    pltpu.make_async_remote_copy(
                        src_ref=block,
                        dst_ref=target.at[slot],
                        send_sem=send.at[n, ms],
                        recv_sem=recv.at[n, slot],
                        device_id=(y * 2 + g % 2, seq_to),
                        device_id_type=MESH,
                    ).start()

                @pl.when(mine)
                def _():
                    pltpu.make_async_copy(block, target.at[slot], local.at[n]).start()

    def wait(n):
        source, target = sources[n], targets[n]
        for ms in range(lay.MS):
            seq_to = (ms * 2 + c) * lay.Cq + g // 2
            mine = jnp.logical_and(seq_to == b, g % 2 == c)
            block = source.at[ms // lay.items, ms % lay.items]

            @pl.when(jnp.logical_not(mine))
            def _():
                pltpu.make_async_remote_copy(
                    src_ref=block,
                    dst_ref=target.at[slot],
                    send_sem=send.at[n, ms],
                    recv_sem=recv.at[n, slot],
                    device_id=(y * 2 + g % 2, seq_to),
                    device_id_type=MESH,
                ).wait_send()

            @pl.when(mine)
            def _():
                pltpu.make_async_copy(block, target.at[slot], local.at[n]).wait()

        for j in range(lay.BL):
            from_b = gm * lay.BL + j
            own = jnp.logical_and(from_b == b, qm % 2 == c)

            @pl.when(jnp.logical_not(own))
            def _():
                pltpu.make_async_remote_copy(
                    src_ref=source.at[0, 0],
                    dst_ref=target.at[j],
                    send_sem=send.at[n, 0],
                    recv_sem=recv.at[n, j],
                    device_id=(y * 2 + qm % 2, from_b),
                    device_id_type=MESH,
                ).wait_recv()

    return begin, wait


def reshard_out(lay, sources, targets, send, recv, local):
    y, c, z, x, b = lay.here()
    g = b // lay.BL
    qm = b // lay.Cq
    gm = (b % lay.Cq) * 2 + c
    ms_to = qm // 2
    m_to, s_to = ms_to // lay.items, ms_to % lay.items

    def copies(n, j):
        from_b = gm * lay.BL + j
        own = jnp.logical_and(from_b == b, qm % 2 == c)
        remote = pltpu.make_async_remote_copy(
            src_ref=sources[n].at[j],
            dst_ref=targets[n].at[m_to, s_to],
            send_sem=send.at[n, j],
            recv_sem=recv.at[n, ms_to],
            device_id=(y * 2 + qm % 2, from_b),
            device_id_type=MESH,
        )
        near = pltpu.make_async_copy(sources[n].at[j], targets[n].at[m_to, s_to], local.at[n])
        return own, remote, near

    def begin(n):
        for j in range(lay.BL):
            own, remote, near = copies(n, j)
            pl.when(jnp.logical_not(own))(remote.start)
            pl.when(own)(near.start)

    def wait(n):
        for j in range(lay.BL):
            own, remote, near = copies(n, j)
            pl.when(jnp.logical_not(own))(remote.wait_send)
            pl.when(own)(near.wait)
        for ms in range(lay.MS):
            seq_at = (ms * 2 + c) * lay.Cq + g // 2
            own = jnp.logical_and(seq_at == b, g % 2 == c)

            @pl.when(jnp.logical_not(own))
            def _():
                pltpu.make_async_remote_copy(
                    src_ref=sources[n].at[0],
                    dst_ref=targets[n].at[ms // lay.items, ms % lay.items],
                    send_sem=send.at[n, 0],
                    recv_sem=recv.at[n, ms],
                    device_id=(y * 2 + g % 2, seq_at),
                    device_id_type=MESH,
                ).wait_recv()

    return begin, wait


def chunks_of(shapes, limit):
    result = []
    for n, shape in enumerate(shapes):
        tiles = shape[-1] // LANES
        cuts = max(1, -(-shape[0] * shape[-1] // limit))
        at = 0
        for cut in range(cuts):
            width = (tiles - at) // (cuts - cut) if cut == cuts - 1 else -(-(tiles - at) // (cuts - cut))
            result.append((n, at * LANES, width * LANES))
            at += width
    return result


def column_blocks(columns, most=768):
    cuts = -(-columns // most)
    while (columns // LANES) % cuts:
        cuts += 1
    width = columns // cuts
    return [(i * width, width) for i in range(cuts)]


def weight_block(full, stage, sem, at, width):
    target = stage.at[:, :, :, :, :, pl.ds(0, width)]
    copy = pltpu.make_async_copy(full.at[:, :, :, :, :, pl.ds(at, width)], target, sem)
    copy.start()
    copy.wait()
    block = stage[:, :, :, :, :, 0:width]
    return block.reshape(-1, width)


def gather_kernel(lay, count, chunks, refs):
    tok, cot = refs[0], refs[1]
    shards = refs[2 : 2 + count]
    tok_out, cot_out = refs[2 + count], refs[3 + count]
    fulls = refs[4 + count : 4 + 2 * count]
    send, recv, local, t_send, t_recv, t_local = refs[4 + 2 * count :]
    y, c, z, x, b = lay.here()
    X, Y, Z = lay.X, lay.Y, lay.Z
    greet(lay)
    wire = Wire(lay, send, recv)
    begin, wait = reshard_in(lay, (tok, cot), (tok_out, cot_out), t_send, t_recv, t_local)
    total = len(chunks)
    owns = []
    for i, (n, at, width) in enumerate(chunks):
        cols = pl.ds(at, width)
        copy = pltpu.make_async_copy(
            shards[n].at[:, cols], fulls[n].at[y, c, z, x, :, cols], local.at[i]
        )
        copy.start()
        owns.append(copy)
    arrived = [dict() for i in range(total)]

    def stage_z(i):
        n, at, width = chunks[i]
        cols = pl.ds(at, width)
        arrived[i]["z"] = [
            wire.start(
                shards[n].at[:, cols],
                fulls[n].at[y, c, z, x, :, cols],
                wire.to(y, c, (z + k) % Z, x),
            )
            for k in range(1, Z)
        ]

    def parts(i):
        n, at, width = chunks[i]
        left = half_columns(width)
        result = [(at, left)]
        if left < width:
            result.append((at + left, width - left))
        return result

    def to_core(i, block):
        arrived[i].setdefault("core", []).append(wire.start(block, block, wire.to(y, 1 - c, z, x)))

    def stage_one(i):
        owns[i].wait()
        for copy in arrived[i]["z"]:
            copy.wait_recv()
        n, first, columns = chunks[i]
        full = fulls[n]
        for half, (at, width) in enumerate(parts(i)):
            block = full.at[y, c, :, x, :, pl.ds(at, width)]
            if half == 0:
                arrived[i]["x0"] = [
                    wire.start(block, block, wire.to(y, c, z, (x + k) % X)) for k in range(1, X)
                ]
            else:
                arrived[i]["y1"] = [
                    wire.start(block, block, wire.to((y + k) % Y, c, z, x)) for k in range(1, Y)
                ]
        to_core(i, full.at[y, c, :, x, :, pl.ds(first, columns)])

    def stage_two(i):
        full = fulls[chunks[i][0]]
        for half, (at, width) in enumerate(parts(i)):
            cols = pl.ds(at, width)
            if half == 0:
                for copy in arrived[i]["x0"]:
                    copy.wait_recv()
                block = full.at[y, c, :, :, :, cols]
                arrived[i]["y0"] = [
                    wire.start(block, block, wire.to((y + k) % Y, c, z, x)) for k in range(1, Y)
                ]
                for k in range(1, X):
                    to_core(i, full.at[y, c, :, (x + X - k) % X, :, cols])
            else:
                for copy in arrived[i]["y1"]:
                    copy.wait_recv()
                block = full.at[:, c, :, x, :, cols]
                arrived[i]["x1"] = [
                    wire.start(block, block, wire.to(y, c, z, (x + k) % X)) for k in range(1, X)
                ]
                for k in range(1, Y):
                    to_core(i, full.at[(y + Y - k) % Y, c, :, x, :, cols])

    def stage_three(i):
        full = fulls[chunks[i][0]]
        for half, (at, width) in enumerate(parts(i)):
            cols = pl.ds(at, width)
            if half == 0:
                for k, copy in enumerate(arrived[i]["y0"], 1):
                    copy.wait_recv()
                    to_core(i, full.at[(y + Y - k) % Y, c, :, :, :, cols])
            else:
                for k, copy in enumerate(arrived[i]["x1"], 1):
                    copy.wait_recv()
                    to_core(i, full.at[:, c, :, (x + X - k) % X, :, cols])

    def finish():
        for i in range(total):
            for copy in arrived[i]["core"]:
                copy.wait_recv()
        wire.finish()

    def gathered(n):
        for i in range(total):
            if chunks[i][0] == n:
                for copy in arrived[i].pop("core"):
                    copy.wait_recv()
                arrived[i]["core"] = []

    return wire, (begin, wait), (stage_z, stage_one, stage_two, stage_three), gathered, finish


def group_copies(lay, send, recv, source, inbox, forward):
    y, c, z, x, b = lay.here()
    q = b // lay.Cq
    g = (b % lay.Cq) * 2 + c
    copies = []
    for k in range(1, lay.G):
        t = (g + (k if forward else lay.G - k)) % lay.G
        copies.append(
            pltpu.make_async_remote_copy(
                src_ref=source,
                dst_ref=inbox.at[k - 1],
                send_sem=send.at[k - 1],
                recv_sem=recv.at[k - 1],
                device_id=(y * 2 + t % 2, q * lay.Cq + t // 2),
                device_id_type=MESH,
            )
        )
    return copies, g


def to_tiles(low, tiles, r0, rows):
    for t in range(tiles.shape[0]):
        tiles[t, pl.ds(r0, rows), :] = low[:, t * LANES : (t + 1) * LANES].astype(F32)


def make_tables(lay, H, pack, raw, table, turned):
    r = pack.shape[4]
    total = lay.Y * 2 * lay.Z * lay.X

    def one(i, carry):
        block = pack[i // (2 * lay.Z * lay.X), i // (lay.Z * lay.X) % 2, i // lay.X % lay.Z, i % lay.X]
        raw[pl.ds(i * r, r), :] = block.astype(F32)
        return carry

    lax.fori_loop(0, total, one, 0)
    for t in range(table.shape[0]):
        v = raw[t * LANES : (t + 1) * LANES, :].T
        turned[t] = v
        leak = jax.nn.sigmoid(v[:H])
        decay = 1.0 - leak * jax.nn.sigmoid(v[H : 2 * H])
        table[t, :H] = decay
        table[t, H : 2 * H] = jnp.log(decay)
        table[t, 2 * H : 3 * H] = leak * v[2 * H : 3 * H] * v[3 * H : 4 * H] * (H ** (-0.5))


def carry_in(lay, H, rows, g, inbox, table, inc, t, later):
    log = table[t, H : 2 * H]
    state = jnp.zeros((H, LANES), F32)
    slope = jnp.zeros((H, LANES), F32)
    for k in range(1, lay.G):
        span = (k - 1) * rows
        valid = (g + k < lay.G) if later else (k <= g)
        s_part = inbox[k - 1, t, :H]
        r_part = s_part * 0.0 if later else inbox[k - 1, t, H : 2 * H]
        if span:
            power = jnp.exp(span * log)
            r_part = power * r_part + (span * jnp.exp((span - 1) * log)) * s_part
            s_part = power * s_part
        state = state + jnp.where(valid, s_part, 0.0)
        slope = slope + jnp.where(valid, r_part, 0.0)
    inc[t, :H] = state
    if not later:
        inc[t, H : 2 * H] = slope


def forward_kernel(lay, count, chunks, H, refs):
    n_in, n_out = 2 + count, 16 + count
    ins = refs[:n_in]
    query_gain, query_bias, key_gain, relative = refs[n_in : n_in + 4]
    refs = refs[n_in + 4 :]
    outs, scratch = refs[:n_out], refs[n_out:]
    tok_out, cot_out = outs[0], outs[1]
    fulls = outs[2 : 2 + count]
    mixed, ema, si, ri, table, turned = outs[2 + count : 8 + count]
    value_pre, base, queries, keys, vals, probs, attended, z_out = outs[8 + count :]
    sems, work = scratch[:6], scratch[6:]
    xt, pack, raw, s_end, r_end, mine, inbox, inc, stage, strip, scores, load, c_send, c_recv = work
    wire, (begin, wait), stages, gathered, finish = gather_kernel(
        lay, count, chunks, ins + (tok_out, cot_out) + tuple(fulls) + sems
    )
    stage_z, stage_one, stage_two, stage_three = stages
    total = len(chunks)
    rows = xt.shape[1]
    tiles = xt.shape[0]
    copies, g = group_copies(lay, c_send.at[0], c_recv.at[0], mine, inbox, True)
    others = pl.ds(1, lay.G - 1)
    vals_copies, g = group_copies(
        lay, c_send.at[1], c_recv.at[1], vals.at[0], vals.at[others], True
    )
    keys_copies, g = group_copies(
        lay, c_send.at[2], c_recv.at[2], keys.at[0], keys.at[others], True
    )
    width = tok_out.shape[2]
    zw = queries.shape[1]

    def value(at, cols):
        v = mm(tok_out[...].reshape(rows, width), weight_block(fulls[1], stage, load, at, cols))
        value_pre[:, at : at + cols] = v
        vals[0, :, at : at + cols] = (v * jax.nn.sigmoid(v)).astype(BF16)

    def send_values():
        for copy in vals_copies:
            copy.start()

    def bias():
        bias_kernel(lay.G * rows, relative.shape[0], relative, strip)

    def base_out(at, cols):
        base[:, at : at + cols] = mm(mixed[...], weight_block(fulls[2], stage, load, at, cols))

    def send_keys():
        z_pre = base[:, :zw]
        z_out[...] = z_pre
        shared = z_pre * jax.nn.sigmoid(z_pre)
        queries[...] = (shared * query_gain[...] + query_bias[...]).astype(BF16)
        keys[0] = (shared * key_gain[...]).astype(BF16)
        for copy in keys_copies:
            copy.start()

    def keys_here():
        for copy in keys_copies + vals_copies:
            copy.wait()

    def attend(part):
        y, c, z, x, b = lay.here()
        q_at = b // lay.Cq
        first = ((y * 2 + q_at % 2) * lay.Z * lay.X) * pack.shape[4]
        marks = raw[pl.ds(first, 1), :]
        lane = lax.broadcasted_iota(jnp.int32, (1, LANES), 1)
        mark = jnp.sum(
            jnp.where(lane == 4 * H + 3 + q_at // 2, marks, 0.0), axis=1, keepdims=True
        )
        far = jnp.where(mark == float(lay.G * rows), 0.0, masked_fill)
        attend_body(lay, g, far, queries, strip, keys, vals, attended, probs, scores, part)

    def tables():
        gathered(0)
        copy = pltpu.make_async_copy(fulls[0], pack, load)
        copy.start()
        copy.wait()
        make_tables(lay, H, pack, raw, table, turned)

    def tokens():
        wait(0)
        for j in range(lay.BL):
            to_tiles(tok_out[j], xt, j * (rows // lay.BL), rows // lay.BL)

    def ends(first, last):
        def one(t, carry):
            ema_ends_kernel(H, xt.at[t], table.at[t], s_end.at[t], r_end.at[t])
            for h in range(H):
                mine[t, pl.ds(h, 1), :] = s_end[t, h, SEG - 1 : SEG, :]
                mine[t, pl.ds(H + h, 1), :] = r_end[t, h, SEG - 1 : SEG, :]
            return carry

        lax.fori_loop(first, last, one, 0)

    def exchange():
        for copy in copies:
            copy.start()

    def carries():
        for copy in copies:
            copy.wait()
        for t in range(tiles):
            carry_in(lay, H, rows, g, inbox, table, inc, t, False)

    def out(first, last):
        def one(t, carry):
            ema_out_kernel(
                H, xt.at[t], table.at[t], turned.at[t, pl.ds(4 * H, 1)], s_end.at[t], r_end.at[t],
                inc.at[t], ema.at[t], si.at[t], ri.at[t],
            )
            return carry

        lax.fori_loop(first, last, one, 0)
        for t in range(first, last):
            for r0 in range(0, rows, 128):
                v = ema[t, pl.ds(r0, 128), :]
                mixed[pl.ds(r0, 128), t * LANES : (t + 1) * LANES] = (
                    v * jax.nn.sigmoid(v)
                ).astype(BF16)

    steps = [lambda: begin(0)]
    last = {}
    for i in range(min(AHEAD, total)):
        steps.append(functools.partial(stage_z, i))
    for turn in range(total + 2 * LAG):
        if 0 <= turn - 2 * LAG < total:
            last[chunks[turn - 2 * LAG][0]] = len(steps)
            steps.append(functools.partial(stage_three, turn - 2 * LAG))
        if 0 <= turn - LAG < total:
            steps.append(functools.partial(stage_two, turn - LAG))
        if turn < total:
            steps.append(functools.partial(stage_one, turn))
        if turn + AHEAD < total:
            steps.append(functools.partial(stage_z, turn + AHEAD))
        if turn == PLAN[5]:
            steps.append(lambda: begin(1))
    base_blocks = column_blocks(base.shape[1])
    todo = [(last[0] + PLAN[0], tables), (PLAN[1], tokens)]
    todo += [(0, functools.partial(ends, t, t + 1)) for t in range(tiles)]
    todo += [(0, exchange)]
    todo += [(last[1] + PLAN[2], lambda: gathered(1))]
    todo += [(0, functools.partial(value, *block)) for block in column_blocks(vals.shape[2])]
    todo += [(0, send_values), (0, carries)]
    todo += [(0, functools.partial(out, t, t + 1)) for t in range(tiles)]
    todo += [(0, bias), (last[2] + PLAN[3], lambda: gathered(2))]
    todo += [(0, functools.partial(base_out, *base_blocks[0])), (0, send_keys)]
    todo += [(0, functools.partial(base_out, *block)) for block in base_blocks[1:]]
    todo += [(0, keys_here)]
    todo += [(0, functools.partial(attend, part)) for part in range(rows // QB)]
    interleave(steps, todo, PLAN[6])
    finish()
    wait(1)


def interleave(steps, todo, most):
    todo = list(todo)
    done = set()

    def run():
        first, piece, name = (todo.pop(0) + (None,))[:3]
        piece()
        done.add(name)

    for number, step in enumerate(steps):
        step, needs = step if isinstance(step, tuple) else (step, None)
        while needs is not None and needs not in done:
            run()
        step()
        for i in range(most):
            if todo and todo[0][0] <= number:
                run()
    while todo:
        run()


PLAN = (1, 12, 1, 1, 0, 9, 1)


def forward_all(lay, H, tokens, cotangent, shards, query_gain, query_bias, key_gain, relative):
    count = len(shards)
    chunks = chunks_of([shard.shape for shard in shards], shards[0].shape[0] * LIMIT)
    micro, items, rows, width = tokens.shape
    per = (lay.Z - 1) + 2 * (lay.X - 1 + lay.Y - 1) + 1 + 2 * (lay.X - 1 + lay.Y - 1)
    blocks = jax.ShapeDtypeStruct((lay.BL, rows, width), BF16)
    fulls = [
        jax.ShapeDtypeStruct((lay.Y, 2, lay.Z, lay.X) + shard.shape, shard.dtype)
        for shard in shards
    ]
    T, R = width // LANES, lay.BL * rows
    state = (T, H, SEG, LANES)
    outs = [blocks, blocks] + fulls
    outs += [
        jax.ShapeDtypeStruct((R, width), BF16),
        jax.ShapeDtypeStruct((T, R, LANES), F32),
        jax.ShapeDtypeStruct(state, F32),
        jax.ShapeDtypeStruct(state, F32),
        jax.ShapeDtypeStruct((T, 3 * H, LANES), F32),
        jax.ShapeDtypeStruct((T, LANES, LANES), F32),
    ]
    V, cols, zw, G = shards[1].shape[1], shards[2].shape[1], query_gain.shape[1], lay.G
    outs += [
        jax.ShapeDtypeStruct((R, V), F32),
        jax.ShapeDtypeStruct((R, cols), F32),
        jax.ShapeDtypeStruct((R, zw), BF16),
        jax.ShapeDtypeStruct((G, R, zw), BF16),
        jax.ShapeDtypeStruct((G, R, V), BF16),
        jax.ShapeDtypeStruct((G, R, R), BF16),
        jax.ShapeDtypeStruct((R, V), F32),
        jax.ShapeDtypeStruct((R, zw), F32),
    ]

    def body(*refs):
        forward_kernel(lay, count, chunks, H, refs)

    result = pl.pallas_call(
        body,
        out_shape=outs,
        in_specs=[ANY] * (2 + count) + [VM] * 3 + [SM],
        out_specs=[VM] + [ANY] * (1 + count) + [VM] * 14,
        scratch_shapes=[
            pltpu.SemaphoreType.DMA((len(chunks) * per,)),
            pltpu.SemaphoreType.DMA((len(chunks) * per,)),
            pltpu.SemaphoreType.DMA((len(chunks),)),
            pltpu.SemaphoreType.DMA((2, lay.MS)),
            pltpu.SemaphoreType.DMA((2, lay.BL)),
            pltpu.SemaphoreType.DMA((2,)),
            pltpu.VMEM((T, R, LANES), F32),
            pltpu.VMEM(fulls[0].shape, fulls[0].dtype),
            pltpu.VMEM((width, LANES), F32),
            pltpu.VMEM(state, F32),
            pltpu.VMEM(state, F32),
            pltpu.VMEM((T, 2 * H, LANES), F32),
            pltpu.VMEM((lay.G - 1, T, 2 * H, LANES), F32),
            pltpu.VMEM((T, 2 * H, LANES), F32),
            pltpu.VMEM((lay.Y, 2, lay.Z, lay.X, shards[1].shape[0], 768), BF16),
            pltpu.VMEM((QB, (G + 1) * R), F32),
            pltpu.VMEM((QB, G * R), F32),
            pltpu.SemaphoreType.DMA,
            pltpu.SemaphoreType.DMA((3, lay.G - 1)),
            pltpu.SemaphoreType.DMA((3, lay.G - 1)),
        ],
        compiler_params=pltpu.CompilerParams(
            collective_id=0, has_side_effects=True, vmem_limit_bytes=58 * 2**20
        ),
        name="forward_all",
    )(tokens, cotangent, *shards, query_gain, query_bias, key_gain, relative)
    return result[0], result[1], result[2 : 2 + count], result[2 + count :]


def add_blocks(total, index, extra, extra_index, counts, width_at):
    size = int(np.prod(counts)) if counts else 1

    def one(i, carry):
        places = []
        for extent in reversed(counts):
            places.insert(0, i % extent)
            i = i // extent
        a, e = index(*places), extra_index(*places)
        total[a] = total[a] + extra[e]
        return carry

    lax.fori_loop(0, size, one, 0)


def scatter_kernel(lay, H, NB, chunks, ins, outs, scratch):
    (
        grads, x_low, d_in, d_att, delta, queries, keys, vals, probs, z_pre, gains_small, mixed, ema,
        base_rest, value_pre, w_base, w_value, pre, gains, table, turned, si, ri, block_out,
    ) = ins
    results, small_out, outs_to, made, dvo, dvi = outs
    bufs, own = scratch[: 6 * len(chunks)], scratch[6 * len(chunks) :]
    small_acc, small_recv, send, recv, local, t_send, t_recv, t_local = own[:8]
    xt, dt, sums, flat, split, l_end, mine, inbox, inc, gx, c_send, c_recv = own[8:20]
    dx = xt
    stage, vstage, bstage, pstage, ds, strip, dq, dko, dki, zlow, mixed_acc, x_acc, load = own[20:33]
    gstage, mixed_t, loads = own[33:36]
    halves = own[36:]
    grads = grads + made + (split,)
    y, c, z, x, b = lay.here()
    X, Y, Z = lay.X, lay.Y, lay.Z
    greet(lay)
    wire = Wire(lay, send, recv)
    begin, wait = reshard_out(lay, (block_out, gx), outs_to, t_send, t_recv, t_local)
    total = len(chunks)
    arrived = [dict() for i in range(total)]

    def buf(i, name):
        return bufs[6 * i + ("acc", "x0", "y1", "y0", "x1", "z").index(name)]

    def parts(i):
        n, at, width = chunks[i]
        left = half_columns(width)
        result = [(0, left)]
        if left < width:
            result.append((left, width - left))
        return result

    def own_half(i):
        n, at, width = chunks[i]
        if n == len(grads) - 1:
            return None
        source = grads[n].at[:, c, :, :, :, pl.ds(at, width)]
        return pltpu.make_async_copy(source, half_of(i), local.at[i])

    def half_of(i):
        n, at, width = chunks[i]
        r = grads[n].shape[4]
        room = [h for h in halves if h.shape[4] == r][0]
        return room.at[i % 2, :, :, :, :, pl.ds(0, width)]

    def prefetch_half(i):
        near = own_half(i) if i < total else None
        if near is not None:
            near.start()

    def stage_core(i):
        n, at, width = chunks[i]
        if n_base <= n < n_base + 2:
            settle()
        if i == 0:
            prefetch_half(0)
        arrived[i]["core"] = wire.start(
            grads[n].at[:, 1 - c, :, :, :, pl.ds(at, width)],
            buf(i, "acc"),
            wire.to(y, 1 - c, z, x),
        )

    def stage_one(i):
        n, first, columns = chunks[i]
        acc = buf(i, "acc")
        near = own_half(i)
        if near is not None:
            near.wait()
        arrived[i]["core"].wait_recv()
        if near is not None:
            mine_half = half_of(i)
            add_blocks(acc, lambda *p: p, mine_half, lambda *p: p, (Y, Z, X), None)
        else:
            add_blocks(
                acc, lambda *p: p, split, lambda p, q, s: (p, c, q, s), (Y, Z, X), None
            )
        prefetch_half(i + 1)
        for half, (at, width) in enumerate(parts(i)):
            cols = pl.ds(at, width)
            if half == 0:
                arrived[i]["x0"] = [
                    wire.start(
                        acc.at[:, :, (x + k) % X, :, cols],
                        buf(i, "x0").at[k - 1],
                        wire.to(y, c, z, (x + k) % X),
                    )
                    for k in range(1, X)
                ]
            else:
                arrived[i]["y1"] = [
                    wire.start(
                        acc.at[(y + k) % Y, :, :, :, cols],
                        buf(i, "y1").at[k - 1],
                        wire.to((y + k) % Y, c, z, x),
                    )
                    for k in range(1, Y)
                ]

    def stage_two(i):
        acc = buf(i, "acc")
        for half, (at, width) in enumerate(parts(i)):
            cols = slice(at, at + width)
            view = pl.ds(at, width)
            if half == 0:
                for k, copy in enumerate(arrived[i]["x0"]):
                    copy.wait_recv()
                    add_blocks(
                        acc,
                        lambda p, q: (p, q, x, slice(None), cols),
                        buf(i, "x0"),
                        lambda p, q: (k, p, q),
                        (Y, Z),
                        None,
                    )
                arrived[i]["y0"] = [
                    wire.start(
                        acc.at[(y + k) % Y, :, x, :, view],
                        buf(i, "y0").at[k - 1],
                        wire.to((y + k) % Y, c, z, x),
                    )
                    for k in range(1, Y)
                ]
            else:
                for k, copy in enumerate(arrived[i]["y1"]):
                    copy.wait_recv()
                    add_blocks(
                        acc,
                        lambda p, q: (y, p, q, slice(None), cols),
                        buf(i, "y1"),
                        lambda p, q: (k, p, q),
                        (Z, X),
                        None,
                    )
                arrived[i]["x1"] = [
                    wire.start(
                        acc.at[y, :, (x + k) % X, :, view],
                        buf(i, "x1").at[k - 1],
                        wire.to(y, c, z, (x + k) % X),
                    )
                    for k in range(1, X)
                ]

    def stage_three(i):
        acc = buf(i, "acc")
        for half, (at, width) in enumerate(parts(i)):
            cols = slice(at, at + width)
            name = "y0" if half == 0 else "x1"
            for k, copy in enumerate(arrived[i][name]):
                copy.wait_recv()
                add_blocks(
                    acc,
                    lambda p: (y, p, x, slice(None), cols),
                    buf(i, name),
                    lambda p: (k, p),
                    (Z,),
                    None,
                )
        arrived[i]["z"] = [
            wire.start(
                acc.at[y, (z + k) % Z, x], buf(i, "z").at[k - 1], wire.to(y, c, (z + k) % Z, x)
            )
            for k in range(1, Z)
        ]

    def stage_four(i):
        n, at, width = chunks[i]
        total = buf(i, "acc")[y, z, x].astype(F32)
        for k, copy in enumerate(arrived[i]["z"]):
            copy.wait_recv()
            total = total + buf(i, "z")[k].astype(F32)
        results[n][:, pl.ds(at, width)] = total

    small_at = [0]

    def small_stage(moves):
        copies = []
        for target in moves:
            slot = small_at[0]
            small_at[0] += 1
            copies.append((slot, wire.start(small_acc, small_recv.at[slot], target)))
        for slot, copy in copies:
            copy.wait_send()
            wire.sent = [other for other in wire.sent if other is not copy]
        for slot, copy in copies:
            copy.wait_recv()
            small_acc[...] += small_recv[slot]

    rows, tiles = xt.shape[1], xt.shape[0]
    per_block = rows // lay.BL
    copies, g = group_copies(lay, c_send.at[0], c_recv.at[0], mine, inbox, False)
    G, zw = lay.G, queries.shape[1]
    D = x_low.shape[2]
    scale = zw ** (-0.5)
    n_base, n_value = len(grads) - 3, len(grads) - 2
    q_at = b // lay.Cq

    def back_copy(k, source, target, kind):
        t = (g + G - k) % G
        return pltpu.make_async_remote_copy(
            src_ref=source,
            dst_ref=target,
            send_sem=c_send.at[kind, k - 1],
            recv_sem=c_recv.at[kind, k - 1],
            device_id=(y * 2 + t % 2, q_at * lay.Cq + t // 2),
            device_id_type=MESH,
        )

    key_copies = [back_copy(k, dko.at[k - 1], dki.at[k - 1], 1) for k in range(1, G)]
    val_copies = [back_copy(k, dvo.at[k - 1], dvi.at[k - 1], 2) for k in range(1, G)]

    def fetch(source, target):
        copy = pltpu.make_async_copy(source, target, load)
        copy.start()
        copy.wait()

    storing = []

    def settle():
        while storing:
            storing.pop().wait()

    def keep_grad(n, at, grad):
        columns = grad.shape[1]
        r = made[n].shape[4]
        low = grad.astype(BF16).reshape(Y, 2, Z, X, r, columns)
        settle()
        gstage[:, :, :, :, :, :columns] = low
        copy = pltpu.make_async_copy(
            gstage.at[:, :, :, :, :, pl.ds(0, columns)],
            made[n].at[:, :, :, :, :, pl.ds(at, columns)],
            loads.at[0],
        )
        copy.start()
        storing.append(copy)

    all_base, all_value = column_blocks(w_base.shape[5]), column_blocks(w_value.shape[5])
    weight_order = [(w_base,) + block for block in all_base[1:] + all_base[:1]]
    weight_order += [(w_value,) + block for block in all_value]
    coming = {}

    def weight_copy(number):
        full, at, columns = weight_order[number]
        return pltpu.make_async_copy(
            full.at[:, :, :, :, :, pl.ds(at, columns)],
            stage.at[:, :, :, :, :, pl.ds(0, columns)],
            loads.at[1],
        )

    def next_weight(number):
        if number < len(weight_order):
            coming["weight"] = weight_copy(number)
            coming["weight"].start()

    def rest_copy(number):
        full, at, columns = weight_order[number]
        if at == 0:
            return pltpu.make_async_copy(
                base_rest.at[:, pl.ds(0, columns - zw)],
                bstage.at[:, pl.ds(zw, columns - zw)],
                loads.at[2],
            )
        return pltpu.make_async_copy(
            base_rest.at[:, pl.ds(at - zw, columns)], bstage.at[:, pl.ds(0, columns)], loads.at[2]
        )

    def next_rest(number):
        if number < len(all_base):
            coming["rest"] = rest_copy(number)
            coming["rest"].start()

    def next_pre(number):
        if number < len(all_value):
            at, columns = all_value[number]
            coming["pre"] = pltpu.make_async_copy(
                value_pre.at[:, pl.ds(at, columns)], pstage.at[:, pl.ds(0, columns)], loads.at[3]
            )
            coming["pre"].start()

    def begin_fetch():
        next_weight(0)
        next_rest(0)
        next_pre(0)
        coming["x"] = pltpu.make_async_copy(pre, x_acc, loads.at[4])
        coming["x"].start()
        mixed_t[...] = mixed[...].astype(F32).T.astype(BF16)

    def weight_here(columns):
        coming["weight"].wait()
        return stage[:, :, :, :, :, 0:columns].reshape(-1, columns)

    def base_block(number):
        full, at, columns = weight_order[number]
        coming["rest"].wait()
        if at == 0:
            bstage[:, :zw] = zlow[...]
        low = bstage[:, :columns]
        keep_grad(0, at, mm(mixed_t[...], low))
        part = mm_t(low, weight_here(columns))
        mixed_acc[...] = part if number == 0 else mixed_acc[...] + part
        next_weight(number + 1)
        next_rest(number + 1)

    def load_values(k):
        fetch(vals.at[k], vstage)
        if k == G - 1:
            strip[...] = jnp.zeros(strip.shape, F32)

    def scores_back(k, i):
        at = i * QB
        here = pl.ds(at, QB)
        owner = lax.rem(g - k + G, G)
        dw = mm_t(d_att[here, :], vstage[...])
        p = probs[k, here, :].astype(F32)
        grad = p * (dw - delta[here, :])
        off = jnp.clip(G * rows - rows * (g - owner) - at, 0, G * rows)
        strip[:, pl.ds(pl.multiple_of(off, LANES), rows)] += grad
        low = grad.astype(BF16)
        ds[here, :] = low
        part = mm(low, keys[k]) * scale
        dq[here, :] = part if k == G - 1 else dq[here, :] + part

    def keys_back(k):
        grad = dot_t(ds[...], queries[...]) * scale
        if k:
            dko[k - 1] = grad.astype(BF16)
            key_copies[k - 1].start()
        else:
            for copy in key_copies:
                copy.wait()
            for j in range(1, G):
                grad = grad + dki[j - 1].astype(F32)
            pre_z = z_pre[...]
            gate = jax.nn.sigmoid(pre_z)
            shared = pre_z * gate
            small_acc[0:1, :] = jnp.sum(dq[...] * shared, axis=0, keepdims=True)
            small_acc[1:2, :] = jnp.sum(dq[...], axis=0, keepdims=True)
            small_acc[2:3, :] = jnp.sum(grad * shared, axis=0, keepdims=True)
            d_shared = dq[...] * gains_small[0:1, :] + grad * gains_small[1:2, :]
            zlow[...] = (d_shared * (gate * (1.0 + pre_z * (1.0 - gate)))).astype(BF16)

    def values_back(k):
        for at, columns in column_blocks(vstage.shape[1]):
            vstage[:, at : at + columns] = dot_t(
                probs[k], d_att[:, at : at + columns]
            ).astype(BF16)
        fetch(vstage, dvo.at[k - 1])
        val_copies[k - 1].start()

    def buckets():
        sums_of = bucket_sums(G * rows, NB, strip)
        lane = lax.broadcasted_iota(jnp.int32, (1, LANES), 1)
        line = jnp.zeros((1, LANES), F32)
        for k in range(NB):
            line = jnp.where(lane == k, jnp.sum(sums_of[k], axis=1, keepdims=True), line)
        small_acc[3:4, :] = line
        small_acc[4:8, :] = jnp.zeros((4, LANES), F32)

    def values_here():
        for copy in val_copies:
            copy.wait()

    def value_block(number):
        full, at, columns = weight_order[len(all_base) + number]
        cols = pl.ds(at, columns)
        if number == 0:
            mixed_t[...] = x_low[...].reshape(rows, D).astype(F32).T.astype(BF16)
            coming["x"].wait()
        grad = dot_t(probs[0], d_att[:, at : at + columns])
        for k in range(1, G):
            fetch(dvi.at[k - 1, :, cols], bstage.at[:, pl.ds(0, columns)])
            grad = grad + bstage[:, :columns].astype(F32)
        coming["pre"].wait()
        v = pstage[:, :columns]
        gate = jax.nn.sigmoid(v)
        low = (grad * (gate * (1.0 + v * (1.0 - gate)))).astype(BF16)
        next_pre(number + 1)
        keep_grad(1, at, mm(mixed_t[...], low))
        x_acc[...] += mm_t(low, weight_here(columns))
        next_weight(len(all_base) + number + 1)

    def d_ema(t):
        v = ema[t]
        gate = jax.nn.sigmoid(v)
        dt[t] = mixed_acc[:, t * LANES : (t + 1) * LANES] * (gate * (1.0 + v * (1.0 - gate)))

    def tile_x():
        for j in range(lay.BL):
            to_tiles(x_low[j], xt, j * per_block, per_block)

    def ends(t):
        ema_back_ends_kernel(H, dt.at[t], table.at[t], l_end.at[t])
        for h in range(H):
            mine[t, pl.ds(h, 1), :] = l_end[t, h, 0:1, :]

    def exchange():
        for copy in copies:
            copy.start()

    def carries():
        for copy in copies:
            copy.wait()
        for t in range(tiles):
            carry_in(lay, H, rows, g, inbox, table, inc, t, True)

    def correlate(t):
        ema_sums_kernel(H, xt.at[t], dt.at[t], table.at[t], si.at[t], ri.at[t], sums.at[t])

    def back(t):
        ema_back_kernel(
            H, dt.at[t], table.at[t], turned.at[t, pl.ds(4 * H, 1)], l_end.at[t], inc.at[t], dx.at[t]
        )
        cols = slice(t * LANES, (t + 1) * LANES)
        for j in range(lay.BL):
            at = pl.ds(j * per_block, per_block)
            gx[j, :, cols] = (x_acc[at, cols] + dx[t, at, :]).astype(BF16)

    def share_sums():
        r = split.shape[4]
        for t in range(tiles):
            sums[t, pl.ds(2 * H + 1, 2), :] = gains[0:2, t * LANES : (t + 1) * LANES]
            flat[t * LANES : (t + 1) * LANES, :] = sums[t].T

        def one(i, carry):
            split[i // (2 * Z * X), i // (Z * X) % 2, i // X % Z, i % X] = flat[pl.ds(i * r, r), :]
            return carry

        lax.fori_loop(0, 2 * X * Y * Z, one, 0)

    sums[...] = jnp.zeros(sums.shape, F32)
    xs = [wire.to(y, c, z, (x + k) % X) for k in range(1, X)]
    ys = [wire.to((y + k) % Y, c, z, x) for k in range(1, Y)]
    zs = [wire.to(y, c, (z + k) % Z, x) for k in range(1, Z)]

    run = functools.partial
    todo = [(0, begin_fetch)]
    for number in range(len(all_base) - 1):
        todo.append((0, run(base_block, number), (n_base, weight_order[number][1])))
    for k in list(range(1, G))[::-1] + [0]:
        todo.append((0, run(load_values, k)))
        todo += [(0, run(scores_back, k, i)) for i in range(rows // QB)]
        todo.append((0, run(keys_back, k)))
        if k:
            todo.append((0, run(values_back, k)))
    todo.append((0, run(base_block, len(all_base) - 1), (n_base, 0)))
    todo += [(0, run(d_ema, t)) for t in range(tiles)]
    todo += [(0, run(ends, t)) for t in range(tiles)]
    todo += [(0, exchange), (0, values_here)]
    for number, block in enumerate(all_value):
        todo.append((0, run(value_block, number), (n_value, block[0])))
    todo.append((0, carries))
    todo += [(0, run(back, t)) for t in range(tiles)]
    todo += [(0, lambda: begin(1)), (0, tile_x), (0, buckets, "small")]
    todo += [(0, run(correlate, t)) for t in range(tiles)]
    todo.append((0, share_sums, (len(grads) - 1, 0)))

    def needs(i):
        n, at, width = chunks[i]
        return (n, at) if n >= n_base else None

    steps = []
    for i in range(min(LEAD, total)):
        steps.append((run(stage_core, i), needs(i)))
    steps.append(lambda: begin(0))
    for turn in range(total + 3 * BLAG):
        for what, lag in ((stage_four, 3), (stage_three, 2), (stage_two, 1), (stage_one, 0)):
            if 0 <= turn - lag * BLAG < total:
                steps.append(run(what, turn - lag * BLAG))
        if turn + LEAD < total:
            steps.append((run(stage_core, turn + LEAD), needs(turn + LEAD)))
        if turn >= total:
            late = turn - total
            moves = ([wire.to(y, 1 - c, z, x)], xs, ys, zs)
            if late < 4:
                steps.append((run(small_stage, moves[late]), "small"))
    interleave(steps, todo, MOST)
    small_out[...] = small_acc[...]
    wait(0)
    wait(1)
    wire.finish()


LEAD = 3
MOST = 1
BLAG = 2


def dot_t(a, b):
    return lax.dot_general(a, b, (((0,), (0,)), ((), ())), preferred_element_type=F32)


def bucket_sums(length, bucket_count, strip):
    edges = bucket_edges(bucket_count)
    lag0 = lax.broadcasted_iota(jnp.int32, (QB, LANES), 0) - lax.broadcasted_iota(
        jnp.int32, (QB, LANES), 1
    )
    totals = [jnp.zeros((1, LANES), F32) for k in range(bucket_count)]
    for t in range((length + QB) // LANES):
        base = length - t * LANES
        low, high = base - LANES + 1, base + QB - 1
        if high < 0:
            continue
        value = strip[:, t * LANES : (t + 1) * LANES]
        for k in range(bucket_count):
            top = edges[k + 1] if k + 1 < bucket_count else length
            if edges[k] <= high and top > low:
                lag = lag0 + base
                inside = (lag >= edges[k]) & (lag < top)
                totals[k] = totals[k] + jnp.sum(jnp.where(inside, value, 0.0), axis=0, keepdims=True)
    return totals


def backward_all(lay, H, NB, grads, fulls, values, share):
    X, Y, Z, G = lay.X, lay.Y, lay.Z, lay.G
    R, V = values["d_att"].shape
    D = values["pre"].shape[1]
    T, zw = D // LANES, values["queries"].shape[1]
    rows = R // lay.BL
    micro = lay.MS // lay.items
    shapes = [grad.shape[-2:] for grad in grads] + [full.shape[-2:] for full in fulls] + [(share, LANES)]
    kinds = [grad.dtype for grad in grads] + [BF16, BF16, F32]
    known = len(grads)
    chunks = chunks_of([shape for shape in shapes[:known]], share * LIMIT)
    base_blocks = column_blocks(shapes[known][1])
    chunks += [(known,) + block for block in base_blocks[1:]]
    chunks += [(known,) + base_blocks[0]]
    chunks += [(known + 1,) + block for block in column_blocks(shapes[known + 1][1])]
    chunks += [(known + 2, 0, LANES)]
    scratch = []
    for n, at, cols in chunks:
        r = shapes[n][0]
        left = half_columns(cols)
        right = cols - left if cols > left else LANES
        kind = kinds[n]
        scratch += [
            pltpu.VMEM((Y, Z, X, r, cols), kind),
            pltpu.VMEM((X - 1, Y, Z, r, left), kind),
            pltpu.VMEM((Y - 1, Z, X, r, right), kind),
            pltpu.VMEM((Y - 1, Z, r, left), kind),
            pltpu.VMEM((X - 1, Z, r, right), kind),
            pltpu.VMEM((Z - 1, r, cols), kind),
        ]
    hops = 1 + (X - 1) + (Y - 1) + (Z - 1)
    per = 1 + 2 * (X - 1 + Y - 1) + Z - 1
    small = (8, LANES)
    outs = [jax.ShapeDtypeStruct(shape, F32) for shape in shapes]
    outs.append(jax.ShapeDtypeStruct(small, F32))
    outs += [jax.ShapeDtypeStruct((micro, lay.items, rows, D), BF16)] * 2
    outs += [jax.ShapeDtypeStruct(full.shape, BF16) for full in fulls]
    outs += [jax.ShapeDtypeStruct((G - 1, R, V), BF16)] * 2
    scratch += [pltpu.VMEM(small, F32), pltpu.VMEM((hops,) + small, F32)]
    heights = sorted({shapes[n][0] for n, at, width in chunks})
    widest = {r: max(w for n, at, w in chunks if shapes[n][0] == r) for r in heights}
    scratch += [
        pltpu.SemaphoreType.DMA((len(chunks) * per + hops,)),
        pltpu.SemaphoreType.DMA((len(chunks) * per + hops,)),
        pltpu.SemaphoreType.DMA((len(chunks),)),
        pltpu.SemaphoreType.DMA((2, lay.BL)),
        pltpu.SemaphoreType.DMA((2, lay.MS)),
        pltpu.SemaphoreType.DMA((2,)),
        pltpu.VMEM((T, R, LANES), F32),
        pltpu.VMEM((T, R, LANES), F32),
        pltpu.VMEM((T, LANES, LANES), F32),
        pltpu.VMEM((D, LANES), F32),
        pltpu.VMEM((Y, 2, Z, X, share, LANES), F32),
        pltpu.VMEM((T, H, SEG, LANES), F32),
        pltpu.VMEM((T, H, LANES), F32),
        pltpu.VMEM((G - 1, T, H, LANES), F32),
        pltpu.VMEM((T, H, LANES), F32),
        pltpu.VMEM((lay.BL, rows, D), BF16),
        pltpu.SemaphoreType.DMA((3, G - 1)),
        pltpu.SemaphoreType.DMA((3, G - 1)),
        pltpu.VMEM((Y, 2, Z, X, share, 768), BF16),
        pltpu.VMEM((R, V), BF16),
        pltpu.VMEM((R, 768), BF16),
        pltpu.VMEM((R, 768), F32),
        pltpu.VMEM((R, R), BF16),
        pltpu.VMEM((QB, (G + 1) * R), F32),
        pltpu.VMEM((R, zw), F32),
        pltpu.VMEM((G - 1, R, zw), BF16),
        pltpu.VMEM((G - 1, R, zw), BF16),
        pltpu.VMEM((R, zw), BF16),
        pltpu.VMEM((R, D), F32),
        pltpu.VMEM((R, D), F32),
        pltpu.SemaphoreType.DMA,
        pltpu.VMEM((Y, 2, Z, X, share, 768), BF16),
        pltpu.VMEM((D, R), BF16),
        pltpu.SemaphoreType.DMA((5,)),
    ]
    scratch += [pltpu.VMEM((2, Y, Z, X, r, widest[r]), BF16) for r in heights]
    order = (
        ("x_blocks", VM), ("d_in", ANY), ("d_att", VM), ("delta", VM), ("queries", VM), ("keys", VM),
        ("vals", ANY), ("probs", VM), ("z_pre", VM), ("gains_small", VM), ("mixed", VM), ("ema", VM),
        ("base_rest", ANY), ("value_pre", ANY), ("w_base", ANY), ("w_value", ANY), ("pre", ANY),
        ("gains", VM), ("table", VM), ("turned", VM), ("si", VM), ("ri", VM), ("block_out", ANY),
    )
    values = dict(values, w_base=fulls[0], w_value=fulls[1])
    order = tuple(item for item in order if item[0] != "d_in")

    def body(*refs):
        named = refs[known : known + len(order)]
        ins = (tuple(refs[:known]), named[0], None) + tuple(named[1:])
        rest = refs[known + len(order) :]
        results, small_out, moved = rest[: known + 3], rest[known + 3], rest[known + 4 : known + 6]
        made, dvo, dvi = rest[known + 6 : known + 8], rest[known + 8], rest[known + 9]
        scatter_kernel(
            lay, H, NB, chunks, ins, (results, small_out, moved, tuple(made), dvo, dvi), rest[known + 10 :]
        )

    result = pl.pallas_call(
        body,
        out_shape=outs,
        in_specs=[ANY] * known + [spec for name, spec in order],
        out_specs=[VM] * (known + 4) + [ANY] * 6,
        scratch_shapes=scratch,
        compiler_params=pltpu.CompilerParams(
            collective_id=1, has_side_effects=True, vmem_limit_bytes=60 * 2**20
        ),
        name="backward_all",
    )(*grads, *[values[name] for name, spec in order])
    return result[: known + 3], result[known + 3], result[known + 4 : known + 6]


def row(ref, index, lanes):
    return jnp.broadcast_to(ref[pl.ds(index, 1), lanes], (SEG, LANES))


def lane_call(kernel, outs, args, name):
    def spec(a):
        lead = len(a.shape) - 1
        return pl.BlockSpec(a.shape[:-1] + (LANES,), lambda i: (0,) * lead + (i,))

    return pl.pallas_call(
        kernel,
        out_shape=outs,
        grid=(args[0].shape[-1] // LANES,),
        in_specs=[spec(a) for a in args],
        out_specs=jax.tree.map(spec, outs),
        compiler_params=pltpu.CompilerParams(vmem_limit_bytes=32 * 2**20),
        name=name,
    )(*args)


def shifted(value, by):
    where = lax.broadcasted_iota(jnp.int32, (SEG, LANES), 0)
    if by > 0:
        return jnp.where(where >= by, pltpu.roll(value, by, 0), 0.0)
    return jnp.where(where < SEG + by, pltpu.roll(value, SEG + by, 0), 0.0)


def ema_ends_kernel(H, x_ref, tab_ref, s_ref, r_ref):
    rows, width = x_ref.shape
    steps = rows // SEG

    def tile(lanes):
        decay = [row(tab_ref, h, lanes) for h in range(H)]

        def step(t, state):
            s, r = state
            xt = x_ref[pl.ds(t, SEG, stride=steps), lanes]
            r = tuple(decay[h] * r[h] + s[h] for h in range(H))
            s = tuple(decay[h] * s[h] + xt for h in range(H))
            return s, r

        zero = tuple(tab_ref[0:SEG, lanes] * 0.0 for h in range(H))
        s, r = lax.fori_loop(0, steps, step, (zero, zero))
        for h in range(H):
            log = row(tab_ref, H + h, lanes)
            sh, rh = s[h], r[h]
            for d in (1, 2, 4):
                span = d * steps
                sd, rd = shifted(sh, d), shifted(rh, d)
                power = jnp.exp(span * log)
                rh = rh + power * rd + (span * jnp.exp((span - 1) * log)) * sd
                sh = sh + power * sd
            s_ref[h, :, lanes] = sh
            r_ref[h, :, lanes] = rh

    tile(slice(None))


def ema_out_kernel(H, x_ref, tab_ref, omega_ref, s_ref, r_ref, inc_ref, ema_ref, si_ref, ri_ref):
    rows, width = x_ref.shape
    steps = rows // SEG

    def tile(lanes):
        decay = [row(tab_ref, h, lanes) for h in range(H)]
        gain = [row(tab_ref, 2 * H + h, lanes) for h in range(H)]
        omega = row(omega_ref, 0, lanes)
        start = []
        span = (lax.broadcasted_iota(jnp.int32, (SEG, LANES), 0) * steps).astype(F32)
        for h in range(H):
            log = row(tab_ref, H + h, lanes)
            s_dev = row(inc_ref, h, lanes)
            r_dev = row(inc_ref, H + h, lanes)
            power = jnp.exp(span * log)
            s_in = shifted(s_ref[h, :, lanes], 1) + power * s_dev
            r_in = (
                shifted(r_ref[h, :, lanes], 1)
                + power * r_dev
                + (span * jnp.exp((span - 1.0) * log)) * s_dev
            )
            si_ref[h, :, lanes] = s_in
            ri_ref[h, :, lanes] = r_in
            start.append(s_in)

        def step(t, s):
            xt = x_ref[pl.ds(t, SEG, stride=steps), lanes]
            s = tuple(decay[h] * s[h] + xt for h in range(H))
            parts = [gain[h] * s[h] for h in range(H)]
            while len(parts) > 1:
                parts = [parts[i] + parts[i + 1] for i in range(0, len(parts), 2)]
            ema_ref[pl.ds(t, SEG, stride=steps), lanes] = parts[0] + omega * xt
            return s

        lax.fori_loop(0, steps, step, tuple(start))

    tile(slice(None))


def ema_back_ends_kernel(H, d_ref, tab_ref, l_ref):
    rows, width = d_ref.shape
    steps = rows // SEG

    def tile(lanes):
        decay = [row(tab_ref, h, lanes) for h in range(H)]

        def step(i, lam):
            dt = d_ref[pl.ds(steps - 1 - i, SEG, stride=steps), lanes]
            return tuple(decay[h] * lam[h] + dt for h in range(H))

        zero = tuple(tab_ref[0:SEG, lanes] * 0.0 for h in range(H))
        lam = lax.fori_loop(0, steps, step, zero)
        for h in range(H):
            log = row(tab_ref, H + h, lanes)
            lh = lam[h]
            for d in (1, 2, 4):
                lh = lh + jnp.exp(d * steps * log) * shifted(lh, -d)
            l_ref[h, :, lanes] = lh

    tile(slice(None))


def ema_sums_kernel(H, x_ref, d_ref, tab_ref, si_ref, ri_ref, out_ref):
    rows, width = x_ref.shape
    steps = rows // SEG
    group = H // 2

    def tile(lanes):
        for first in range(0, H, group):
            decay = [row(tab_ref, first + h, lanes) for h in range(group)]

            def step(t, state):
                s, r, c, q, o = state
                xt = x_ref[pl.ds(t, SEG, stride=steps), lanes]
                dt = d_ref[pl.ds(t, SEG, stride=steps), lanes]
                r = tuple(decay[h] * r[h] + s[h] for h in range(group))
                s = tuple(decay[h] * s[h] + xt for h in range(group))
                c = tuple(c[h] + dt * s[h] for h in range(group))
                q = tuple(q[h] + dt * r[h] for h in range(group))
                return s, r, c, q, o + dt * xt

            zero = tuple(tab_ref[0:SEG, lanes] * 0.0 for h in range(group))
            s = tuple(si_ref[first + h, :, lanes] for h in range(group))
            r = tuple(ri_ref[first + h, :, lanes] for h in range(group))
            s, r, c, q, o = lax.fori_loop(0, steps, step, (s, r, zero, zero, zero[0]))
            for h in range(group):
                out_ref[pl.ds(first + h, 1), lanes] = jnp.sum(c[h], axis=0, keepdims=True)
                out_ref[pl.ds(H + first + h, 1), lanes] = jnp.sum(q[h], axis=0, keepdims=True)
            out_ref[pl.ds(2 * H, 1), lanes] = jnp.sum(o, axis=0, keepdims=True)

    tile(slice(None))


def ema_back_kernel(H, d_ref, tab_ref, omega_ref, l_ref, inc_ref, dx_ref):
    rows, width = d_ref.shape
    steps = rows // SEG

    def tile(lanes):
        decay = [row(tab_ref, h, lanes) for h in range(H)]
        gain = [row(tab_ref, 2 * H + h, lanes) for h in range(H)]
        omega = row(omega_ref, 0, lanes)
        start = []
        span = ((SEG - 1 - lax.broadcasted_iota(jnp.int32, (SEG, LANES), 0)) * steps).astype(F32)
        for h in range(H):
            log = row(tab_ref, H + h, lanes)
            l_dev = row(inc_ref, h, lanes)
            start.append(shifted(l_ref[h, :, lanes], -1) + jnp.exp(span * log) * l_dev)

        def step(i, lam):
            at = pl.ds(steps - 1 - i, SEG, stride=steps)
            dt = d_ref[at, lanes]
            lam = tuple(decay[h] * lam[h] + dt for h in range(H))
            parts = [gain[h] * lam[h] for h in range(H)]
            while len(parts) > 1:
                parts = [parts[i] + parts[i + 1] for i in range(0, len(parts), 2)]
            dx_ref[at, lanes] = parts[0] + omega * dt
            return lam

        lax.fori_loop(0, steps, step, tuple(start))

    tile(slice(None))


def call(kernel, outs, args, specs=None, scratch=(), vmem=58, name=None):
    return pl.pallas_call(
        kernel,
        out_shape=outs,
        in_specs=specs or [VM] * len(args),
        out_specs=jax.tree.map(lambda o: VM, outs),
        scratch_shapes=list(scratch),
        compiler_params=pltpu.CompilerParams(vmem_limit_bytes=vmem * 2**20),
        name=name,
    )(*args)


QB = 256
STRETCH = 128


def bias_kernel(length, bucket_count, bias_ref, strip_ref):
    edges = bucket_edges(bucket_count)
    tiles = length // LANES + QB // LANES
    lag0 = lax.broadcasted_iota(jnp.int32, (QB, LANES), 0) - lax.broadcasted_iota(
        jnp.int32, (QB, LANES), 1
    )
    for t in range(strip_ref.shape[1] // LANES):
        base = length - t * LANES
        low, high = base - LANES + 1, base + QB - 1
        start = max([k for k in range(bucket_count) if edges[k] <= low], default=0)
        value = jnp.full((QB, LANES), bias_ref[start], F32)
        for k in range(start + 1, bucket_count):
            if edges[k] <= high:
                value = jnp.where(lag0 + base >= edges[k], bias_ref[k], value)
        strip_ref[:, t * LANES : (t + 1) * LANES] = value


def attend_body(lay, g, far, q_ref, strip_ref, keys, vals, att_ref, probs_ref, scores, part):
    G = lay.G
    rows, zw = q_ref.shape
    length = G * rows
    r0 = lax.broadcasted_iota(jnp.int32, (QB, rows), 0)
    c0 = lax.broadcasted_iota(jnp.int32, (QB, rows), 1)

    def one(i, carry):
        at = i * QB
        q = q_ref[pl.ds(at, QB), :]
        for k in range(G):
            owner = lax.rem(g - k + G, G)
            s = mm_t(q, keys[k])
            off = jnp.clip(length - rows * (g - owner) - at, 0, length)
            s = s * (zw ** (-0.5)) + strip_ref[:, pl.ds(pl.multiple_of(off, LANES), rows)]
            if k == 0:
                pos = r0 + at
                s = jnp.where(pos // STRETCH == c0 // STRETCH, s, s + far)
                s = jnp.where(c0 <= pos, s, masked_fill)
            else:
                s = s + jnp.where(k <= g, far, masked_fill)
            scores[:, k * rows : (k + 1) * rows] = s
        s = scores[...]
        p = jnp.exp(s - jnp.max(s, axis=1, keepdims=True))
        p = p * (1.0 / jnp.sum(p, axis=1, keepdims=True))
        total = jnp.zeros((QB, att_ref.shape[1]), F32)
        for k in range(G):
            low = p[:, k * rows : (k + 1) * rows].astype(BF16)
            probs_ref[k, pl.ds(at, QB), :] = low
            total += mm(low, vals[k])
        att_ref[pl.ds(at, QB), :] = total
        return carry

    one(part, 0)


def attend_back_kernel(lay, bucket_count, flag_ref, q_ref, da_ref, delta_ref, probs_ref, *refs):
    G = lay.G
    keys, vals, dq_ref, dk_ref, dv_ref, dko_ref, dvo_ref, bucket_ref, strip, ds_ref = refs
    rows, zw = q_ref.shape
    length = G * rows
    g = flag_ref[1]
    scale = zw ** (-0.5)
    edges = bucket_edges(bucket_count)
    strip[...] = jnp.zeros(strip.shape, F32)

    def one(i, carry):
        at = pl.multiple_of(i * QB, QB)
        da = da_ref[pl.ds(at, QB), :]
        dq = jnp.zeros((QB, zw), F32)
        for k in range(G):
            owner = lax.rem(g - k + G, G)
            dw = mm_t(da, vals[k])
            p = probs_ref[k, pl.ds(at, QB), :].astype(F32)
            ds = p * (dw - delta_ref[pl.ds(at, QB), :])
            off = jnp.clip(length - rows * (g - owner) - at, 0, length)
            strip[:, pl.ds(pl.multiple_of(off, LANES), rows)] += ds
            low = ds.astype(BF16)
            dq += mm(low, keys[k])
            ds_ref[k, pl.ds(at, QB), :] = low
        dq_ref[pl.ds(at, QB), :] = dq * scale
        return carry

    lax.fori_loop(0, rows // QB, one, 0)
    for k in range(G):
        dk = lax.dot_general(
            ds_ref[k], q_ref[...], (((0,), (0,)), ((), ())), preferred_element_type=F32
        )
        dv = lax.dot_general(
            probs_ref[k], da_ref[...], (((0,), (0,)), ((), ())), preferred_element_type=F32
        )
        if k == 0:
            dk_ref[...] = dk * scale
            dv_ref[...] = dv
        else:
            dko_ref[k - 1] = (dk * scale).astype(BF16)
            dvo_ref[k - 1] = dv.astype(BF16)
    lag0 = lax.broadcasted_iota(jnp.int32, (QB, LANES), 0) - lax.broadcasted_iota(
        jnp.int32, (QB, LANES), 1
    )
    sums = [jnp.zeros((1, LANES), F32) for k in range(bucket_count)]
    for t in range((length + QB) // LANES):
        base = length - t * LANES
        low, high = base - LANES + 1, base + QB - 1
        if high < 0:
            continue
        value = strip[:, t * LANES : (t + 1) * LANES]
        for k in range(bucket_count):
            top = edges[k + 1] if k + 1 < bucket_count else length
            if edges[k] <= high and top > low:
                lag = lag0 + base
                inside = (lag >= edges[k]) & (lag < top)
                sums[k] = sums[k] + jnp.sum(jnp.where(inside, value, 0.0), axis=0, keepdims=True)
    for k in range(bucket_count):
        bucket_ref[pl.ds(k, 1), :] = sums[k]


def silu_slope(values):
    gate_value = jax.nn.sigmoid(values)
    return gate_value * (1.0 + values * (1.0 - gate_value))


def normalize(seq_rows):
    centered = seq_rows - jnp.mean(seq_rows, axis=-1, keepdims=True)
    inverse = lax.rsqrt(jnp.mean(centered * centered, axis=-1, keepdims=True) + epsilon)
    return (centered * inverse, inverse)


def normalize_back(grad_scaled, unit_rows, inverse):
    return inverse * (
        grad_scaled
        - jnp.mean(grad_scaled, axis=-1, keepdims=True)
        - unit_rows * jnp.mean(grad_scaled * unit_rows, axis=-1, keepdims=True)
    )


def mm(a, b):
    return jnp.dot(a, b, preferred_element_type=F32)


def mm_t(a, b):
    return lax.dot_general(a, b, (((1,), (1,)), ((), ())), preferred_element_type=F32)


def wgrad(a, b):
    return lax.dot_general(a, b, (((0,), (0,)), ((), ())), preferred_element_type=F32).astype(BF16)


def shards(
    lay,
    tokens,
    cotangent,
    stretch_size,
    w_value,
    w_base,
    w_out,
    w_up,
    w_down,
    ema_delta,
    ema_alpha,
    ema_beta,
    ema_gamma,
    ema_omega,
    first_gain,
    second_gain,
    query_gain,
    query_bias,
    key_gain,
    relative_bias,
):
    micro, items, seq_len, D = tokens.shape
    H = ema_delta.shape[1]
    zw = query_gain.shape[0]
    V = w_value.shape[1]
    NB = relative_bias.shape[0]
    length = seq_len * lay.S
    G = lay.G
    R = lay.BL * seq_len
    d_at, b_at = lax.axis_index("dp"), lax.axis_index("seq")
    c_at, y_at = d_at % 2, d_at // 2
    q_at = b_at // lay.Cq
    g_at = (b_at % lay.Cq) * 2 + c_at
    share = ema_delta.shape[0]

    def group_perm(k):
        pairs = []
        for y in range(lay.Y):
            for q in range(lay.Q):
                for g in range(G):
                    t = (g + k) % G
                    src = (y * 2 + g % 2) * lay.S + q * lay.Cq + g // 2
                    dst = (y * 2 + t % 2) * lay.S + q * lay.Cq + t // 2
                    pairs.append((src, dst))
        return pairs

    def shift(value, k):
        return lax.ppermute(value, ("dp", "seq"), group_perm(k % G))

    marks = jnp.broadcast_to(stretch_size.reshape(-1, 1).astype(BF16), (lay.MS, share))
    used = 4 * H + 3 + lay.MS
    pack = jnp.concatenate(
        [
            ema_delta.T,
            ema_alpha.T,
            ema_beta.T,
            ema_gamma.T,
            ema_omega[None],
            first_gain[None],
            second_gain[None],
            marks,
            jnp.zeros((LANES - used, share), BF16),
        ],
        0,
    ).T
    x_blocks, cot_blocks, fulls, rest = forward_all(
        lay, H, tokens, cotangent, (pack, w_value, w_base, w_out, w_up, w_down),
        query_gain[None], query_bias[None], key_gain[None], relative_bias,
    )
    mixed, ema_tiles, s_in, r_in, table, turned = rest[:6]
    value_pre, base, queries, keys_all, vals_all, probs, attended, z_pre = rest[6:]
    flags = jnp.stack([g_at, g_at])
    mats = [full.reshape(-1, full.shape[-1]) for full in fulls[1:]]
    mat_value, mat_base, mat_out, mat_up, mat_down = mats
    gain_first = turned[:, 4 * H + 1].reshape(D)
    gain_second = turned[:, 4 * H + 2].reshape(D)

    x_low = x_blocks.reshape(R, D)
    x = x_low.astype(F32)
    grad_out = cot_blocks.reshape(R, D).astype(F32)

    reset_pre = base[:, zw : zw + V]
    cand_pre = base[:, zw + V : zw + V + D]
    update_pre = base[:, zw + V + D :]
    reset_gate = jax.nn.silu(reset_pre)
    update = jax.nn.sigmoid(update_pre)
    gated = (attended * reset_gate).astype(BF16)
    cand_in = cand_pre + mm(gated, mat_out)
    candidate = jax.nn.silu(cand_in)
    first_sum = x + update * (candidate - x)
    unit_first, inverse_first = normalize(first_sum)
    normed = unit_first * gain_first
    normed_low = normed.astype(BF16)
    hidden_pre = mm(normed_low, mat_up)
    hidden = jax.nn.silu(hidden_pre).astype(BF16)
    second_sum = normed + mm(hidden, mat_down)
    unit_second, inverse_second = normalize(second_sum)
    block_out = (unit_second * gain_second).astype(BF16)

    grad_gain_second = jnp.sum(grad_out * unit_second, axis=0)
    grad_second = normalize_back(grad_out * gain_second, unit_second, inverse_second)
    branch = grad_second.astype(BF16)
    grad_mat_down = wgrad(hidden, branch)
    hidden_grad = (mm_t(branch, mat_down) * silu_slope(hidden_pre)).astype(BF16)
    grad_mat_up = wgrad(normed_low, hidden_grad)
    grad_normed = grad_second + mm_t(hidden_grad, mat_up)
    grad_gain_first = jnp.sum(grad_normed * unit_first, axis=0)
    grad_first = normalize_back(grad_normed * gain_first, unit_first, inverse_first)
    cand_low = (grad_first * update * silu_slope(cand_in)).astype(BF16)
    grad_mat_out = wgrad(gated, cand_low)
    grad_gated = mm_t(cand_low, mat_out)
    att_low = (grad_gated * reset_gate).astype(BF16)
    grad_reset = grad_gated * attended * silu_slope(reset_pre)
    grad_update = grad_first * (candidate - x) * update * (1.0 - update)
    delta = jnp.sum(att_low.astype(F32) * attended, axis=1, keepdims=True)
    base_rest = jnp.concatenate(
        [grad_reset.astype(BF16), cand_low, grad_update.astype(BF16)], 1
    )
    pre = grad_first * (1.0 - update)
    gains = jnp.concatenate(
        [grad_gain_first[None], grad_gain_second[None], jnp.zeros((6, D), F32)]
    )
    shape = (lay.Y, 2, lay.Z, lay.X)

    def split(grad):
        return grad.reshape(shape + (-1, grad.shape[-1]))

    reduced, small_total, moved = backward_all(
        lay,
        H,
        NB,
        [split(grad_mat_down), split(grad_mat_up), split(grad_mat_out)],
        [fulls[2], fulls[1]],
        dict(
            x_blocks=x_blocks, d_att=att_low, delta=delta, queries=queries, keys=keys_all,
            vals=vals_all, probs=probs, z_pre=z_pre,
            gains_small=jnp.concatenate([query_gain[None], key_gain[None], jnp.zeros((6, zw), F32)]),
            mixed=mixed, ema=ema_tiles, base_rest=base_rest, value_pre=value_pre, pre=pre, gains=gains,
            table=table, turned=turned, si=s_in, ri=r_in,
            block_out=block_out.reshape(lay.BL, seq_len, D),
        ),
        share,
    )
    own = reduced[5].T
    corr, lagged = own[:H], own[H : 2 * H]
    p = jax.nn.sigmoid(ema_delta.T.astype(F32))
    a = jax.nn.sigmoid(ema_alpha.T.astype(F32))
    beta = ema_beta.T.astype(F32)
    read = ema_gamma.T.astype(F32) * (H ** (-0.5))
    q_grad = read * p * beta * lagged
    return (
        moved[0],
        moved[1].astype(F32),
        reduced[4],
        reduced[3],
        reduced[2],
        reduced[1],
        reduced[0],
        ((read * beta * corr - a * q_grad) * p * (1.0 - p)).T,
        (-p * q_grad * a * (1.0 - a)).T,
        (p * read * corr).T,
        (p * beta * corr * (H ** (-0.5))).T,
        own[2 * H],
        own[2 * H + 1],
        own[2 * H + 2],
        small_total[0, :zw],
        small_total[1, :zw],
        small_total[2, :zw],
        small_total[3, :NB],
    )


def solution(mesh):
    rows = P(None, "dp", "seq", None)
    part2, part1 = P(("dp", "seq"), None), P(("dp", "seq"))
    in_specs = (rows, rows, P(None, "dp")) + (part2,) * 9 + (part1,) * 3 + (P(),) * 4
    out_specs = (rows, rows) + (part2,) * 9 + (part1,) * 3 + (P(),) * 4

    def whole(tokens, *rest):
        micro, seqs = tokens.shape[:2]
        lay = Layout(mesh.shape["dp"], mesh.shape["seq"], micro, seqs // mesh.shape["dp"])
        return jax.shard_map(
            functools.partial(shards, lay),
            mesh=mesh,
            in_specs=in_specs,
            out_specs=out_specs,
            check_vma=False,
        )(tokens, *rest)

    return whole
```

```python
import functools

import jax
import jax.numpy as jnp
import numpy as np
from jax import lax
from jax.experimental import pallas as pl
from jax.experimental.pallas import tpu as pltpu
from jax.sharding import PartitionSpec as P

epsilon = 1e-05
masked_fill = -1e30
MESH = pl.DeviceIdType.MESH
ANY = pl.BlockSpec(memory_space=pl.ANY)
VM = pl.BlockSpec(memory_space=pltpu.VMEM)
SM = pl.BlockSpec(memory_space=pltpu.SMEM)
F32 = jnp.float32
BF16 = jnp.bfloat16
SEG = 8
LANES = 128


def bucket_edges(bucket_count):
    edge_list = [0]
    middle = bucket_count // 2
    for number in range(1, bucket_count):
        edge_list.append(number if number < middle else int(middle * 2 ** ((number - middle) / 2)))
    return edge_list


class Layout:
    def __init__(self, dp, seq, micro, items):
        self.dp, self.S = dp, seq
        self.C = 2
        self.Y = dp // 2
        self.X = min(self.Y, seq)
        self.Z = seq // self.X
        self.items = items
        self.MS = micro * items
        self.Q = 2 * self.MS
        self.Cq = seq // self.Q
        self.G = 2 * self.Cq
        self.BL = seq // self.G

    def here(self):
        d, b = lax.axis_index("dp"), lax.axis_index("seq")
        return d // 2, d % 2, b // self.X, b % self.X, b


class Wire:
    def __init__(self, lay, send, recv):
        self.lay, self.send, self.recv, self.count = lay, send, recv, 0
        self.sent = []

    def to(self, y, c, z, x):
        return (y * 2 + c, z * self.lay.X + x)

    def start(self, src, dst, target):
        number = self.count
        self.count += 1
        copy = pltpu.make_async_remote_copy(
            src_ref=src,
            dst_ref=dst,
            send_sem=self.send.at[number],
            recv_sem=self.recv.at[number],
            device_id=target,
            device_id_type=MESH,
        )
        copy.start()
        self.sent.append(copy)
        return copy

    def finish(self):
        for copy in self.sent:
            copy.wait_send()


def greet(lay):
    y, c, z, x, b = lay.here()
    barrier = pltpu.get_barrier_semaphore()
    plane = 2 * lay.S

    def one(k, carry):
        other = (c * lay.S + b + k) % plane
        pl.semaphore_signal(
            barrier, inc=1, device_id=(y * 2 + other // lay.S, other % lay.S), device_id_type=MESH
        )
        return carry

    lax.fori_loop(1, plane, one, 0)
    for k in range(1, lay.Y):
        pl.semaphore_signal(
            barrier, inc=1, device_id=(((y + k) % lay.Y) * 2 + c, b), device_id_type=MESH
        )
    pl.semaphore_wait(barrier, plane - 1 + lay.Y - 1)


ALPHA = 0.5
AHEAD = 3
LAG = 3
ORDER = 1
LIMIT = 800


def half_columns(columns):
    return max(1, int(columns // LANES * ALPHA + 0.5)) * LANES


def reshard_in(lay, sources, targets, send, recv, local):
    y, c, z, x, b = lay.here()
    g = b // lay.BL
    slot = b % lay.BL
    qm = b // lay.Cq
    gm = (b % lay.Cq) * 2 + c

    def begin(n):
        for source, target in ((sources[n], targets[n]),):
            for ms in range(lay.MS):
                seq_to = (ms * 2 + c) * lay.Cq + g // 2
                mine = jnp.logical_and(seq_to == b, g % 2 == c)
                block = source.at[ms // lay.items, ms % lay.items]

                @pl.when(jnp.logical_not(mine))
                def _():
                    pltpu.make_async_remote_copy(
                        src_ref=block,
                        dst_ref=target.at[slot],
                        send_sem=send.at[n, ms],
                        recv_sem=recv.at[n, slot],
                        device_id=(y * 2 + g % 2, seq_to),
                        device_id_type=MESH,
                    ).start()

                @pl.when(mine)
                def _():
                    pltpu.make_async_copy(block, target.at[slot], local.at[n]).start()

    def wait(n):
        source, target = sources[n], targets[n]
        for ms in range(lay.MS):
            seq_to = (ms * 2 + c) * lay.Cq + g // 2
            mine = jnp.logical_and(seq_to == b, g % 2 == c)
            block = source.at[ms // lay.items, ms % lay.items]

            @pl.when(jnp.logical_not(mine))
            def _():
                pltpu.make_async_remote_copy(
                    src_ref=block,
                    dst_ref=target.at[slot],
                    send_sem=send.at[n, ms],
                    recv_sem=recv.at[n, slot],
                    device_id=(y * 2 + g % 2, seq_to),
                    device_id_type=MESH,
                ).wait_send()

            @pl.when(mine)
            def _():
                pltpu.make_async_copy(block, target.at[slot], local.at[n]).wait()

        for j in range(lay.BL):
            from_b = gm * lay.BL + j
            own = jnp.logical_and(from_b == b, qm % 2 == c)

            @pl.when(jnp.logical_not(own))
            def _():
                pltpu.make_async_remote_copy(
                    src_ref=source.at[0, 0],
                    dst_ref=target.at[j],
                    send_sem=send.at[n, 0],
                    recv_sem=recv.at[n, j],
                    device_id=(y * 2 + qm % 2, from_b),
                    device_id_type=MESH,
                ).wait_recv()

    return begin, wait


def reshard_out(lay, sources, targets, send, recv, local):
    y, c, z, x, b = lay.here()
    g = b // lay.BL
    qm = b // lay.Cq
    gm = (b % lay.Cq) * 2 + c
    ms_to = qm // 2
    m_to, s_to = ms_to // lay.items, ms_to % lay.items

    def copies(n, j):
        from_b = gm * lay.BL + j
        own = jnp.logical_and(from_b == b, qm % 2 == c)
        remote = pltpu.make_async_remote_copy(
            src_ref=sources[n].at[j],
            dst_ref=targets[n].at[m_to, s_to],
            send_sem=send.at[n, j],
            recv_sem=recv.at[n, ms_to],
            device_id=(y * 2 + qm % 2, from_b),
            device_id_type=MESH,
        )
        near = pltpu.make_async_copy(sources[n].at[j], targets[n].at[m_to, s_to], local.at[n])
        return own, remote, near

    def begin(n):
        for j in range(lay.BL):
            own, remote, near = copies(n, j)
            pl.when(jnp.logical_not(own))(remote.start)
            pl.when(own)(near.start)

    def wait(n):
        for j in range(lay.BL):
            own, remote, near = copies(n, j)
            pl.when(jnp.logical_not(own))(remote.wait_send)
            pl.when(own)(near.wait)
        for ms in range(lay.MS):
            seq_at = (ms * 2 + c) * lay.Cq + g // 2
            own = jnp.logical_and(seq_at == b, g % 2 == c)

            @pl.when(jnp.logical_not(own))
            def _():
                pltpu.make_async_remote_copy(
                    src_ref=sources[n].at[0],
                    dst_ref=targets[n].at[ms // lay.items, ms % lay.items],
                    send_sem=send.at[n, 0],
                    recv_sem=recv.at[n, ms],
                    device_id=(y * 2 + g % 2, seq_at),
                    device_id_type=MESH,
                ).wait_recv()

    return begin, wait


def chunks_of(shapes, limit):
    result = []
    for n, shape in enumerate(shapes):
        tiles = shape[-1] // LANES
        cuts = max(1, -(-shape[0] * shape[-1] // limit))
        at = 0
        for cut in range(cuts):
            width = (tiles - at) // (cuts - cut) if cut == cuts - 1 else -(-(tiles - at) // (cuts - cut))
            result.append((n, at * LANES, width * LANES))
            at += width
    return result


def column_blocks(columns, most=768):
    cuts = -(-columns // most)
    while (columns // LANES) % cuts:
        cuts += 1
    width = columns // cuts
    return [(i * width, width) for i in range(cuts)]


def weight_block(full, stage, sem, at, width):
    target = stage.at[:, :, :, :, :, pl.ds(0, width)]
    copy = pltpu.make_async_copy(full.at[:, :, :, :, :, pl.ds(at, width)], target, sem)
    copy.start()
    copy.wait()
    block = stage[:, :, :, :, :, 0:width]
    return block.reshape(-1, width)


def gather_kernel(lay, count, chunks, refs):
    tok, cot = refs[0], refs[1]
    shards = refs[2 : 2 + count]
    tok_out, cot_out = refs[2 + count], refs[3 + count]
    fulls = refs[4 + count : 4 + 2 * count]
    send, recv, local, t_send, t_recv, t_local = refs[4 + 2 * count :]
    y, c, z, x, b = lay.here()
    X, Y, Z = lay.X, lay.Y, lay.Z
    greet(lay)
    wire = Wire(lay, send, recv)
    begin, wait = reshard_in(lay, (tok, cot), (tok_out, cot_out), t_send, t_recv, t_local)
    total = len(chunks)
    owns = []
    for i, (n, at, width) in enumerate(chunks):
        cols = pl.ds(at, width)
        copy = pltpu.make_async_copy(
            shards[n].at[:, cols], fulls[n].at[y, c, z, x, :, cols], local.at[i]
        )
        copy.start()
        owns.append(copy)
    arrived = [dict() for i in range(total)]

    def stage_z(i):
        n, at, width = chunks[i]
        cols = pl.ds(at, width)
        arrived[i]["z"] = [
            wire.start(
                shards[n].at[:, cols],
                fulls[n].at[y, c, z, x, :, cols],
                wire.to(y, c, (z + k) % Z, x),
            )
            for k in range(1, Z)
        ]

    def parts(i):
        n, at, width = chunks[i]
        left = half_columns(width)
        result = [(at, left)]
        if left < width:
            result.append((at + left, width - left))
        return result

    def to_core(i, block):
        arrived[i].setdefault("core", []).append(wire.start(block, block, wire.to(y, 1 - c, z, x)))

    def stage_one(i):
        owns[i].wait()
        for copy in arrived[i]["z"]:
            copy.wait_recv()
        n, first, columns = chunks[i]
        full = fulls[n]
        for half, (at, width) in enumerate(parts(i)):
            block = full.at[y, c, :, x, :, pl.ds(at, width)]
            if half == 0:
                arrived[i]["x0"] = [
                    wire.start(block, block, wire.to(y, c, z, (x + k) % X)) for k in range(1, X)
                ]
            else:
                arrived[i]["y1"] = [
                    wire.start(block, block, wire.to((y + k) % Y, c, z, x)) for k in range(1, Y)
                ]
        to_core(i, full.at[y, c, :, x, :, pl.ds(first, columns)])

    def stage_two(i):
        full = fulls[chunks[i][0]]
        for half, (at, width) in enumerate(parts(i)):
            cols = pl.ds(at, width)
            if half == 0:
                for copy in arrived[i]["x0"]:
                    copy.wait_recv()
                block = full.at[y, c, :, :, :, cols]
                arrived[i]["y0"] = [
                    wire.start(block, block, wire.to((y + k) % Y, c, z, x)) for k in range(1, Y)
                ]
                for k in range(1, X):
                    to_core(i, full.at[y, c, :, (x + X - k) % X, :, cols])
            else:
                for copy in arrived[i]["y1"]:
                    copy.wait_recv()
                block = full.at[:, c, :, x, :, cols]
                arrived[i]["x1"] = [
                    wire.start(block, block, wire.to(y, c, z, (x + k) % X)) for k in range(1, X)
                ]
                for k in range(1, Y):
                    to_core(i, full.at[(y + Y - k) % Y, c, :, x, :, cols])

    def stage_three(i):
        full = fulls[chunks[i][0]]
        for half, (at, width) in enumerate(parts(i)):
            cols = pl.ds(at, width)
            if half == 0:
                for k, copy in enumerate(arrived[i]["y0"], 1):
                    copy.wait_recv()
                    to_core(i, full.at[(y + Y - k) % Y, c, :, :, :, cols])
            else:
                for k, copy in enumerate(arrived[i]["x1"], 1):
                    copy.wait_recv()
                    to_core(i, full.at[:, c, :, (x + X - k) % X, :, cols])

    def finish():
        for i in range(total):
            for copy in arrived[i]["core"]:
                copy.wait_recv()
        wire.finish()

    def gathered(n):
        for i in range(total):
            if chunks[i][0] == n:
                for copy in arrived[i].pop("core"):
                    copy.wait_recv()
                arrived[i]["core"] = []

    return wire, (begin, wait), (stage_z, stage_one, stage_two, stage_three), gathered, finish


def group_copies(lay, send, recv, source, inbox, forward):
    y, c, z, x, b = lay.here()
    q = b // lay.Cq
    g = (b % lay.Cq) * 2 + c
    copies = []
    for k in range(1, lay.G):
        t = (g + (k if forward else lay.G - k)) % lay.G
        copies.append(
            pltpu.make_async_remote_copy(
                src_ref=source,
                dst_ref=inbox.at[k - 1],
                send_sem=send.at[k - 1],
                recv_sem=recv.at[k - 1],
                device_id=(y * 2 + t % 2, q * lay.Cq + t // 2),
                device_id_type=MESH,
            )
        )
    return copies, g


def to_tiles(low, tiles, r0, rows):
    for t in range(tiles.shape[0]):
        tiles[t, pl.ds(r0, rows), :] = low[:, t * LANES : (t + 1) * LANES].astype(F32)


def make_tables(lay, H, pack, raw, table, turned):
    r = pack.shape[4]
    total = lay.Y * 2 * lay.Z * lay.X

    def one(i, carry):
        block = pack[i // (2 * lay.Z * lay.X), i // (lay.Z * lay.X) % 2, i // lay.X % lay.Z, i % lay.X]
        raw[pl.ds(i * r, r), :] = block.astype(F32)
        return carry

    lax.fori_loop(0, total, one, 0)
    for t in range(table.shape[0]):
        v = raw[t * LANES : (t + 1) * LANES, :].T
        turned[t] = v
        leak = jax.nn.sigmoid(v[:H])
        decay = 1.0 - leak * jax.nn.sigmoid(v[H : 2 * H])
        table[t, :H] = decay
        table[t, H : 2 * H] = jnp.log(decay)
        table[t, 2 * H : 3 * H] = leak * v[2 * H : 3 * H] * v[3 * H : 4 * H] * (H ** (-0.5))


def carry_in(lay, H, rows, g, inbox, table, inc, t, later):
    log = table[t, H : 2 * H]
    state = jnp.zeros((H, LANES), F32)
    slope = jnp.zeros((H, LANES), F32)
    for k in range(1, lay.G):
        span = (k - 1) * rows
        valid = (g + k < lay.G) if later else (k <= g)
        s_part = inbox[k - 1, t, :H]
        r_part = s_part * 0.0 if later else inbox[k - 1, t, H : 2 * H]
        if span:
            power = jnp.exp(span * log)
            r_part = power * r_part + (span * jnp.exp((span - 1) * log)) * s_part
            s_part = power * s_part
        state = state + jnp.where(valid, s_part, 0.0)
        slope = slope + jnp.where(valid, r_part, 0.0)
    inc[t, :H] = state
    if not later:
        inc[t, H : 2 * H] = slope


def forward_kernel(lay, count, chunks, H, refs):
    n_in, n_out = 2 + count, 16 + count
    ins = refs[:n_in]
    query_gain, query_bias, key_gain, relative = refs[n_in : n_in + 4]
    refs = refs[n_in + 4 :]
    outs, scratch = refs[:n_out], refs[n_out:]
    tok_out, cot_out = outs[0], outs[1]
    fulls = outs[2 : 2 + count]
    mixed, ema, si, ri, table, turned = outs[2 + count : 8 + count]
    value_pre, base, queries, keys, vals, probs, attended, z_out = outs[8 + count :]
    sems, work = scratch[:6], scratch[6:]
    xt, pack, raw, s_end, r_end, mine, inbox, inc, stage, strip, scores, load, c_send, c_recv = work
    wire, (begin, wait), stages, gathered, finish = gather_kernel(
        lay, count, chunks, ins + (tok_out, cot_out) + tuple(fulls) + sems
    )
    stage_z, stage_one, stage_two, stage_three = stages
    total = len(chunks)
    rows = xt.shape[1]
    tiles = xt.shape[0]
    copies, g = group_copies(lay, c_send.at[0], c_recv.at[0], mine, inbox, True)
    others = pl.ds(1, lay.G - 1)
    vals_copies, g = group_copies(
        lay, c_send.at[1], c_recv.at[1], vals.at[0], vals.at[others], True
    )
    keys_copies, g = group_copies(
        lay, c_send.at[2], c_recv.at[2], keys.at[0], keys.at[others], True
    )
    width = tok_out.shape[2]
    zw = queries.shape[1]

    def value(at, cols):
        v = mm(tok_out[...].reshape(rows, width), weight_block(fulls[1], stage, load, at, cols))
        value_pre[:, at : at + cols] = v
        vals[0, :, at : at + cols] = (v * jax.nn.sigmoid(v)).astype(BF16)

    def send_values():
        for copy in vals_copies:
            copy.start()

    def bias():
        bias_kernel(lay.G * rows, relative.shape[0], relative, strip)

    def base_out(at, cols):
        base[:, at : at + cols] = mm(mixed[...], weight_block(fulls[2], stage, load, at, cols))

    def send_keys():
        z_pre = base[:, :zw]
        z_out[...] = z_pre
        shared = z_pre * jax.nn.sigmoid(z_pre)
        queries[...] = (shared * query_gain[...] + query_bias[...]).astype(BF16)
        keys[0] = (shared * key_gain[...]).astype(BF16)
        for copy in keys_copies:
            copy.start()

    def keys_here():
        for copy in keys_copies + vals_copies:
            copy.wait()

    def attend(part):
        y, c, z, x, b = lay.here()
        q_at = b // lay.Cq
        first = ((y * 2 + q_at % 2) * lay.Z * lay.X) * pack.shape[4]
        marks = raw[pl.ds(first, 1), :]
        lane = lax.broadcasted_iota(jnp.int32, (1, LANES), 1)
        mark = jnp.sum(
            jnp.where(lane == 4 * H + 3 + q_at // 2, marks, 0.0), axis=1, keepdims=True
        )
        far = jnp.where(mark == float(lay.G * rows), 0.0, masked_fill)
        attend_body(lay, g, far, queries, strip, keys, vals, attended, probs, scores, part)

    def tables():
        gathered(0)
        copy = pltpu.make_async_copy(fulls[0], pack, load)
        copy.start()
        copy.wait()
        make_tables(lay, H, pack, raw, table, turned)

    def tokens():
        wait(0)
        for j in range(lay.BL):
            to_tiles(tok_out[j], xt, j * (rows // lay.BL), rows // lay.BL)

    def ends(first, last):
        def one(t, carry):
            ema_ends_kernel(H, xt.at[t], table.at[t], s_end.at[t], r_end.at[t])
            for h in range(H):
                mine[t, pl.ds(h, 1), :] = s_end[t, h, SEG - 1 : SEG, :]
                mine[t, pl.ds(H + h, 1), :] = r_end[t, h, SEG - 1 : SEG, :]
            return carry

        lax.fori_loop(first, last, one, 0)

    def exchange():
        for copy in copies:
            copy.start()

    def carries():
        for copy in copies:
            copy.wait()
        for t in range(tiles):
            carry_in(lay, H, rows, g, inbox, table, inc, t, False)

    def out(first, last):
        def one(t, carry):
            ema_out_kernel(
                H, xt.at[t], table.at[t], turned.at[t, pl.ds(4 * H, 1)], s_end.at[t], r_end.at[t],
                inc.at[t], ema.at[t], si.at[t], ri.at[t],
            )
            return carry

        lax.fori_loop(first, last, one, 0)
        for t in range(first, last):
            for r0 in range(0, rows, 128):
                v = ema[t, pl.ds(r0, 128), :]
                mixed[pl.ds(r0, 128), t * LANES : (t + 1) * LANES] = (
                    v * jax.nn.sigmoid(v)
                ).astype(BF16)

    steps = [lambda: begin(0)]
    last = {}
    for i in range(min(AHEAD, total)):
        steps.append(functools.partial(stage_z, i))
    for turn in range(total + 2 * LAG):
        if 0 <= turn - 2 * LAG < total:
            last[chunks[turn - 2 * LAG][0]] = len(steps)
            steps.append(functools.partial(stage_three, turn - 2 * LAG))
        if 0 <= turn - LAG < total:
            steps.append(functools.partial(stage_two, turn - LAG))
        if turn < total:
            steps.append(functools.partial(stage_one, turn))
        if turn + AHEAD < total:
            steps.append(functools.partial(stage_z, turn + AHEAD))
        if turn == PLAN[5]:
            steps.append(lambda: begin(1))
    base_blocks = column_blocks(base.shape[1])
    todo = [(last[0] + PLAN[0], tables), (PLAN[1], tokens)]
    todo += [(0, functools.partial(ends, t, t + 1)) for t in range(tiles)]
    todo += [(0, exchange)]
    todo += [(last[1] + PLAN[2], lambda: gathered(1))]
    todo += [(0, functools.partial(value, *block)) for block in column_blocks(vals.shape[2])]
    todo += [(0, send_values), (0, carries)]
    todo += [(0, functools.partial(out, t, t + 1)) for t in range(tiles)]
    todo += [(0, bias), (last[2] + PLAN[3], lambda: gathered(2))]
    todo += [(0, functools.partial(base_out, *base_blocks[0])), (0, send_keys)]
    todo += [(0, functools.partial(base_out, *block)) for block in base_blocks[1:]]
    todo += [(0, keys_here)]
    todo += [(0, functools.partial(attend, part)) for part in range(rows // QB)]
    interleave(steps, todo, PLAN[6])
    finish()
    wait(1)


def interleave(steps, todo, most):
    todo = list(todo)
    done = set()

    def run():
        first, piece, name = (todo.pop(0) + (None,))[:3]
        piece()
        done.add(name)

    for number, step in enumerate(steps):
        step, needs = step if isinstance(step, tuple) else (step, None)
        while needs is not None and needs not in done:
            run()
        step()
        for i in range(most):
            if todo and todo[0][0] <= number:
                run()
    while todo:
        run()


PLAN = (1, 12, 1, 1, 0, 9, 1)


def forward_all(lay, H, tokens, cotangent, shards, query_gain, query_bias, key_gain, relative):
    count = len(shards)
    chunks = chunks_of([shard.shape for shard in shards], shards[0].shape[0] * LIMIT)
    micro, items, rows, width = tokens.shape
    per = (lay.Z - 1) + 2 * (lay.X - 1 + lay.Y - 1) + 1 + 2 * (lay.X - 1 + lay.Y - 1)
    blocks = jax.ShapeDtypeStruct((lay.BL, rows, width), BF16)
    fulls = [
        jax.ShapeDtypeStruct((lay.Y, 2, lay.Z, lay.X) + shard.shape, shard.dtype)
        for shard in shards
    ]
    T, R = width // LANES, lay.BL * rows
    state = (T, H, SEG, LANES)
    outs = [blocks, blocks] + fulls
    outs += [
        jax.ShapeDtypeStruct((R, width), BF16),
        jax.ShapeDtypeStruct((T, R, LANES), F32),
        jax.ShapeDtypeStruct(state, F32),
        jax.ShapeDtypeStruct(state, F32),
        jax.ShapeDtypeStruct((T, 3 * H, LANES), F32),
        jax.ShapeDtypeStruct((T, LANES, LANES), F32),
    ]
    V, cols, zw, G = shards[1].shape[1], shards[2].shape[1], query_gain.shape[1], lay.G
    outs += [
        jax.ShapeDtypeStruct((R, V), F32),
        jax.ShapeDtypeStruct((R, cols), F32),
        jax.ShapeDtypeStruct((R, zw), BF16),
        jax.ShapeDtypeStruct((G, R, zw), BF16),
        jax.ShapeDtypeStruct((G, R, V), BF16),
        jax.ShapeDtypeStruct((G, R, R), BF16),
        jax.ShapeDtypeStruct((R, V), F32),
        jax.ShapeDtypeStruct((R, zw), F32),
    ]

    def body(*refs):
        forward_kernel(lay, count, chunks, H, refs)

    result = pl.pallas_call(
        body,
        out_shape=outs,
        in_specs=[ANY] * (2 + count) + [VM] * 3 + [SM],
        out_specs=[VM] + [ANY] * (1 + count) + [VM] * 14,
        scratch_shapes=[
            pltpu.SemaphoreType.DMA((len(chunks) * per,)),
            pltpu.SemaphoreType.DMA((len(chunks) * per,)),
            pltpu.SemaphoreType.DMA((len(chunks),)),
            pltpu.SemaphoreType.DMA((2, lay.MS)),
            pltpu.SemaphoreType.DMA((2, lay.BL)),
            pltpu.SemaphoreType.DMA((2,)),
            pltpu.VMEM((T, R, LANES), F32),
            pltpu.VMEM(fulls[0].shape, fulls[0].dtype),
            pltpu.VMEM((width, LANES), F32),
            pltpu.VMEM(state, F32),
            pltpu.VMEM(state, F32),
            pltpu.VMEM((T, 2 * H, LANES), F32),
            pltpu.VMEM((lay.G - 1, T, 2 * H, LANES), F32),
            pltpu.VMEM((T, 2 * H, LANES), F32),
            pltpu.VMEM((lay.Y, 2, lay.Z, lay.X, shards[1].shape[0], 768), BF16),
            pltpu.VMEM((QB, (G + 1) * R), F32),
            pltpu.VMEM((QB, G * R), F32),
            pltpu.SemaphoreType.DMA,
            pltpu.SemaphoreType.DMA((3, lay.G - 1)),
            pltpu.SemaphoreType.DMA((3, lay.G - 1)),
        ],
        compiler_params=pltpu.CompilerParams(
            collective_id=0, has_side_effects=True, vmem_limit_bytes=58 * 2**20
        ),
        name="forward_all",
    )(tokens, cotangent, *shards, query_gain, query_bias, key_gain, relative)
    return result[0], result[1], result[2 : 2 + count], result[2 + count :]


def add_blocks(total, index, extra, extra_index, counts, width_at):
    size = int(np.prod(counts)) if counts else 1

    def one(i, carry):
        places = []
        for extent in reversed(counts):
            places.insert(0, i % extent)
            i = i // extent
        a, e = index(*places), extra_index(*places)
        total[a] = total[a] + extra[e]
        return carry

    lax.fori_loop(0, size, one, 0)


def scatter_kernel(lay, H, NB, chunks, ins, outs, scratch):
    (
        grads, x_low, d_in, d_att, delta, queries, keys, vals, probs, z_pre, gains_small, mixed, ema,
        base_rest, value_pre, w_base, w_value, pre, gains, table, turned, si, ri, block_out,
    ) = ins
    results, small_out, outs_to, made, dvo, dvi = outs
    bufs, own = scratch[: 6 * len(chunks)], scratch[6 * len(chunks) :]
    small_acc, small_recv, send, recv, local, t_send, t_recv, t_local = own[:8]
    xt, dt, sums, flat, split, l_end, mine, inbox, inc, gx, c_send, c_recv = own[8:20]
    dx = xt
    stage, vstage, bstage, pstage, ds, strip, dq, dko, dki, zlow, mixed_acc, x_acc, load = own[20:33]
    gstage, mixed_t, loads = own[33:36]
    halves = own[36:]
    grads = grads + made + (split,)
    y, c, z, x, b = lay.here()
    X, Y, Z = lay.X, lay.Y, lay.Z
    greet(lay)
    wire = Wire(lay, send, recv)
    begin, wait = reshard_out(lay, (block_out, gx), outs_to, t_send, t_recv, t_local)
    total = len(chunks)
    arrived = [dict() for i in range(total)]

    def buf(i, name):
        return bufs[6 * i + ("acc", "x0", "y1", "y0", "x1", "z").index(name)]

    def parts(i):
        n, at, width = chunks[i]
        left = half_columns(width)
        result = [(0, left)]
        if left < width:
            result.append((left, width - left))
        return result

    def own_half(i):
        n, at, width = chunks[i]
        if n == len(grads) - 1:
            return None
        source = grads[n].at[:, c, :, :, :, pl.ds(at, width)]
        return pltpu.make_async_copy(source, half_of(i), local.at[i])

    def half_of(i):
        n, at, width = chunks[i]
        r = grads[n].shape[4]
        room = [h for h in halves if h.shape[4] == r][0]
        return room.at[i % 2, :, :, :, :, pl.ds(0, width)]

    def prefetch_half(i):
        near = own_half(i) if i < total else None
        if near is not None:
            near.start()

    def stage_core(i):
        n, at, width = chunks[i]
        if n_base <= n < n_base + 2:
            settle()
        if i == 0:
            prefetch_half(0)
        arrived[i]["core"] = wire.start(
            grads[n].at[:, 1 - c, :, :, :, pl.ds(at, width)],
            buf(i, "acc"),
            wire.to(y, 1 - c, z, x),
        )

    def stage_one(i):
        n, first, columns = chunks[i]
        acc = buf(i, "acc")
        near = own_half(i)
        if near is not None:
            near.wait()
        arrived[i]["core"].wait_recv()
        if near is not None:
            mine_half = half_of(i)
            add_blocks(acc, lambda *p: p, mine_half, lambda *p: p, (Y, Z, X), None)
        else:
            add_blocks(
                acc, lambda *p: p, split, lambda p, q, s: (p, c, q, s), (Y, Z, X), None
            )
        prefetch_half(i + 1)
        for half, (at, width) in enumerate(parts(i)):
            cols = pl.ds(at, width)
            if half == 0:
                arrived[i]["x0"] = [
                    wire.start(
                        acc.at[:, :, (x + k) % X, :, cols],
                        buf(i, "x0").at[k - 1],
                        wire.to(y, c, z, (x + k) % X),
                    )
                    for k in range(1, X)
                ]
            else:
                arrived[i]["y1"] = [
                    wire.start(
                        acc.at[(y + k) % Y, :, :, :, cols],
                        buf(i, "y1").at[k - 1],
                        wire.to((y + k) % Y, c, z, x),
                    )
                    for k in range(1, Y)
                ]

    def stage_two(i):
        acc = buf(i, "acc")
        for half, (at, width) in enumerate(parts(i)):
            cols = slice(at, at + width)
            view = pl.ds(at, width)
            if half == 0:
                for k, copy in enumerate(arrived[i]["x0"]):
                    copy.wait_recv()
                    add_blocks(
                        acc,
                        lambda p, q: (p, q, x, slice(None), cols),
                        buf(i, "x0"),
                        lambda p, q: (k, p, q),
                        (Y, Z),
                        None,
                    )
                arrived[i]["y0"] = [
                    wire.start(
                        acc.at[(y + k) % Y, :, x, :, view],
                        buf(i, "y0").at[k - 1],
                        wire.to((y + k) % Y, c, z, x),
                    )
                    for k in range(1, Y)
                ]
            else:
                for k, copy in enumerate(arrived[i]["y1"]):
                    copy.wait_recv()
                    add_blocks(
                        acc,
                        lambda p, q: (y, p, q, slice(None), cols),
                        buf(i, "y1"),
                        lambda p, q: (k, p, q),
                        (Z, X),
                        None,
                    )
                arrived[i]["x1"] = [
                    wire.start(
                        acc.at[y, :, (x + k) % X, :, view],
                        buf(i, "x1").at[k - 1],
                        wire.to(y, c, z, (x + k) % X),
                    )
                    for k in range(1, X)
                ]

    def stage_three(i):
        acc = buf(i, "acc")
        for half, (at, width) in enumerate(parts(i)):
            cols = slice(at, at + width)
            name = "y0" if half == 0 else "x1"
            for k, copy in enumerate(arrived[i][name]):
                copy.wait_recv()
                add_blocks(
                    acc,
                    lambda p: (y, p, x, slice(None), cols),
                    buf(i, name),
                    lambda p: (k, p),
                    (Z,),
                    None,
                )
        arrived[i]["z"] = [
            wire.start(
                acc.at[y, (z + k) % Z, x], buf(i, "z").at[k - 1], wire.to(y, c, (z + k) % Z, x)
            )
            for k in range(1, Z)
        ]

    def stage_four(i):
        n, at, width = chunks[i]
        total = buf(i, "acc")[y, z, x].astype(F32)
        for k, copy in enumerate(arrived[i]["z"]):
            copy.wait_recv()
            total = total + buf(i, "z")[k].astype(F32)
        results[n][:, pl.ds(at, width)] = total

    small_at = [0]

    def small_stage(moves):
        copies = []
        for target in moves:
            slot = small_at[0]
            small_at[0] += 1
            copies.append((slot, wire.start(small_acc, small_recv.at[slot], target)))
        for slot, copy in copies:
            copy.wait_send()
            wire.sent = [other for other in wire.sent if other is not copy]
        for slot, copy in copies:
            copy.wait_recv()
            small_acc[...] += small_recv[slot]

    rows, tiles = xt.shape[1], xt.shape[0]
    per_block = rows // lay.BL
    copies, g = group_copies(lay, c_send.at[0], c_recv.at[0], mine, inbox, False)
    G, zw = lay.G, queries.shape[1]
    D = x_low.shape[2]
    scale = zw ** (-0.5)
    n_base, n_value = len(grads) - 3, len(grads) - 2
    q_at = b // lay.Cq

    def back_copy(k, source, target, kind):
        t = (g + G - k) % G
        return pltpu.make_async_remote_copy(
            src_ref=source,
            dst_ref=target,
            send_sem=c_send.at[kind, k - 1],
            recv_sem=c_recv.at[kind, k - 1],
            device_id=(y * 2 + t % 2, q_at * lay.Cq + t // 2),
            device_id_type=MESH,
        )

    key_copies = [back_copy(k, dko.at[k - 1], dki.at[k - 1], 1) for k in range(1, G)]
    val_copies = [back_copy(k, dvo.at[k - 1], dvi.at[k - 1], 2) for k in range(1, G)]

    def fetch(source, target):
        copy = pltpu.make_async_copy(source, target, load)
        copy.start()
        copy.wait()

    storing = []

    def settle():
        while storing:
            storing.pop().wait()

    def keep_grad(n, at, grad):
        columns = grad.shape[1]
        r = made[n].shape[4]
        low = grad.astype(BF16).reshape(Y, 2, Z, X, r, columns)
        settle()
        gstage[:, :, :, :, :, :columns] = low
        copy = pltpu.make_async_copy(
            gstage.at[:, :, :, :, :, pl.ds(0, columns)],
            made[n].at[:, :, :, :, :, pl.ds(at, columns)],
            loads.at[0],
        )
        copy.start()
        storing.append(copy)

    all_base, all_value = column_blocks(w_base.shape[5]), column_blocks(w_value.shape[5])
    weight_order = [(w_base,) + block for block in all_base[1:] + all_base[:1]]
    weight_order += [(w_value,) + block for block in all_value]
    coming = {}

    def weight_copy(number):
        full, at, columns = weight_order[number]
        return pltpu.make_async_copy(
            full.at[:, :, :, :, :, pl.ds(at, columns)],
            stage.at[:, :, :, :, :, pl.ds(0, columns)],
            loads.at[1],
        )

    def next_weight(number):
        if number < len(weight_order):
            coming["weight"] = weight_copy(number)
            coming["weight"].start()

    def rest_copy(number):
        full, at, columns = weight_order[number]
        if at == 0:
            return pltpu.make_async_copy(
                base_rest.at[:, pl.ds(0, columns - zw)],
                bstage.at[:, pl.ds(zw, columns - zw)],
                loads.at[2],
            )
        return pltpu.make_async_copy(
            base_rest.at[:, pl.ds(at - zw, columns)], bstage.at[:, pl.ds(0, columns)], loads.at[2]
        )

    def next_rest(number):
        if number < len(all_base):
            coming["rest"] = rest_copy(number)
            coming["rest"].start()

    def next_pre(number):
        if number < len(all_value):
            at, columns = all_value[number]
            coming["pre"] = pltpu.make_async_copy(
                value_pre.at[:, pl.ds(at, columns)], pstage.at[:, pl.ds(0, columns)], loads.at[3]
            )
            coming["pre"].start()

    def begin_fetch():
        next_weight(0)
        next_rest(0)
        next_pre(0)
        coming["x"] = pltpu.make_async_copy(pre, x_acc, loads.at[4])
        coming["x"].start()
        mixed_t[...] = mixed[...].astype(F32).T.astype(BF16)

    def weight_here(columns):
        coming["weight"].wait()
        return stage[:, :, :, :, :, 0:columns].reshape(-1, columns)

    def base_block(number):
        full, at, columns = weight_order[number]
        coming["rest"].wait()
        if at == 0:
            bstage[:, :zw] = zlow[...]
        low = bstage[:, :columns]
        keep_grad(0, at, mm(mixed_t[...], low))
        part = mm_t(low, weight_here(columns))
        mixed_acc[...] = part if number == 0 else mixed_acc[...] + part
        next_weight(number + 1)
        next_rest(number + 1)

    def load_values(k):
        fetch(vals.at[k], vstage)
        if k == G - 1:
            strip[...] = jnp.zeros(strip.shape, F32)

    def scores_back(k, i):
        at = i * QB
        here = pl.ds(at, QB)
        owner = lax.rem(g - k + G, G)
        dw = mm_t(d_att[here, :], vstage[...])
        p = probs[k, here, :].astype(F32)
        grad = p * (dw - delta[here, :])
        off = jnp.clip(G * rows - rows * (g - owner) - at, 0, G * rows)
        strip[:, pl.ds(pl.multiple_of(off, LANES), rows)] += grad
        low = grad.astype(BF16)
        ds[here, :] = low
        part = mm(low, keys[k]) * scale
        dq[here, :] = part if k == G - 1 else dq[here, :] + part

    def keys_back(k):
        grad = dot_t(ds[...], queries[...]) * scale
        if k:
            dko[k - 1] = grad.astype(BF16)
            key_copies[k - 1].start()
        else:
            for copy in key_copies:
                copy.wait()
            for j in range(1, G):
                grad = grad + dki[j - 1].astype(F32)
            pre_z = z_pre[...]
            gate = jax.nn.sigmoid(pre_z)
            shared = pre_z * gate
            small_acc[0:1, :] = jnp.sum(dq[...] * shared, axis=0, keepdims=True)
            small_acc[1:2, :] = jnp.sum(dq[...], axis=0, keepdims=True)
            small_acc[2:3, :] = jnp.sum(grad * shared, axis=0, keepdims=True)
            d_shared = dq[...] * gains_small[0:1, :] + grad * gains_small[1:2, :]
            zlow[...] = (d_shared * (gate * (1.0 + pre_z * (1.0 - gate)))).astype(BF16)

    def values_back(k):
        for at, columns in column_blocks(vstage.shape[1]):
            vstage[:, at : at + columns] = dot_t(
                probs[k], d_att[:, at : at + columns]
            ).astype(BF16)
        fetch(vstage, dvo.at[k - 1])
        val_copies[k - 1].start()

    def buckets():
        sums_of = bucket_sums(G * rows, NB, strip)
        lane = lax.broadcasted_iota(jnp.int32, (1, LANES), 1)
        line = jnp.zeros((1, LANES), F32)
        for k in range(NB):
            line = jnp.where(lane == k, jnp.sum(sums_of[k], axis=1, keepdims=True), line)
        small_acc[3:4, :] = line
        small_acc[4:8, :] = jnp.zeros((4, LANES), F32)

    def values_here():
        for copy in val_copies:
            copy.wait()

    def value_block(number):
        full, at, columns = weight_order[len(all_base) + number]
        cols = pl.ds(at, columns)
        if number == 0:
            mixed_t[...] = x_low[...].reshape(rows, D).astype(F32).T.astype(BF16)
            coming["x"].wait()
        grad = dot_t(probs[0], d_att[:, at : at + columns])
        for k in range(1, G):
            fetch(dvi.at[k - 1, :, cols], bstage.at[:, pl.ds(0, columns)])
            grad = grad + bstage[:, :columns].astype(F32)
        coming["pre"].wait()
        v = pstage[:, :columns]
        gate = jax.nn.sigmoid(v)
        low = (grad * (gate * (1.0 + v * (1.0 - gate)))).astype(BF16)
        next_pre(number + 1)
        keep_grad(1, at, mm(mixed_t[...], low))
        x_acc[...] += mm_t(low, weight_here(columns))
        next_weight(len(all_base) + number + 1)

    def d_ema(t):
        v = ema[t]
        gate = jax.nn.sigmoid(v)
        dt[t] = mixed_acc[:, t * LANES : (t + 1) * LANES] * (gate * (1.0 + v * (1.0 - gate)))

    def tile_x():
        for j in range(lay.BL):
            to_tiles(x_low[j], xt, j * per_block, per_block)

    def ends(t):
        ema_back_ends_kernel(H, dt.at[t], table.at[t], l_end.at[t])
        for h in range(H):
            mine[t, pl.ds(h, 1), :] = l_end[t, h, 0:1, :]

    def exchange():
        for copy in copies:
            copy.start()

    def carries():
        for copy in copies:
            copy.wait()
        for t in range(tiles):
            carry_in(lay, H, rows, g, inbox, table, inc, t, True)

    def correlate(t):
        ema_sums_kernel(H, xt.at[t], dt.at[t], table.at[t], si.at[t], ri.at[t], sums.at[t])

    def back(t):
        ema_back_kernel(
            H, dt.at[t], table.at[t], turned.at[t, pl.ds(4 * H, 1)], l_end.at[t], inc.at[t], dx.at[t]
        )
        cols = slice(t * LANES, (t + 1) * LANES)
        for j in range(lay.BL):
            at = pl.ds(j * per_block, per_block)
            gx[j, :, cols] = (x_acc[at, cols] + dx[t, at, :]).astype(BF16)

    def share_sums():
        r = split.shape[4]
        for t in range(tiles):
            sums[t, pl.ds(2 * H + 1, 2), :] = gains[0:2, t * LANES : (t + 1) * LANES]
            flat[t * LANES : (t + 1) * LANES, :] = sums[t].T

        def one(i, carry):
            split[i // (2 * Z * X), i // (Z * X) % 2, i // X % Z, i % X] = flat[pl.ds(i * r, r), :]
            return carry

        lax.fori_loop(0, 2 * X * Y * Z, one, 0)

    sums[...] = jnp.zeros(sums.shape, F32)
    xs = [wire.to(y, c, z, (x + k) % X) for k in range(1, X)]
    ys = [wire.to((y + k) % Y, c, z, x) for k in range(1, Y)]
    zs = [wire.to(y, c, (z + k) % Z, x) for k in range(1, Z)]

    run = functools.partial
    todo = [(0, begin_fetch)]
    for number in range(len(all_base) - 1):
        todo.append((0, run(base_block, number), (n_base, weight_order[number][1])))
    for k in list(range(1, G))[::-1] + [0]:
        todo.append((0, run(load_values, k)))
        todo += [(0, run(scores_back, k, i)) for i in range(rows // QB)]
        todo.append((0, run(keys_back, k)))
        if k:
            todo.append((0, run(values_back, k)))
    todo.append((0, run(base_block, len(all_base) - 1), (n_base, 0)))
    todo += [(0, run(d_ema, t)) for t in range(tiles)]
    todo += [(0, run(ends, t)) for t in range(tiles)]
    todo += [(0, exchange), (0, values_here)]
    for number, block in enumerate(all_value):
        todo.append((0, run(value_block, number), (n_value, block[0])))
    todo.append((0, carries))
    todo += [(0, run(back, t)) for t in range(tiles)]
    todo += [(0, lambda: begin(1)), (0, tile_x), (0, buckets, "small")]
    todo += [(0, run(correlate, t)) for t in range(tiles)]
    todo.append((0, share_sums, (len(grads) - 1, 0)))

    def needs(i):
        n, at, width = chunks[i]
        return (n, at) if n >= n_base else None

    steps = []
    for i in range(min(LEAD, total)):
        steps.append((run(stage_core, i), needs(i)))
    steps.append(lambda: begin(0))
    for turn in range(total + 3 * BLAG):
        for what, lag in ((stage_four, 3), (stage_three, 2), (stage_two, 1), (stage_one, 0)):
            if 0 <= turn - lag * BLAG < total:
                steps.append(run(what, turn - lag * BLAG))
        if turn + LEAD < total:
            steps.append((run(stage_core, turn + LEAD), needs(turn + LEAD)))
        if turn >= total:
            late = turn - total
            moves = ([wire.to(y, 1 - c, z, x)], xs, ys, zs)
            if late < 4:
                steps.append((run(small_stage, moves[late]), "small"))
    interleave(steps, todo, MOST)
    small_out[...] = small_acc[...]
    wait(0)
    wait(1)
    wire.finish()


LEAD = 2
MOST = 1
BLAG = 3


def dot_t(a, b):
    return lax.dot_general(a, b, (((0,), (0,)), ((), ())), preferred_element_type=F32)


def bucket_sums(length, bucket_count, strip):
    edges = bucket_edges(bucket_count)
    lag0 = lax.broadcasted_iota(jnp.int32, (QB, LANES), 0) - lax.broadcasted_iota(
        jnp.int32, (QB, LANES), 1
    )
    totals = [jnp.zeros((1, LANES), F32) for k in range(bucket_count)]
    for t in range((length + QB) // LANES):
        base = length - t * LANES
        low, high = base - LANES + 1, base + QB - 1
        if high < 0:
            continue
        value = strip[:, t * LANES : (t + 1) * LANES]
        for k in range(bucket_count):
            top = edges[k + 1] if k + 1 < bucket_count else length
            if edges[k] <= high and top > low:
                lag = lag0 + base
                inside = (lag >= edges[k]) & (lag < top)
                totals[k] = totals[k] + jnp.sum(jnp.where(inside, value, 0.0), axis=0, keepdims=True)
    return totals


def backward_all(lay, H, NB, grads, fulls, values, share):
    X, Y, Z, G = lay.X, lay.Y, lay.Z, lay.G
    R, V = values["d_att"].shape
    D = values["pre"].shape[1]
    T, zw = D // LANES, values["queries"].shape[1]
    rows = R // lay.BL
    micro = lay.MS // lay.items
    shapes = [grad.shape[-2:] for grad in grads] + [full.shape[-2:] for full in fulls] + [(share, LANES)]
    kinds = [grad.dtype for grad in grads] + [BF16, BF16, F32]
    known = len(grads)
    chunks = chunks_of([shape for shape in shapes[:known]], share * LIMIT)
    base_blocks = column_blocks(shapes[known][1])
    chunks += [(known,) + block for block in base_blocks[1:]]
    chunks += [(known,) + base_blocks[0]]
    chunks += [(known + 1,) + block for block in column_blocks(shapes[known + 1][1])]
    chunks += [(known + 2, 0, LANES)]
    scratch = []
    for n, at, cols in chunks:
        r = shapes[n][0]
        left = half_columns(cols)
        right = cols - left if cols > left else LANES
        kind = kinds[n]
        scratch += [
            pltpu.VMEM((Y, Z, X, r, cols), kind),
            pltpu.VMEM((X - 1, Y, Z, r, left), kind),
            pltpu.VMEM((Y - 1, Z, X, r, right), kind),
            pltpu.VMEM((Y - 1, Z, r, left), kind),
            pltpu.VMEM((X - 1, Z, r, right), kind),
            pltpu.VMEM((Z - 1, r, cols), kind),
        ]
    hops = 1 + (X - 1) + (Y - 1) + (Z - 1)
    per = 1 + 2 * (X - 1 + Y - 1) + Z - 1
    small = (8, LANES)
    outs = [jax.ShapeDtypeStruct(shape, F32) for shape in shapes]
    outs.append(jax.ShapeDtypeStruct(small, F32))
    outs += [jax.ShapeDtypeStruct((micro, lay.items, rows, D), BF16)] * 2
    outs += [jax.ShapeDtypeStruct(full.shape, BF16) for full in fulls]
    outs += [jax.ShapeDtypeStruct((G - 1, R, V), BF16)] * 2
    scratch += [pltpu.VMEM(small, F32), pltpu.VMEM((hops,) + small, F32)]
    heights = sorted({shapes[n][0] for n, at, width in chunks})
    widest = {r: max(w for n, at, w in chunks if shapes[n][0] == r) for r in heights}
    scratch += [
        pltpu.SemaphoreType.DMA((len(chunks) * per + hops,)),
        pltpu.SemaphoreType.DMA((len(chunks) * per + hops,)),
        pltpu.SemaphoreType.DMA((len(chunks),)),
        pltpu.SemaphoreType.DMA((2, lay.BL)),
        pltpu.SemaphoreType.DMA((2, lay.MS)),
        pltpu.SemaphoreType.DMA((2,)),
        pltpu.VMEM((T, R, LANES), F32),
        pltpu.VMEM((T, R, LANES), F32),
        pltpu.VMEM((T, LANES, LANES), F32),
        pltpu.VMEM((D, LANES), F32),
        pltpu.VMEM((Y, 2, Z, X, share, LANES), F32),
        pltpu.VMEM((T, H, SEG, LANES), F32),
        pltpu.VMEM((T, H, LANES), F32),
        pltpu.VMEM((G - 1, T, H, LANES), F32),
        pltpu.VMEM((T, H, LANES), F32),
        pltpu.VMEM((lay.BL, rows, D), BF16),
        pltpu.SemaphoreType.DMA((3, G - 1)),
        pltpu.SemaphoreType.DMA((3, G - 1)),
        pltpu.VMEM((Y, 2, Z, X, share, 768), BF16),
        pltpu.VMEM((R, V), BF16),
        pltpu.VMEM((R, 768), BF16),
        pltpu.VMEM((R, 768), F32),
        pltpu.VMEM((R, R), BF16),
        pltpu.VMEM((QB, (G + 1) * R), F32),
        pltpu.VMEM((R, zw), F32),
        pltpu.VMEM((G - 1, R, zw), BF16),
        pltpu.VMEM((G - 1, R, zw), BF16),
        pltpu.VMEM((R, zw), BF16),
        pltpu.VMEM((R, D), F32),
        pltpu.VMEM((R, D), F32),
        pltpu.SemaphoreType.DMA,
        pltpu.VMEM((Y, 2, Z, X, share, 768), BF16),
        pltpu.VMEM((D, R), BF16),
        pltpu.SemaphoreType.DMA((5,)),
    ]
    scratch += [pltpu.VMEM((2, Y, Z, X, r, widest[r]), BF16) for r in heights]
    order = (
        ("x_blocks", VM), ("d_in", ANY), ("d_att", VM), ("delta", VM), ("queries", VM), ("keys", VM),
        ("vals", ANY), ("probs", VM), ("z_pre", VM), ("gains_small", VM), ("mixed", VM), ("ema", VM),
        ("base_rest", ANY), ("value_pre", ANY), ("w_base", ANY), ("w_value", ANY), ("pre", ANY),
        ("gains", VM), ("table", VM), ("turned", VM), ("si", VM), ("ri", VM), ("block_out", ANY),
    )
    values = dict(values, w_base=fulls[0], w_value=fulls[1])
    order = tuple(item for item in order if item[0] != "d_in")

    def body(*refs):
        named = refs[known : known + len(order)]
        ins = (tuple(refs[:known]), named[0], None) + tuple(named[1:])
        rest = refs[known + len(order) :]
        results, small_out, moved = rest[: known + 3], rest[known + 3], rest[known + 4 : known + 6]
        made, dvo, dvi = rest[known + 6 : known + 8], rest[known + 8], rest[known + 9]
        scatter_kernel(
            lay, H, NB, chunks, ins, (results, small_out, moved, tuple(made), dvo, dvi), rest[known + 10 :]
        )

    result = pl.pallas_call(
        body,
        out_shape=outs,
        in_specs=[ANY] * known + [spec for name, spec in order],
        out_specs=[VM] * (known + 4) + [ANY] * 6,
        scratch_shapes=scratch,
        compiler_params=pltpu.CompilerParams(
            collective_id=1, has_side_effects=True, vmem_limit_bytes=60 * 2**20
        ),
        name="backward_all",
    )(*grads, *[values[name] for name, spec in order])
    return result[: known + 3], result[known + 3], result[known + 4 : known + 6]


def row(ref, index, lanes):
    return jnp.broadcast_to(ref[pl.ds(index, 1), lanes], (SEG, LANES))


def lane_call(kernel, outs, args, name):
    def spec(a):
        lead = len(a.shape) - 1
        return pl.BlockSpec(a.shape[:-1] + (LANES,), lambda i: (0,) * lead + (i,))

    return pl.pallas_call(
        kernel,
        out_shape=outs,
        grid=(args[0].shape[-1] // LANES,),
        in_specs=[spec(a) for a in args],
        out_specs=jax.tree.map(spec, outs),
        compiler_params=pltpu.CompilerParams(vmem_limit_bytes=32 * 2**20),
        name=name,
    )(*args)


def shifted(value, by):
    where = lax.broadcasted_iota(jnp.int32, (SEG, LANES), 0)
    if by > 0:
        return jnp.where(where >= by, pltpu.roll(value, by, 0), 0.0)
    return jnp.where(where < SEG + by, pltpu.roll(value, SEG + by, 0), 0.0)


def ema_ends_kernel(H, x_ref, tab_ref, s_ref, r_ref):
    rows, width = x_ref.shape
    steps = rows // SEG

    def tile(lanes):
        decay = [row(tab_ref, h, lanes) for h in range(H)]

        def step(t, state):
            s, r = state
            xt = x_ref[pl.ds(t, SEG, stride=steps), lanes]
            r = tuple(decay[h] * r[h] + s[h] for h in range(H))
            s = tuple(decay[h] * s[h] + xt for h in range(H))
            return s, r

        zero = tuple(tab_ref[0:SEG, lanes] * 0.0 for h in range(H))
        s, r = lax.fori_loop(0, steps, step, (zero, zero))
        for h in range(H):
            log = row(tab_ref, H + h, lanes)
            sh, rh = s[h], r[h]
            for d in (1, 2, 4):
                span = d * steps
                sd, rd = shifted(sh, d), shifted(rh, d)
                power = jnp.exp(span * log)
                rh = rh + power * rd + (span * jnp.exp((span - 1) * log)) * sd
                sh = sh + power * sd
            s_ref[h, :, lanes] = sh
            r_ref[h, :, lanes] = rh

    tile(slice(None))


def ema_out_kernel(H, x_ref, tab_ref, omega_ref, s_ref, r_ref, inc_ref, ema_ref, si_ref, ri_ref):
    rows, width = x_ref.shape
    steps = rows // SEG

    def tile(lanes):
        decay = [row(tab_ref, h, lanes) for h in range(H)]
        gain = [row(tab_ref, 2 * H + h, lanes) for h in range(H)]
        omega = row(omega_ref, 0, lanes)
        start = []
        span = (lax.broadcasted_iota(jnp.int32, (SEG, LANES), 0) * steps).astype(F32)
        for h in range(H):
            log = row(tab_ref, H + h, lanes)
            s_dev = row(inc_ref, h, lanes)
            r_dev = row(inc_ref, H + h, lanes)
            power = jnp.exp(span * log)
            s_in = shifted(s_ref[h, :, lanes], 1) + power * s_dev
            r_in = (
                shifted(r_ref[h, :, lanes], 1)
                + power * r_dev
                + (span * jnp.exp((span - 1.0) * log)) * s_dev
            )
            si_ref[h, :, lanes] = s_in
            ri_ref[h, :, lanes] = r_in
            start.append(s_in)

        def step(t, s):
            xt = x_ref[pl.ds(t, SEG, stride=steps), lanes]
            s = tuple(decay[h] * s[h] + xt for h in range(H))
            parts = [gain[h] * s[h] for h in range(H)]
            while len(parts) > 1:
                parts = [parts[i] + parts[i + 1] for i in range(0, len(parts), 2)]
            ema_ref[pl.ds(t, SEG, stride=steps), lanes] = parts[0] + omega * xt
            return s

        lax.fori_loop(0, steps, step, tuple(start))

    tile(slice(None))


def ema_back_ends_kernel(H, d_ref, tab_ref, l_ref):
    rows, width = d_ref.shape
    steps = rows // SEG

    def tile(lanes):
        decay = [row(tab_ref, h, lanes) for h in range(H)]

        def step(i, lam):
            dt = d_ref[pl.ds(steps - 1 - i, SEG, stride=steps), lanes]
            return tuple(decay[h] * lam[h] + dt for h in range(H))

        zero = tuple(tab_ref[0:SEG, lanes] * 0.0 for h in range(H))
        lam = lax.fori_loop(0, steps, step, zero)
        for h in range(H):
            log = row(tab_ref, H + h, lanes)
            lh = lam[h]
            for d in (1, 2, 4):
                lh = lh + jnp.exp(d * steps * log) * shifted(lh, -d)
            l_ref[h, :, lanes] = lh

    tile(slice(None))


def ema_sums_kernel(H, x_ref, d_ref, tab_ref, si_ref, ri_ref, out_ref):
    rows, width = x_ref.shape
    steps = rows // SEG
    group = H // 2

    def tile(lanes):
        for first in range(0, H, group):
            decay = [row(tab_ref, first + h, lanes) for h in range(group)]

            def step(t, state):
                s, r, c, q, o = state
                xt = x_ref[pl.ds(t, SEG, stride=steps), lanes]
                dt = d_ref[pl.ds(t, SEG, stride=steps), lanes]
                r = tuple(decay[h] * r[h] + s[h] for h in range(group))
                s = tuple(decay[h] * s[h] + xt for h in range(group))
                c = tuple(c[h] + dt * s[h] for h in range(group))
                q = tuple(q[h] + dt * r[h] for h in range(group))
                return s, r, c, q, o + dt * xt

            zero = tuple(tab_ref[0:SEG, lanes] * 0.0 for h in range(group))
            s = tuple(si_ref[first + h, :, lanes] for h in range(group))
            r = tuple(ri_ref[first + h, :, lanes] for h in range(group))
            s, r, c, q, o = lax.fori_loop(0, steps, step, (s, r, zero, zero, zero[0]))
            for h in range(group):
                out_ref[pl.ds(first + h, 1), lanes] = jnp.sum(c[h], axis=0, keepdims=True)
                out_ref[pl.ds(H + first + h, 1), lanes] = jnp.sum(q[h], axis=0, keepdims=True)
            out_ref[pl.ds(2 * H, 1), lanes] = jnp.sum(o, axis=0, keepdims=True)

    tile(slice(None))


def ema_back_kernel(H, d_ref, tab_ref, omega_ref, l_ref, inc_ref, dx_ref):
    rows, width = d_ref.shape
    steps = rows // SEG

    def tile(lanes):
        decay = [row(tab_ref, h, lanes) for h in range(H)]
        gain = [row(tab_ref, 2 * H + h, lanes) for h in range(H)]
        omega = row(omega_ref, 0, lanes)
        start = []
        span = ((SEG - 1 - lax.broadcasted_iota(jnp.int32, (SEG, LANES), 0)) * steps).astype(F32)
        for h in range(H):
            log = row(tab_ref, H + h, lanes)
            l_dev = row(inc_ref, h, lanes)
            start.append(shifted(l_ref[h, :, lanes], -1) + jnp.exp(span * log) * l_dev)

        def step(i, lam):
            at = pl.ds(steps - 1 - i, SEG, stride=steps)
            dt = d_ref[at, lanes]
            lam = tuple(decay[h] * lam[h] + dt for h in range(H))
            parts = [gain[h] * lam[h] for h in range(H)]
            while len(parts) > 1:
                parts = [parts[i] + parts[i + 1] for i in range(0, len(parts), 2)]
            dx_ref[at, lanes] = parts[0] + omega * dt
            return lam

        lax.fori_loop(0, steps, step, tuple(start))

    tile(slice(None))


def call(kernel, outs, args, specs=None, scratch=(), vmem=58, name=None):
    return pl.pallas_call(
        kernel,
        out_shape=outs,
        in_specs=specs or [VM] * len(args),
        out_specs=jax.tree.map(lambda o: VM, outs),
        scratch_shapes=list(scratch),
        compiler_params=pltpu.CompilerParams(vmem_limit_bytes=vmem * 2**20),
        name=name,
    )(*args)


QB = 256
STRETCH = 128


def bias_kernel(length, bucket_count, bias_ref, strip_ref):
    edges = bucket_edges(bucket_count)
    tiles = length // LANES + QB // LANES
    lag0 = lax.broadcasted_iota(jnp.int32, (QB, LANES), 0) - lax.broadcasted_iota(
        jnp.int32, (QB, LANES), 1
    )
    for t in range(strip_ref.shape[1] // LANES):
        base = length - t * LANES
        low, high = base - LANES + 1, base + QB - 1
        start = max([k for k in range(bucket_count) if edges[k] <= low], default=0)
        value = jnp.full((QB, LANES), bias_ref[start], F32)
        for k in range(start + 1, bucket_count):
            if edges[k] <= high:
                value = jnp.where(lag0 + base >= edges[k], bias_ref[k], value)
        strip_ref[:, t * LANES : (t + 1) * LANES] = value


def attend_body(lay, g, far, q_ref, strip_ref, keys, vals, att_ref, probs_ref, scores, part):
    G = lay.G
    rows, zw = q_ref.shape
    length = G * rows
    r0 = lax.broadcasted_iota(jnp.int32, (QB, rows), 0)
    c0 = lax.broadcasted_iota(jnp.int32, (QB, rows), 1)

    def one(i, carry):
        at = i * QB
        q = q_ref[pl.ds(at, QB), :]
        for k in range(G):
            owner = lax.rem(g - k + G, G)
            s = mm_t(q, keys[k])
            off = jnp.clip(length - rows * (g - owner) - at, 0, length)
            s = s * (zw ** (-0.5)) + strip_ref[:, pl.ds(pl.multiple_of(off, LANES), rows)]
            if k == 0:
                pos = r0 + at
                s = jnp.where(pos // STRETCH == c0 // STRETCH, s, s + far)
                s = jnp.where(c0 <= pos, s, masked_fill)
            else:
                s = s + jnp.where(k <= g, far, masked_fill)
            scores[:, k * rows : (k + 1) * rows] = s
        s = scores[...]
        p = jnp.exp(s - jnp.max(s, axis=1, keepdims=True))
        p = p * (1.0 / jnp.sum(p, axis=1, keepdims=True))
        total = jnp.zeros((QB, att_ref.shape[1]), F32)
        for k in range(G):
            low = p[:, k * rows : (k + 1) * rows].astype(BF16)
            probs_ref[k, pl.ds(at, QB), :] = low
            total += mm(low, vals[k])
        att_ref[pl.ds(at, QB), :] = total
        return carry

    one(part, 0)


def attend_back_kernel(lay, bucket_count, flag_ref, q_ref, da_ref, delta_ref, probs_ref, *refs):
    G = lay.G
    keys, vals, dq_ref, dk_ref, dv_ref, dko_ref, dvo_ref, bucket_ref, strip, ds_ref = refs
    rows, zw = q_ref.shape
    length = G * rows
    g = flag_ref[1]
    scale = zw ** (-0.5)
    edges = bucket_edges(bucket_count)
    strip[...] = jnp.zeros(strip.shape, F32)

    def one(i, carry):
        at = pl.multiple_of(i * QB, QB)
        da = da_ref[pl.ds(at, QB), :]
        dq = jnp.zeros((QB, zw), F32)
        for k in range(G):
            owner = lax.rem(g - k + G, G)
            dw = mm_t(da, vals[k])
            p = probs_ref[k, pl.ds(at, QB), :].astype(F32)
            ds = p * (dw - delta_ref[pl.ds(at, QB), :])
            off = jnp.clip(length - rows * (g - owner) - at, 0, length)
            strip[:, pl.ds(pl.multiple_of(off, LANES), rows)] += ds
            low = ds.astype(BF16)
            dq += mm(low, keys[k])
            ds_ref[k, pl.ds(at, QB), :] = low
        dq_ref[pl.ds(at, QB), :] = dq * scale
        return carry

    lax.fori_loop(0, rows // QB, one, 0)
    for k in range(G):
        dk = lax.dot_general(
            ds_ref[k], q_ref[...], (((0,), (0,)), ((), ())), preferred_element_type=F32
        )
        dv = lax.dot_general(
            probs_ref[k], da_ref[...], (((0,), (0,)), ((), ())), preferred_element_type=F32
        )
        if k == 0:
            dk_ref[...] = dk * scale
            dv_ref[...] = dv
        else:
            dko_ref[k - 1] = (dk * scale).astype(BF16)
            dvo_ref[k - 1] = dv.astype(BF16)
    lag0 = lax.broadcasted_iota(jnp.int32, (QB, LANES), 0) - lax.broadcasted_iota(
        jnp.int32, (QB, LANES), 1
    )
    sums = [jnp.zeros((1, LANES), F32) for k in range(bucket_count)]
    for t in range((length + QB) // LANES):
        base = length - t * LANES
        low, high = base - LANES + 1, base + QB - 1
        if high < 0:
            continue
        value = strip[:, t * LANES : (t + 1) * LANES]
        for k in range(bucket_count):
            top = edges[k + 1] if k + 1 < bucket_count else length
            if edges[k] <= high and top > low:
                lag = lag0 + base
                inside = (lag >= edges[k]) & (lag < top)
                sums[k] = sums[k] + jnp.sum(jnp.where(inside, value, 0.0), axis=0, keepdims=True)
    for k in range(bucket_count):
        bucket_ref[pl.ds(k, 1), :] = sums[k]


def silu_slope(values):
    gate_value = jax.nn.sigmoid(values)
    return gate_value * (1.0 + values * (1.0 - gate_value))


def normalize(seq_rows):
    centered = seq_rows - jnp.mean(seq_rows, axis=-1, keepdims=True)
    inverse = lax.rsqrt(jnp.mean(centered * centered, axis=-1, keepdims=True) + epsilon)
    return (centered * inverse, inverse)


def normalize_back(grad_scaled, unit_rows, inverse):
    return inverse * (
        grad_scaled
        - jnp.mean(grad_scaled, axis=-1, keepdims=True)
        - unit_rows * jnp.mean(grad_scaled * unit_rows, axis=-1, keepdims=True)
    )


def mm(a, b):
    return jnp.dot(a, b, preferred_element_type=F32)


def mm_t(a, b):
    return lax.dot_general(a, b, (((1,), (1,)), ((), ())), preferred_element_type=F32)


def wgrad(a, b):
    return lax.dot_general(a, b, (((0,), (0,)), ((), ())), preferred_element_type=F32).astype(BF16)


def shards(
    lay,
    tokens,
    cotangent,
    stretch_size,
    w_value,
    w_base,
    w_out,
    w_up,
    w_down,
    ema_delta,
    ema_alpha,
    ema_beta,
    ema_gamma,
    ema_omega,
    first_gain,
    second_gain,
    query_gain,
    query_bias,
    key_gain,
    relative_bias,
):
    micro, items, seq_len, D = tokens.shape
    H = ema_delta.shape[1]
    zw = query_gain.shape[0]
    V = w_value.shape[1]
    NB = relative_bias.shape[0]
    length = seq_len * lay.S
    G = lay.G
    R = lay.BL * seq_len
    d_at, b_at = lax.axis_index("dp"), lax.axis_index("seq")
    c_at, y_at = d_at % 2, d_at // 2
    q_at = b_at // lay.Cq
    g_at = (b_at % lay.Cq) * 2 + c_at
    share = ema_delta.shape[0]

    def group_perm(k):
        pairs = []
        for y in range(lay.Y):
            for q in range(lay.Q):
                for g in range(G):
                    t = (g + k) % G
                    src = (y * 2 + g % 2) * lay.S + q * lay.Cq + g // 2
                    dst = (y * 2 + t % 2) * lay.S + q * lay.Cq + t // 2
                    pairs.append((src, dst))
        return pairs

    def shift(value, k):
        return lax.ppermute(value, ("dp", "seq"), group_perm(k % G))

    marks = jnp.broadcast_to(stretch_size.reshape(-1, 1).astype(BF16), (lay.MS, share))
    used = 4 * H + 3 + lay.MS
    pack = jnp.concatenate(
        [
            ema_delta.T,
            ema_alpha.T,
            ema_beta.T,
            ema_gamma.T,
            ema_omega[None],
            first_gain[None],
            second_gain[None],
            marks,
            jnp.zeros((LANES - used, share), BF16),
        ],
        0,
    ).T
    x_blocks, cot_blocks, fulls, rest = forward_all(
        lay, H, tokens, cotangent, (pack, w_value, w_base, w_out, w_up, w_down),
        query_gain[None], query_bias[None], key_gain[None], relative_bias,
    )
    mixed, ema_tiles, s_in, r_in, table, turned = rest[:6]
    value_pre, base, queries, keys_all, vals_all, probs, attended, z_pre = rest[6:]
    flags = jnp.stack([g_at, g_at])
    mats = [full.reshape(-1, full.shape[-1]) for full in fulls[1:]]
    mat_value, mat_base, mat_out, mat_up, mat_down = mats
    gain_first = turned[:, 4 * H + 1].reshape(D)
    gain_second = turned[:, 4 * H + 2].reshape(D)

    x_low = x_blocks.reshape(R, D)
    x = x_low.astype(F32)
    grad_out = cot_blocks.reshape(R, D).astype(F32)

    reset_pre = base[:, zw : zw + V]
    cand_pre = base[:, zw + V : zw + V + D]
    update_pre = base[:, zw + V + D :]
    reset_gate = jax.nn.silu(reset_pre)
    update = jax.nn.sigmoid(update_pre)
    gated = (attended * reset_gate).astype(BF16)
    cand_in = cand_pre + mm(gated, mat_out)
    candidate = jax.nn.silu(cand_in)
    first_sum = x + update * (candidate - x)
    unit_first, inverse_first = normalize(first_sum)
    normed = unit_first * gain_first
    normed_low = normed.astype(BF16)
    hidden_pre = mm(normed_low, mat_up)
    hidden = jax.nn.silu(hidden_pre).astype(BF16)
    second_sum = normed + mm(hidden, mat_down)
    unit_second, inverse_second = normalize(second_sum)
    block_out = (unit_second * gain_second).astype(BF16)

    grad_gain_second = jnp.sum(grad_out * unit_second, axis=0)
    grad_second = normalize_back(grad_out * gain_second, unit_second, inverse_second)
    branch = grad_second.astype(BF16)
    grad_mat_down = wgrad(hidden, branch)
    hidden_grad = (mm_t(branch, mat_down) * silu_slope(hidden_pre)).astype(BF16)
    grad_mat_up = wgrad(normed_low, hidden_grad)
    grad_normed = grad_second + mm_t(hidden_grad, mat_up)
    grad_gain_first = jnp.sum(grad_normed * unit_first, axis=0)
    grad_first = normalize_back(grad_normed * gain_first, unit_first, inverse_first)
    cand_low = (grad_first * update * silu_slope(cand_in)).astype(BF16)
    grad_mat_out = wgrad(gated, cand_low)
    grad_gated = mm_t(cand_low, mat_out)
    att_low = (grad_gated * reset_gate).astype(BF16)
    grad_reset = grad_gated * attended * silu_slope(reset_pre)
    grad_update = grad_first * (candidate - x) * update * (1.0 - update)
    delta = jnp.sum(att_low.astype(F32) * attended, axis=1, keepdims=True)
    base_rest = jnp.concatenate(
        [grad_reset.astype(BF16), cand_low, grad_update.astype(BF16)], 1
    )
    pre = grad_first * (1.0 - update)
    gains = jnp.concatenate(
        [grad_gain_first[None], grad_gain_second[None], jnp.zeros((6, D), F32)]
    )
    shape = (lay.Y, 2, lay.Z, lay.X)

    def split(grad):
        return grad.reshape(shape + (-1, grad.shape[-1]))

    reduced, small_total, moved = backward_all(
        lay,
        H,
        NB,
        [split(grad_mat_down), split(grad_mat_up), split(grad_mat_out)],
        [fulls[2], fulls[1]],
        dict(
            x_blocks=x_blocks, d_att=att_low, delta=delta, queries=queries, keys=keys_all,
            vals=vals_all, probs=probs, z_pre=z_pre,
            gains_small=jnp.concatenate([query_gain[None], key_gain[None], jnp.zeros((6, zw), F32)]),
            mixed=mixed, ema=ema_tiles, base_rest=base_rest, value_pre=value_pre, pre=pre, gains=gains,
            table=table, turned=turned, si=s_in, ri=r_in,
            block_out=block_out.reshape(lay.BL, seq_len, D),
        ),
        share,
    )
    own = reduced[5].T
    corr, lagged = own[:H], own[H : 2 * H]
    p = jax.nn.sigmoid(ema_delta.T.astype(F32))
    a = jax.nn.sigmoid(ema_alpha.T.astype(F32))
    beta = ema_beta.T.astype(F32)
    read = ema_gamma.T.astype(F32) * (H ** (-0.5))
    q_grad = read * p * beta * lagged
    return (
        moved[0],
        moved[1].astype(F32),
        reduced[4],
        reduced[3],
        reduced[2],
        reduced[1],
        reduced[0],
        ((read * beta * corr - a * q_grad) * p * (1.0 - p)).T,
        (-p * q_grad * a * (1.0 - a)).T,
        (p * read * corr).T,
        (p * beta * corr * (H ** (-0.5))).T,
        own[2 * H],
        own[2 * H + 1],
        own[2 * H + 2],
        small_total[0, :zw],
        small_total[1, :zw],
        small_total[2, :zw],
        small_total[3, :NB],
    )


def solution(mesh):
    rows = P(None, "dp", "seq", None)
    part2, part1 = P(("dp", "seq"), None), P(("dp", "seq"))
    in_specs = (rows, rows, P(None, "dp")) + (part2,) * 9 + (part1,) * 3 + (P(),) * 4
    out_specs = (rows, rows) + (part2,) * 9 + (part1,) * 3 + (P(),) * 4

    def whole(tokens, *rest):
        micro, seqs = tokens.shape[:2]
        lay = Layout(mesh.shape["dp"], mesh.shape["seq"], micro, seqs // mesh.shape["dp"])
        return jax.shard_map(
            functools.partial(shards, lay),
            mesh=mesh,
            in_specs=in_specs,
            out_specs=out_specs,
            check_vma=False,
        )(tokens, *rest)

    return whole
```

```python
import functools

import jax
import jax.numpy as jnp
import numpy as np
from jax import lax
from jax.experimental import pallas as pl
from jax.experimental.pallas import tpu as pltpu
from jax.sharding import PartitionSpec as P

epsilon = 1e-05
masked_fill = -1e30
MESH = pl.DeviceIdType.MESH
ANY = pl.BlockSpec(memory_space=pl.ANY)
VM = pl.BlockSpec(memory_space=pltpu.VMEM)
SM = pl.BlockSpec(memory_space=pltpu.SMEM)
F32 = jnp.float32
BF16 = jnp.bfloat16
SEG = 8
LANES = 128


def bucket_edges(bucket_count):
    edge_list = [0]
    middle = bucket_count // 2
    for number in range(1, bucket_count):
        edge_list.append(number if number < middle else int(middle * 2 ** ((number - middle) / 2)))
    return edge_list


class Layout:
    def __init__(self, dp, seq, micro, items):
        self.dp, self.S = dp, seq
        self.C = 2
        self.Y = dp // 2
        self.X = min(self.Y, seq)
        self.Z = seq // self.X
        self.items = items
        self.MS = micro * items
        self.Q = 2 * self.MS
        self.Cq = seq // self.Q
        self.G = 2 * self.Cq
        self.BL = seq // self.G

    def here(self):
        d, b = lax.axis_index("dp"), lax.axis_index("seq")
        return d // 2, d % 2, b // self.X, b % self.X, b


class Wire:
    def __init__(self, lay, send, recv):
        self.lay, self.send, self.recv, self.count = lay, send, recv, 0
        self.sent = []

    def to(self, y, c, z, x):
        return (y * 2 + c, z * self.lay.X + x)

    def start(self, src, dst, target):
        number = self.count
        self.count += 1
        copy = pltpu.make_async_remote_copy(
            src_ref=src,
            dst_ref=dst,
            send_sem=self.send.at[number],
            recv_sem=self.recv.at[number],
            device_id=target,
            device_id_type=MESH,
        )
        copy.start()
        self.sent.append(copy)
        return copy

    def finish(self):
        for copy in self.sent:
            copy.wait_send()


def greet(lay):
    y, c, z, x, b = lay.here()
    barrier = pltpu.get_barrier_semaphore()
    plane = 2 * lay.S

    def one(k, carry):
        other = (c * lay.S + b + k) % plane
        pl.semaphore_signal(
            barrier, inc=1, device_id=(y * 2 + other // lay.S, other % lay.S), device_id_type=MESH
        )
        return carry

    lax.fori_loop(1, plane, one, 0)
    for k in range(1, lay.Y):
        pl.semaphore_signal(
            barrier, inc=1, device_id=(((y + k) % lay.Y) * 2 + c, b), device_id_type=MESH
        )
    pl.semaphore_wait(barrier, plane - 1 + lay.Y - 1)


ALPHA = 0.5
AHEAD = 3
LAG = 3
ORDER = 1
LIMIT = 800


def half_columns(columns):
    return max(1, int(columns // LANES * ALPHA + 0.5)) * LANES


def reshard_in(lay, sources, targets, send, recv, local):
    y, c, z, x, b = lay.here()
    g = b // lay.BL
    slot = b % lay.BL
    qm = b // lay.Cq
    gm = (b % lay.Cq) * 2 + c

    def begin(n):
        for source, target in ((sources[n], targets[n]),):
            for ms in range(lay.MS):
                seq_to = (ms * 2 + c) * lay.Cq + g // 2
                mine = jnp.logical_and(seq_to == b, g % 2 == c)
                block = source.at[ms // lay.items, ms % lay.items]

                @pl.when(jnp.logical_not(mine))
                def _():
                    pltpu.make_async_remote_copy(
                        src_ref=block,
                        dst_ref=target.at[slot],
                        send_sem=send.at[n, ms],
                        recv_sem=recv.at[n, slot],
                        device_id=(y * 2 + g % 2, seq_to),
                        device_id_type=MESH,
                    ).start()

                @pl.when(mine)
                def _():
                    pltpu.make_async_copy(block, target.at[slot], local.at[n]).start()

    def wait(n):
        source, target = sources[n], targets[n]
        for ms in range(lay.MS):
            seq_to = (ms * 2 + c) * lay.Cq + g // 2
            mine = jnp.logical_and(seq_to == b, g % 2 == c)
            block = source.at[ms // lay.items, ms % lay.items]

            @pl.when(jnp.logical_not(mine))
            def _():
                pltpu.make_async_remote_copy(
                    src_ref=block,
                    dst_ref=target.at[slot],
                    send_sem=send.at[n, ms],
                    recv_sem=recv.at[n, slot],
                    device_id=(y * 2 + g % 2, seq_to),
                    device_id_type=MESH,
                ).wait_send()

            @pl.when(mine)
            def _():
                pltpu.make_async_copy(block, target.at[slot], local.at[n]).wait()

        for j in range(lay.BL):
            from_b = gm * lay.BL + j
            own = jnp.logical_and(from_b == b, qm % 2 == c)

            @pl.when(jnp.logical_not(own))
            def _():
                pltpu.make_async_remote_copy(
                    src_ref=source.at[0, 0],
                    dst_ref=target.at[j],
                    send_sem=send.at[n, 0],
                    recv_sem=recv.at[n, j],
                    device_id=(y * 2 + qm % 2, from_b),
                    device_id_type=MESH,
                ).wait_recv()

    return begin, wait


def reshard_out(lay, sources, targets, send, recv, local):
    y, c, z, x, b = lay.here()
    g = b // lay.BL
    qm = b // lay.Cq
    gm = (b % lay.Cq) * 2 + c
    ms_to = qm // 2
    m_to, s_to = ms_to // lay.items, ms_to % lay.items

    def copies(n, j):
        from_b = gm * lay.BL + j
        own = jnp.logical_and(from_b == b, qm % 2 == c)
        remote = pltpu.make_async_remote_copy(
            src_ref=sources[n].at[j],
            dst_ref=targets[n].at[m_to, s_to],
            send_sem=send.at[n, j],
            recv_sem=recv.at[n, ms_to],
            device_id=(y * 2 + qm % 2, from_b),
            device_id_type=MESH,
        )
        near = pltpu.make_async_copy(sources[n].at[j], targets[n].at[m_to, s_to], local.at[n])
        return own, remote, near

    def begin(n):
        for j in range(lay.BL):
            own, remote, near = copies(n, j)
            pl.when(jnp.logical_not(own))(remote.start)
            pl.when(own)(near.start)

    def wait(n):
        for j in range(lay.BL):
            own, remote, near = copies(n, j)
            pl.when(jnp.logical_not(own))(remote.wait_send)
            pl.when(own)(near.wait)
        for ms in range(lay.MS):
            seq_at = (ms * 2 + c) * lay.Cq + g // 2
            own = jnp.logical_and(seq_at == b, g % 2 == c)

            @pl.when(jnp.logical_not(own))
            def _():
                pltpu.make_async_remote_copy(
                    src_ref=sources[n].at[0],
                    dst_ref=targets[n].at[ms // lay.items, ms % lay.items],
                    send_sem=send.at[n, 0],
                    recv_sem=recv.at[n, ms],
                    device_id=(y * 2 + g % 2, seq_at),
                    device_id_type=MESH,
                ).wait_recv()

    return begin, wait


def chunks_of(shapes, limit):
    result = []
    for n, shape in enumerate(shapes):
        tiles = shape[-1] // LANES
        cuts = max(1, -(-shape[0] * shape[-1] // limit))
        at = 0
        for cut in range(cuts):
            width = (tiles - at) // (cuts - cut) if cut == cuts - 1 else -(-(tiles - at) // (cuts - cut))
            result.append((n, at * LANES, width * LANES))
            at += width
    return result


def column_blocks(columns, most=768):
    cuts = -(-columns // most)
    while (columns // LANES) % cuts:
        cuts += 1
    width = columns // cuts
    return [(i * width, width) for i in range(cuts)]


def weight_block(full, stage, sem, at, width):
    target = stage.at[:, :, :, :, :, pl.ds(0, width)]
    copy = pltpu.make_async_copy(full.at[:, :, :, :, :, pl.ds(at, width)], target, sem)
    copy.start()
    copy.wait()
    block = stage[:, :, :, :, :, 0:width]
    return block.reshape(-1, width)


def gather_kernel(lay, count, chunks, refs):
    tok, cot = refs[0], refs[1]
    shards = refs[2 : 2 + count]
    tok_out, cot_out = refs[2 + count], refs[3 + count]
    fulls = refs[4 + count : 4 + 2 * count]
    send, recv, local, t_send, t_recv, t_local = refs[4 + 2 * count :]
    y, c, z, x, b = lay.here()
    X, Y, Z = lay.X, lay.Y, lay.Z
    greet(lay)
    wire = Wire(lay, send, recv)
    begin, wait = reshard_in(lay, (tok, cot), (tok_out, cot_out), t_send, t_recv, t_local)
    total = len(chunks)
    owns = []
    for i, (n, at, width) in enumerate(chunks):
        cols = pl.ds(at, width)
        copy = pltpu.make_async_copy(
            shards[n].at[:, cols], fulls[n].at[y, c, z, x, :, cols], local.at[i]
        )
        copy.start()
        owns.append(copy)
    arrived = [dict() for i in range(total)]

    def stage_z(i):
        n, at, width = chunks[i]
        cols = pl.ds(at, width)
        arrived[i]["z"] = [
            wire.start(
                shards[n].at[:, cols],
                fulls[n].at[y, c, z, x, :, cols],
                wire.to(y, c, (z + k) % Z, x),
            )
            for k in range(1, Z)
        ]

    def parts(i):
        n, at, width = chunks[i]
        left = half_columns(width)
        result = [(at, left)]
        if left < width:
            result.append((at + left, width - left))
        return result

    def to_core(i, block):
        arrived[i].setdefault("core", []).append(wire.start(block, block, wire.to(y, 1 - c, z, x)))

    def stage_one(i):
        owns[i].wait()
        for copy in arrived[i]["z"]:
            copy.wait_recv()
        n, first, columns = chunks[i]
        full = fulls[n]
        for half, (at, width) in enumerate(parts(i)):
            block = full.at[y, c, :, x, :, pl.ds(at, width)]
            if half == 0:
                arrived[i]["x0"] = [
                    wire.start(block, block, wire.to(y, c, z, (x + k) % X)) for k in range(1, X)
                ]
            else:
                arrived[i]["y1"] = [
                    wire.start(block, block, wire.to((y + k) % Y, c, z, x)) for k in range(1, Y)
                ]
        to_core(i, full.at[y, c, :, x, :, pl.ds(first, columns)])

    def stage_two(i):
        full = fulls[chunks[i][0]]
        for half, (at, width) in enumerate(parts(i)):
            cols = pl.ds(at, width)
            if half == 0:
                for copy in arrived[i]["x0"]:
                    copy.wait_recv()
                block = full.at[y, c, :, :, :, cols]
                arrived[i]["y0"] = [
                    wire.start(block, block, wire.to((y + k) % Y, c, z, x)) for k in range(1, Y)
                ]
                for k in range(1, X):
                    to_core(i, full.at[y, c, :, (x + X - k) % X, :, cols])
            else:
                for copy in arrived[i]["y1"]:
                    copy.wait_recv()
                block = full.at[:, c, :, x, :, cols]
                arrived[i]["x1"] = [
                    wire.start(block, block, wire.to(y, c, z, (x + k) % X)) for k in range(1, X)
                ]
                for k in range(1, Y):
                    to_core(i, full.at[(y + Y - k) % Y, c, :, x, :, cols])

    def stage_three(i):
        full = fulls[chunks[i][0]]
        for half, (at, width) in enumerate(parts(i)):
            cols = pl.ds(at, width)
            if half == 0:
                for k, copy in enumerate(arrived[i]["y0"], 1):
                    copy.wait_recv()
                    to_core(i, full.at[(y + Y - k) % Y, c, :, :, :, cols])
            else:
                for k, copy in enumerate(arrived[i]["x1"], 1):
                    copy.wait_recv()
                    to_core(i, full.at[:, c, :, (x + X - k) % X, :, cols])

    def finish():
        for i in range(total):
            for copy in arrived[i]["core"]:
                copy.wait_recv()
        wire.finish()

    def gathered(n):
        for i in range(total):
            if chunks[i][0] == n:
                for copy in arrived[i].pop("core"):
                    copy.wait_recv()
                arrived[i]["core"] = []

    return wire, (begin, wait), (stage_z, stage_one, stage_two, stage_three), gathered, finish


def group_copies(lay, send, recv, source, inbox, forward):
    y, c, z, x, b = lay.here()
    q = b // lay.Cq
    g = (b % lay.Cq) * 2 + c
    copies = []
    for k in range(1, lay.G):
        t = (g + (k if forward else lay.G - k)) % lay.G
        copies.append(
            pltpu.make_async_remote_copy(
                src_ref=source,
                dst_ref=inbox.at[k - 1],
                send_sem=send.at[k - 1],
                recv_sem=recv.at[k - 1],
                device_id=(y * 2 + t % 2, q * lay.Cq + t // 2),
                device_id_type=MESH,
            )
        )
    return copies, g


def to_tiles(low, tiles, r0, rows):
    for t in range(tiles.shape[0]):
        tiles[t, pl.ds(r0, rows), :] = low[:, t * LANES : (t + 1) * LANES].astype(F32)


def make_tables(lay, H, pack, raw, table, turned):
    r = pack.shape[4]
    total = lay.Y * 2 * lay.Z * lay.X

    def one(i, carry):
        block = pack[i // (2 * lay.Z * lay.X), i // (lay.Z * lay.X) % 2, i // lay.X % lay.Z, i % lay.X]
        raw[pl.ds(i * r, r), :] = block.astype(F32)
        return carry

    lax.fori_loop(0, total, one, 0)
    for t in range(table.shape[0]):
        v = raw[t * LANES : (t + 1) * LANES, :].T
        turned[t] = v
        leak = jax.nn.sigmoid(v[:H])
        decay = 1.0 - leak * jax.nn.sigmoid(v[H : 2 * H])
        table[t, :H] = decay
        table[t, H : 2 * H] = jnp.log(decay)
        table[t, 2 * H : 3 * H] = leak * v[2 * H : 3 * H] * v[3 * H : 4 * H] * (H ** (-0.5))


def carry_in(lay, H, rows, g, inbox, table, inc, t, later):
    log = table[t, H : 2 * H]
    state = jnp.zeros((H, LANES), F32)
    slope = jnp.zeros((H, LANES), F32)
    for k in range(1, lay.G):
        span = (k - 1) * rows
        valid = (g + k < lay.G) if later else (k <= g)
        s_part = inbox[k - 1, t, :H]
        r_part = s_part * 0.0 if later else inbox[k - 1, t, H : 2 * H]
        if span:
            power = jnp.exp(span * log)
            r_part = power * r_part + (span * jnp.exp((span - 1) * log)) * s_part
            s_part = power * s_part
        state = state + jnp.where(valid, s_part, 0.0)
        slope = slope + jnp.where(valid, r_part, 0.0)
    inc[t, :H] = state
    if not later:
        inc[t, H : 2 * H] = slope


def forward_kernel(lay, count, chunks, H, refs):
    n_in, n_out = 2 + count, 16 + count
    ins = refs[:n_in]
    query_gain, query_bias, key_gain, relative = refs[n_in : n_in + 4]
    refs = refs[n_in + 4 :]
    outs, scratch = refs[:n_out], refs[n_out:]
    tok_out, cot_out = outs[0], outs[1]
    fulls = outs[2 : 2 + count]
    mixed, ema, si, ri, table, turned = outs[2 + count : 8 + count]
    value_pre, base, queries, keys, vals, probs, attended, z_out = outs[8 + count :]
    sems, work = scratch[:6], scratch[6:]
    xt, pack, raw, s_end, r_end, mine, inbox, inc, stage, strip, scores, load, c_send, c_recv = work
    wire, (begin, wait), stages, gathered, finish = gather_kernel(
        lay, count, chunks, ins + (tok_out, cot_out) + tuple(fulls) + sems
    )
    stage_z, stage_one, stage_two, stage_three = stages
    total = len(chunks)
    rows = xt.shape[1]
    tiles = xt.shape[0]
    copies, g = group_copies(lay, c_send.at[0], c_recv.at[0], mine, inbox, True)
    others = pl.ds(1, lay.G - 1)
    vals_copies, g = group_copies(
        lay, c_send.at[1], c_recv.at[1], vals.at[0], vals.at[others], True
    )
    keys_copies, g = group_copies(
        lay, c_send.at[2], c_recv.at[2], keys.at[0], keys.at[others], True
    )
    width = tok_out.shape[2]
    zw = queries.shape[1]

    def value(at, cols):
        v = mm(tok_out[...].reshape(rows, width), weight_block(fulls[1], stage, load, at, cols))
        value_pre[:, at : at + cols] = v
        vals[0, :, at : at + cols] = (v * jax.nn.sigmoid(v)).astype(BF16)

    def send_values():
        for copy in vals_copies:
            copy.start()

    def bias():
        bias_kernel(lay.G * rows, relative.shape[0], relative, strip)

    def base_out(at, cols):
        base[:, at : at + cols] = mm(mixed[...], weight_block(fulls[2], stage, load, at, cols))

    def send_keys():
        z_pre = base[:, :zw]
        z_out[...] = z_pre
        shared = z_pre * jax.nn.sigmoid(z_pre)
        queries[...] = (shared * query_gain[...] + query_bias[...]).astype(BF16)
        keys[0] = (shared * key_gain[...]).astype(BF16)
        for copy in keys_copies:
            copy.start()

    def keys_here():
        for copy in keys_copies + vals_copies:
            copy.wait()

    def attend(part):
        y, c, z, x, b = lay.here()
        q_at = b // lay.Cq
        first = ((y * 2 + q_at % 2) * lay.Z * lay.X) * pack.shape[4]
        marks = raw[pl.ds(first, 1), :]
        lane = lax.broadcasted_iota(jnp.int32, (1, LANES), 1)
        mark = jnp.sum(
            jnp.where(lane == 4 * H + 3 + q_at // 2, marks, 0.0), axis=1, keepdims=True
        )
        far = jnp.where(mark == float(lay.G * rows), 0.0, masked_fill)
        attend_body(lay, g, far, queries, strip, keys, vals, attended, probs, scores, part)

    def tables():
        gathered(0)
        copy = pltpu.make_async_copy(fulls[0], pack, load)
        copy.start()
        copy.wait()
        make_tables(lay, H, pack, raw, table, turned)

    def tokens():
        wait(0)
        for j in range(lay.BL):
            to_tiles(tok_out[j], xt, j * (rows // lay.BL), rows // lay.BL)

    def ends(first, last):
        def one(t, carry):
            ema_ends_kernel(H, xt.at[t], table.at[t], s_end.at[t], r_end.at[t])
            for h in range(H):
                mine[t, pl.ds(h, 1), :] = s_end[t, h, SEG - 1 : SEG, :]
                mine[t, pl.ds(H + h, 1), :] = r_end[t, h, SEG - 1 : SEG, :]
            return carry

        lax.fori_loop(first, last, one, 0)

    def exchange():
        for copy in copies:
            copy.start()

    def carries():
        for copy in copies:
            copy.wait()
        for t in range(tiles):
            carry_in(lay, H, rows, g, inbox, table, inc, t, False)

    def out(first, last):
        def one(t, carry):
            ema_out_kernel(
                H, xt.at[t], table.at[t], turned.at[t, pl.ds(4 * H, 1)], s_end.at[t], r_end.at[t],
                inc.at[t], ema.at[t], si.at[t], ri.at[t],
            )
            return carry

        lax.fori_loop(first, last, one, 0)
        for t in range(first, last):
            for r0 in range(0, rows, 128):
                v = ema[t, pl.ds(r0, 128), :]
                mixed[pl.ds(r0, 128), t * LANES : (t + 1) * LANES] = (
                    v * jax.nn.sigmoid(v)
                ).astype(BF16)

    steps = [lambda: begin(0)]
    last = {}
    for i in range(min(AHEAD, total)):
        steps.append(functools.partial(stage_z, i))
    for turn in range(total + 2 * LAG):
        if 0 <= turn - 2 * LAG < total:
            last[chunks[turn - 2 * LAG][0]] = len(steps)
            steps.append(functools.partial(stage_three, turn - 2 * LAG))
        if 0 <= turn - LAG < total:
            steps.append(functools.partial(stage_two, turn - LAG))
        if turn < total:
            steps.append(functools.partial(stage_one, turn))
        if turn + AHEAD < total:
            steps.append(functools.partial(stage_z, turn + AHEAD))
        if turn == PLAN[5]:
            steps.append(lambda: begin(1))
    base_blocks = column_blocks(base.shape[1])
    todo = [(last[0] + PLAN[0], tables), (PLAN[1], tokens)]
    todo += [(0, functools.partial(ends, t, t + 1)) for t in range(tiles)]
    todo += [(0, exchange)]
    todo += [(last[1] + PLAN[2], lambda: gathered(1))]
    todo += [(0, functools.partial(value, *block)) for block in column_blocks(vals.shape[2])]
    todo += [(0, send_values), (0, carries)]
    todo += [(0, functools.partial(out, t, t + 1)) for t in range(tiles)]
    todo += [(0, bias), (last[2] + PLAN[3], lambda: gathered(2))]
    todo += [(0, functools.partial(base_out, *base_blocks[0])), (0, send_keys)]
    todo += [(0, functools.partial(base_out, *block)) for block in base_blocks[1:]]
    todo += [(0, keys_here)]
    todo += [(0, functools.partial(attend, part)) for part in range(rows // QB)]
    interleave(steps, todo, PLAN[6])
    finish()
    wait(1)


def interleave(steps, todo, most):
    todo = list(todo)
    done = set()

    def run():
        first, piece, name = (todo.pop(0) + (None,))[:3]
        piece()
        done.add(name)

    for number, step in enumerate(steps):
        step, needs = step if isinstance(step, tuple) else (step, None)
        while needs is not None and needs not in done:
            run()
        step()
        for i in range(most):
            if todo and todo[0][0] <= number:
                run()
    while todo:
        run()


PLAN = (1, 12, 1, 1, 0, 9, 1)


def forward_all(lay, H, tokens, cotangent, shards, query_gain, query_bias, key_gain, relative):
    count = len(shards)
    chunks = chunks_of([shard.shape for shard in shards], shards[0].shape[0] * LIMIT)
    micro, items, rows, width = tokens.shape
    per = (lay.Z - 1) + 2 * (lay.X - 1 + lay.Y - 1) + 1 + 2 * (lay.X - 1 + lay.Y - 1)
    blocks = jax.ShapeDtypeStruct((lay.BL, rows, width), BF16)
    fulls = [
        jax.ShapeDtypeStruct((lay.Y, 2, lay.Z, lay.X) + shard.shape, shard.dtype)
        for shard in shards
    ]
    T, R = width // LANES, lay.BL * rows
    state = (T, H, SEG, LANES)
    outs = [blocks, blocks] + fulls
    outs += [
        jax.ShapeDtypeStruct((R, width), BF16),
        jax.ShapeDtypeStruct((T, R, LANES), F32),
        jax.ShapeDtypeStruct(state, F32),
        jax.ShapeDtypeStruct(state, F32),
        jax.ShapeDtypeStruct((T, 3 * H, LANES), F32),
        jax.ShapeDtypeStruct((T, LANES, LANES), F32),
    ]
    V, cols, zw, G = shards[1].shape[1], shards[2].shape[1], query_gain.shape[1], lay.G
    outs += [
        jax.ShapeDtypeStruct((R, V), F32),
        jax.ShapeDtypeStruct((R, cols), F32),
        jax.ShapeDtypeStruct((R, zw), BF16),
        jax.ShapeDtypeStruct((G, R, zw), BF16),
        jax.ShapeDtypeStruct((G, R, V), BF16),
        jax.ShapeDtypeStruct((G, R, R), BF16),
        jax.ShapeDtypeStruct((R, V), F32),
        jax.ShapeDtypeStruct((R, zw), F32),
    ]

    def body(*refs):
        forward_kernel(lay, count, chunks, H, refs)

    result = pl.pallas_call(
        body,
        out_shape=outs,
        in_specs=[ANY] * (2 + count) + [VM] * 3 + [SM],
        out_specs=[VM] + [ANY] * (1 + count) + [VM] * 14,
        scratch_shapes=[
            pltpu.SemaphoreType.DMA((len(chunks) * per,)),
            pltpu.SemaphoreType.DMA((len(chunks) * per,)),
            pltpu.SemaphoreType.DMA((len(chunks),)),
            pltpu.SemaphoreType.DMA((2, lay.MS)),
            pltpu.SemaphoreType.DMA((2, lay.BL)),
            pltpu.SemaphoreType.DMA((2,)),
            pltpu.VMEM((T, R, LANES), F32),
            pltpu.VMEM(fulls[0].shape, fulls[0].dtype),
            pltpu.VMEM((width, LANES), F32),
            pltpu.VMEM(state, F32),
            pltpu.VMEM(state, F32),
            pltpu.VMEM((T, 2 * H, LANES), F32),
            pltpu.VMEM((lay.G - 1, T, 2 * H, LANES), F32),
            pltpu.VMEM((T, 2 * H, LANES), F32),
            pltpu.VMEM((lay.Y, 2, lay.Z, lay.X, shards[1].shape[0], 768), BF16),
            pltpu.VMEM((QB, (G + 1) * R), F32),
            pltpu.VMEM((QB, G * R), F32),
            pltpu.SemaphoreType.DMA,
            pltpu.SemaphoreType.DMA((3, lay.G - 1)),
            pltpu.SemaphoreType.DMA((3, lay.G - 1)),
        ],
        compiler_params=pltpu.CompilerParams(
            collective_id=0, has_side_effects=True, vmem_limit_bytes=58 * 2**20
        ),
        name="forward_all",
    )(tokens, cotangent, *shards, query_gain, query_bias, key_gain, relative)
    return result[0], result[1], result[2 : 2 + count], result[2 + count :]


def add_blocks(total, index, extra, extra_index, counts, width_at):
    size = int(np.prod(counts)) if counts else 1

    def one(i, carry):
        places = []
        for extent in reversed(counts):
            places.insert(0, i % extent)
            i = i // extent
        a, e = index(*places), extra_index(*places)
        total[a] = total[a] + extra[e]
        return carry

    lax.fori_loop(0, size, one, 0)


def scatter_kernel(lay, H, NB, chunks, ins, outs, scratch):
    (
        grads, x_low, d_in, d_att, delta, queries, keys, vals, probs, z_pre, gains_small, mixed, ema,
        base_rest, value_pre, w_base, w_value, pre, gains, table, turned, si, ri, block_out,
    ) = ins
    results, small_out, outs_to, made, dvo, dvi = outs
    bufs, own = scratch[: 6 * len(chunks)], scratch[6 * len(chunks) :]
    small_acc, small_recv, send, recv, local, t_send, t_recv, t_local = own[:8]
    xt, dt, sums, flat, split, l_end, mine, inbox, inc, gx, c_send, c_recv = own[8:20]
    dx = xt
    stage, vstage, bstage, pstage, ds, strip, dq, dko, dki, zlow, mixed_acc, x_acc, load = own[20:33]
    gstage, mixed_t, loads = own[33:36]
    halves = own[36:]
    grads = grads + made + (split,)
    y, c, z, x, b = lay.here()
    X, Y, Z = lay.X, lay.Y, lay.Z
    greet(lay)
    wire = Wire(lay, send, recv)
    begin, wait = reshard_out(lay, (block_out, gx), outs_to, t_send, t_recv, t_local)
    total = len(chunks)
    arrived = [dict() for i in range(total)]

    def buf(i, name):
        return bufs[6 * i + ("acc", "x0", "y1", "y0", "x1", "z").index(name)]

    def parts(i):
        n, at, width = chunks[i]
        left = half_columns(width)
        result = [(0, left)]
        if left < width:
            result.append((left, width - left))
        return result

    def own_half(i):
        n, at, width = chunks[i]
        if n == len(grads) - 1:
            return None
        source = grads[n].at[:, c, :, :, :, pl.ds(at, width)]
        return pltpu.make_async_copy(source, half_of(i), local.at[i])

    def half_of(i):
        n, at, width = chunks[i]
        r = grads[n].shape[4]
        room = [h for h in halves if h.shape[4] == r][0]
        return room.at[i % 2, :, :, :, :, pl.ds(0, width)]

    def prefetch_half(i):
        near = own_half(i) if i < total else None
        if near is not None:
            near.start()

    def stage_core(i):
        n, at, width = chunks[i]
        if n_base <= n < n_base + 2:
            settle()
        if i == 0:
            prefetch_half(0)
        arrived[i]["core"] = wire.start(
            grads[n].at[:, 1 - c, :, :, :, pl.ds(at, width)],
            buf(i, "acc"),
            wire.to(y, 1 - c, z, x),
        )

    def stage_one(i):
        n, first, columns = chunks[i]
        acc = buf(i, "acc")
        near = own_half(i)
        if near is not None:
            near.wait()
        arrived[i]["core"].wait_recv()
        if near is not None:
            mine_half = half_of(i)
            add_blocks(acc, lambda *p: p, mine_half, lambda *p: p, (Y, Z, X), None)
        else:
            add_blocks(
                acc, lambda *p: p, split, lambda p, q, s: (p, c, q, s), (Y, Z, X), None
            )
        prefetch_half(i + 1)
        for half, (at, width) in enumerate(parts(i)):
            cols = pl.ds(at, width)
            if half == 0:
                arrived[i]["x0"] = [
                    wire.start(
                        acc.at[:, :, (x + k) % X, :, cols],
                        buf(i, "x0").at[k - 1],
                        wire.to(y, c, z, (x + k) % X),
                    )
                    for k in range(1, X)
                ]
            else:
                arrived[i]["y1"] = [
                    wire.start(
                        acc.at[(y + k) % Y, :, :, :, cols],
                        buf(i, "y1").at[k - 1],
                        wire.to((y + k) % Y, c, z, x),
                    )
                    for k in range(1, Y)
                ]

    def stage_two(i):
        acc = buf(i, "acc")
        for half, (at, width) in enumerate(parts(i)):
            cols = slice(at, at + width)
            view = pl.ds(at, width)
            if half == 0:
                for k, copy in enumerate(arrived[i]["x0"]):
                    copy.wait_recv()
                    add_blocks(
                        acc,
                        lambda p, q: (p, q, x, slice(None), cols),
                        buf(i, "x0"),
                        lambda p, q: (k, p, q),
                        (Y, Z),
                        None,
                    )
                arrived[i]["y0"] = [
                    wire.start(
                        acc.at[(y + k) % Y, :, x, :, view],
                        buf(i, "y0").at[k - 1],
                        wire.to((y + k) % Y, c, z, x),
                    )
                    for k in range(1, Y)
                ]
            else:
                for k, copy in enumerate(arrived[i]["y1"]):
                    copy.wait_recv()
                    add_blocks(
                        acc,
                        lambda p, q: (y, p, q, slice(None), cols),
                        buf(i, "y1"),
                        lambda p, q: (k, p, q),
                        (Z, X),
                        None,
                    )
                arrived[i]["x1"] = [
                    wire.start(
                        acc.at[y, :, (x + k) % X, :, view],
                        buf(i, "x1").at[k - 1],
                        wire.to(y, c, z, (x + k) % X),
                    )
                    for k in range(1, X)
                ]

    def stage_three(i):
        acc = buf(i, "acc")
        for half, (at, width) in enumerate(parts(i)):
            cols = slice(at, at + width)
            name = "y0" if half == 0 else "x1"
            for k, copy in enumerate(arrived[i][name]):
                copy.wait_recv()
                add_blocks(
                    acc,
                    lambda p: (y, p, x, slice(None), cols),
                    buf(i, name),
                    lambda p: (k, p),
                    (Z,),
                    None,
                )
        arrived[i]["z"] = [
            wire.start(
                acc.at[y, (z + k) % Z, x], buf(i, "z").at[k - 1], wire.to(y, c, (z + k) % Z, x)
            )
            for k in range(1, Z)
        ]

    def stage_four(i):
        n, at, width = chunks[i]
        total = buf(i, "acc")[y, z, x].astype(F32)
        for k, copy in enumerate(arrived[i]["z"]):
            copy.wait_recv()
            total = total + buf(i, "z")[k].astype(F32)
        results[n][:, pl.ds(at, width)] = total

    small_at = [0]

    small_open = []

    def small_begin(moves):
        for target in moves:
            slot = small_at[0]
            small_at[0] += 1
            small_open.append((slot, wire.start(small_acc, small_recv.at[slot], target)))

    def small_end():
        for slot, copy in small_open:
            copy.wait_send()
            wire.sent = [other for other in wire.sent if other is not copy]
        for slot, copy in small_open:
            copy.wait_recv()
            small_acc[...] += small_recv[slot]
        small_open.clear()

    rows, tiles = xt.shape[1], xt.shape[0]
    per_block = rows // lay.BL
    copies, g = group_copies(lay, c_send.at[0], c_recv.at[0], mine, inbox, False)
    G, zw = lay.G, queries.shape[1]
    D = x_low.shape[2]
    scale = zw ** (-0.5)
    n_base, n_value = len(grads) - 3, len(grads) - 2
    q_at = b // lay.Cq

    def back_copy(k, source, target, kind):
        t = (g + G - k) % G
        return pltpu.make_async_remote_copy(
            src_ref=source,
            dst_ref=target,
            send_sem=c_send.at[kind, k - 1],
            recv_sem=c_recv.at[kind, k - 1],
            device_id=(y * 2 + t % 2, q_at * lay.Cq + t // 2),
            device_id_type=MESH,
        )

    key_copies = [back_copy(k, dko.at[k - 1], dki.at[k - 1], 1) for k in range(1, G)]
    val_copies = [back_copy(k, dvo.at[k - 1], dvi.at[k - 1], 2) for k in range(1, G)]

    def fetch(source, target):
        copy = pltpu.make_async_copy(source, target, load)
        copy.start()
        copy.wait()

    storing = []

    def settle():
        while storing:
            storing.pop().wait()

    def keep_grad(n, at, grad):
        columns = grad.shape[1]
        r = made[n].shape[4]
        low = grad.astype(BF16).reshape(Y, 2, Z, X, r, columns)
        settle()
        gstage[:, :, :, :, :, :columns] = low
        copy = pltpu.make_async_copy(
            gstage.at[:, :, :, :, :, pl.ds(0, columns)],
            made[n].at[:, :, :, :, :, pl.ds(at, columns)],
            loads.at[0],
        )
        copy.start()
        storing.append(copy)

    all_base, all_value = column_blocks(w_base.shape[5]), column_blocks(w_value.shape[5])
    weight_order = [(w_base,) + block for block in all_base[1:] + all_base[:1]]
    weight_order += [(w_value,) + block for block in all_value]
    coming = {}

    def weight_copy(number):
        full, at, columns = weight_order[number]
        return pltpu.make_async_copy(
            full.at[:, :, :, :, :, pl.ds(at, columns)],
            stage.at[:, :, :, :, :, pl.ds(0, columns)],
            loads.at[1],
        )

    def next_weight(number):
        if number < len(weight_order):
            coming["weight"] = weight_copy(number)
            coming["weight"].start()

    def rest_copy(number):
        full, at, columns = weight_order[number]
        if at == 0:
            return pltpu.make_async_copy(
                base_rest.at[:, pl.ds(0, columns - zw)],
                bstage.at[:, pl.ds(zw, columns - zw)],
                loads.at[2],
            )
        return pltpu.make_async_copy(
            base_rest.at[:, pl.ds(at - zw, columns)], bstage.at[:, pl.ds(0, columns)], loads.at[2]
        )

    def next_rest(number):
        if number < len(all_base):
            coming["rest"] = rest_copy(number)
            coming["rest"].start()

    def next_pre(number):
        if number < len(all_value):
            at, columns = all_value[number]
            coming["pre"] = pltpu.make_async_copy(
                value_pre.at[:, pl.ds(at, columns)], pstage.at[:, pl.ds(0, columns)], loads.at[3]
            )
            coming["pre"].start()

    def begin_fetch():
        next_weight(0)
        next_rest(0)
        next_pre(0)
        coming["x"] = pltpu.make_async_copy(pre, x_acc, loads.at[4])
        coming["x"].start()
        mixed_t[...] = mixed[...].astype(F32).T.astype(BF16)

    def weight_here(columns):
        coming["weight"].wait()
        return stage[:, :, :, :, :, 0:columns].reshape(-1, columns)

    def base_block(number):
        full, at, columns = weight_order[number]
        coming["rest"].wait()
        if at == 0:
            bstage[:, :zw] = zlow[...]
        low = bstage[:, :columns]
        keep_grad(0, at, mm(mixed_t[...], low))
        part = mm_t(low, weight_here(columns))
        mixed_acc[...] = part if number == 0 else mixed_acc[...] + part
        next_weight(number + 1)
        next_rest(number + 1)

    def load_values(k):
        fetch(vals.at[k], vstage)
        if k == G - 1:
            strip[...] = jnp.zeros(strip.shape, F32)

    def scores_back(k, i):
        at = i * QB
        here = pl.ds(at, QB)
        owner = lax.rem(g - k + G, G)
        dw = mm_t(d_att[here, :], vstage[...])
        p = probs[k, here, :].astype(F32)
        grad = p * (dw - delta[here, :])
        off = jnp.clip(G * rows - rows * (g - owner) - at, 0, G * rows)
        strip[:, pl.ds(pl.multiple_of(off, LANES), rows)] += grad
        low = grad.astype(BF16)
        ds[here, :] = low
        part = mm(low, keys[k]) * scale
        dq[here, :] = part if k == G - 1 else dq[here, :] + part

    def keys_back(k):
        grad = dot_t(ds[...], queries[...]) * scale
        if k:
            dko[k - 1] = grad.astype(BF16)
            key_copies[k - 1].start()
        else:
            for copy in key_copies:
                copy.wait()
            for j in range(1, G):
                grad = grad + dki[j - 1].astype(F32)
            pre_z = z_pre[...]
            gate = jax.nn.sigmoid(pre_z)
            shared = pre_z * gate
            small_acc[0:1, :] = jnp.sum(dq[...] * shared, axis=0, keepdims=True)
            small_acc[1:2, :] = jnp.sum(dq[...], axis=0, keepdims=True)
            small_acc[2:3, :] = jnp.sum(grad * shared, axis=0, keepdims=True)
            d_shared = dq[...] * gains_small[0:1, :] + grad * gains_small[1:2, :]
            zlow[...] = (d_shared * (gate * (1.0 + pre_z * (1.0 - gate)))).astype(BF16)

    def values_back(k):
        for at, columns in column_blocks(vstage.shape[1]):
            vstage[:, at : at + columns] = dot_t(
                probs[k], d_att[:, at : at + columns]
            ).astype(BF16)
        fetch(vstage, dvo.at[k - 1])
        val_copies[k - 1].start()

    def buckets():
        sums_of = bucket_sums(G * rows, NB, strip)
        lane = lax.broadcasted_iota(jnp.int32, (1, LANES), 1)
        line = jnp.zeros((1, LANES), F32)
        for k in range(NB):
            line = jnp.where(lane == k, jnp.sum(sums_of[k], axis=1, keepdims=True), line)
        small_acc[3:4, :] = line
        small_acc[4:8, :] = jnp.zeros((4, LANES), F32)

    def values_here():
        for copy in val_copies:
            copy.wait()

    def value_block(number):
        full, at, columns = weight_order[len(all_base) + number]
        cols = pl.ds(at, columns)
        if number == 0:
            mixed_t[...] = x_low[...].reshape(rows, D).astype(F32).T.astype(BF16)
            coming["x"].wait()
        grad = dot_t(probs[0], d_att[:, at : at + columns])
        for k in range(1, G):
            fetch(dvi.at[k - 1, :, cols], bstage.at[:, pl.ds(0, columns)])
            grad = grad + bstage[:, :columns].astype(F32)
        coming["pre"].wait()
        v = pstage[:, :columns]
        gate = jax.nn.sigmoid(v)
        low = (grad * (gate * (1.0 + v * (1.0 - gate)))).astype(BF16)
        next_pre(number + 1)
        keep_grad(1, at, mm(mixed_t[...], low))
        x_acc[...] += mm_t(low, weight_here(columns))
        next_weight(len(all_base) + number + 1)

    def d_ema(t):
        v = ema[t]
        gate = jax.nn.sigmoid(v)
        dt[t] = mixed_acc[:, t * LANES : (t + 1) * LANES] * (gate * (1.0 + v * (1.0 - gate)))

    def tile_x():
        for j in range(lay.BL):
            to_tiles(x_low[j], xt, j * per_block, per_block)

    def ends(t):
        ema_back_ends_kernel(H, dt.at[t], table.at[t], l_end.at[t])
        for h in range(H):
            mine[t, pl.ds(h, 1), :] = l_end[t, h, 0:1, :]

    def exchange():
        for copy in copies:
            copy.start()

    def carries():
        for copy in copies:
            copy.wait()
        for t in range(tiles):
            carry_in(lay, H, rows, g, inbox, table, inc, t, True)

    def correlate(t):
        ema_sums_kernel(H, xt.at[t], dt.at[t], table.at[t], si.at[t], ri.at[t], sums.at[t])

    def back(t):
        ema_back_kernel(
            H, dt.at[t], table.at[t], turned.at[t, pl.ds(4 * H, 1)], l_end.at[t], inc.at[t], dx.at[t]
        )
        cols = slice(t * LANES, (t + 1) * LANES)
        for j in range(lay.BL):
            at = pl.ds(j * per_block, per_block)
            gx[j, :, cols] = (x_acc[at, cols] + dx[t, at, :]).astype(BF16)

    def share_sums():
        r = split.shape[4]
        for t in range(tiles):
            sums[t, pl.ds(2 * H + 1, 2), :] = gains[0:2, t * LANES : (t + 1) * LANES]
            flat[t * LANES : (t + 1) * LANES, :] = sums[t].T

        def one(i, carry):
            split[i // (2 * Z * X), i // (Z * X) % 2, i // X % Z, i % X] = flat[pl.ds(i * r, r), :]
            return carry

        lax.fori_loop(0, 2 * X * Y * Z, one, 0)

    sums[...] = jnp.zeros(sums.shape, F32)
    xs = [wire.to(y, c, z, (x + k) % X) for k in range(1, X)]
    ys = [wire.to((y + k) % Y, c, z, x) for k in range(1, Y)]
    zs = [wire.to(y, c, (z + k) % Z, x) for k in range(1, Z)]

    run = functools.partial
    todo = [(0, begin_fetch)]
    for number in range(len(all_base) - 1):
        todo.append((0, run(base_block, number), (n_base, weight_order[number][1])))
    for k in list(range(1, G))[::-1] + [0]:
        todo.append((0, run(load_values, k)))
        todo += [(0, run(scores_back, k, i)) for i in range(rows // QB)]
        todo.append((0, run(keys_back, k)))
        if k:
            todo.append((0, run(values_back, k)))
    todo.append((0, buckets, "small"))
    todo.append((0, run(base_block, len(all_base) - 1), (n_base, 0)))
    todo += [(0, run(d_ema, t)) for t in range(tiles)]
    todo += [(0, run(ends, t)) for t in range(tiles)]
    todo += [(0, exchange), (0, values_here)]
    for number, block in enumerate(all_value):
        todo.append((0, run(value_block, number), (n_value, block[0])))
    todo.append((0, carries))
    todo += [(0, run(back, t)) for t in range(tiles)]
    todo += [(0, lambda: begin(1)), (0, tile_x)]
    todo += [(0, run(correlate, t)) for t in range(tiles)]
    todo.append((0, share_sums, (len(grads) - 1, 0)))

    def needs(i):
        n, at, width = chunks[i]
        return (n, at) if n >= n_base else None

    steps = []
    for i in range(min(LEAD, total)):
        steps.append((run(stage_core, i), needs(i)))
    steps.append(lambda: begin(0))
    for turn in range(total + 3 * BLAG):
        for what, lag in ((stage_four, 3), (stage_three, 2), (stage_two, 1), (stage_one, 0)):
            if 0 <= turn - lag * BLAG < total:
                steps.append(run(what, turn - lag * BLAG))
        if turn + LEAD < total:
            steps.append((run(stage_core, turn + LEAD), needs(turn + LEAD)))
        hop = turn - (total - 4)
        moves = ([wire.to(y, 1 - c, z, x)], xs, ys, zs)
        if 1 <= hop <= len(moves):
            steps.append(small_end)
        if 0 <= hop < len(moves):
            steps.append((run(small_begin, moves[hop]), "small"))
    interleave(steps, todo, MOST)
    small_out[...] = small_acc[...]
    wait(0)
    wait(1)
    wire.finish()


LEAD = 2
MOST = 1
BLAG = 3


def dot_t(a, b):
    return lax.dot_general(a, b, (((0,), (0,)), ((), ())), preferred_element_type=F32)


def bucket_sums(length, bucket_count, strip):
    edges = bucket_edges(bucket_count)
    lag0 = lax.broadcasted_iota(jnp.int32, (QB, LANES), 0) - lax.broadcasted_iota(
        jnp.int32, (QB, LANES), 1
    )
    totals = [jnp.zeros((1, LANES), F32) for k in range(bucket_count)]
    for t in range((length + QB) // LANES):
        base = length - t * LANES
        low, high = base - LANES + 1, base + QB - 1
        if high < 0:
            continue
        value = strip[:, t * LANES : (t + 1) * LANES]
        for k in range(bucket_count):
            top = edges[k + 1] if k + 1 < bucket_count else length
            if edges[k] <= high and top > low:
                lag = lag0 + base
                inside = (lag >= edges[k]) & (lag < top)
                totals[k] = totals[k] + jnp.sum(jnp.where(inside, value, 0.0), axis=0, keepdims=True)
    return totals


def backward_all(lay, H, NB, grads, fulls, values, share):
    X, Y, Z, G = lay.X, lay.Y, lay.Z, lay.G
    R, V = values["d_att"].shape
    D = values["pre"].shape[1]
    T, zw = D // LANES, values["queries"].shape[1]
    rows = R // lay.BL
    micro = lay.MS // lay.items
    shapes = [grad.shape[-2:] for grad in grads] + [full.shape[-2:] for full in fulls] + [(share, LANES)]
    kinds = [grad.dtype for grad in grads] + [BF16, BF16, F32]
    known = len(grads)
    chunks = chunks_of([shape for shape in shapes[:known]], share * LIMIT)
    base_blocks = column_blocks(shapes[known][1])
    chunks += [(known,) + block for block in base_blocks[1:]]
    chunks += [(known,) + base_blocks[0]]
    chunks += [(known + 1,) + block for block in column_blocks(shapes[known + 1][1])]
    chunks += [(known + 2, 0, LANES)]
    scratch = []
    for n, at, cols in chunks:
        r = shapes[n][0]
        left = half_columns(cols)
        right = cols - left if cols > left else LANES
        kind = kinds[n]
        scratch += [
            pltpu.VMEM((Y, Z, X, r, cols), kind),
            pltpu.VMEM((X - 1, Y, Z, r, left), kind),
            pltpu.VMEM((Y - 1, Z, X, r, right), kind),
            pltpu.VMEM((Y - 1, Z, r, left), kind),
            pltpu.VMEM((X - 1, Z, r, right), kind),
            pltpu.VMEM((Z - 1, r, cols), kind),
        ]
    hops = 1 + (X - 1) + (Y - 1) + (Z - 1)
    per = 1 + 2 * (X - 1 + Y - 1) + Z - 1
    small = (8, LANES)
    outs = [jax.ShapeDtypeStruct(shape, F32) for shape in shapes]
    outs.append(jax.ShapeDtypeStruct(small, F32))
    outs += [jax.ShapeDtypeStruct((micro, lay.items, rows, D), BF16)] * 2
    outs += [jax.ShapeDtypeStruct(full.shape, BF16) for full in fulls]
    outs += [jax.ShapeDtypeStruct((G - 1, R, V), BF16)] * 2
    scratch += [pltpu.VMEM(small, F32), pltpu.VMEM((hops,) + small, F32)]
    heights = sorted({shapes[n][0] for n, at, width in chunks})
    widest = {r: max(w for n, at, w in chunks if shapes[n][0] == r) for r in heights}
    scratch += [
        pltpu.SemaphoreType.DMA((len(chunks) * per + hops,)),
        pltpu.SemaphoreType.DMA((len(chunks) * per + hops,)),
        pltpu.SemaphoreType.DMA((len(chunks),)),
        pltpu.SemaphoreType.DMA((2, lay.BL)),
        pltpu.SemaphoreType.DMA((2, lay.MS)),
        pltpu.SemaphoreType.DMA((2,)),
        pltpu.VMEM((T, R, LANES), F32),
        pltpu.VMEM((T, R, LANES), F32),
        pltpu.VMEM((T, LANES, LANES), F32),
        pltpu.VMEM((D, LANES), F32),
        pltpu.VMEM((Y, 2, Z, X, share, LANES), F32),
        pltpu.VMEM((T, H, SEG, LANES), F32),
        pltpu.VMEM((T, H, LANES), F32),
        pltpu.VMEM((G - 1, T, H, LANES), F32),
        pltpu.VMEM((T, H, LANES), F32),
        pltpu.VMEM((lay.BL, rows, D), BF16),
        pltpu.SemaphoreType.DMA((3, G - 1)),
        pltpu.SemaphoreType.DMA((3, G - 1)),
        pltpu.VMEM((Y, 2, Z, X, share, 768), BF16),
        pltpu.VMEM((R, V), BF16),
        pltpu.VMEM((R, 768), BF16),
        pltpu.VMEM((R, 768), F32),
        pltpu.VMEM((R, R), BF16),
        pltpu.VMEM((QB, (G + 1) * R), F32),
        pltpu.VMEM((R, zw), F32),
        pltpu.VMEM((G - 1, R, zw), BF16),
        pltpu.VMEM((G - 1, R, zw), BF16),
        pltpu.VMEM((R, zw), BF16),
        pltpu.VMEM((R, D), F32),
        pltpu.VMEM((R, D), F32),
        pltpu.SemaphoreType.DMA,
        pltpu.VMEM((Y, 2, Z, X, share, 768), BF16),
        pltpu.VMEM((D, R), BF16),
        pltpu.SemaphoreType.DMA((5,)),
    ]
    scratch += [pltpu.VMEM((2, Y, Z, X, r, widest[r]), BF16) for r in heights]
    order = (
        ("x_blocks", VM), ("d_in", ANY), ("d_att", VM), ("delta", VM), ("queries", VM), ("keys", VM),
        ("vals", ANY), ("probs", VM), ("z_pre", VM), ("gains_small", VM), ("mixed", VM), ("ema", VM),
        ("base_rest", ANY), ("value_pre", ANY), ("w_base", ANY), ("w_value", ANY), ("pre", ANY),
        ("gains", VM), ("table", VM), ("turned", VM), ("si", VM), ("ri", VM), ("block_out", ANY),
    )
    values = dict(values, w_base=fulls[0], w_value=fulls[1])
    order = tuple(item for item in order if item[0] != "d_in")

    def body(*refs):
        named = refs[known : known + len(order)]
        ins = (tuple(refs[:known]), named[0], None) + tuple(named[1:])
        rest = refs[known + len(order) :]
        results, small_out, moved = rest[: known + 3], rest[known + 3], rest[known + 4 : known + 6]
        made, dvo, dvi = rest[known + 6 : known + 8], rest[known + 8], rest[known + 9]
        scatter_kernel(
            lay, H, NB, chunks, ins, (results, small_out, moved, tuple(made), dvo, dvi), rest[known + 10 :]
        )

    result = pl.pallas_call(
        body,
        out_shape=outs,
        in_specs=[ANY] * known + [spec for name, spec in order],
        out_specs=[VM] * (known + 4) + [ANY] * 6,
        scratch_shapes=scratch,
        compiler_params=pltpu.CompilerParams(
            collective_id=1, has_side_effects=True, vmem_limit_bytes=60 * 2**20
        ),
        name="backward_all",
    )(*grads, *[values[name] for name, spec in order])
    return result[: known + 3], result[known + 3], result[known + 4 : known + 6]


def row(ref, index, lanes):
    return jnp.broadcast_to(ref[pl.ds(index, 1), lanes], (SEG, LANES))


def lane_call(kernel, outs, args, name):
    def spec(a):
        lead = len(a.shape) - 1
        return pl.BlockSpec(a.shape[:-1] + (LANES,), lambda i: (0,) * lead + (i,))

    return pl.pallas_call(
        kernel,
        out_shape=outs,
        grid=(args[0].shape[-1] // LANES,),
        in_specs=[spec(a) for a in args],
        out_specs=jax.tree.map(spec, outs),
        compiler_params=pltpu.CompilerParams(vmem_limit_bytes=32 * 2**20),
        name=name,
    )(*args)


def shifted(value, by):
    where = lax.broadcasted_iota(jnp.int32, (SEG, LANES), 0)
    if by > 0:
        return jnp.where(where >= by, pltpu.roll(value, by, 0), 0.0)
    return jnp.where(where < SEG + by, pltpu.roll(value, SEG + by, 0), 0.0)


def ema_ends_kernel(H, x_ref, tab_ref, s_ref, r_ref):
    rows, width = x_ref.shape
    steps = rows // SEG

    def tile(lanes):
        decay = [row(tab_ref, h, lanes) for h in range(H)]

        def step(t, state):
            s, r = state
            xt = x_ref[pl.ds(t, SEG, stride=steps), lanes]
            r = tuple(decay[h] * r[h] + s[h] for h in range(H))
            s = tuple(decay[h] * s[h] + xt for h in range(H))
            return s, r

        zero = tuple(tab_ref[0:SEG, lanes] * 0.0 for h in range(H))
        s, r = lax.fori_loop(0, steps, step, (zero, zero))
        for h in range(H):
            log = row(tab_ref, H + h, lanes)
            sh, rh = s[h], r[h]
            for d in (1, 2, 4):
                span = d * steps
                sd, rd = shifted(sh, d), shifted(rh, d)
                power = jnp.exp(span * log)
                rh = rh + power * rd + (span * jnp.exp((span - 1) * log)) * sd
                sh = sh + power * sd
            s_ref[h, :, lanes] = sh
            r_ref[h, :, lanes] = rh

    tile(slice(None))


def ema_out_kernel(H, x_ref, tab_ref, omega_ref, s_ref, r_ref, inc_ref, ema_ref, si_ref, ri_ref):
    rows, width = x_ref.shape
    steps = rows // SEG

    def tile(lanes):
        decay = [row(tab_ref, h, lanes) for h in range(H)]
        gain = [row(tab_ref, 2 * H + h, lanes) for h in range(H)]
        omega = row(omega_ref, 0, lanes)
        start = []
        span = (lax.broadcasted_iota(jnp.int32, (SEG, LANES), 0) * steps).astype(F32)
        for h in range(H):
            log = row(tab_ref, H + h, lanes)
            s_dev = row(inc_ref, h, lanes)
            r_dev = row(inc_ref, H + h, lanes)
            power = jnp.exp(span * log)
            s_in = shifted(s_ref[h, :, lanes], 1) + power * s_dev
            r_in = (
                shifted(r_ref[h, :, lanes], 1)
                + power * r_dev
                + (span * jnp.exp((span - 1.0) * log)) * s_dev
            )
            si_ref[h, :, lanes] = s_in
            ri_ref[h, :, lanes] = r_in
            start.append(s_in)

        def step(t, s):
            xt = x_ref[pl.ds(t, SEG, stride=steps), lanes]
            s = tuple(decay[h] * s[h] + xt for h in range(H))
            parts = [gain[h] * s[h] for h in range(H)]
            while len(parts) > 1:
                parts = [parts[i] + parts[i + 1] for i in range(0, len(parts), 2)]
            ema_ref[pl.ds(t, SEG, stride=steps), lanes] = parts[0] + omega * xt
            return s

        lax.fori_loop(0, steps, step, tuple(start))

    tile(slice(None))


def ema_back_ends_kernel(H, d_ref, tab_ref, l_ref):
    rows, width = d_ref.shape
    steps = rows // SEG

    def tile(lanes):
        decay = [row(tab_ref, h, lanes) for h in range(H)]

        def step(i, lam):
            dt = d_ref[pl.ds(steps - 1 - i, SEG, stride=steps), lanes]
            return tuple(decay[h] * lam[h] + dt for h in range(H))

        zero = tuple(tab_ref[0:SEG, lanes] * 0.0 for h in range(H))
        lam = lax.fori_loop(0, steps, step, zero)
        for h in range(H):
            log = row(tab_ref, H + h, lanes)
            lh = lam[h]
            for d in (1, 2, 4):
                lh = lh + jnp.exp(d * steps * log) * shifted(lh, -d)
            l_ref[h, :, lanes] = lh

    tile(slice(None))


def ema_sums_kernel(H, x_ref, d_ref, tab_ref, si_ref, ri_ref, out_ref):
    rows, width = x_ref.shape
    steps = rows // SEG
    group = H // 2

    def tile(lanes):
        for first in range(0, H, group):
            decay = [row(tab_ref, first + h, lanes) for h in range(group)]

            def step(t, state):
                s, r, c, q, o = state
                xt = x_ref[pl.ds(t, SEG, stride=steps), lanes]
                dt = d_ref[pl.ds(t, SEG, stride=steps), lanes]
                r = tuple(decay[h] * r[h] + s[h] for h in range(group))
                s = tuple(decay[h] * s[h] + xt for h in range(group))
                c = tuple(c[h] + dt * s[h] for h in range(group))
                q = tuple(q[h] + dt * r[h] for h in range(group))
                return s, r, c, q, o + dt * xt

            zero = tuple(tab_ref[0:SEG, lanes] * 0.0 for h in range(group))
            s = tuple(si_ref[first + h, :, lanes] for h in range(group))
            r = tuple(ri_ref[first + h, :, lanes] for h in range(group))
            s, r, c, q, o = lax.fori_loop(0, steps, step, (s, r, zero, zero, zero[0]))
            for h in range(group):
                out_ref[pl.ds(first + h, 1), lanes] = jnp.sum(c[h], axis=0, keepdims=True)
                out_ref[pl.ds(H + first + h, 1), lanes] = jnp.sum(q[h], axis=0, keepdims=True)
            out_ref[pl.ds(2 * H, 1), lanes] = jnp.sum(o, axis=0, keepdims=True)

    tile(slice(None))


def ema_back_kernel(H, d_ref, tab_ref, omega_ref, l_ref, inc_ref, dx_ref):
    rows, width = d_ref.shape
    steps = rows // SEG

    def tile(lanes):
        decay = [row(tab_ref, h, lanes) for h in range(H)]
        gain = [row(tab_ref, 2 * H + h, lanes) for h in range(H)]
        omega = row(omega_ref, 0, lanes)
        start = []
        span = ((SEG - 1 - lax.broadcasted_iota(jnp.int32, (SEG, LANES), 0)) * steps).astype(F32)
        for h in range(H):
            log = row(tab_ref, H + h, lanes)
            l_dev = row(inc_ref, h, lanes)
            start.append(shifted(l_ref[h, :, lanes], -1) + jnp.exp(span * log) * l_dev)

        def step(i, lam):
            at = pl.ds(steps - 1 - i, SEG, stride=steps)
            dt = d_ref[at, lanes]
            lam = tuple(decay[h] * lam[h] + dt for h in range(H))
            parts = [gain[h] * lam[h] for h in range(H)]
            while len(parts) > 1:
                parts = [parts[i] + parts[i + 1] for i in range(0, len(parts), 2)]
            dx_ref[at, lanes] = parts[0] + omega * dt
            return lam

        lax.fori_loop(0, steps, step, tuple(start))

    tile(slice(None))


def call(kernel, outs, args, specs=None, scratch=(), vmem=58, name=None):
    return pl.pallas_call(
        kernel,
        out_shape=outs,
        in_specs=specs or [VM] * len(args),
        out_specs=jax.tree.map(lambda o: VM, outs),
        scratch_shapes=list(scratch),
        compiler_params=pltpu.CompilerParams(vmem_limit_bytes=vmem * 2**20),
        name=name,
    )(*args)


QB = 256
STRETCH = 128


def bias_kernel(length, bucket_count, bias_ref, strip_ref):
    edges = bucket_edges(bucket_count)
    tiles = length // LANES + QB // LANES
    lag0 = lax.broadcasted_iota(jnp.int32, (QB, LANES), 0) - lax.broadcasted_iota(
        jnp.int32, (QB, LANES), 1
    )
    for t in range(strip_ref.shape[1] // LANES):
        base = length - t * LANES
        low, high = base - LANES + 1, base + QB - 1
        start = max([k for k in range(bucket_count) if edges[k] <= low], default=0)
        value = jnp.full((QB, LANES), bias_ref[start], F32)
        for k in range(start + 1, bucket_count):
            if edges[k] <= high:
                value = jnp.where(lag0 + base >= edges[k], bias_ref[k], value)
        strip_ref[:, t * LANES : (t + 1) * LANES] = value


def attend_body(lay, g, far, q_ref, strip_ref, keys, vals, att_ref, probs_ref, scores, part):
    G = lay.G
    rows, zw = q_ref.shape
    length = G * rows
    r0 = lax.broadcasted_iota(jnp.int32, (QB, rows), 0)
    c0 = lax.broadcasted_iota(jnp.int32, (QB, rows), 1)

    def one(i, carry):
        at = i * QB
        q = q_ref[pl.ds(at, QB), :]
        for k in range(G):
            owner = lax.rem(g - k + G, G)
            s = mm_t(q, keys[k])
            off = jnp.clip(length - rows * (g - owner) - at, 0, length)
            s = s * (zw ** (-0.5)) + strip_ref[:, pl.ds(pl.multiple_of(off, LANES), rows)]
            if k == 0:
                pos = r0 + at
                s = jnp.where(pos // STRETCH == c0 // STRETCH, s, s + far)
                s = jnp.where(c0 <= pos, s, masked_fill)
            else:
                s = s + jnp.where(k <= g, far, masked_fill)
            scores[:, k * rows : (k + 1) * rows] = s
        s = scores[...]
        p = jnp.exp(s - jnp.max(s, axis=1, keepdims=True))
        p = p * (1.0 / jnp.sum(p, axis=1, keepdims=True))
        total = jnp.zeros((QB, att_ref.shape[1]), F32)
        for k in range(G):
            low = p[:, k * rows : (k + 1) * rows].astype(BF16)
            probs_ref[k, pl.ds(at, QB), :] = low
            total += mm(low, vals[k])
        att_ref[pl.ds(at, QB), :] = total
        return carry

    one(part, 0)


def attend_back_kernel(lay, bucket_count, flag_ref, q_ref, da_ref, delta_ref, probs_ref, *refs):
    G = lay.G
    keys, vals, dq_ref, dk_ref, dv_ref, dko_ref, dvo_ref, bucket_ref, strip, ds_ref = refs
    rows, zw = q_ref.shape
    length = G * rows
    g = flag_ref[1]
    scale = zw ** (-0.5)
    edges = bucket_edges(bucket_count)
    strip[...] = jnp.zeros(strip.shape, F32)

    def one(i, carry):
        at = pl.multiple_of(i * QB, QB)
        da = da_ref[pl.ds(at, QB), :]
        dq = jnp.zeros((QB, zw), F32)
        for k in range(G):
            owner = lax.rem(g - k + G, G)
            dw = mm_t(da, vals[k])
            p = probs_ref[k, pl.ds(at, QB), :].astype(F32)
            ds = p * (dw - delta_ref[pl.ds(at, QB), :])
            off = jnp.clip(length - rows * (g - owner) - at, 0, length)
            strip[:, pl.ds(pl.multiple_of(off, LANES), rows)] += ds
            low = ds.astype(BF16)
            dq += mm(low, keys[k])
            ds_ref[k, pl.ds(at, QB), :] = low
        dq_ref[pl.ds(at, QB), :] = dq * scale
        return carry

    lax.fori_loop(0, rows // QB, one, 0)
    for k in range(G):
        dk = lax.dot_general(
            ds_ref[k], q_ref[...], (((0,), (0,)), ((), ())), preferred_element_type=F32
        )
        dv = lax.dot_general(
            probs_ref[k], da_ref[...], (((0,), (0,)), ((), ())), preferred_element_type=F32
        )
        if k == 0:
            dk_ref[...] = dk * scale
            dv_ref[...] = dv
        else:
            dko_ref[k - 1] = (dk * scale).astype(BF16)
            dvo_ref[k - 1] = dv.astype(BF16)
    lag0 = lax.broadcasted_iota(jnp.int32, (QB, LANES), 0) - lax.broadcasted_iota(
        jnp.int32, (QB, LANES), 1
    )
    sums = [jnp.zeros((1, LANES), F32) for k in range(bucket_count)]
    for t in range((length + QB) // LANES):
        base = length - t * LANES
        low, high = base - LANES + 1, base + QB - 1
        if high < 0:
            continue
        value = strip[:, t * LANES : (t + 1) * LANES]
        for k in range(bucket_count):
            top = edges[k + 1] if k + 1 < bucket_count else length
            if edges[k] <= high and top > low:
                lag = lag0 + base
                inside = (lag >= edges[k]) & (lag < top)
                sums[k] = sums[k] + jnp.sum(jnp.where(inside, value, 0.0), axis=0, keepdims=True)
    for k in range(bucket_count):
        bucket_ref[pl.ds(k, 1), :] = sums[k]


def silu_slope(values):
    gate_value = jax.nn.sigmoid(values)
    return gate_value * (1.0 + values * (1.0 - gate_value))


def normalize(seq_rows):
    centered = seq_rows - jnp.mean(seq_rows, axis=-1, keepdims=True)
    inverse = lax.rsqrt(jnp.mean(centered * centered, axis=-1, keepdims=True) + epsilon)
    return (centered * inverse, inverse)


def normalize_back(grad_scaled, unit_rows, inverse):
    return inverse * (
        grad_scaled
        - jnp.mean(grad_scaled, axis=-1, keepdims=True)
        - unit_rows * jnp.mean(grad_scaled * unit_rows, axis=-1, keepdims=True)
    )


def mm(a, b):
    return jnp.dot(a, b, preferred_element_type=F32)


def mm_t(a, b):
    return lax.dot_general(a, b, (((1,), (1,)), ((), ())), preferred_element_type=F32)


def wgrad(a, b):
    return lax.dot_general(a, b, (((0,), (0,)), ((), ())), preferred_element_type=F32).astype(BF16)


def shards(
    lay,
    tokens,
    cotangent,
    stretch_size,
    w_value,
    w_base,
    w_out,
    w_up,
    w_down,
    ema_delta,
    ema_alpha,
    ema_beta,
    ema_gamma,
    ema_omega,
    first_gain,
    second_gain,
    query_gain,
    query_bias,
    key_gain,
    relative_bias,
):
    micro, items, seq_len, D = tokens.shape
    H = ema_delta.shape[1]
    zw = query_gain.shape[0]
    V = w_value.shape[1]
    NB = relative_bias.shape[0]
    length = seq_len * lay.S
    G = lay.G
    R = lay.BL * seq_len
    d_at, b_at = lax.axis_index("dp"), lax.axis_index("seq")
    c_at, y_at = d_at % 2, d_at // 2
    q_at = b_at // lay.Cq
    g_at = (b_at % lay.Cq) * 2 + c_at
    share = ema_delta.shape[0]

    def group_perm(k):
        pairs = []
        for y in range(lay.Y):
            for q in range(lay.Q):
                for g in range(G):
                    t = (g + k) % G
                    src = (y * 2 + g % 2) * lay.S + q * lay.Cq + g // 2
                    dst = (y * 2 + t % 2) * lay.S + q * lay.Cq + t // 2
                    pairs.append((src, dst))
        return pairs

    def shift(value, k):
        return lax.ppermute(value, ("dp", "seq"), group_perm(k % G))

    marks = jnp.broadcast_to(stretch_size.reshape(-1, 1).astype(BF16), (lay.MS, share))
    used = 4 * H + 3 + lay.MS
    pack = jnp.concatenate(
        [
            ema_delta.T,
            ema_alpha.T,
            ema_beta.T,
            ema_gamma.T,
            ema_omega[None],
            first_gain[None],
            second_gain[None],
            marks,
            jnp.zeros((LANES - used, share), BF16),
        ],
        0,
    ).T
    x_blocks, cot_blocks, fulls, rest = forward_all(
        lay, H, tokens, cotangent, (pack, w_value, w_base, w_out, w_up, w_down),
        query_gain[None], query_bias[None], key_gain[None], relative_bias,
    )
    mixed, ema_tiles, s_in, r_in, table, turned = rest[:6]
    value_pre, base, queries, keys_all, vals_all, probs, attended, z_pre = rest[6:]
    flags = jnp.stack([g_at, g_at])
    mats = [full.reshape(-1, full.shape[-1]) for full in fulls[1:]]
    mat_value, mat_base, mat_out, mat_up, mat_down = mats
    gain_first = turned[:, 4 * H + 1].reshape(D)
    gain_second = turned[:, 4 * H + 2].reshape(D)

    x_low = x_blocks.reshape(R, D)
    x = x_low.astype(F32)
    grad_out = cot_blocks.reshape(R, D).astype(F32)

    reset_pre = base[:, zw : zw + V]
    cand_pre = base[:, zw + V : zw + V + D]
    update_pre = base[:, zw + V + D :]
    reset_gate = jax.nn.silu(reset_pre)
    update = jax.nn.sigmoid(update_pre)
    gated = (attended * reset_gate).astype(BF16)
    cand_in = cand_pre + mm(gated, mat_out)
    candidate = jax.nn.silu(cand_in)
    first_sum = x + update * (candidate - x)
    unit_first, inverse_first = normalize(first_sum)
    normed = unit_first * gain_first
    normed_low = normed.astype(BF16)
    hidden_pre = mm(normed_low, mat_up)
    hidden = jax.nn.silu(hidden_pre).astype(BF16)
    second_sum = normed + mm(hidden, mat_down)
    unit_second, inverse_second = normalize(second_sum)
    block_out = (unit_second * gain_second).astype(BF16)

    grad_gain_second = jnp.sum(grad_out * unit_second, axis=0)
    grad_second = normalize_back(grad_out * gain_second, unit_second, inverse_second)
    branch = grad_second.astype(BF16)
    grad_mat_down = wgrad(hidden, branch)
    hidden_grad = (mm_t(branch, mat_down) * silu_slope(hidden_pre)).astype(BF16)
    grad_mat_up = wgrad(normed_low, hidden_grad)
    grad_normed = grad_second + mm_t(hidden_grad, mat_up)
    grad_gain_first = jnp.sum(grad_normed * unit_first, axis=0)
    grad_first = normalize_back(grad_normed * gain_first, unit_first, inverse_first)
    cand_low = (grad_first * update * silu_slope(cand_in)).astype(BF16)
    grad_mat_out = wgrad(gated, cand_low)
    grad_gated = mm_t(cand_low, mat_out)
    att_low = (grad_gated * reset_gate).astype(BF16)
    grad_reset = grad_gated * attended * silu_slope(reset_pre)
    grad_update = grad_first * (candidate - x) * update * (1.0 - update)
    delta = jnp.sum(att_low.astype(F32) * attended, axis=1, keepdims=True)
    base_rest = jnp.concatenate(
        [grad_reset.astype(BF16), cand_low, grad_update.astype(BF16)], 1
    )
    pre = grad_first * (1.0 - update)
    gains = jnp.concatenate(
        [grad_gain_first[None], grad_gain_second[None], jnp.zeros((6, D), F32)]
    )
    shape = (lay.Y, 2, lay.Z, lay.X)

    def split(grad):
        return grad.reshape(shape + (-1, grad.shape[-1]))

    reduced, small_total, moved = backward_all(
        lay,
        H,
        NB,
        [split(grad_mat_down), split(grad_mat_up), split(grad_mat_out)],
        [fulls[2], fulls[1]],
        dict(
            x_blocks=x_blocks, d_att=att_low, delta=delta, queries=queries, keys=keys_all,
            vals=vals_all, probs=probs, z_pre=z_pre,
            gains_small=jnp.concatenate([query_gain[None], key_gain[None], jnp.zeros((6, zw), F32)]),
            mixed=mixed, ema=ema_tiles, base_rest=base_rest, value_pre=value_pre, pre=pre, gains=gains,
            table=table, turned=turned, si=s_in, ri=r_in,
            block_out=block_out.reshape(lay.BL, seq_len, D),
        ),
        share,
    )
    own = reduced[5].T
    corr, lagged = own[:H], own[H : 2 * H]
    p = jax.nn.sigmoid(ema_delta.T.astype(F32))
    a = jax.nn.sigmoid(ema_alpha.T.astype(F32))
    beta = ema_beta.T.astype(F32)
    read = ema_gamma.T.astype(F32) * (H ** (-0.5))
    q_grad = read * p * beta * lagged
    return (
        moved[0],
        moved[1].astype(F32),
        reduced[4],
        reduced[3],
        reduced[2],
        reduced[1],
        reduced[0],
        ((read * beta * corr - a * q_grad) * p * (1.0 - p)).T,
        (-p * q_grad * a * (1.0 - a)).T,
        (p * read * corr).T,
        (p * beta * corr * (H ** (-0.5))).T,
        own[2 * H],
        own[2 * H + 1],
        own[2 * H + 2],
        small_total[0, :zw],
        small_total[1, :zw],
        small_total[2, :zw],
        small_total[3, :NB],
    )


def solution(mesh):
    rows = P(None, "dp", "seq", None)
    part2, part1 = P(("dp", "seq"), None), P(("dp", "seq"))
    in_specs = (rows, rows, P(None, "dp")) + (part2,) * 9 + (part1,) * 3 + (P(),) * 4
    out_specs = (rows, rows) + (part2,) * 9 + (part1,) * 3 + (P(),) * 4

    def whole(tokens, *rest):
        micro, seqs = tokens.shape[:2]
        lay = Layout(mesh.shape["dp"], mesh.shape["seq"], micro, seqs // mesh.shape["dp"])
        return jax.shard_map(
            functools.partial(shards, lay),
            mesh=mesh,
            in_specs=in_specs,
            out_specs=out_specs,
            check_vma=False,
        )(tokens, *rest)

    return whole
```
